256 devices in a mesh: lon: 8 (over x, y_lo), lat: 32 (over y_hi, z, core).
Axes of the slice: x: 4, y: 4 (y_hi: 2, y_lo: 2; y = y_hi * 2 + y_lo), z: 8, core: 2. Of those that a mesh axis runs over, the one named last changes fastest.
Arguments:
- queries: bfloat16 [2, 64, 256, 2048], P(None, 'lat', 'lon'), may hold values from -4.5 to 4.5
- key_states: bfloat16 [2, 64, 256, 2048], P(None, 'lat', 'lon'), may hold values from -4.5 to 4.5
- value_states: bfloat16 [2, 64, 256, 2048], P(None, 'lat', 'lon'), may hold values from -6 to 6
- out_grad: bfloat16 [2, 64, 256, 2048], P(None, 'lat', 'lon'), may hold values from -6 to 6
- block_lists: int32 [32, 3], replicated, may hold values from -1 to 31, as said below
- row_widths: int32 [64], replicated, may hold values from 1 to 8, as said below
Outputs:
- attended: bfloat16 [2, 64, 256, 2048], P(None, 'lat', 'lon')
- query_grad: bfloat16 [2, 64, 256, 2048], P(None, 'lat', 'lon')
- key_grad: bfloat16 [2, 64, 256, 2048], P(None, 'lat', 'lon')
- value_grad: bfloat16 [2, 64, 256, 2048], P(None, 'lat', 'lon')
The draws below stay inside these ranges and needn't reach their ends.
Inputs may be any that keep to these rules, and one draw needn't show every extreme that they name: `block_lists`: row t lists tile t itself and possibly t - 1 and t + 1 where they exist, each at most once, in any order; unused slots hold -1. The two tiles nearest each end list every existing neighbour. `row_widths`: the first and last 8 rows have half-width 8.
All inputs are finite; a program needn't handle non-finite values.
Results may differ from the reference program's by a relative error of at most 0.0067.
Values may be sent and summed in bfloat16 or wider, within the bound.
A program may use at most 64 MiB of HBM per device.

```python
import jax
import jax.numpy as jnp
from jax import lax

IMAGES = 2
ROWS_DEV = 2
COLS_DEV = 32
HALO = 8
HEADS = 16
HDIM = 128
NT = 32
NR = 64
NC = 256
HD = 2048


def draw_queries(key, part):
    key = jax.random.fold_in(key, 1)
    full_shape = (IMAGES, NR, NC, HEADS * HDIM)
    return jnp.clip(jax.random.normal(key, full_shape, jnp.float32), -4.5, 4.5).astype(jnp.bfloat16)


def draw_key_states(key, part):
    key = jax.random.fold_in(key, 2)
    full_shape = (IMAGES, NR, NC, HEADS * HDIM)
    return jnp.clip(jax.random.normal(key, full_shape, jnp.float32), -4.5, 4.5).astype(jnp.bfloat16)


def draw_block_lists(key, part):
    key = jax.random.fold_in(key, 3)
    reach_key, order_key = jax.random.split(key)
    tile_ids = jnp.arange(NT, dtype=jnp.int32)
    polar = (tile_ids < 2) | (tile_ids >= NT - 2)
    reach = jnp.where(polar, 1, jax.random.randint(reach_key, (NT,), 0, 2))
    offsets = jnp.arange(-1, 2, dtype=jnp.int32)
    target = tile_ids[:, None] + offsets[None, :]
    valid = (jnp.abs(offsets)[None, :] <= reach[:, None]) & (target >= 0) & (target < NT)
    listed = jnp.where(valid, target, -1).astype(jnp.int32)
    row_keys = jax.random.split(order_key, NT)
    return jax.vmap(lambda row_key, listed_row: jax.random.permutation(row_key, listed_row))(row_keys, listed).astype(jnp.int32)


def draw_row_widths(key, part):
    key = jax.random.fold_in(key, 4)
    row_ids = jnp.arange(NR, dtype=jnp.int32)
    polar = (row_ids < NR // 8) | (row_ids >= NR - NR // 8)
    return jnp.where(polar, HALO, jax.random.randint(key, (NR,), 1, HALO + 1)).astype(jnp.int32)


def shard_levels(own_key, dims, pieces, least, high):
    factor_of, own = 1.0, jax.random.fold_in(own_key, 6)
    for position, blocks in pieces:
        heights = jnp.exp(jax.random.uniform(jax.random.fold_in(own, position), (blocks,), jnp.float32, least / len(pieces), high / len(pieces)))
        factor_of = factor_of * jnp.repeat(heights, dims[position] // blocks).reshape([-1 if axis == position else 1 for axis in range(len(dims))])
    return factor_of


def centred(key, dims, spread, bound, cuts=(), kind=jnp.bfloat16):
    entries = jax.random.normal(key, dims, jnp.float32) * spread
    if len(cuts) > 0:
        entries = shard_levels(key, dims, cuts, -0.22, 0.18) * entries
    return jnp.clip(entries, min=-bound, max=bound).astype(kind)


def setup_inputs(seed: int = 0) -> dict:
    seeds = jax.random.split(jax.random.key(seed), 7)
    queries = draw_queries(jax.random.fold_in(seeds[6], 71), 0)
    key_states = draw_key_states(jax.random.fold_in(seeds[6], 71), 0)
    value_states = centred(seeds[2], (IMAGES, NR, NC, HD), 1.0, 6.0, ((1, 32), (2, 8)))
    out_grad = centred(seeds[3], (IMAGES, NR, NC, HD), 1.0, 6.0, ((1, 32), (2, 8)))
    block_lists = draw_block_lists(jax.random.fold_in(seeds[6], 71), 0)
    row_widths = draw_row_widths(jax.random.fold_in(seeds[6], 71), 0)
    return dict(queries=queries, key_states=key_states, value_states=value_states, out_grad=out_grad, block_lists=block_lists, row_widths=row_widths)


def contract(pattern, first_operand, second_operand):
    return jnp.einsum(pattern, first_operand.astype(jnp.float32), second_operand.astype(jnp.float32), precision=lax.Precision.HIGHEST)


def index_corner(values):
    return tuple(jnp.asarray(value).astype(jnp.int32) for value in values)


def column_mask(width_rows, columns, margin):
    query_cols = jnp.arange(columns, dtype=jnp.int32)[:, None]
    panel_cols = jnp.arange(columns + 2 * margin, dtype=jnp.int32)[None, :] - margin
    return jnp.abs(query_cols - panel_cols)[None, :, :] <= width_rows[:, None, None]


def widen(field):
    wrapped = jnp.concatenate([field[:, :, NC - HALO:], field, field[:, :, :HALO]], axis=2)
    padding = [(0, 0), (ROWS_DEV, ROWS_DEV)] + [(0, 0)] * (field.ndim - 2)
    return jnp.pad(wrapped, padding)


def assemble(stacked):
    tile_count = NR // ROWS_DEV
    sectors = NC // COLS_DEV
    shaped = stacked.reshape((tile_count, sectors) + stacked.shape[1:])
    shaped = jnp.transpose(shaped, (2, 0, 3, 1, 4, 5))
    return shaped.reshape(shaped.shape[0], NR, NC, shaped.shape[-1])


def rounded_term(term):
    return lax.optimization_barrier(term.astype(jnp.bfloat16)).astype(jnp.float32)


def reference(queries, key_states, value_states, out_grad, block_lists, row_widths):
    images = queries.shape[0]
    channels = queries.shape[3]
    panel_width = COLS_DEV + 2 * HALO
    block_size = ROWS_DEV * panel_width
    tile_count = NR // ROWS_DEV
    sectors = NC // COLS_DEV
    score_scale = HDIM ** -0.5
    near_shape = (images, ROWS_DEV * COLS_DEV, HEADS, HDIM)
    far_shape = (images, 3 * block_size, HEADS, HDIM)
    key_panel = widen(key_states)
    value_panel = widen(value_states)

    def query_side(index):
        tile_index = (index // sectors).astype(jnp.int32)
        sector = (index % sectors).astype(jnp.int32)
        row_start = (tile_index * ROWS_DEV).astype(jnp.int32)
        col_start = (sector * COLS_DEV).astype(jnp.int32)
        corner = index_corner((0, row_start, col_start, 0))
        query_tile = lax.dynamic_slice(queries, corner, (images, ROWS_DEV, COLS_DEV, channels)).reshape(near_shape)
        grad_tile = lax.dynamic_slice(out_grad, corner, (images, ROWS_DEV, COLS_DEV, channels)).reshape(near_shape)
        key_tile = lax.dynamic_slice(key_panel, corner, (images, 3 * ROWS_DEV, panel_width, channels)).reshape(far_shape)
        value_tile = lax.dynamic_slice(value_panel, corner, (images, 3 * ROWS_DEV, panel_width, channels)).reshape(far_shape)
        own_list = block_lists[tile_index]
        targets = tile_index + jnp.arange(-1, 2, dtype=jnp.int32)
        active = (targets >= 0) & (targets < tile_count) & jnp.any(own_list[None, :] == targets[:, None], axis=1)
        widths_here = lax.dynamic_slice(row_widths, index_corner((row_start,)), (ROWS_DEV,))
        near_mask = column_mask(widths_here, COLS_DEV, HALO)
        near_mask = jnp.broadcast_to(near_mask[:, :, None, :], (ROWS_DEV, COLS_DEV, ROWS_DEV, panel_width)).reshape(ROWS_DEV * COLS_DEV, block_size)
        full_mask = jnp.transpose(active[:, None, None] & near_mask[None], (1, 0, 2)).reshape(ROWS_DEV * COLS_DEV, 3 * block_size)
        raw = score_scale * contract("bqhd,bkhd->bhqk", query_tile, key_tile)
        hidden = jnp.where(full_mask, raw, -jnp.inf)
        row_top = jnp.max(hidden, axis=3, keepdims=True)
        row_total = jnp.sum(jnp.exp(hidden - row_top), axis=3, keepdims=True)
        log_total = row_top + jnp.log(row_total)
        weights = jnp.where(full_mask, jnp.exp(raw - log_total), 0.0)
        weights_low = weights.astype(jnp.bfloat16)
        attended = contract("bhqk,bkhd->bqhd", weights_low, value_tile).astype(jnp.bfloat16)
        grad_scores = contract("bqhd,bkhd->bhqk", grad_tile, value_tile)
        balance = jnp.sum(weights * grad_scores, axis=3, keepdims=True)
        dscore_low = (weights * (grad_scores - balance)).astype(jnp.bfloat16)
        query_grad = (score_scale * contract("bhqk,bkhd->bqhd", dscore_low, key_tile)).astype(jnp.bfloat16)
        stats = jnp.concatenate([log_total, balance], axis=3)
        stats = jnp.transpose(stats.reshape(images, HEADS, ROWS_DEV, COLS_DEV, 2), (0, 2, 3, 1, 4))
        stats = stats.reshape(images, ROWS_DEV, COLS_DEV, 2 * HEADS)
        return (attended.reshape(images, ROWS_DEV, COLS_DEV, channels), query_grad.reshape(images, ROWS_DEV, COLS_DEV, channels), stats)

    indices = jnp.arange(tile_count * sectors, dtype=jnp.int32)
    attended_parts, query_parts, stat_parts = lax.map(query_side, indices)
    attended = assemble(attended_parts)
    query_grad = assemble(query_parts)
    stats_panel = widen(assemble(stat_parts))
    query_panel = widen(queries)
    grad_panel = widen(out_grad)
    width_panel = jnp.pad(row_widths, (ROWS_DEV, ROWS_DEV))

    def key_side(index):
        tile_index = (index // sectors).astype(jnp.int32)
        sector = (index % sectors).astype(jnp.int32)
        row_start = (tile_index * ROWS_DEV).astype(jnp.int32)
        col_start = (sector * COLS_DEV).astype(jnp.int32)
        corner = index_corner((0, row_start, col_start, 0))
        key_tile = lax.dynamic_slice(key_states, corner, (images, ROWS_DEV, COLS_DEV, channels)).reshape(near_shape)
        value_tile = lax.dynamic_slice(value_states, corner, (images, ROWS_DEV, COLS_DEV, channels)).reshape(near_shape)
        query_tile = lax.dynamic_slice(query_panel, corner, (images, 3 * ROWS_DEV, panel_width, channels)).reshape(far_shape)
        grad_tile = lax.dynamic_slice(grad_panel, corner, (images, 3 * ROWS_DEV, panel_width, channels)).reshape(far_shape)
        stats_tile = lax.dynamic_slice(stats_panel, corner, (images, 3 * ROWS_DEV, panel_width, 2 * HEADS)).reshape(images, 3 * block_size, HEADS, 2)
        log_total = jnp.transpose(stats_tile[..., 0], (0, 2, 1))[..., None]
        balance = jnp.transpose(stats_tile[..., 1], (0, 2, 1))[..., None]
        sources = tile_index + jnp.arange(-1, 2, dtype=jnp.int32)
        source_lists = block_lists[jnp.clip(sources, 0, tile_count - 1)]
        active = (sources >= 0) & (sources < tile_count) & jnp.any(source_lists == tile_index, axis=1)
        widths_here = lax.dynamic_slice(width_panel, index_corner((row_start,)), (3 * ROWS_DEV,))
        far_mask = jnp.transpose(column_mask(widths_here, COLS_DEV, HALO), (0, 2, 1))
        far_mask = jnp.broadcast_to(far_mask[:, :, None, :], (3 * ROWS_DEV, panel_width, ROWS_DEV, COLS_DEV)).reshape(3 * block_size, ROWS_DEV * COLS_DEV)
        far_mask = far_mask & jnp.repeat(active, block_size)[:, None]
        raw = score_scale * contract("bqhd,bkhd->bhqk", query_tile, key_tile)
        weights = jnp.where(far_mask, jnp.exp(raw - log_total), 0.0)
        weights_low = weights.astype(jnp.bfloat16)
        grad_scores = contract("bqhd,bkhd->bhqk", grad_tile, value_tile)
        dscore_low = (weights * (grad_scores - balance)).astype(jnp.bfloat16)
        query_six = query_tile.reshape(images, 3, ROWS_DEV, panel_width, HEADS, HDIM)
        grad_six = grad_tile.reshape(images, 3, ROWS_DEV, panel_width, HEADS, HDIM)
        dscore_six = dscore_low.reshape(images, HEADS, 3, ROWS_DEV, panel_width, ROWS_DEV * COLS_DEV)
        weight_six = weights_low.reshape(images, HEADS, 3, ROWS_DEV, panel_width, ROWS_DEV * COLS_DEV)
        key_grad = jnp.zeros(near_shape, jnp.float32)
        value_grad = jnp.zeros(near_shape, jnp.float32)
        for low, high in ((0, HALO), (HALO, panel_width - HALO), (panel_width - HALO, panel_width)):
            key_term = score_scale * contract("bhtrpk,btrphd->btkhd", dscore_six[:, :, :, :, low:high], query_six[:, :, :, low:high])
            value_term = contract("bhtrpk,btrphd->btkhd", weight_six[:, :, :, :, low:high], grad_six[:, :, :, low:high])
            key_grad = key_grad + jnp.sum(rounded_term(key_term), axis=1)
            value_grad = value_grad + jnp.sum(rounded_term(value_term), axis=1)
        return (key_grad.astype(jnp.bfloat16).reshape(images, ROWS_DEV, COLS_DEV, channels), value_grad.astype(jnp.bfloat16).reshape(images, ROWS_DEV, COLS_DEV, channels))

    key_parts, value_parts = lax.map(key_side, indices)
    return attended, query_grad, assemble(key_parts), assemble(value_parts)
```

```python
import functools
import math

import jax
import jax.numpy as jnp
from jax import lax
from jax.experimental import pallas as pl
from jax.experimental.pallas import tpu as pltpu
from jax.sharding import PartitionSpec as P

MESH = pl.DeviceIdType.MESH
HALO = 8
HDIM = 128
GROUPS = 4
HIDDEN = -1e30
FLOOR = -1e29


def nt(a, b):
    return lax.dot_general(a, b, (((1,), (1,)), ((), ())), preferred_element_type=jnp.float32)


def tn(a, b):
    return lax.dot_general(a, b, (((0,), (0,)), ((), ())), preferred_element_type=jnp.float32)


def nn(a, b):
    return jnp.dot(a, b, preferred_element_type=jnp.float32)


def kernel(
    lon_count,
    lat_count,
    lists_ref,
    widths_ref,
    q_hbm,
    k_hbm,
    v_hbm,
    g_hbm,
    att_hbm,
    dq_hbm,
    dk_hbm,
    dv_hbm,
    near,
    far,
    edge_out,
    bias,
    exps,
    dps,
    stats,
    stats_in,
    factors,
    near_acc,
    part_out,
    part_in,
    far_acc,
    term_out,
    term_in,
    outs,
    own_sem,
    kv_send,
    kv_recv,
    edge_send,
    edge_recv,
    stat_send,
    stat_recv,
    part_send,
    part_recv,
    term_send,
    term_recv,
    out_sem,
):
    lon = lax.axis_index("lon")
    lat = lax.axis_index("lat")
    left = lax.rem(lon + lon_count - 1, lon_count)
    right = lax.rem(lon + 1, lon_count)
    has_above = lat > 0
    has_below = lat < lat_count - 1
    images, tokens, channels = q_hbm.shape
    heads = channels // HDIM
    group_heads = heads // GROUPS
    group_items = images * group_heads
    group_lanes = group_heads * HDIM
    scale = HDIM ** -0.5

    sides = ({"lon": left}, {"lon": right})
    tiles = ({"lat": lat - 1}, {"lat": lat + 1})
    exists = (has_above, has_below)

    own_copies = [
        pltpu.make_async_copy(q_hbm, near.at[0, :, 0:tokens, :], own_sem.at[0]),
        pltpu.make_async_copy(g_hbm, near.at[1, :, 0:tokens, :], own_sem.at[1]),
        pltpu.make_async_copy(k_hbm, far.at[0, :, tokens : 2 * tokens, :], own_sem.at[2]),
        pltpu.make_async_copy(v_hbm, far.at[1, :, tokens : 2 * tokens, :], own_sem.at[3]),
    ]
    for copy in own_copies:
        copy.start()

    barrier = pltpu.get_barrier_semaphore()
    for side in sides:
        pl.semaphore_signal(barrier, inc=1, device_id=side, device_id_type=MESH)
    for there, tile in zip(exists, tiles):
        @pl.when(there)
        def _():
            pl.semaphore_signal(barrier, inc=1, device_id=tile, device_id_type=MESH)
    pl.semaphore_wait(barrier, 2 + jnp.where(has_above, 1, 0) + jnp.where(has_below, 1, 0))

    def lanes(group):
        return pl.ds(group * group_lanes, group_lanes)

    def kv_copy(group, way, which):
        source = (k_hbm, v_hbm)[which]
        start = 2 * tokens if way == 0 else 0
        return pltpu.make_async_remote_copy(
            src_ref=source.at[:, :, lanes(group)],
            dst_ref=far.at[which, :, start : start + tokens, lanes(group)],
            send_sem=kv_send.at[group, way, which],
            recv_sem=kv_recv.at[group, 1 - way, which],
            device_id=tiles[way],
            device_id_type=MESH,
        )

    def kv_landed(group, origin, which):
        start = 0 if origin == 0 else 2 * tokens
        piece = far.at[which, :, start : start + tokens, lanes(group)]
        return pltpu.make_async_remote_copy(
            src_ref=piece,
            dst_ref=piece,
            send_sem=kv_send.at[group, 1 - origin, which],
            recv_sem=kv_recv.at[group, origin, which],
            device_id=tiles[origin],
            device_id_type=MESH,
        )

    def edge_copy(group, way):
        start = tokens + 2 * HALO if way == 0 else tokens
        return pltpu.make_async_remote_copy(
            src_ref=edge_out.at[way, :, :, :, lanes(group)],
            dst_ref=near.at[:, :, start : start + 2 * HALO, lanes(group)],
            send_sem=edge_send.at[group, way],
            recv_sem=edge_recv.at[group, 1 - way],
            device_id=sides[way],
            device_id_type=MESH,
        )

    def edge_landed(group, origin):
        start = tokens if origin == 0 else tokens + 2 * HALO
        piece = near.at[:, :, start : start + 2 * HALO, lanes(group)]
        return pltpu.make_async_remote_copy(
            src_ref=piece,
            dst_ref=piece,
            send_sem=edge_send.at[group, 1 - origin],
            recv_sem=edge_recv.at[group, origin],
            device_id=sides[origin],
            device_id_type=MESH,
        )

    def stat_copy(group, way):
        return pltpu.make_async_remote_copy(
            src_ref=stats.at[group],
            dst_ref=stats_in.at[1 - way, group],
            send_sem=stat_send.at[group, way],
            recv_sem=stat_recv.at[group, 1 - way],
            device_id=sides[way],
            device_id_type=MESH,
        )

    def part_copy(group, way):
        return pltpu.make_async_remote_copy(
            src_ref=part_out.at[way, :, :, :, lanes(group)],
            dst_ref=part_in.at[1 - way, :, :, :, lanes(group)],
            send_sem=part_send.at[group, way],
            recv_sem=part_recv.at[group, 1 - way],
            device_id=sides[way],
            device_id_type=MESH,
        )

    def term_copy(group, way):
        return pltpu.make_async_remote_copy(
            src_ref=term_out.at[way, :, :, :, lanes(group)],
            dst_ref=term_in.at[1 - way, :, :, :, lanes(group)],
            send_sem=term_send.at[group, way],
            recv_sem=term_recv.at[group, 1 - way],
            device_id=tiles[way],
            device_id_type=MESH,
        )

    for group in range(GROUPS):
        for way in range(2):
            @pl.when(exists[way])
            def _():
                kv_copy(group, way, 0).start()
                kv_copy(group, way, 1).start()

    own_copies[0].wait()
    own_copies[1].wait()
    for group in range(GROUPS):
        for which in range(2):
            for image in range(images):
                def half(start, low):
                    block = near[which, image, start : start + 16, lanes(group)].astype(jnp.float32)
                    return block[low : low + HALO]

                edge_out[0, which, image, :, lanes(group)] = jnp.concatenate(
                    [half(0, 0), half(32, 0)], axis=0
                ).astype(jnp.bfloat16)
                edge_out[1, which, image, :, lanes(group)] = jnp.concatenate(
                    [half(16, HALO), half(48, HALO)], axis=0
                ).astype(jnp.bfloat16)
        for way in range(2):
            edge_copy(group, way).start()

    near[:, :, tokens + 4 * HALO :, :] = jnp.zeros(
        (2, images, near.shape[2] - tokens - 4 * HALO, channels), jnp.bfloat16
    )
    for way in range(2):
        @pl.when(jnp.logical_not(exists[way]))
        def _():
            start = 0 if way == 0 else 2 * tokens
            far[:, :, start : start + tokens, :] = jnp.zeros((2, images, tokens, channels), jnp.bfloat16)
            term_in[way] = jnp.zeros((2, images, tokens, channels), jnp.bfloat16)

    def listed(target):
        found = (
            (lists_ref[0, lat] == target)
            | (lists_ref[1, lat] == target)
            | (lists_ref[2, lat] == target)
        ) & (target >= 0)
        return jnp.where(found, 1, 0)

    shape = bias.shape
    key = lax.broadcasted_iota(jnp.int32, shape, 0)
    query = lax.broadcasted_iota(jnp.int32, shape, 1)
    key_tile = key >> 6
    key_col = key & 31
    edge = query - tokens
    is_own = query < tokens
    from_left = edge < 2 * HALO
    query_col = jnp.where(is_own, query & 31, jnp.where(from_left, (edge & 7) - HALO, 32 + (edge & 7)))
    query_row = jnp.where(is_own, query >> 5, (edge >> 3) & 1)
    width = jnp.where(query_row == 0, widths_ref[2 * lat], widths_ref[2 * lat + 1])
    active = jnp.where(
        key_tile == 0, listed(lat - 1), jnp.where(key_tile == 1, listed(lat), listed(lat + 1))
    )
    seen = (jnp.abs(query_col - key_col) <= width) & (active == 1) & (edge < 4 * HALO)
    bias[...] = jnp.where(seen, 0.0, HIDDEN)

    own_copies[2].wait()
    own_copies[3].wait()

    def place(group, item):
        image = item // group_heads
        head = item % group_heads
        return image, pl.ds(pl.multiple_of(group * group_lanes + head * HDIM, HDIM), HDIM)

    def scores(group):
        for origin in range(2):
            @pl.when(exists[origin])
            def _():
                kv_landed(group, origin, 0).wait_recv()
                kv_landed(group, origin, 1).wait_recv()
        for origin in range(2):
            edge_landed(group, origin).wait_recv()

        def body(item, carry):
            image, cols = place(group, item)
            queries = near[0, image, :, cols]
            grads = near[1, image, :, cols]
            keys = far[0, image, :, cols]
            values = far[1, image, :, cols]
            raw = nt(keys, queries) * (scale * math.log2(math.e)) + bias[...]
            dp = nt(values, grads)
            top = jnp.maximum(jnp.max(raw, axis=0, keepdims=True), FLOOR)
            e = jnp.exp2(raw - top)
            slot = group * group_items + item
            exps[slot] = e
            dps[slot] = dp
            stats[group, pl.ds(item, 1), :] = top
            stats[group, pl.ds(group_items + item, 1), :] = jnp.sum(e, axis=0, keepdims=True)
            stats[group, pl.ds(2 * group_items + item, 1), :] = jnp.sum(e * dp, axis=0, keepdims=True)
            return carry

        lax.fori_loop(0, group_items, body, 0, unroll=2)
        for way in range(2):
            stat_copy(group, way).start()

    def combine(group):
        for way in range(2):
            stat_copy(group, way).wait_recv()
        from_l = stats_in[0, group]
        from_r = stats_in[1, group]
        lane = lax.broadcasted_iota(jnp.int32, from_l.shape, 1)
        row = lax.broadcasted_iota(jnp.int32, from_l.shape, 0)
        other = jnp.where(row < group_items, FLOOR, 0.0)
        moves = (
            (from_l, 80, 0),
            (from_l, 88, 32),
            (from_r, 64, 24),
            (from_r, 72, 56),
            (from_l, 24, 64),
            (from_l, 56, 72),
            (from_r, 0, 80),
            (from_r, 32, 88),
        )
        for source, old, new in moves:
            shifted = pltpu.roll(source, (new - old) % HDIM, 1)
            other = jnp.where((lane >= new) & (lane < new + HALO), shifted, other)
        here = stats[group]
        n = group_items
        top, total, balance = here[0:n], here[n : 2 * n], here[2 * n : 3 * n]
        top2, total2, balance2 = other[0:n], other[n : 2 * n], other[2 * n : 3 * n]
        high = jnp.maximum(top, top2)
        part = jnp.exp2(top - high)
        part2 = jnp.exp2(top2 - high)
        inverse = 1.0 / jnp.maximum(part * total + part2 * total2, 0.5)
        factors[group, 0] = part * inverse
        factors[group, 1] = (part * balance + part2 * balance2) * inverse

    def gradients(group):
        def body(item, carry):
            image, cols = place(group, item)
            queries = near[0, image, :, cols]
            grads = near[1, image, :, cols]
            keys = far[0, image, :, cols]
            values = far[1, image, :, cols]
            slot = group * group_items + item
            w = exps[slot] * factors[group, 0, pl.ds(item, 1), :]
            ds = w * (dps[slot] - factors[group, 1, pl.ds(item, 1), :])
            w = w.astype(jnp.bfloat16)
            ds = ds.astype(jnp.bfloat16)
            att = tn(w, values)
            dq = tn(ds, keys) * scale
            dv = nn(w, grads)
            dk = nn(ds, queries) * scale
            for which, x in enumerate((att, dq)):
                near_acc[which, image, :, cols] = x[0:tokens]
                for way in range(2):
                    start = tokens + 2 * HALO * way
                    part_out[way, which, image, :, cols] = x[start : start + 2 * HALO].astype(jnp.bfloat16)
            for which, x in enumerate((dk, dv)):
                far_acc[which, image, :, cols] = x[tokens : 2 * tokens]
                term_out[0, which, image, :, cols] = x[0:tokens].astype(jnp.bfloat16)
                term_out[1, which, image, :, cols] = x[2 * tokens :].astype(jnp.bfloat16)
            return carry

        lax.fori_loop(0, group_items, body, 0, unroll=2)
        for way in range(2):
            @pl.when(exists[way])
            def _():
                term_copy(group, way).start()
        for way in range(2):
            part_copy(group, way).start()

    def out_copies(group):
        return [
            pltpu.make_async_copy(
                outs.at[which, :, :, lanes(group)], ref.at[:, :, lanes(group)], out_sem.at[group, which]
            )
            for which, ref in enumerate((att_hbm, dq_hbm, dk_hbm, dv_hbm))
        ]

    def finish(group):
        for way in range(2):
            part_copy(group, way).wait_recv()
        for way in range(2):
            @pl.when(exists[way])
            def _():
                term_copy(group, 1 - way).wait_recv()

        def body(item, carry):
            image, cols = place(group, item)
            for which in range(2):
                acc = near_acc[which, image, :, cols]
                add_l = part_in[0, which, image, :, cols].astype(jnp.float32)
                add_r = part_in[1, which, image, :, cols].astype(jnp.float32)
                rows = []
                for r in range(2):
                    here = acc[32 * r : 32 * r + 32]
                    rows.append(here[0:8] + add_l[8 * r : 8 * r + 8])
                    rows.append(here[8:24])
                    rows.append(here[24:32] + add_r[8 * r : 8 * r + 8])
                outs[which, image, :, cols] = jnp.concatenate(rows, axis=0).astype(jnp.bfloat16)
            for which in range(2):
                total = far_acc[which, image, :, cols]
                for way in range(2):
                    total = total + term_in[way, which, image, :, cols].astype(jnp.float32)
                outs[2 + which, image, :, cols] = total.astype(jnp.bfloat16)
            return carry

        lax.fori_loop(0, group_items, body, 0, unroll=2)
        for copy in out_copies(group):
            copy.start()

    scores(0)
    for group in range(1, GROUPS):
        scores(group)
        combine(group - 1)
        gradients(group - 1)
        if group >= 3:
            finish(group - 3)
    combine(GROUPS - 1)
    gradients(GROUPS - 1)
    for group in range(max(GROUPS - 3, 0), GROUPS):
        finish(group)

    for group in range(GROUPS):
        for copy in out_copies(group):
            copy.wait()
        for way in range(2):
            edge_copy(group, way).wait_send()
            stat_copy(group, way).wait_send()
            part_copy(group, way).wait_send()

            @pl.when(exists[way])
            def _():
                kv_copy(group, way, 0).wait_send()
                kv_copy(group, way, 1).wait_send()
                term_copy(group, way).wait_send()


def solution(mesh):
    lon_count = mesh.shape["lon"]
    lat_count = mesh.shape["lat"]

    def on_device(queries, key_states, value_states, out_grad, block_lists, row_widths):
        images, rows, columns, channels = queries.shape
        tokens = rows * columns
        flat = (images, tokens, channels)
        items = images * channels // HDIM
        group_items = items // GROUPS
        bf16, f32 = jnp.bfloat16, jnp.float32
        any_spec = pl.BlockSpec(memory_space=pltpu.HBM)
        smem_spec = pl.BlockSpec(memory_space=pltpu.SMEM)
        dma = pltpu.SemaphoreType.DMA
        results = pl.pallas_call(
            functools.partial(kernel, lon_count, lat_count),
            out_shape=[jax.ShapeDtypeStruct(flat, bf16)] * 4,
            in_specs=[smem_spec, smem_spec] + [any_spec] * 4,
            out_specs=[any_spec] * 4,
            scratch_shapes=[
                pltpu.VMEM((2, images, 2 * tokens, channels), bf16),
                pltpu.VMEM((2, images, 3 * tokens, channels), bf16),
                pltpu.VMEM((2, 2, images, 2 * HALO, channels), bf16),
                pltpu.VMEM((3 * tokens, 2 * tokens), f32),
                pltpu.VMEM((items, 3 * tokens, 2 * tokens), f32),
                pltpu.VMEM((items, 3 * tokens, 2 * tokens), f32),
                pltpu.VMEM((GROUPS, 3 * group_items, 2 * tokens), f32),
                pltpu.VMEM((2, GROUPS, 3 * group_items, 2 * tokens), f32),
                pltpu.VMEM((GROUPS, 2, group_items, 2 * tokens), f32),
                pltpu.VMEM((2, images, tokens, channels), f32),
                pltpu.VMEM((2, 2, images, 2 * HALO, channels), bf16),
                pltpu.VMEM((2, 2, images, 2 * HALO, channels), bf16),
                pltpu.VMEM((2, images, tokens, channels), f32),
                pltpu.VMEM((2, 2, images, tokens, channels), bf16),
                pltpu.VMEM((2, 2, images, tokens, channels), bf16),
                pltpu.VMEM((4, images, tokens, channels), bf16),
                dma((4,)),
                dma((GROUPS, 2, 2)),
                dma((GROUPS, 2, 2)),
                dma((GROUPS, 2)),
                dma((GROUPS, 2)),
                dma((GROUPS, 2)),
                dma((GROUPS, 2)),
                dma((GROUPS, 2)),
                dma((GROUPS, 2)),
                dma((GROUPS, 2)),
                dma((GROUPS, 2)),
                dma((GROUPS, 4)),
            ],
            compiler_params=pltpu.CompilerParams(
                collective_id=0, has_side_effects=True, vmem_limit_bytes=48 * 1024 * 1024
            ),
            cost_estimate=pl.CostEstimate(
                flops=12 * items * 192 * 128 * 128, bytes_accessed=8 * images * tokens * channels * 2, transcendentals=items * 192 * 128
            ),
        )(
            block_lists.T,
            row_widths,
            queries.reshape(flat),
            key_states.reshape(flat),
            value_states.reshape(flat),
            out_grad.reshape(flat),
        )
        return tuple(x.reshape(queries.shape) for x in results)

    split = P(None, "lat", "lon", None)
    return jax.shard_map(
        on_device,
        mesh=mesh,
        in_specs=(split, split, split, split, P(), P()),
        out_specs=(split, split, split, split),
        check_vma=False,
    )
```

```python
import functools
import math

import jax
import jax.numpy as jnp
from jax import lax
from jax.experimental import pallas as pl
from jax.experimental.pallas import tpu as pltpu
from jax.sharding import PartitionSpec as P

MESH = pl.DeviceIdType.MESH
HALO = 8
HDIM = 128
GROUPS = 4
AHEAD = 2
HIDDEN = -1e30
FLOOR = -1e29


def nt(a, b):
    return lax.dot_general(a, b, (((1,), (1,)), ((), ())), preferred_element_type=jnp.float32)


def tn(a, b):
    return lax.dot_general(a, b, (((0,), (0,)), ((), ())), preferred_element_type=jnp.float32)


def nn(a, b):
    return jnp.dot(a, b, preferred_element_type=jnp.float32)


def window(x, old, new, size, rest):
    lane = lax.broadcasted_iota(jnp.int32, x.shape, 1)
    shifted = x if old == new else pltpu.roll(x, (new - old) % HDIM, 1)
    return jnp.where((lane >= new) & (lane < new + size), shifted, rest)


def kernel(
    lon_count,
    lat_count,
    lists_ref,
    widths_ref,
    q_hbm,
    k_hbm,
    v_hbm,
    g_hbm,
    out_hbm,
    near,
    far,
    edge_out,
    bias,
    exps,
    dps,
    stats,
    stats_out,
    stats_in,
    factors,
    near_acc,
    part_out,
    part_in,
    far_acc,
    term_out,
    term_in,
    outs,
    own_sem,
    kv_send,
    kv_recv,
    edge_send,
    edge_recv,
    stat_send,
    stat_recv,
    part_send,
    part_recv,
    term_send,
    term_recv,
    out_sem,
):
    lon = lax.axis_index("lon")
    lat = lax.axis_index("lat")
    left = lax.rem(lon + lon_count - 1, lon_count)
    right = lax.rem(lon + 1, lon_count)
    has_above = lat > 0
    has_below = lat < lat_count - 1
    images, tokens, channels = q_hbm.shape
    heads = channels // HDIM
    group_heads = heads // GROUPS
    group_items = images * group_heads
    group_lanes = group_heads * HDIM
    scale = HDIM ** -0.5

    sides = ({"lon": left}, {"lon": right})
    tiles = ({"lat": lat - 1}, {"lat": lat + 1})
    exists = (has_above, has_below)

    own_copies = [
        pltpu.make_async_copy(q_hbm, near.at[0, :, 0:tokens, :], own_sem.at[0]),
        pltpu.make_async_copy(g_hbm, near.at[1, :, 0:tokens, :], own_sem.at[1]),
        pltpu.make_async_copy(k_hbm, far.at[0, :, tokens : 2 * tokens, :], own_sem.at[2]),
        pltpu.make_async_copy(v_hbm, far.at[1, :, tokens : 2 * tokens, :], own_sem.at[3]),
    ]
    for copy in own_copies:
        copy.start()

    barrier = pltpu.get_barrier_semaphore()
    for side in sides:
        pl.semaphore_signal(barrier, inc=1, device_id=side, device_id_type=MESH)
    for there, tile in zip(exists, tiles):
        @pl.when(there)
        def _():
            pl.semaphore_signal(barrier, inc=1, device_id=tile, device_id_type=MESH)
    pl.semaphore_wait(barrier, 2 + jnp.where(has_above, 1, 0) + jnp.where(has_below, 1, 0))

    def lanes(group):
        start = group * group_lanes
        return pl.ds(start if isinstance(group, int) else pl.multiple_of(start, HDIM), group_lanes)

    def remote(source, target, send, recv, device):
        return pltpu.make_async_remote_copy(
            src_ref=source, dst_ref=target, send_sem=send, recv_sem=recv, device_id=device, device_id_type=MESH
        )

    def kv_copy(group, way, which):
        start = 2 * tokens if way == 0 else 0
        return remote(
            (k_hbm, v_hbm)[which].at[:, :, lanes(group)],
            far.at[which, :, start : start + tokens, lanes(group)],
            kv_send.at[group, way, which],
            kv_recv.at[group, 1 - way, which],
            tiles[way],
        )

    def edge_copy(group, way):
        start = tokens + 2 * HALO if way == 0 else tokens
        return remote(
            edge_out.at[way, :, :, :, lanes(group)],
            near.at[:, :, start : start + 2 * HALO, lanes(group)],
            edge_send.at[group, way],
            edge_recv.at[group, 1 - way],
            sides[way],
        )

    def stat_copy(group, way):
        return remote(
            stats_out.at[way, group],
            stats_in.at[1 - way, group],
            stat_send.at[group, way],
            stat_recv.at[group, 1 - way],
            sides[way],
        )

    def part_copy(group, way):
        return remote(
            part_out.at[way, :, :, :, lanes(group)],
            part_in.at[1 - way, :, :, :, lanes(group)],
            part_send.at[group, way],
            part_recv.at[group, 1 - way],
            sides[way],
        )

    def term_copy(group, way):
        return remote(
            term_out.at[way, :, :, :, lanes(group)],
            term_in.at[1 - way, :, :, :, lanes(group)],
            term_send.at[group, way],
            term_recv.at[group, 1 - way],
            tiles[way],
        )

    def out_copy(group):
        return pltpu.make_async_copy(
            outs.at[:, :, :, lanes(group)], out_hbm.at[:, :, :, lanes(group)], out_sem.at[group]
        )

    def send_kv(group):
        for way in range(2):
            @pl.when(exists[way])
            def _():
                kv_copy(group, way, 0).start()
                kv_copy(group, way, 1).start()

    def send_edges(group):
        for which in range(2):
            for image in range(images):
                def half(start, low):
                    block = near[which, image, start : start + 16, lanes(group)].astype(jnp.float32)
                    return block[low : low + HALO]

                edge_out[0, which, image, :, lanes(group)] = jnp.concatenate(
                    [half(0, 0), half(32, 0)], axis=0
                ).astype(jnp.bfloat16)
                edge_out[1, which, image, :, lanes(group)] = jnp.concatenate(
                    [half(16, HALO), half(48, HALO)], axis=0
                ).astype(jnp.bfloat16)
        for way in range(2):
            edge_copy(group, way).start()

    for group in range(AHEAD):
        send_kv(group)
    own_copies[0].wait()
    own_copies[1].wait()
    for group in range(AHEAD):
        send_edges(group)

    near[:, :, tokens + 4 * HALO :, :] = jnp.zeros(
        (2, images, near.shape[2] - tokens - 4 * HALO, channels), jnp.bfloat16
    )
    for way in range(2):
        @pl.when(jnp.logical_not(exists[way]))
        def _():
            start = 0 if way == 0 else 2 * tokens
            far[:, :, start : start + tokens, :] = jnp.zeros((2, images, tokens, channels), jnp.bfloat16)
            term_in[way] = jnp.zeros((2, images, tokens, channels), jnp.bfloat16)

    def listed(target):
        found = (
            (lists_ref[0, lat] == target)
            | (lists_ref[1, lat] == target)
            | (lists_ref[2, lat] == target)
        ) & (target >= 0)
        return jnp.where(found, 1, 0)

    shape = bias.shape
    key = lax.broadcasted_iota(jnp.int32, shape, 0)
    query = lax.broadcasted_iota(jnp.int32, shape, 1)
    key_tile = key >> 6
    key_col = key & 31
    edge = query - tokens
    is_own = query < tokens
    from_left = edge < 2 * HALO
    query_col = jnp.where(is_own, query & 31, jnp.where(from_left, (edge & 7) - HALO, 32 + (edge & 7)))
    query_row = jnp.where(is_own, query >> 5, (edge >> 3) & 1)
    width = jnp.where(query_row == 0, widths_ref[2 * lat], widths_ref[2 * lat + 1])
    active = jnp.where(
        key_tile == 0, listed(lat - 1), jnp.where(key_tile == 1, listed(lat), listed(lat + 1))
    )
    seen = (jnp.abs(query_col - key_col) <= width) & (active == 1) & (edge < 4 * HALO)
    bias[...] = jnp.where(seen, 0.0, HIDDEN)

    own_copies[2].wait()
    own_copies[3].wait()

    def place(group, item):
        image = item // group_heads
        head = item % group_heads
        return image, pl.ds(pl.multiple_of(group * group_lanes + head * HDIM, HDIM), HDIM)

    def wait_inputs(group):
        for origin in range(2):
            @pl.when(exists[origin])
            def _():
                kv_copy(group, 1 - origin, 0).wait_recv()
                kv_copy(group, 1 - origin, 1).wait_recv()
        for origin in range(2):
            edge_copy(group, 1 - origin).wait_recv()

    def scores(group):
        def body(item, carry):
            image, cols = place(group, item)
            queries = near[0, image, :, cols]
            grads = near[1, image, :, cols]
            keys = far[0, image, :, cols]
            values = far[1, image, :, cols]
            raw = nt(keys, queries) * (scale * math.log2(math.e)) + bias[...]
            dp = nt(values, grads)
            top = jnp.maximum(jnp.max(raw, axis=0, keepdims=True), FLOOR)
            e = jnp.exp2(raw - top)
            slot = group * group_items + item
            exps[slot] = e
            dps[slot] = dp
            stats[group, 0, pl.ds(item, 1), :] = top
            stats[group, 1, pl.ds(item, 1), :] = jnp.sum(e, axis=0, keepdims=True)
            stats[group, 2, pl.ds(item, 1), :] = jnp.sum(e * dp, axis=0, keepdims=True)
            return carry

        lax.fori_loop(0, group_items, body, 0, unroll=2)
        for way, moves in enumerate((((0, 0, 8), (32, 8, 8), (64, 16, 16)), ((24, 0, 8), (56, 8, 8), (80, 16, 16)))):
            packed = jnp.zeros((8, HDIM), jnp.float32)
            for kind in range(3):
                for old, new, size in moves:
                    packed = window(stats[group, kind], old, 32 * kind + new, size, packed)
            stats_out[way, group] = packed
        for way in range(2):
            stat_copy(group, way).start()

    def combine(group):
        for way in range(2):
            stat_copy(group, way).wait_recv()
        others = []
        for kind in range(3):
            other = jnp.full((8, HDIM), FLOOR if kind == 0 else 0.0, jnp.float32)
            for origin, moves in enumerate((((0, 64, 16), (16, 0, 8), (24, 32, 8)), ((0, 80, 16), (16, 24, 8), (24, 56, 8)))):
                for old, new, size in moves:
                    other = window(stats_in[origin, group], 32 * kind + old, new, size, other)
            others.append(other)
        top, total, balance = (stats[group, kind] for kind in range(3))
        top2, total2, balance2 = others
        high = jnp.maximum(top, top2)
        part = jnp.exp2(top - high)
        part2 = jnp.exp2(top2 - high)
        inverse = 1.0 / jnp.maximum(part * total + part2 * total2, 0.5)
        factors[group, 0] = part * inverse
        factors[group, 1] = (part * balance + part2 * balance2) * inverse

    def gradients(group):
        def body(item, carry):
            image, cols = place(group, item)
            queries = near[0, image, :, cols]
            grads = near[1, image, :, cols]
            keys = far[0, image, :, cols]
            values = far[1, image, :, cols]
            slot = group * group_items + item
            w = exps[slot] * factors[group, 0, pl.ds(item, 1), :]
            ds = w * (dps[slot] - factors[group, 1, pl.ds(item, 1), :])
            w = w.astype(jnp.bfloat16)
            ds = ds.astype(jnp.bfloat16)
            att = tn(w, values)
            dq = tn(ds, keys) * scale
            dv = nn(w, grads)
            dk = nn(ds, queries) * scale
            for which, x in enumerate((att, dq)):
                near_acc[which, image, :, cols] = x[0:tokens]
                for way in range(2):
                    start = tokens + 2 * HALO * way
                    part_out[way, which, image, :, cols] = x[start : start + 2 * HALO].astype(jnp.bfloat16)
            for which, x in enumerate((dk, dv)):
                far_acc[which, image, :, cols] = x[tokens : 2 * tokens]
                term_out[0, which, image, :, cols] = x[0:tokens].astype(jnp.bfloat16)
                term_out[1, which, image, :, cols] = x[2 * tokens :].astype(jnp.bfloat16)
            return carry

        lax.fori_loop(0, group_items, body, 0, unroll=2)
        for way in range(2):
            @pl.when(exists[way])
            def _():
                term_copy(group, way).start()
        for way in range(2):
            part_copy(group, way).start()

    def finish(group):
        for way in range(2):
            part_copy(group, way).wait_recv()
        for way in range(2):
            @pl.when(exists[way])
            def _():
                term_copy(group, 1 - way).wait_recv()

        def body(item, carry):
            image, cols = place(group, item)
            for which in range(2):
                acc = near_acc[which, image, :, cols]
                add_l = part_in[0, which, image, :, cols].astype(jnp.float32)
                add_r = part_in[1, which, image, :, cols].astype(jnp.float32)
                rows = []
                for r in range(2):
                    here = acc[32 * r : 32 * r + 32]
                    rows.append(here[0:8] + add_l[8 * r : 8 * r + 8])
                    rows.append(here[8:24])
                    rows.append(here[24:32] + add_r[8 * r : 8 * r + 8])
                outs[which, image, :, cols] = jnp.concatenate(rows, axis=0).astype(jnp.bfloat16)
            for which in range(2):
                total = far_acc[which, image, :, cols]
                for way in range(2):
                    total = total + term_in[way, which, image, :, cols].astype(jnp.float32)
                outs[2 + which, image, :, cols] = total.astype(jnp.bfloat16)
            return carry

        lax.fori_loop(0, group_items, body, 0, unroll=2)
        out_copy(group).start()

    def step(index, carry):
        @pl.when(index < GROUPS)
        def _():
            wait_inputs(index)

            @pl.when(index + AHEAD < GROUPS)
            def _():
                send_kv(index + AHEAD)
                send_edges(index + AHEAD)

            scores(index)

        @pl.when((index >= 1) & (index <= GROUPS))
        def _():
            combine(index - 1)
            gradients(index - 1)

        @pl.when(index >= 2)
        def _():
            finish(index - 2)

        return carry

    lax.fori_loop(0, GROUPS + 2, step, 0)

    def drain(group, carry):
        out_copy(group).wait()
        for way in range(2):
            edge_copy(group, way).wait_send()
            stat_copy(group, way).wait_send()
            part_copy(group, way).wait_send()

            @pl.when(exists[way])
            def _():
                kv_copy(group, way, 0).wait_send()
                kv_copy(group, way, 1).wait_send()
                term_copy(group, way).wait_send()

        return carry

    lax.fori_loop(0, GROUPS, drain, 0)


def split_kernel(from_hbm, *refs):
    outs, sem = refs[:4], refs[4]
    copies = [pltpu.make_async_copy(from_hbm.at[i], outs[i], sem.at[i]) for i in range(4)]
    for copy in copies:
        copy.start()
    for copy in copies:
        copy.wait()


def solution(mesh):
    lon_count = mesh.shape["lon"]
    lat_count = mesh.shape["lat"]

    def on_device(queries, key_states, value_states, out_grad, block_lists, row_widths):
        images, rows, columns, channels = queries.shape
        tokens = rows * columns
        flat = (images, tokens, channels)
        items = images * channels // HDIM
        bf16, f32 = jnp.bfloat16, jnp.float32
        hbm_spec = pl.BlockSpec(memory_space=pltpu.HBM)
        smem_spec = pl.BlockSpec(memory_space=pltpu.SMEM)
        dma = pltpu.SemaphoreType.DMA
        stacked = pl.pallas_call(
            functools.partial(kernel, lon_count, lat_count),
            out_shape=jax.ShapeDtypeStruct((4,) + flat, bf16),
            in_specs=[smem_spec, smem_spec] + [hbm_spec] * 4,
            out_specs=hbm_spec,
            scratch_shapes=[
                pltpu.VMEM((2, images, 2 * tokens, channels), bf16),
                pltpu.VMEM((2, images, 3 * tokens, channels), bf16),
                pltpu.VMEM((2, 2, images, 2 * HALO, channels), bf16),
                pltpu.VMEM((3 * tokens, 2 * tokens), f32),
                pltpu.VMEM((items, 3 * tokens, 2 * tokens), f32),
                pltpu.VMEM((items, 3 * tokens, 2 * tokens), f32),
                pltpu.VMEM((GROUPS, 3, 8, 2 * tokens), f32),
                pltpu.VMEM((2, GROUPS, 8, 2 * tokens), f32),
                pltpu.VMEM((2, GROUPS, 8, 2 * tokens), f32),
                pltpu.VMEM((GROUPS, 2, 8, 2 * tokens), f32),
                pltpu.VMEM((2, images, tokens, channels), f32),
                pltpu.VMEM((2, 2, images, 2 * HALO, channels), bf16),
                pltpu.VMEM((2, 2, images, 2 * HALO, channels), bf16),
                pltpu.VMEM((2, images, tokens, channels), f32),
                pltpu.VMEM((2, 2, images, tokens, channels), bf16),
                pltpu.VMEM((2, 2, images, tokens, channels), bf16),
                pltpu.VMEM((4, images, tokens, channels), bf16),
                dma((4,)),
                dma((GROUPS, 2, 2)),
                dma((GROUPS, 2, 2)),
                dma((GROUPS, 2)),
                dma((GROUPS, 2)),
                dma((GROUPS, 2)),
                dma((GROUPS, 2)),
                dma((GROUPS, 2)),
                dma((GROUPS, 2)),
                dma((GROUPS, 2)),
                dma((GROUPS, 2)),
                dma((GROUPS,)),
            ],
            compiler_params=pltpu.CompilerParams(
                collective_id=0, has_side_effects=True, vmem_limit_bytes=60 * 1024 * 1024
            ),
            cost_estimate=pl.CostEstimate(
                flops=12 * items * 192 * 128 * 128,
                bytes_accessed=8 * images * tokens * channels * 2,
                transcendentals=items * 192 * 128,
            ),
        )(
            block_lists.T,
            row_widths,
            queries.reshape(flat),
            key_states.reshape(flat),
            value_states.reshape(flat),
            out_grad.reshape(flat),
        )
        results = pl.pallas_call(
            split_kernel,
            out_shape=[jax.ShapeDtypeStruct(flat, bf16)] * 4,
            in_specs=[hbm_spec],
            out_specs=[hbm_spec] * 4,
            scratch_shapes=[dma((4,))],
            compiler_params=pltpu.CompilerParams(vmem_limit_bytes=60 * 1024 * 1024),
        )(stacked)
        return tuple(x.reshape(queries.shape) for x in results)

    split = P(None, "lat", "lon", None)
    return jax.shard_map(
        on_device,
        mesh=mesh,
        in_specs=(split, split, split, split, P(), P()),
        out_specs=(split, split, split, split),
        check_vma=False,
    )
```

```python
import functools
import math

import jax
import jax.numpy as jnp
from jax import lax
from jax.experimental import pallas as pl
from jax.experimental.pallas import tpu as pltpu
from jax.sharding import PartitionSpec as P

MESH = pl.DeviceIdType.MESH
HALO = 8
HDIM = 128
GROUPS = 4
AHEAD = 2
HIDDEN = -1e30
FLOOR = -1e29


def nt(a, b):
    return lax.dot_general(a, b, (((1,), (1,)), ((), ())), preferred_element_type=jnp.float32)


def tn(a, b):
    return lax.dot_general(a, b, (((0,), (0,)), ((), ())), preferred_element_type=jnp.float32)


def nn(a, b):
    return jnp.dot(a, b, preferred_element_type=jnp.float32)


def window(x, old, new, size, rest):
    lane = lax.broadcasted_iota(jnp.int32, x.shape, 1)
    shifted = x if old == new else pltpu.roll(x, (new - old) % HDIM, 1)
    return jnp.where((lane >= new) & (lane < new + size), shifted, rest)


def kernel(
    lon_count,
    lat_count,
    lists_ref,
    widths_ref,
    q_hbm,
    k_hbm,
    v_hbm,
    g_hbm,
    outs,
    near,
    far,
    edge_out,
    bias,
    exps,
    dps,
    stats,
    stats_out,
    stats_in,
    factors,
    near_acc,
    part_out,
    part_in,
    far_acc,
    term_out,
    term_in,
    own_sem,
    kv_send,
    kv_recv,
    edge_send,
    edge_recv,
    stat_send,
    stat_recv,
    part_send,
    part_recv,
    term_send,
    term_recv,
):
    lon = lax.axis_index("lon")
    lat = lax.axis_index("lat")
    left = lax.rem(lon + lon_count - 1, lon_count)
    right = lax.rem(lon + 1, lon_count)
    has_above = lat > 0
    has_below = lat < lat_count - 1
    images, tokens, channels = q_hbm.shape
    heads = channels // HDIM
    group_heads = heads // GROUPS
    group_items = images * group_heads
    group_lanes = group_heads * HDIM
    scale = HDIM ** -0.5

    sides = ({"lon": left}, {"lon": right})
    tiles = ({"lat": lat - 1}, {"lat": lat + 1})
    exists = (has_above, has_below)

    own_copies = [
        pltpu.make_async_copy(q_hbm, near.at[0, :, 0:tokens, :], own_sem.at[0]),
        pltpu.make_async_copy(g_hbm, near.at[1, :, 0:tokens, :], own_sem.at[1]),
        pltpu.make_async_copy(k_hbm, far.at[0, :, tokens : 2 * tokens, :], own_sem.at[2]),
        pltpu.make_async_copy(v_hbm, far.at[1, :, tokens : 2 * tokens, :], own_sem.at[3]),
    ]
    for copy in own_copies:
        copy.start()

    barrier = pltpu.get_barrier_semaphore()
    for side in sides:
        pl.semaphore_signal(barrier, inc=1, device_id=side, device_id_type=MESH)
    for there, tile in zip(exists, tiles):
        @pl.when(there)
        def _():
            pl.semaphore_signal(barrier, inc=1, device_id=tile, device_id_type=MESH)
    pl.semaphore_wait(barrier, 2 + jnp.where(has_above, 1, 0) + jnp.where(has_below, 1, 0))

    def lanes(group):
        start = group * group_lanes
        return pl.ds(start if isinstance(group, int) else pl.multiple_of(start, HDIM), group_lanes)

    def remote(source, target, send, recv, device):
        return pltpu.make_async_remote_copy(
            src_ref=source, dst_ref=target, send_sem=send, recv_sem=recv, device_id=device, device_id_type=MESH
        )

    def kv_copy(group, way, which):
        start = 2 * tokens if way == 0 else 0
        return remote(
            (k_hbm, v_hbm)[which].at[:, :, lanes(group)],
            far.at[which, :, start : start + tokens, lanes(group)],
            kv_send.at[group, way, which],
            kv_recv.at[group, 1 - way, which],
            tiles[way],
        )

    def edge_copy(group, way):
        start = tokens + 2 * HALO if way == 0 else tokens
        return remote(
            edge_out.at[way, :, :, :, lanes(group)],
            near.at[:, :, start : start + 2 * HALO, lanes(group)],
            edge_send.at[group, way],
            edge_recv.at[group, 1 - way],
            sides[way],
        )

    def stat_copy(group, way):
        return remote(
            stats_out.at[way, group],
            stats_in.at[1 - way, group],
            stat_send.at[group, way],
            stat_recv.at[group, 1 - way],
            sides[way],
        )

    def part_copy(group, way):
        return remote(
            part_out.at[way, :, :, :, lanes(group)],
            part_in.at[1 - way, :, :, :, lanes(group)],
            part_send.at[group, way],
            part_recv.at[group, 1 - way],
            sides[way],
        )

    def term_copy(group, way):
        return remote(
            term_out.at[way, :, :, :, lanes(group)],
            term_in.at[1 - way, :, :, :, lanes(group)],
            term_send.at[group, way],
            term_recv.at[group, 1 - way],
            tiles[way],
        )

    def send_kv(group):
        for way in range(2):
            @pl.when(exists[way])
            def _():
                kv_copy(group, way, 0).start()
                kv_copy(group, way, 1).start()

    def send_edges(group):
        for which in range(2):
            for image in range(images):
                def half(start, low):
                    block = near[which, image, start : start + 16, lanes(group)].astype(jnp.float32)
                    return block[low : low + HALO]

                edge_out[0, which, image, :, lanes(group)] = jnp.concatenate(
                    [half(0, 0), half(32, 0)], axis=0
                ).astype(jnp.bfloat16)
                edge_out[1, which, image, :, lanes(group)] = jnp.concatenate(
                    [half(16, HALO), half(48, HALO)], axis=0
                ).astype(jnp.bfloat16)
        for way in range(2):
            edge_copy(group, way).start()

    for group in range(AHEAD):
        send_kv(group)
    own_copies[0].wait()
    own_copies[1].wait()
    for group in range(AHEAD):
        send_edges(group)

    near[:, :, tokens + 4 * HALO :, :] = jnp.zeros(
        (2, images, near.shape[2] - tokens - 4 * HALO, channels), jnp.bfloat16
    )
    for way in range(2):
        @pl.when(jnp.logical_not(exists[way]))
        def _():
            start = 0 if way == 0 else 2 * tokens
            far[:, :, start : start + tokens, :] = jnp.zeros((2, images, tokens, channels), jnp.bfloat16)
            term_in[way] = jnp.zeros((2, images, tokens, channels), jnp.bfloat16)

    def listed(target):
        found = (
            (lists_ref[0, lat] == target)
            | (lists_ref[1, lat] == target)
            | (lists_ref[2, lat] == target)
        ) & (target >= 0)
        return jnp.where(found, 1, 0)

    shape = bias.shape
    key = lax.broadcasted_iota(jnp.int32, shape, 0)
    query = lax.broadcasted_iota(jnp.int32, shape, 1)
    key_tile = key >> 6
    key_col = key & 31
    edge = query - tokens
    is_own = query < tokens
    from_left = edge < 2 * HALO
    query_col = jnp.where(is_own, query & 31, jnp.where(from_left, (edge & 7) - HALO, 32 + (edge & 7)))
    query_row = jnp.where(is_own, query >> 5, (edge >> 3) & 1)
    width = jnp.where(query_row == 0, widths_ref[2 * lat], widths_ref[2 * lat + 1])
    active = jnp.where(
        key_tile == 0, listed(lat - 1), jnp.where(key_tile == 1, listed(lat), listed(lat + 1))
    )
    seen = (jnp.abs(query_col - key_col) <= width) & (active == 1) & (edge < 4 * HALO)
    bias[...] = jnp.where(seen, 0.0, HIDDEN)

    own_copies[2].wait()
    own_copies[3].wait()

    def place(group, item):
        image = item // group_heads
        head = item % group_heads
        return image, pl.ds(pl.multiple_of(group * group_lanes + head * HDIM, HDIM), HDIM)

    def wait_inputs(group):
        for origin in range(2):
            @pl.when(exists[origin])
            def _():
                kv_copy(group, 1 - origin, 0).wait_recv()
                kv_copy(group, 1 - origin, 1).wait_recv()
        for origin in range(2):
            edge_copy(group, 1 - origin).wait_recv()

    def scores(group):
        def body(item, carry):
            image, cols = place(group, item)
            queries = near[0, image, :, cols]
            grads = near[1, image, :, cols]
            keys = far[0, image, :, cols]
            values = far[1, image, :, cols]
            raw = nt(keys, queries) * (scale * math.log2(math.e)) + bias[...]
            dp = nt(values, grads)
            top = jnp.maximum(jnp.max(raw, axis=0, keepdims=True), FLOOR)
            e = jnp.exp2(raw - top)
            slot = group * group_items + item
            exps[slot] = e
            dps[slot] = dp
            stats[group, 0, pl.ds(item, 1), :] = top
            stats[group, 1, pl.ds(item, 1), :] = jnp.sum(e, axis=0, keepdims=True)
            stats[group, 2, pl.ds(item, 1), :] = jnp.sum(e * dp, axis=0, keepdims=True)
            return carry

        lax.fori_loop(0, group_items, body, 0, unroll=4)
        for way, moves in enumerate((((0, 0, 8), (32, 8, 8), (64, 16, 16)), ((24, 0, 8), (56, 8, 8), (80, 16, 16)))):
            packed = jnp.zeros((8, HDIM), jnp.float32)
            for kind in range(3):
                for old, new, size in moves:
                    packed = window(stats[group, kind], old, 32 * kind + new, size, packed)
            stats_out[way, group] = packed
        for way in range(2):
            stat_copy(group, way).start()

    def combine(group):
        for way in range(2):
            stat_copy(group, way).wait_recv()
        others = []
        for kind in range(3):
            other = jnp.full((8, HDIM), FLOOR if kind == 0 else 0.0, jnp.float32)
            for origin, moves in enumerate((((0, 64, 16), (16, 0, 8), (24, 32, 8)), ((0, 80, 16), (16, 24, 8), (24, 56, 8)))):
                for old, new, size in moves:
                    other = window(stats_in[origin, group], 32 * kind + old, new, size, other)
            others.append(other)
        top, total, balance = (stats[group, kind] for kind in range(3))
        top2, total2, balance2 = others
        high = jnp.maximum(top, top2)
        part = jnp.exp2(top - high)
        part2 = jnp.exp2(top2 - high)
        inverse = 1.0 / jnp.maximum(part * total + part2 * total2, 0.5)
        factors[group, 0] = part * inverse
        factors[group, 1] = (part * balance + part2 * balance2) * inverse

    def gradients(group):
        def body(item, carry):
            image, cols = place(group, item)
            queries = near[0, image, :, cols]
            grads = near[1, image, :, cols]
            keys = far[0, image, :, cols]
            values = far[1, image, :, cols]
            slot = group * group_items + item
            w = exps[slot] * factors[group, 0, pl.ds(item, 1), :]
            ds = w * (dps[slot] - factors[group, 1, pl.ds(item, 1), :])
            w = w.astype(jnp.bfloat16)
            ds = ds.astype(jnp.bfloat16)
            att = tn(w, values)
            dq = tn(ds, keys) * scale
            dv = nn(w, grads)
            dk = nn(ds, queries) * scale
            for which, x in enumerate((att, dq)):
                near_acc[which, image, :, cols] = x[0:tokens]
                for way in range(2):
                    start = tokens + 2 * HALO * way
                    part_out[way, which, image, :, cols] = x[start : start + 2 * HALO].astype(jnp.bfloat16)
            for which, x in enumerate((dk, dv)):
                far_acc[which, image, :, cols] = x[tokens : 2 * tokens]
                term_out[0, which, image, :, cols] = x[0:tokens].astype(jnp.bfloat16)
                term_out[1, which, image, :, cols] = x[2 * tokens :].astype(jnp.bfloat16)
            return carry

        lax.fori_loop(0, group_items, body, 0, unroll=4)
        for way in range(2):
            @pl.when(exists[way])
            def _():
                term_copy(group, way).start()
        for way in range(2):
            part_copy(group, way).start()

    def finish(group):
        for way in range(2):
            part_copy(group, way).wait_recv()
        for way in range(2):
            @pl.when(exists[way])
            def _():
                term_copy(group, 1 - way).wait_recv()

        def body(item, carry):
            image, cols = place(group, item)
            for which in range(2):
                acc = near_acc[which, image, :, cols]
                add_l = part_in[0, which, image, :, cols].astype(jnp.float32)
                add_r = part_in[1, which, image, :, cols].astype(jnp.float32)
                rows = []
                for r in range(2):
                    here = acc[32 * r : 32 * r + 32]
                    rows.append(here[0:8] + add_l[8 * r : 8 * r + 8])
                    rows.append(here[8:24])
                    rows.append(here[24:32] + add_r[8 * r : 8 * r + 8])
                outs[which, image, :, cols] = jnp.concatenate(rows, axis=0).astype(jnp.bfloat16)
            for which in range(2):
                total = far_acc[which, image, :, cols]
                for way in range(2):
                    total = total + term_in[way, which, image, :, cols].astype(jnp.float32)
                outs[2 + which, image, :, cols] = total.astype(jnp.bfloat16)
            return carry

        lax.fori_loop(0, group_items, body, 0, unroll=4)

    def step(index, carry):
        @pl.when(index < GROUPS)
        def _():
            wait_inputs(index)

            @pl.when(index + AHEAD < GROUPS)
            def _():
                send_kv(index + AHEAD)
                send_edges(index + AHEAD)

            scores(index)

        @pl.when((index >= 1) & (index <= GROUPS))
        def _():
            combine(index - 1)
            gradients(index - 1)

        @pl.when(index >= 2)
        def _():
            finish(index - 2)

        return carry

    lax.fori_loop(0, GROUPS + 2, step, 0)

    def drain(group, carry):
        for way in range(2):
            edge_copy(group, way).wait_send()
            stat_copy(group, way).wait_send()
            part_copy(group, way).wait_send()

            @pl.when(exists[way])
            def _():
                kv_copy(group, way, 0).wait_send()
                kv_copy(group, way, 1).wait_send()
                term_copy(group, way).wait_send()

        return carry

    lax.fori_loop(0, GROUPS, drain, 0)


def split_kernel(stacked, *refs):
    outs, sem = refs[:4], refs[4]
    copies = [pltpu.make_async_copy(stacked.at[i], outs[i], sem.at[i]) for i in range(4)]
    for copy in copies:
        copy.start()
    for copy in copies:
        copy.wait()


def solution(mesh):
    lon_count = mesh.shape["lon"]
    lat_count = mesh.shape["lat"]

    def on_device(queries, key_states, value_states, out_grad, block_lists, row_widths):
        images, rows, columns, channels = queries.shape
        tokens = rows * columns
        flat = (images, tokens, channels)
        items = images * channels // HDIM
        bf16, f32 = jnp.bfloat16, jnp.float32
        hbm_spec = pl.BlockSpec(memory_space=pltpu.HBM)
        vmem_spec = pl.BlockSpec(memory_space=pltpu.VMEM)
        smem_spec = pl.BlockSpec(memory_space=pltpu.SMEM)
        dma = pltpu.SemaphoreType.DMA
        stacked = pl.pallas_call(
            functools.partial(kernel, lon_count, lat_count),
            out_shape=pltpu.VMEM((4,) + flat, bf16),
            in_specs=[smem_spec, smem_spec] + [hbm_spec] * 4,
            out_specs=vmem_spec,
            scratch_shapes=[
                pltpu.VMEM((2, images, 2 * tokens, channels), bf16),
                pltpu.VMEM((2, images, 3 * tokens, channels), bf16),
                pltpu.VMEM((2, 2, images, 2 * HALO, channels), bf16),
                pltpu.VMEM((3 * tokens, 2 * tokens), f32),
                pltpu.VMEM((items, 3 * tokens, 2 * tokens), f32),
                pltpu.VMEM((items, 3 * tokens, 2 * tokens), f32),
                pltpu.VMEM((GROUPS, 3, 8, 2 * tokens), f32),
                pltpu.VMEM((2, GROUPS, 8, 2 * tokens), f32),
                pltpu.VMEM((2, GROUPS, 8, 2 * tokens), f32),
                pltpu.VMEM((GROUPS, 2, 8, 2 * tokens), f32),
                pltpu.VMEM((2, images, tokens, channels), f32),
                pltpu.VMEM((2, 2, images, 2 * HALO, channels), bf16),
                pltpu.VMEM((2, 2, images, 2 * HALO, channels), bf16),
                pltpu.VMEM((2, images, tokens, channels), f32),
                pltpu.VMEM((2, 2, images, tokens, channels), bf16),
                pltpu.VMEM((2, 2, images, tokens, channels), bf16),
                dma((4,)),
                dma((GROUPS, 2, 2)),
                dma((GROUPS, 2, 2)),
                dma((GROUPS, 2)),
                dma((GROUPS, 2)),
                dma((GROUPS, 2)),
                dma((GROUPS, 2)),
                dma((GROUPS, 2)),
                dma((GROUPS, 2)),
                dma((GROUPS, 2)),
                dma((GROUPS, 2)),
            ],
            compiler_params=pltpu.CompilerParams(
                collective_id=0, has_side_effects=True, vmem_limit_bytes=60 * 1024 * 1024
            ),
            cost_estimate=pl.CostEstimate(
                flops=12 * items * 192 * 128 * 128,
                bytes_accessed=8 * images * tokens * channels * 2,
                transcendentals=items * 192 * 128,
            ),
        )(
            block_lists.T,
            row_widths,
            queries.reshape(flat),
            key_states.reshape(flat),
            value_states.reshape(flat),
            out_grad.reshape(flat),
        )
        results = pl.pallas_call(
            split_kernel,
            out_shape=[jax.ShapeDtypeStruct(flat, bf16)] * 4,
            in_specs=[pl.BlockSpec(memory_space=pl.ANY)],
            out_specs=[hbm_spec] * 4,
            scratch_shapes=[dma((4,))],
            compiler_params=pltpu.CompilerParams(vmem_limit_bytes=8 * 1024 * 1024),
        )(stacked)
        return tuple(x.reshape(queries.shape) for x in results)

    split = P(None, "lat", "lon", None)
    return jax.shard_map(
        on_device,
        mesh=mesh,
        in_specs=(split, split, split, split, P(), P()),
        out_specs=(split, split, split, split),
        check_vma=False,
    )
```

```python
import functools
import math

import jax
import jax.numpy as jnp
from jax import lax
from jax.experimental import pallas as pl
from jax.experimental.pallas import tpu as pltpu
from jax.sharding import PartitionSpec as P

MESH = pl.DeviceIdType.MESH
HALO = 8
HDIM = 128
GROUPS = 4
AHEAD = 2
HIDDEN = -1e30
FLOOR = -1e29


def nt(a, b):
    return lax.dot_general(a, b, (((1,), (1,)), ((), ())), preferred_element_type=jnp.float32)


def tn(a, b):
    return lax.dot_general(a, b, (((0,), (0,)), ((), ())), preferred_element_type=jnp.float32)


def nn(a, b):
    return jnp.dot(a, b, preferred_element_type=jnp.float32)


def window(x, old, new, size, rest):
    lane = lax.broadcasted_iota(jnp.int32, x.shape, 1)
    shifted = x if old == new else pltpu.roll(x, (new - old) % HDIM, 1)
    return jnp.where((lane >= new) & (lane < new + size), shifted, rest)


def kernel(
    lon_count,
    lat_count,
    lists_ref,
    widths_ref,
    q_hbm,
    k_hbm,
    v_hbm,
    g_hbm,
    outs,
    near,
    far,
    edge_out,
    bias,
    exps,
    dps,
    stats,
    stats_out,
    stats_in,
    factors,
    near_acc,
    part_out,
    part_in,
    far_acc,
    term_out,
    term_in,
    relay,
    own_sem,
    kv_send,
    kv_recv,
    edge_send,
    edge_recv,
    stat_send,
    stat_recv,
    part_send,
    part_recv,
    term_send,
    term_recv,
    pass_send,
    pass_recv,
    relay_send,
):
    lon = lax.axis_index("lon")
    lat = lax.axis_index("lat")
    left = lax.rem(lon + lon_count - 1, lon_count)
    right = lax.rem(lon + 1, lon_count)
    has_above = lat > 0
    has_below = lat < lat_count - 1
    middle = lat_count // 2
    beside = lon + 1 - 2 * lax.rem(lon, 2)
    is_middle = (lat == middle - 1) | (lat == middle)
    is_end = (lat == 0) | (lat == lat_count - 1)
    routes = ((middle, 0, middle - 1), (middle - 1, lat_count - 1, middle))
    images, tokens, channels = q_hbm.shape
    heads = channels // HDIM
    group_heads = heads // GROUPS
    group_items = images * group_heads
    group_lanes = group_heads * HDIM
    scale = HDIM ** -0.5

    sides = ({"lon": left}, {"lon": right})
    tiles = ({"lat": lat - 1}, {"lat": lat + 1})
    exists = (has_above, has_below)

    own_copies = [
        pltpu.make_async_copy(q_hbm, near.at[0, :, 0:tokens, :], own_sem.at[0]),
        pltpu.make_async_copy(g_hbm, near.at[1, :, 0:tokens, :], own_sem.at[1]),
        pltpu.make_async_copy(k_hbm, far.at[0, :, tokens : 2 * tokens, :], own_sem.at[2]),
        pltpu.make_async_copy(v_hbm, far.at[1, :, tokens : 2 * tokens, :], own_sem.at[3]),
    ]
    for copy in own_copies:
        copy.start()

    barrier = pltpu.get_barrier_semaphore()
    for side in sides:
        pl.semaphore_signal(barrier, inc=1, device_id=side, device_id_type=MESH)
    for there, tile in zip(exists, tiles):
        @pl.when(there)
        def _():
            pl.semaphore_signal(barrier, inc=1, device_id=tile, device_id_type=MESH)
    for here, far_lats in ((is_middle, (0, lat_count - 1)), (is_end, (middle - 1, middle))):
        @pl.when(here)
        def _():
            for far_lat in far_lats:
                pl.semaphore_signal(barrier, inc=1, device_id={"lat": far_lat, "lon": beside}, device_id_type=MESH)
    pl.semaphore_wait(
        barrier,
        2
        + jnp.where(has_above, 1, 0)
        + jnp.where(has_below, 1, 0)
        + jnp.where(is_middle | is_end, 2, 0),
    )

    def lanes(group):
        start = group * group_lanes
        return pl.ds(start if isinstance(group, int) else pl.multiple_of(start, HDIM), group_lanes)

    def remote(source, target, send, recv, device):
        return pltpu.make_async_remote_copy(
            src_ref=source, dst_ref=target, send_sem=send, recv_sem=recv, device_id=device, device_id_type=MESH
        )

    def kv_copy(group, way, which):
        start = 2 * tokens if way == 0 else 0
        return remote(
            (k_hbm, v_hbm)[which].at[:, :, lanes(group)],
            far.at[which, :, start : start + tokens, lanes(group)],
            kv_send.at[group, way, which],
            kv_recv.at[group, 1 - way, which],
            tiles[way],
        )

    def edge_copy(group, way):
        start = tokens + 2 * HALO if way == 0 else tokens
        return remote(
            edge_out.at[way, :, :, :, lanes(group)],
            near.at[:, :, start : start + 2 * HALO, lanes(group)],
            edge_send.at[group, way],
            edge_recv.at[group, 1 - way],
            sides[way],
        )

    def stat_copy(group, way):
        return remote(
            stats_out.at[way, group],
            stats_in.at[1 - way, group],
            stat_send.at[group, way],
            stat_recv.at[group, 1 - way],
            sides[way],
        )

    def part_copy(group, way):
        return remote(
            part_out.at[way, :, :, :, lanes(group)],
            part_in.at[1 - way, :, :, :, lanes(group)],
            part_send.at[group, way],
            part_recv.at[group, 1 - way],
            sides[way],
        )

    def term_copy(group, way, which):
        return remote(
            term_out.at[way, which, :, :, lanes(group)],
            term_in.at[1 - way, which, :, :, lanes(group)],
            term_send.at[group, way, which],
            term_recv.at[group, 1 - way, which],
            tiles[way],
        )

    def pass_copy(group, way, kind):
        return remote(
            v_hbm.at[:, :, lanes(group)] if kind == 0 else term_out.at[way, 1, :, :, lanes(group)],
            relay.at[kind, :, :, lanes(group)],
            pass_send.at[group, kind],
            pass_recv.at[group, kind],
            {"lat": routes[way][1], "lon": beside},
        )

    def relay_copy(group, way, kind):
        start = 2 * tokens if way == 0 else 0
        target = far.at[1, :, start : start + tokens, lanes(group)]
        return remote(
            relay.at[kind, :, :, lanes(group)],
            target if kind == 0 else term_in.at[1 - way, 1, :, :, lanes(group)],
            relay_send.at[group, kind],
            (kv_recv if kind == 0 else term_recv).at[group, 1 - way, 1],
            {"lat": routes[way][2], "lon": beside},
        )

    def relayed(group, kind):
        return True if kind == 0 else group < GROUPS - 1

    def each_way(group, kind, direct, passing):
        for way in range(2):
            by_relay = (lat == routes[way][0]) & relayed(group, kind)

            @pl.when(exists[way] & jnp.logical_not(by_relay))
            def _():
                direct(way)

            @pl.when(by_relay)
            def _():
                passing(way)

    def forward(group, kind):
        for way in range(2):
            @pl.when((lat == routes[way][1]) & relayed(group, kind))
            def _():
                pass_copy(group, way, kind).wait_recv()
                relay_copy(group, way, kind).start()

    def send_kv(group):
        for way in range(2):
            @pl.when(exists[way])
            def _():
                kv_copy(group, way, 0).start()

        each_way(
            group,
            0,
            lambda way: kv_copy(group, way, 1).start(),
            lambda way: pass_copy(group, way, 0).start(),
        )

    def send_edges(group):
        for which in range(2):
            for image in range(images):
                def half(start, low):
                    block = near[which, image, start : start + 16, lanes(group)].astype(jnp.float32)
                    return block[low : low + HALO]

                edge_out[0, which, image, :, lanes(group)] = jnp.concatenate(
                    [half(0, 0), half(32, 0)], axis=0
                ).astype(jnp.bfloat16)
                edge_out[1, which, image, :, lanes(group)] = jnp.concatenate(
                    [half(16, HALO), half(48, HALO)], axis=0
                ).astype(jnp.bfloat16)
        for way in range(2):
            edge_copy(group, way).start()

    for group in range(AHEAD):
        send_kv(group)
    own_copies[0].wait()
    own_copies[1].wait()
    for group in range(AHEAD):
        send_edges(group)

    near[:, :, tokens + 4 * HALO :, :] = jnp.zeros(
        (2, images, near.shape[2] - tokens - 4 * HALO, channels), jnp.bfloat16
    )
    for way in range(2):
        @pl.when(jnp.logical_not(exists[way]))
        def _():
            start = 0 if way == 0 else 2 * tokens
            far[:, :, start : start + tokens, :] = jnp.zeros((2, images, tokens, channels), jnp.bfloat16)
            term_in[way] = jnp.zeros((2, images, tokens, channels), jnp.bfloat16)

    def listed(target):
        found = (
            (lists_ref[0, lat] == target)
            | (lists_ref[1, lat] == target)
            | (lists_ref[2, lat] == target)
        ) & (target >= 0)
        return jnp.where(found, 1, 0)

    shape = bias.shape
    key = lax.broadcasted_iota(jnp.int32, shape, 0)
    query = lax.broadcasted_iota(jnp.int32, shape, 1)
    key_tile = key >> 6
    key_col = key & 31
    edge = query - tokens
    is_own = query < tokens
    from_left = edge < 2 * HALO
    query_col = jnp.where(is_own, query & 31, jnp.where(from_left, (edge & 7) - HALO, 32 + (edge & 7)))
    query_row = jnp.where(is_own, query >> 5, (edge >> 3) & 1)
    width = jnp.where(query_row == 0, widths_ref[2 * lat], widths_ref[2 * lat + 1])
    active = jnp.where(
        key_tile == 0, listed(lat - 1), jnp.where(key_tile == 1, listed(lat), listed(lat + 1))
    )
    seen = (jnp.abs(query_col - key_col) <= width) & (active == 1) & (edge < 4 * HALO)
    bias[...] = jnp.where(seen, 0.0, HIDDEN)

    own_copies[2].wait()
    own_copies[3].wait()

    def place(group, item):
        image = item // group_heads
        head = item % group_heads
        return image, pl.ds(pl.multiple_of(group * group_lanes + head * HDIM, HDIM), HDIM)

    def wait_inputs(group):
        for origin in range(2):
            @pl.when(exists[origin])
            def _():
                kv_copy(group, 1 - origin, 0).wait_recv()
                kv_copy(group, 1 - origin, 1).wait_recv()
        for origin in range(2):
            edge_copy(group, 1 - origin).wait_recv()

    def scores(group):
        def body(item, carry):
            image, cols = place(group, item)
            queries = near[0, image, :, cols]
            grads = near[1, image, :, cols]
            keys = far[0, image, :, cols]
            values = far[1, image, :, cols]
            raw = nt(keys, queries) * (scale * math.log2(math.e)) + bias[...]
            dp = nt(values, grads)
            top = jnp.maximum(jnp.max(raw, axis=0, keepdims=True), FLOOR)
            e = jnp.exp2(raw - top)
            slot = group * group_items + item
            exps[slot] = e
            dps[slot] = dp
            stats[group, 0, pl.ds(item, 1), :] = top
            stats[group, 1, pl.ds(item, 1), :] = jnp.sum(e, axis=0, keepdims=True)
            stats[group, 2, pl.ds(item, 1), :] = jnp.sum(e * dp, axis=0, keepdims=True)
            return carry

        lax.fori_loop(0, group_items, body, 0, unroll=4)
        for way, moves in enumerate((((0, 0, 8), (32, 8, 8), (64, 16, 16)), ((24, 0, 8), (56, 8, 8), (80, 16, 16)))):
            packed = jnp.zeros((8, HDIM), jnp.float32)
            for kind in range(3):
                for old, new, size in moves:
                    packed = window(stats[group, kind], old, 32 * kind + new, size, packed)
            stats_out[way, group] = packed
        for way in range(2):
            stat_copy(group, way).start()

    def combine(group):
        for way in range(2):
            stat_copy(group, way).wait_recv()
        others = []
        for kind in range(3):
            other = jnp.full((8, HDIM), FLOOR if kind == 0 else 0.0, jnp.float32)
            for origin, moves in enumerate((((0, 64, 16), (16, 0, 8), (24, 32, 8)), ((0, 80, 16), (16, 24, 8), (24, 56, 8)))):
                for old, new, size in moves:
                    other = window(stats_in[origin, group], 32 * kind + old, new, size, other)
            others.append(other)
        top, total, balance = (stats[group, kind] for kind in range(3))
        top2, total2, balance2 = others
        high = jnp.maximum(top, top2)
        part = jnp.exp2(top - high)
        part2 = jnp.exp2(top2 - high)
        inverse = 1.0 / jnp.maximum(part * total + part2 * total2, 0.5)
        factors[group, 0] = part * inverse
        factors[group, 1] = (part * balance + part2 * balance2) * inverse

    def gradients(group):
        def body(item, carry):
            image, cols = place(group, item)
            queries = near[0, image, :, cols]
            grads = near[1, image, :, cols]
            keys = far[0, image, :, cols]
            values = far[1, image, :, cols]
            slot = group * group_items + item
            w = exps[slot] * factors[group, 0, pl.ds(item, 1), :]
            ds = w * (dps[slot] - factors[group, 1, pl.ds(item, 1), :])
            w = w.astype(jnp.bfloat16)
            ds = ds.astype(jnp.bfloat16)
            att = tn(w, values)
            dq = tn(ds, keys) * scale
            dv = nn(w, grads)
            dk = nn(ds, queries) * scale
            for which, x in enumerate((att, dq)):
                near_acc[which, image, :, cols] = x[0:tokens]
                for way in range(2):
                    start = tokens + 2 * HALO * way
                    part_out[way, which, image, :, cols] = x[start : start + 2 * HALO].astype(jnp.bfloat16)
            for which, x in enumerate((dk, dv)):
                far_acc[which, image, :, cols] = x[tokens : 2 * tokens]
                term_out[0, which, image, :, cols] = x[0:tokens].astype(jnp.bfloat16)
                term_out[1, which, image, :, cols] = x[2 * tokens :].astype(jnp.bfloat16)
            return carry

        lax.fori_loop(0, group_items, body, 0, unroll=4)
        for way in range(2):
            @pl.when(exists[way])
            def _():
                term_copy(group, way, 0).start()

        each_way(
            group,
            1,
            lambda way: term_copy(group, way, 1).start(),
            lambda way: pass_copy(group, way, 1).start(),
        )
        for way in range(2):
            part_copy(group, way).start()

    def finish(group):
        for way in range(2):
            part_copy(group, way).wait_recv()
        for way in range(2):
            @pl.when(exists[way])
            def _():
                term_copy(group, 1 - way, 0).wait_recv()
                term_copy(group, 1 - way, 1).wait_recv()

        def body(item, carry):
            image, cols = place(group, item)
            for which in range(2):
                acc = near_acc[which, image, :, cols]
                add_l = part_in[0, which, image, :, cols].astype(jnp.float32)
                add_r = part_in[1, which, image, :, cols].astype(jnp.float32)
                rows = []
                for r in range(2):
                    here = acc[32 * r : 32 * r + 32]
                    rows.append(here[0:8] + add_l[8 * r : 8 * r + 8])
                    rows.append(here[8:24])
                    rows.append(here[24:32] + add_r[8 * r : 8 * r + 8])
                outs[which, image, :, cols] = jnp.concatenate(rows, axis=0).astype(jnp.bfloat16)
            for which in range(2):
                total = far_acc[which, image, :, cols]
                for way in range(2):
                    total = total + term_in[way, which, image, :, cols].astype(jnp.float32)
                outs[2 + which, image, :, cols] = total.astype(jnp.bfloat16)
            return carry

        lax.fori_loop(0, group_items, body, 0, unroll=4)

    def step(index, carry):
        @pl.when(index < GROUPS)
        def _():
            wait_inputs(index)

            @pl.when(index + AHEAD < GROUPS)
            def _():
                send_kv(index + AHEAD)
                send_edges(index + AHEAD)

            forward(index, 0)
            scores(index)

        @pl.when((index >= 2) & (index <= GROUPS))
        def _():
            forward(index - 2, 1)

        @pl.when((index >= 1) & (index <= GROUPS))
        def _():
            combine(index - 1)
            gradients(index - 1)

        @pl.when(index >= 2)
        def _():
            finish(index - 2)

        return carry

    lax.fori_loop(0, GROUPS + 2, step, 0)

    def drain(group, carry):
        for way in range(2):
            edge_copy(group, way).wait_send()
            stat_copy(group, way).wait_send()
            part_copy(group, way).wait_send()

            @pl.when(exists[way])
            def _():
                kv_copy(group, way, 0).wait_send()
                term_copy(group, way, 0).wait_send()

        each_way(
            group,
            0,
            lambda way: kv_copy(group, way, 1).wait_send(),
            lambda way: pass_copy(group, way, 0).wait_send(),
        )
        each_way(
            group,
            1,
            lambda way: term_copy(group, way, 1).wait_send(),
            lambda way: pass_copy(group, way, 1).wait_send(),
        )
        for way in range(2):
            for kind in range(2):
                @pl.when((lat == routes[way][1]) & relayed(group, kind))
                def _():
                    relay_copy(group, way, kind).wait_send()

        return carry

    lax.fori_loop(0, GROUPS, drain, 0)


def split_kernel(stacked, *refs):
    outs, sem = refs[:4], refs[4]
    copies = [pltpu.make_async_copy(stacked.at[i], outs[i], sem.at[i]) for i in range(4)]
    for copy in copies:
        copy.start()
    for copy in copies:
        copy.wait()


def solution(mesh):
    lon_count = mesh.shape["lon"]
    lat_count = mesh.shape["lat"]

    def on_device(queries, key_states, value_states, out_grad, block_lists, row_widths):
        images, rows, columns, channels = queries.shape
        tokens = rows * columns
        flat = (images, tokens, channels)
        items = images * channels // HDIM
        bf16, f32 = jnp.bfloat16, jnp.float32
        hbm_spec = pl.BlockSpec(memory_space=pltpu.HBM)
        vmem_spec = pl.BlockSpec(memory_space=pltpu.VMEM)
        smem_spec = pl.BlockSpec(memory_space=pltpu.SMEM)
        dma = pltpu.SemaphoreType.DMA
        stacked = pl.pallas_call(
            functools.partial(kernel, lon_count, lat_count),
            out_shape=pltpu.VMEM((4,) + flat, bf16),
            in_specs=[smem_spec, smem_spec] + [hbm_spec] * 4,
            out_specs=vmem_spec,
            scratch_shapes=[
                pltpu.VMEM((2, images, 2 * tokens, channels), bf16),
                pltpu.VMEM((2, images, 3 * tokens, channels), bf16),
                pltpu.VMEM((2, 2, images, 2 * HALO, channels), bf16),
                pltpu.VMEM((3 * tokens, 2 * tokens), f32),
                pltpu.VMEM((items, 3 * tokens, 2 * tokens), f32),
                pltpu.VMEM((items, 3 * tokens, 2 * tokens), f32),
                pltpu.VMEM((GROUPS, 3, 8, 2 * tokens), f32),
                pltpu.VMEM((2, GROUPS, 8, 2 * tokens), f32),
                pltpu.VMEM((2, GROUPS, 8, 2 * tokens), f32),
                pltpu.VMEM((GROUPS, 2, 8, 2 * tokens), f32),
                pltpu.VMEM((2, images, tokens, channels), f32),
                pltpu.VMEM((2, 2, images, 2 * HALO, channels), bf16),
                pltpu.VMEM((2, 2, images, 2 * HALO, channels), bf16),
                pltpu.VMEM((2, images, tokens, channels), f32),
                pltpu.VMEM((2, 2, images, tokens, channels), bf16),
                pltpu.VMEM((2, 2, images, tokens, channels), bf16),
                pltpu.VMEM((2, images, tokens, channels), bf16),
                dma((4,)),
                dma((GROUPS, 2, 2)),
                dma((GROUPS, 2, 2)),
                dma((GROUPS, 2)),
                dma((GROUPS, 2)),
                dma((GROUPS, 2)),
                dma((GROUPS, 2)),
                dma((GROUPS, 2)),
                dma((GROUPS, 2)),
                dma((GROUPS, 2, 2)),
                dma((GROUPS, 2, 2)),
                dma((GROUPS, 2)),
                dma((GROUPS, 2)),
                dma((GROUPS, 2)),
            ],
            compiler_params=pltpu.CompilerParams(
                collective_id=0, has_side_effects=True, vmem_limit_bytes=60 * 1024 * 1024
            ),
            cost_estimate=pl.CostEstimate(
                flops=12 * items * 192 * 128 * 128,
                bytes_accessed=8 * images * tokens * channels * 2,
                transcendentals=items * 192 * 128,
            ),
        )(
            block_lists.T,
            row_widths,
            queries.reshape(flat),
            key_states.reshape(flat),
            value_states.reshape(flat),
            out_grad.reshape(flat),
        )
        results = pl.pallas_call(
            split_kernel,
            out_shape=[jax.ShapeDtypeStruct(flat, bf16)] * 4,
            in_specs=[pl.BlockSpec(memory_space=pl.ANY)],
            out_specs=[hbm_spec] * 4,
            scratch_shapes=[dma((4,))],
            compiler_params=pltpu.CompilerParams(vmem_limit_bytes=8 * 1024 * 1024),
        )(stacked)
        return tuple(x.reshape(queries.shape) for x in results)

    split = P(None, "lat", "lon", None)
    return jax.shard_map(
        on_device,
        mesh=mesh,
        in_specs=(split, split, split, split, P(), P()),
        out_specs=(split, split, split, split),
        check_vma=False,
    )
```

```python
import functools
import math

import jax
import jax.numpy as jnp
from jax import lax
from jax.experimental import pallas as pl
from jax.experimental.pallas import tpu as pltpu
from jax.sharding import PartitionSpec as P

MESH = pl.DeviceIdType.MESH
HALO = 8
HDIM = 128
GROUPS = 8
AHEAD = 3
LAG = 4
HIDDEN = -1e30
FLOOR = -1e29


def nt(a, b):
    return lax.dot_general(a, b, (((1,), (1,)), ((), ())), preferred_element_type=jnp.float32)


def tn(a, b):
    return lax.dot_general(a, b, (((0,), (0,)), ((), ())), preferred_element_type=jnp.float32)


def nn(a, b):
    return jnp.dot(a, b, preferred_element_type=jnp.float32)


def window(x, old, new, size, rest):
    lane = lax.broadcasted_iota(jnp.int32, x.shape, 1)
    shifted = x if old == new else pltpu.roll(x, (new - old) % HDIM, 1)
    return jnp.where((lane >= new) & (lane < new + size), shifted, rest)


def kernel(
    lon_count,
    lat_count,
    lists_ref,
    widths_ref,
    q_hbm,
    k_hbm,
    v_hbm,
    g_hbm,
    outs,
    near,
    far,
    edge_out,
    bias,
    exps,
    dps,
    stats,
    stats_out,
    stats_in,
    factors,
    near_acc,
    part_out,
    part_in,
    far_acc,
    term_out,
    term_in,
    relay,
    own_sem,
    kv_send,
    kv_recv,
    edge_send,
    edge_recv,
    stat_send,
    stat_recv,
    part_send,
    part_recv,
    term_send,
    term_recv,
    pass_send,
    pass_recv,
    relay_send,
):
    lon = lax.axis_index("lon")
    lat = lax.axis_index("lat")
    left = lax.rem(lon + lon_count - 1, lon_count)
    right = lax.rem(lon + 1, lon_count)
    has_above = lat > 0
    has_below = lat < lat_count - 1
    middle = lat_count // 2
    beside = lon + 1 - 2 * lax.rem(lon, 2)
    is_middle = (lat == middle - 1) | (lat == middle)
    is_end = (lat == 0) | (lat == lat_count - 1)
    routes = ((middle, 0, middle - 1), (middle - 1, lat_count - 1, middle))
    images, tokens, channels = q_hbm.shape
    heads = channels // HDIM
    group_heads = heads // GROUPS
    group_items = images * group_heads
    group_lanes = group_heads * HDIM
    scale = HDIM ** -0.5
    half = images // 2
    whole, direct, passing = slice(0, images), slice(0, half), slice(half, images)

    sides = ({"lon": left}, {"lon": right})
    tiles = ({"lat": lat - 1}, {"lat": lat + 1})
    exists = (has_above, has_below)

    own_copies = [
        pltpu.make_async_copy(k_hbm, far.at[0, :, tokens : 2 * tokens, :], own_sem.at[0]),
        pltpu.make_async_copy(v_hbm, far.at[1, :, tokens : 2 * tokens, :], own_sem.at[1]),
        pltpu.make_async_copy(q_hbm, near.at[0, :, 0:tokens, :], own_sem.at[2]),
        pltpu.make_async_copy(g_hbm, near.at[1, :, 0:tokens, :], own_sem.at[3]),
    ]
    for copy in own_copies:
        copy.start()

    barrier = pltpu.get_barrier_semaphore()
    for side in sides:
        pl.semaphore_signal(barrier, inc=1, device_id=side, device_id_type=MESH)
    for there, tile in zip(exists, tiles):
        @pl.when(there)
        def _():
            pl.semaphore_signal(barrier, inc=1, device_id=tile, device_id_type=MESH)
    for here, far_lats in ((is_middle, (0, lat_count - 1)), (is_end, (middle - 1, middle))):
        @pl.when(here)
        def _():
            for far_lat in far_lats:
                pl.semaphore_signal(barrier, inc=1, device_id={"lat": far_lat, "lon": beside}, device_id_type=MESH)
    pl.semaphore_wait(
        barrier,
        2
        + jnp.where(has_above, 1, 0)
        + jnp.where(has_below, 1, 0)
        + jnp.where(is_middle | is_end, 2, 0),
    )

    def lanes(group):
        start = group * group_lanes
        return pl.ds(start if isinstance(group, int) else pl.multiple_of(start, HDIM), group_lanes)

    def remote(source, target, send, recv, device):
        return pltpu.make_async_remote_copy(
            src_ref=source, dst_ref=target, send_sem=send, recv_sem=recv, device_id=device, device_id_type=MESH
        )

    def kv_copy(group, way, some):
        start = 2 * tokens if way == 0 else 0
        return remote(
            far.at[:, some, tokens : 2 * tokens, lanes(group)],
            far.at[:, some, start : start + tokens, lanes(group)],
            kv_send.at[group, way],
            kv_recv.at[group, 1 - way],
            tiles[way],
        )

    def edge_copy(group, way):
        start = tokens + 2 * HALO if way == 0 else tokens
        return remote(
            edge_out.at[way, :, :, :, lanes(group)],
            near.at[:, :, start : start + 2 * HALO, lanes(group)],
            edge_send.at[group, way],
            edge_recv.at[group, 1 - way],
            sides[way],
        )

    def stat_copy(group, way):
        return remote(
            stats_out.at[way, group],
            stats_in.at[1 - way, group],
            stat_send.at[group, way],
            stat_recv.at[group, 1 - way],
            sides[way],
        )

    def part_copy(group, way):
        return remote(
            part_out.at[way, :, :, :, lanes(group)],
            part_in.at[1 - way, :, :, :, lanes(group)],
            part_send.at[group, way],
            part_recv.at[group, 1 - way],
            sides[way],
        )

    def term_copy(group, way, some):
        return remote(
            term_out.at[way, :, some, :, lanes(group)],
            term_in.at[1 - way, :, some, :, lanes(group)],
            term_send.at[group, way],
            term_recv.at[group, 1 - way],
            tiles[way],
        )

    def pass_copy(group, way, kind):
        return remote(
            far.at[:, passing, tokens : 2 * tokens, lanes(group)]
            if kind == 0
            else term_out.at[way, :, passing, :, lanes(group)],
            relay.at[kind, :, :, :, lanes(group)],
            pass_send.at[group, kind],
            pass_recv.at[group, kind],
            {"lat": routes[way][1], "lon": beside},
        )

    def relay_copy(group, way, kind):
        start = 2 * tokens if way == 0 else 0
        return remote(
            relay.at[kind, :, :, :, lanes(group)],
            far.at[:, passing, start : start + tokens, lanes(group)]
            if kind == 0
            else term_in.at[1 - way, :, passing, :, lanes(group)],
            relay_send.at[group, kind],
            (kv_recv if kind == 0 else term_recv).at[group, 1 - way],
            {"lat": routes[way][2], "lon": beside},
        )

    def relayed(group, kind):
        return True if kind == 0 else group < GROUPS - 1

    def to_tiles(group, kind, act):
        copy = (kv_copy, term_copy)[kind]
        for way in range(2):
            crossing = (lat == routes[way][0]) & relayed(group, kind)

            @pl.when(exists[way] & jnp.logical_not(crossing))
            def _():
                act(copy(group, way, whole))

            @pl.when(crossing)
            def _():
                act(copy(group, way, direct))
                act(pass_copy(group, way, kind))

    def from_tiles(group, kind):
        copy = (kv_copy, term_copy)[kind]
        for origin in range(2):
            @pl.when(exists[origin])
            def _():
                copy(group, 1 - origin, whole).wait_recv()

    def forward(group, kind):
        for way in range(2):
            @pl.when((lat == routes[way][1]) & relayed(group, kind))
            def _():
                pass_copy(group, way, kind).wait_recv()
                relay_copy(group, way, kind).start()

    def start(copy):
        copy.start()

    def wait_send(copy):
        copy.wait_send()

    def send_edges(group):
        for which in range(2):
            for image in range(images):
                def half(start, low):
                    block = near[which, image, start : start + 16, lanes(group)].astype(jnp.float32)
                    return block[low : low + HALO]

                edge_out[0, which, image, :, lanes(group)] = jnp.concatenate(
                    [half(0, 0), half(32, 0)], axis=0
                ).astype(jnp.bfloat16)
                edge_out[1, which, image, :, lanes(group)] = jnp.concatenate(
                    [half(16, HALO), half(48, HALO)], axis=0
                ).astype(jnp.bfloat16)
        for way in range(2):
            edge_copy(group, way).start()

    own_copies[0].wait()
    own_copies[1].wait()
    for group in range(AHEAD):
        to_tiles(group, 0, start)
    own_copies[2].wait()
    own_copies[3].wait()
    for group in range(AHEAD):
        send_edges(group)

    near[:, :, tokens + 4 * HALO :, :] = jnp.zeros(
        (2, images, near.shape[2] - tokens - 4 * HALO, channels), jnp.bfloat16
    )
    for way in range(2):
        @pl.when(jnp.logical_not(exists[way]))
        def _():
            start = 0 if way == 0 else 2 * tokens
            far[:, :, start : start + tokens, :] = jnp.zeros((2, images, tokens, channels), jnp.bfloat16)
            term_in[way] = jnp.zeros((2, images, tokens, channels), jnp.bfloat16)

    def listed(target):
        found = (
            (lists_ref[0, lat] == target)
            | (lists_ref[1, lat] == target)
            | (lists_ref[2, lat] == target)
        ) & (target >= 0)
        return jnp.where(found, 1, 0)

    shape = bias.shape
    key = lax.broadcasted_iota(jnp.int32, shape, 0)
    query = lax.broadcasted_iota(jnp.int32, shape, 1)
    key_tile = key >> 6
    key_col = key & 31
    edge = query - tokens
    is_own = query < tokens
    from_left = edge < 2 * HALO
    query_col = jnp.where(is_own, query & 31, jnp.where(from_left, (edge & 7) - HALO, 32 + (edge & 7)))
    query_row = jnp.where(is_own, query >> 5, (edge >> 3) & 1)
    width = jnp.where(query_row == 0, widths_ref[2 * lat], widths_ref[2 * lat + 1])
    active = jnp.where(
        key_tile == 0, listed(lat - 1), jnp.where(key_tile == 1, listed(lat), listed(lat + 1))
    )
    seen = (jnp.abs(query_col - key_col) <= width) & (active == 1) & (edge < 4 * HALO)
    bias[...] = jnp.where(seen, 0.0, HIDDEN)

    places = [(image, head) for image in range(images) for head in range(group_heads)]

    def cols(group, head):
        return pl.ds(pl.multiple_of(group * group_lanes + head * HDIM, HDIM), HDIM)

    def scores(group):
        raws, dvals = [], []
        for image, head in places:
            at = cols(group, head)
            raws.append(nt(far[0, image, :, at], near[0, image, :, at]))
            dvals.append(nt(far[1, image, :, at], near[1, image, :, at]))
        mask = bias[...]
        tops, exs, sums, balances = [], [], [], []
        for raw, dp in zip(raws, dvals):
            raw = raw * (scale * math.log2(math.e)) + mask
            top = jnp.maximum(jnp.max(raw, axis=0, keepdims=True), FLOOR)
            e = jnp.exp2(raw - top)
            tops.append(top)
            exs.append(e)
            sums.append(jnp.sum(e, axis=0, keepdims=True))
            balances.append(jnp.sum(e * dp, axis=0, keepdims=True))
        for item, (e, dp) in enumerate(zip(exs, dvals)):
            slot = group * group_items + item
            exps[slot] = e
            dps[slot] = dp
        for kind, found in enumerate((tops, sums, balances)):
            rows = found + [jnp.zeros_like(found[0])] * (8 - len(found))
            stats[group, kind] = jnp.concatenate(rows, axis=0)
        for way, moves in enumerate((((0, 0, 8), (32, 8, 8), (64, 16, 16)), ((24, 0, 8), (56, 8, 8), (80, 16, 16)))):
            packed = jnp.zeros((8, HDIM), jnp.float32)
            for kind in range(3):
                for old, new, size in moves:
                    packed = window(stats[group, kind], old, 32 * kind + new, size, packed)
            stats_out[way, group] = packed
        for way in range(2):
            stat_copy(group, way).start()

    def combine(group):
        for way in range(2):
            stat_copy(group, way).wait_recv()
        others = []
        for kind in range(3):
            other = jnp.full((8, HDIM), FLOOR if kind == 0 else 0.0, jnp.float32)
            for origin, moves in enumerate((((0, 64, 16), (16, 0, 8), (24, 32, 8)), ((0, 80, 16), (16, 24, 8), (24, 56, 8)))):
                for old, new, size in moves:
                    other = window(stats_in[origin, group], 32 * kind + old, new, size, other)
            others.append(other)
        top, total, balance = (stats[group, kind] for kind in range(3))
        top2, total2, balance2 = others
        high = jnp.maximum(top, top2)
        part = jnp.exp2(top - high)
        part2 = jnp.exp2(top2 - high)
        inverse = 1.0 / jnp.maximum(part * total + part2 * total2, 0.5)
        factors[group, 0] = part * inverse
        factors[group, 1] = (part * balance + part2 * balance2) * inverse

    def gradients(group):
        lows, dlows = [], []
        for item in range(group_items):
            slot = group * group_items + item
            w = exps[slot] * factors[group, 0, item : item + 1, :]
            ds = w * (dps[slot] - factors[group, 1, item : item + 1, :])
            lows.append(w.astype(jnp.bfloat16))
            dlows.append(ds.astype(jnp.bfloat16))
        results = []
        for (image, head), w, ds in zip(places, lows, dlows):
            at = cols(group, head)
            att = tn(w, far[1, image, :, at])
            dq = tn(ds, far[0, image, :, at]) * scale
            dk = nn(ds, near[0, image, :, at]) * scale
            dv = nn(w, near[1, image, :, at])
            results.append(((att, dq), (dk, dv)))
        for (image, head), (for_near, for_far) in zip(places, results):
            at = cols(group, head)
            for which, x in enumerate(for_near):
                near_acc[which, image, :, at] = x[0:tokens]
                for way in range(2):
                    low = tokens + 2 * HALO * way
                    part_out[way, which, image, :, at] = x[low : low + 2 * HALO].astype(jnp.bfloat16)
            for which, x in enumerate(for_far):
                far_acc[which, image, :, at] = x[tokens : 2 * tokens]
                term_out[0, which, image, :, at] = x[0:tokens].astype(jnp.bfloat16)
                term_out[1, which, image, :, at] = x[2 * tokens :].astype(jnp.bfloat16)
        to_tiles(group, 1, start)
        for way in range(2):
            part_copy(group, way).start()

    def finish(group):
        for way in range(2):
            part_copy(group, way).wait_recv()
        from_tiles(group, 1)
        at = lanes(group)
        for image in range(images):
            for which in range(2):
                acc = near_acc[which, image, :, at]
                add_l = part_in[0, which, image, :, at].astype(jnp.float32)
                add_r = part_in[1, which, image, :, at].astype(jnp.float32)
                rows = []
                for r in range(2):
                    here = acc[32 * r : 32 * r + 32]
                    rows.append(here[0:8] + add_l[8 * r : 8 * r + 8])
                    rows.append(here[8:24])
                    rows.append(here[24:32] + add_r[8 * r : 8 * r + 8])
                outs[which, image, :, at] = jnp.concatenate(rows, axis=0).astype(jnp.bfloat16)
            for which in range(2):
                total = far_acc[which, image, :, at]
                for way in range(2):
                    total = total + term_in[way, which, image, :, at].astype(jnp.float32)
                outs[2 + which, image, :, at] = total.astype(jnp.bfloat16)

    def step(index, carry):
        @pl.when(index < GROUPS)
        def _():
            from_tiles(index, 0)
            for origin in range(2):
                edge_copy(index, 1 - origin).wait_recv()

            @pl.when(index + AHEAD < GROUPS)
            def _():
                to_tiles(index + AHEAD, 0, start)
                send_edges(index + AHEAD)

            forward(index, 0)
            scores(index)

        @pl.when((index >= 3) & (index <= GROUPS + 1))
        def _():
            forward(index - 3, 1)

        @pl.when((index >= 1) & (index <= GROUPS))
        def _():
            combine(index - 1)
            gradients(index - 1)

        @pl.when(index >= LAG)
        def _():
            finish(index - LAG)

        return carry

    lax.fori_loop(0, GROUPS + LAG, step, 0)

    def drain(group, carry):
        for way in range(2):
            edge_copy(group, way).wait_send()
            stat_copy(group, way).wait_send()
            part_copy(group, way).wait_send()
        for kind in range(2):
            to_tiles(group, kind, wait_send)
            for way in range(2):
                @pl.when((lat == routes[way][1]) & relayed(group, kind))
                def _():
                    relay_copy(group, way, kind).wait_send()
        return carry

    lax.fori_loop(0, GROUPS, drain, 0)


def split_kernel(stacked, *refs):
    outs, sem = refs[:4], refs[4]
    copies = [pltpu.make_async_copy(stacked.at[i], outs[i], sem.at[i]) for i in range(4)]
    for copy in copies:
        copy.start()
    for copy in copies:
        copy.wait()


def solution(mesh):
    lon_count = mesh.shape["lon"]
    lat_count = mesh.shape["lat"]

    def on_device(queries, key_states, value_states, out_grad, block_lists, row_widths):
        images, rows, columns, channels = queries.shape
        tokens = rows * columns
        flat = (images, tokens, channels)
        items = images * channels // HDIM
        bf16, f32 = jnp.bfloat16, jnp.float32
        hbm_spec = pl.BlockSpec(memory_space=pltpu.HBM)
        vmem_spec = pl.BlockSpec(memory_space=pltpu.VMEM)
        smem_spec = pl.BlockSpec(memory_space=pltpu.SMEM)
        dma = pltpu.SemaphoreType.DMA
        stacked = pl.pallas_call(
            functools.partial(kernel, lon_count, lat_count),
            out_shape=pltpu.VMEM((4,) + flat, bf16),
            in_specs=[smem_spec, smem_spec] + [hbm_spec] * 4,
            out_specs=vmem_spec,
            scratch_shapes=[
                pltpu.VMEM((2, images, 2 * tokens, channels), bf16),
                pltpu.VMEM((2, images, 3 * tokens, channels), bf16),
                pltpu.VMEM((2, 2, images, 2 * HALO, channels), bf16),
                pltpu.VMEM((3 * tokens, 2 * tokens), f32),
                pltpu.VMEM((items, 3 * tokens, 2 * tokens), f32),
                pltpu.VMEM((items, 3 * tokens, 2 * tokens), f32),
                pltpu.VMEM((GROUPS, 3, 8, 2 * tokens), f32),
                pltpu.VMEM((2, GROUPS, 8, 2 * tokens), f32),
                pltpu.VMEM((2, GROUPS, 8, 2 * tokens), f32),
                pltpu.VMEM((GROUPS, 2, 8, 2 * tokens), f32),
                pltpu.VMEM((2, images, tokens, channels), f32),
                pltpu.VMEM((2, 2, images, 2 * HALO, channels), bf16),
                pltpu.VMEM((2, 2, images, 2 * HALO, channels), bf16),
                pltpu.VMEM((2, images, tokens, channels), f32),
                pltpu.VMEM((2, 2, images, tokens, channels), bf16),
                pltpu.VMEM((2, 2, images, tokens, channels), bf16),
                pltpu.VMEM((2, 2, images - images // 2, tokens, channels), bf16),
                dma((4,)),
                dma((GROUPS, 2)),
                dma((GROUPS, 2)),
                dma((GROUPS, 2)),
                dma((GROUPS, 2)),
                dma((GROUPS, 2)),
                dma((GROUPS, 2)),
                dma((GROUPS, 2)),
                dma((GROUPS, 2)),
                dma((GROUPS, 2)),
                dma((GROUPS, 2)),
                dma((GROUPS, 2)),
                dma((GROUPS, 2)),
                dma((GROUPS, 2)),
            ],
            compiler_params=pltpu.CompilerParams(
                collective_id=0, has_side_effects=True, vmem_limit_bytes=60 * 1024 * 1024
            ),
            cost_estimate=pl.CostEstimate(
                flops=12 * items * 192 * 128 * 128,
                bytes_accessed=8 * images * tokens * channels * 2,
                transcendentals=items * 192 * 128,
            ),
        )(
            block_lists.T,
            row_widths,
            queries.reshape(flat),
            key_states.reshape(flat),
            value_states.reshape(flat),
            out_grad.reshape(flat),
        )
        results = pl.pallas_call(
            split_kernel,
            out_shape=[jax.ShapeDtypeStruct(flat, bf16)] * 4,
            in_specs=[pl.BlockSpec(memory_space=pl.ANY)],
            out_specs=[hbm_spec] * 4,
            scratch_shapes=[dma((4,))],
            compiler_params=pltpu.CompilerParams(vmem_limit_bytes=8 * 1024 * 1024),
        )(stacked)
        return tuple(x.reshape(queries.shape) for x in results)

    split = P(None, "lat", "lon", None)
    return jax.shard_map(
        on_device,
        mesh=mesh,
        in_specs=(split, split, split, split, P(), P()),
        out_specs=(split, split, split, split),
        check_vma=False,
    )
```

```python
import functools
import math

import jax
import jax.numpy as jnp
from jax import lax
from jax.experimental import pallas as pl
from jax.experimental.pallas import tpu as pltpu
from jax.sharding import PartitionSpec as P

MESH = pl.DeviceIdType.MESH
HALO = 8
HDIM = 128
GROUPS = 8
AHEAD = 2
LAG = 4
HIDDEN = -1e30
FLOOR = -1e29


def nt(a, b):
    return lax.dot_general(a, b, (((1,), (1,)), ((), ())), preferred_element_type=jnp.float32)


def nn(a, b):
    return jnp.dot(a, b, preferred_element_type=jnp.float32)


def window(x, old, new, size, rest):
    lane = lax.broadcasted_iota(jnp.int32, x.shape, 1)
    shifted = x if old == new else pltpu.roll(x, (new - old) % HDIM, 1)
    return jnp.where((lane >= new) & (lane < new + size), shifted, rest)


def kernel(
    lon_count,
    lat_count,
    lists_ref,
    widths_ref,
    q_hbm,
    k_hbm,
    v_hbm,
    g_hbm,
    outs,
    near,
    far,
    edge_out,
    bias,
    bias_t,
    exps,
    dps,
    stats,
    stats_out,
    stats_in,
    factors,
    columns,
    near_acc,
    part_out,
    part_in,
    far_acc,
    term_out,
    term_in,
    relay,
    own_sem,
    kv_send,
    kv_recv,
    edge_send,
    edge_recv,
    stat_send,
    stat_recv,
    part_send,
    part_recv,
    term_send,
    term_recv,
    pass_send,
    pass_recv,
    relay_send,
):
    lon = lax.axis_index("lon")
    lat = lax.axis_index("lat")
    left = lax.rem(lon + lon_count - 1, lon_count)
    right = lax.rem(lon + 1, lon_count)
    has_above = lat > 0
    has_below = lat < lat_count - 1
    middle = lat_count // 2
    beside = lon + 1 - 2 * lax.rem(lon, 2)
    is_middle = (lat == middle - 1) | (lat == middle)
    is_end = (lat == 0) | (lat == lat_count - 1)
    routes = ((middle, 0, middle - 1), (middle - 1, lat_count - 1, middle))
    images, tokens, channels = q_hbm.shape
    heads = channels // HDIM
    group_heads = heads // GROUPS
    group_items = images * group_heads
    group_lanes = group_heads * HDIM
    scale = HDIM ** -0.5
    half = images // 2
    whole, direct, passing = slice(0, images), slice(0, half), slice(half, images)

    sides = ({"lon": left}, {"lon": right})
    tiles = ({"lat": lat - 1}, {"lat": lat + 1})
    exists = (has_above, has_below)

    own_copies = [
        pltpu.make_async_copy(k_hbm, far.at[0, :, tokens : 2 * tokens, :], own_sem.at[0]),
        pltpu.make_async_copy(v_hbm, far.at[1, :, tokens : 2 * tokens, :], own_sem.at[1]),
        pltpu.make_async_copy(q_hbm, near.at[0, :, 0:tokens, :], own_sem.at[2]),
        pltpu.make_async_copy(g_hbm, near.at[1, :, 0:tokens, :], own_sem.at[3]),
    ]
    for copy in own_copies:
        copy.start()

    barrier = pltpu.get_barrier_semaphore()
    for side in sides:
        pl.semaphore_signal(barrier, inc=1, device_id=side, device_id_type=MESH)
    for there, tile in zip(exists, tiles):
        @pl.when(there)
        def _():
            pl.semaphore_signal(barrier, inc=1, device_id=tile, device_id_type=MESH)
    for here, far_lats in ((is_middle, (0, lat_count - 1)), (is_end, (middle - 1, middle))):
        @pl.when(here)
        def _():
            for far_lat in far_lats:
                pl.semaphore_signal(barrier, inc=1, device_id={"lat": far_lat, "lon": beside}, device_id_type=MESH)
    pl.semaphore_wait(
        barrier,
        2
        + jnp.where(has_above, 1, 0)
        + jnp.where(has_below, 1, 0)
        + jnp.where(is_middle | is_end, 2, 0),
    )

    def lanes(group):
        start = group * group_lanes
        return pl.ds(start if isinstance(group, int) else pl.multiple_of(start, HDIM), group_lanes)

    def remote(source, target, send, recv, device):
        return pltpu.make_async_remote_copy(
            src_ref=source, dst_ref=target, send_sem=send, recv_sem=recv, device_id=device, device_id_type=MESH
        )

    def kv_copy(group, way, some):
        start = 2 * tokens if way == 0 else 0
        return remote(
            far.at[:, some, tokens : 2 * tokens, lanes(group)],
            far.at[:, some, start : start + tokens, lanes(group)],
            kv_send.at[group, way],
            kv_recv.at[group, 1 - way],
            tiles[way],
        )

    def edge_copy(group, way):
        start = tokens + 2 * HALO if way == 0 else tokens
        return remote(
            edge_out.at[way, :, :, :, lanes(group)],
            near.at[:, :, start : start + 2 * HALO, lanes(group)],
            edge_send.at[group, way],
            edge_recv.at[group, 1 - way],
            sides[way],
        )

    def stat_copy(group, way):
        return remote(
            stats_out.at[way, group],
            stats_in.at[1 - way, group],
            stat_send.at[group, way],
            stat_recv.at[group, 1 - way],
            sides[way],
        )

    def part_copy(group, way):
        return remote(
            part_out.at[way, :, :, :, lanes(group)],
            part_in.at[1 - way, :, :, :, lanes(group)],
            part_send.at[group, way],
            part_recv.at[group, 1 - way],
            sides[way],
        )

    def term_copy(group, way, some):
        return remote(
            term_out.at[way, :, some, :, lanes(group)],
            term_in.at[1 - way, :, some, :, lanes(group)],
            term_send.at[group, way],
            term_recv.at[group, 1 - way],
            tiles[way],
        )

    def pass_copy(group, way, kind):
        return remote(
            far.at[:, passing, tokens : 2 * tokens, lanes(group)]
            if kind == 0
            else term_out.at[way, :, passing, :, lanes(group)],
            relay.at[kind, :, :, :, lanes(group)],
            pass_send.at[group, kind],
            pass_recv.at[group, kind],
            {"lat": routes[way][1], "lon": beside},
        )

    def relay_copy(group, way, kind):
        start = 2 * tokens if way == 0 else 0
        return remote(
            relay.at[kind, :, :, :, lanes(group)],
            far.at[:, passing, start : start + tokens, lanes(group)]
            if kind == 0
            else term_in.at[1 - way, :, passing, :, lanes(group)],
            relay_send.at[group, kind],
            (kv_recv if kind == 0 else term_recv).at[group, 1 - way],
            {"lat": routes[way][2], "lon": beside},
        )

    def relayed(group, kind):
        return True if kind == 0 else group < GROUPS - 1

    def to_tiles(group, kind, act):
        copy = (kv_copy, term_copy)[kind]
        for way in range(2):
            crossing = (lat == routes[way][0]) & relayed(group, kind)

            @pl.when(exists[way] & jnp.logical_not(crossing))
            def _():
                act(copy(group, way, whole))

            @pl.when(crossing)
            def _():
                act(copy(group, way, direct))
                act(pass_copy(group, way, kind))

    def from_tiles(group, kind):
        copy = (kv_copy, term_copy)[kind]
        for origin in range(2):
            @pl.when(exists[origin])
            def _():
                copy(group, 1 - origin, whole).wait_recv()

    def forward(group, kind):
        for way in range(2):
            @pl.when((lat == routes[way][1]) & relayed(group, kind))
            def _():
                pass_copy(group, way, kind).wait_recv()
                relay_copy(group, way, kind).start()

    def start(copy):
        copy.start()

    def wait_send(copy):
        copy.wait_send()

    def send_edges(group):
        for which in range(2):
            for image in range(images):
                def half(start, low):
                    block = near[which, image, start : start + 16, lanes(group)].astype(jnp.float32)
                    return block[low : low + HALO]

                edge_out[0, which, image, :, lanes(group)] = jnp.concatenate(
                    [half(0, 0), half(32, 0)], axis=0
                ).astype(jnp.bfloat16)
                edge_out[1, which, image, :, lanes(group)] = jnp.concatenate(
                    [half(16, HALO), half(48, HALO)], axis=0
                ).astype(jnp.bfloat16)
        for way in range(2):
            edge_copy(group, way).start()

    own_copies[0].wait()
    own_copies[1].wait()
    for group in range(AHEAD):
        to_tiles(group, 0, start)
    own_copies[2].wait()
    own_copies[3].wait()
    for group in range(AHEAD):
        send_edges(group)

    near[:, :, tokens + 4 * HALO :, :] = jnp.zeros(
        (2, images, near.shape[2] - tokens - 4 * HALO, channels), jnp.bfloat16
    )
    for way in range(2):
        @pl.when(jnp.logical_not(exists[way]))
        def _():
            start = 0 if way == 0 else 2 * tokens
            far[:, :, start : start + tokens, :] = jnp.zeros((2, images, tokens, channels), jnp.bfloat16)
            term_in[way] = jnp.zeros((2, images, tokens, channels), jnp.bfloat16)

    def listed(target):
        found = (
            (lists_ref[0, lat] == target)
            | (lists_ref[1, lat] == target)
            | (lists_ref[2, lat] == target)
        ) & (target >= 0)
        return jnp.where(found, 1, 0)

    def mask(shape, key_axis):
        key = lax.broadcasted_iota(jnp.int32, shape, key_axis)
        query = lax.broadcasted_iota(jnp.int32, shape, 1 - key_axis)
        key_tile = key >> 6
        key_col = key & 31
        edge = query - tokens
        is_own = query < tokens
        from_left = edge < 2 * HALO
        query_col = jnp.where(
            is_own, query & 31, jnp.where(from_left, (edge & 7) - HALO, 32 + (edge & 7))
        )
        query_row = jnp.where(is_own, query >> 5, (edge >> 3) & 1)
        width = jnp.where(query_row == 0, widths_ref[2 * lat], widths_ref[2 * lat + 1])
        active = jnp.where(
            key_tile == 0, listed(lat - 1), jnp.where(key_tile == 1, listed(lat), listed(lat + 1))
        )
        seen = (jnp.abs(query_col - key_col) <= width) & (active == 1) & (edge < 4 * HALO)
        return jnp.where(seen, 0.0, HIDDEN)

    bias[...] = mask(bias.shape, 0)
    bias_t[...] = mask(bias_t.shape, 1)

    places = [(image, head) for image in range(images) for head in range(group_heads)]

    def cols(group, head):
        return pl.ds(pl.multiple_of(group * group_lanes + head * HDIM, HDIM), HDIM)

    to_log2 = scale * math.log2(math.e)

    def scores(group):
        tops, sums, balances = [], [], []
        for item, (image, head) in enumerate(places):
            at = cols(group, head)
            raw = nt(far[0, image, :, at], near[0, image, :, at]) * to_log2 + bias[...]
            dp = nt(far[1, image, :, at], near[1, image, :, at])
            top = jnp.maximum(jnp.max(raw, axis=0, keepdims=True), FLOOR)
            e = jnp.exp2(raw - top)
            slot = group * group_items + item
            exps[slot] = e
            dps[slot] = dp
            tops.append(top)
            sums.append(jnp.sum(e, axis=0, keepdims=True))
            balances.append(jnp.sum(e * dp, axis=0, keepdims=True))
        for kind, found in enumerate((tops, sums, balances)):
            rows = found + [jnp.zeros_like(found[0])] * (8 - len(found))
            stats[group, kind] = jnp.concatenate(rows, axis=0)
        for way, moves in enumerate((((0, 0, 8), (32, 8, 8), (64, 16, 16)), ((24, 0, 8), (56, 8, 8), (80, 16, 16)))):
            packed = jnp.zeros((8, HDIM), jnp.float32)
            for kind in range(3):
                for old, new, size in moves:
                    packed = window(stats[group, kind], old, 32 * kind + new, size, packed)
            stats_out[way, group] = packed
        for way in range(2):
            stat_copy(group, way).start()

    def combine(group):
        for way in range(2):
            stat_copy(group, way).wait_recv()
        others = []
        for kind in range(3):
            other = jnp.full((8, HDIM), FLOOR if kind == 0 else 0.0, jnp.float32)
            for origin, moves in enumerate((((0, 64, 16), (16, 0, 8), (24, 32, 8)), ((0, 80, 16), (16, 24, 8), (24, 56, 8)))):
                for old, new, size in moves:
                    other = window(stats_in[origin, group], 32 * kind + old, new, size, other)
            others.append(other)
        top, total, balance = (stats[group, kind] for kind in range(3))
        top2, total2, balance2 = others
        high = jnp.maximum(top, top2)
        part = jnp.exp2(top - high)
        part2 = jnp.exp2(top2 - high)
        whole_sum = jnp.maximum(part * total + part2 * total2, 0.5)
        inverse = 1.0 / whole_sum
        balance = (part * balance + part2 * balance2) * inverse
        factors[group, 0] = part * inverse
        factors[group, 1] = balance
        columns[group, 0] = jnp.transpose(high + jnp.log2(whole_sum))
        columns[group, 1] = jnp.transpose(balance)

    def gradients(group):
        seen = tokens + 4 * HALO
        for item, (image, head) in enumerate(places):
            at = cols(group, head)
            slot = group * group_items + item
            keys, values = far[0, image, :, at], far[1, image, :, at]
            queries, grads = near[0, image, :, at], near[1, image, :, at]
            w = exps[slot] * factors[group, 0, item : item + 1, :]
            ds = w * (dps[slot] - factors[group, 1, item : item + 1, :])
            dk = nn(ds.astype(jnp.bfloat16), queries) * scale
            dv = nn(w.astype(jnp.bfloat16), grads)
            for which, x in enumerate((dk, dv)):
                far_acc[which, image, :, at] = x[tokens : 2 * tokens]
                term_out[0, which, image, :, at] = x[0:tokens].astype(jnp.bfloat16)
                term_out[1, which, image, :, at] = x[2 * tokens :].astype(jnp.bfloat16)
            raw = nt(queries[0:seen], keys) * to_log2 + bias_t[...]
            dp = nt(grads[0:seen], values)
            w = jnp.exp2(raw - columns[group, 0, 0:seen, item : item + 1])
            ds = w * (dp - columns[group, 1, 0:seen, item : item + 1])
            att = nn(w.astype(jnp.bfloat16), values)
            dq = nn(ds.astype(jnp.bfloat16), keys) * scale
            for which, x in enumerate((att, dq)):
                near_acc[which, image, :, at] = x[0:tokens]
                for way in range(2):
                    low = tokens + 2 * HALO * way
                    part_out[way, which, image, :, at] = x[low : low + 2 * HALO].astype(jnp.bfloat16)
        to_tiles(group, 1, start)
        for way in range(2):
            part_copy(group, way).start()

    def finish(group):
        for way in range(2):
            part_copy(group, way).wait_recv()
        from_tiles(group, 1)
        at = lanes(group)
        for image in range(images):
            for which in range(2):
                acc = near_acc[which, image, :, at]
                add_l = part_in[0, which, image, :, at].astype(jnp.float32)
                add_r = part_in[1, which, image, :, at].astype(jnp.float32)
                rows = []
                for r in range(2):
                    here = acc[32 * r : 32 * r + 32]
                    rows.append(here[0:8] + add_l[8 * r : 8 * r + 8])
                    rows.append(here[8:24])
                    rows.append(here[24:32] + add_r[8 * r : 8 * r + 8])
                outs[which, image, :, at] = jnp.concatenate(rows, axis=0).astype(jnp.bfloat16)
            for which in range(2):
                total = far_acc[which, image, :, at]
                for way in range(2):
                    total = total + term_in[way, which, image, :, at].astype(jnp.float32)
                outs[2 + which, image, :, at] = total.astype(jnp.bfloat16)

    def step(index, carry):
        @pl.when(index < GROUPS)
        def _():
            from_tiles(index, 0)
            for origin in range(2):
                edge_copy(index, 1 - origin).wait_recv()

            @pl.when(index + AHEAD < GROUPS)
            def _():
                to_tiles(index + AHEAD, 0, start)
                send_edges(index + AHEAD)

            forward(index, 0)
            scores(index)

        @pl.when((index >= 3) & (index <= GROUPS + 1))
        def _():
            forward(index - 3, 1)

        @pl.when((index >= 2) & (index <= GROUPS + 1))
        def _():
            combine(index - 2)
            gradients(index - 2)

        @pl.when(index >= LAG)
        def _():
            finish(index - LAG)

        return carry

    lax.fori_loop(0, GROUPS + LAG, step, 0)

    def drain(group, carry):
        for way in range(2):
            edge_copy(group, way).wait_send()
            stat_copy(group, way).wait_send()
            part_copy(group, way).wait_send()
        for kind in range(2):
            to_tiles(group, kind, wait_send)
            for way in range(2):
                @pl.when((lat == routes[way][1]) & relayed(group, kind))
                def _():
                    relay_copy(group, way, kind).wait_send()
        return carry

    lax.fori_loop(0, GROUPS, drain, 0)


def split_kernel(stacked, *refs):
    outs, sem = refs[:4], refs[4]
    copies = [pltpu.make_async_copy(stacked.at[i], outs[i], sem.at[i]) for i in range(4)]
    for copy in copies:
        copy.start()
    for copy in copies:
        copy.wait()


def solution(mesh):
    lon_count = mesh.shape["lon"]
    lat_count = mesh.shape["lat"]

    def on_device(queries, key_states, value_states, out_grad, block_lists, row_widths):
        images, rows, columns, channels = queries.shape
        tokens = rows * columns
        flat = (images, tokens, channels)
        items = images * channels // HDIM
        bf16, f32 = jnp.bfloat16, jnp.float32
        hbm_spec = pl.BlockSpec(memory_space=pltpu.HBM)
        vmem_spec = pl.BlockSpec(memory_space=pltpu.VMEM)
        smem_spec = pl.BlockSpec(memory_space=pltpu.SMEM)
        dma = pltpu.SemaphoreType.DMA
        stacked = pl.pallas_call(
            functools.partial(kernel, lon_count, lat_count),
            out_shape=pltpu.VMEM((4,) + flat, bf16),
            in_specs=[smem_spec, smem_spec] + [hbm_spec] * 4,
            out_specs=vmem_spec,
            scratch_shapes=[
                pltpu.VMEM((2, images, 2 * tokens, channels), bf16),
                pltpu.VMEM((2, images, 3 * tokens, channels), bf16),
                pltpu.VMEM((2, 2, images, 2 * HALO, channels), bf16),
                pltpu.VMEM((3 * tokens, 2 * tokens), f32),
                pltpu.VMEM((tokens + 4 * HALO, 3 * tokens), f32),
                pltpu.VMEM((items, 3 * tokens, 2 * tokens), f32),
                pltpu.VMEM((items, 3 * tokens, 2 * tokens), f32),
                pltpu.VMEM((GROUPS, 3, 8, 2 * tokens), f32),
                pltpu.VMEM((2, GROUPS, 8, 2 * tokens), f32),
                pltpu.VMEM((2, GROUPS, 8, 2 * tokens), f32),
                pltpu.VMEM((GROUPS, 2, 8, 2 * tokens), f32),
                pltpu.VMEM((GROUPS, 2, 2 * tokens, 8), f32),
                pltpu.VMEM((2, images, tokens, channels), f32),
                pltpu.VMEM((2, 2, images, 2 * HALO, channels), bf16),
                pltpu.VMEM((2, 2, images, 2 * HALO, channels), bf16),
                pltpu.VMEM((2, images, tokens, channels), f32),
                pltpu.VMEM((2, 2, images, tokens, channels), bf16),
                pltpu.VMEM((2, 2, images, tokens, channels), bf16),
                pltpu.VMEM((2, 2, images - images // 2, tokens, channels), bf16),
                dma((4,)),
                dma((GROUPS, 2)),
                dma((GROUPS, 2)),
                dma((GROUPS, 2)),
                dma((GROUPS, 2)),
                dma((GROUPS, 2)),
                dma((GROUPS, 2)),
                dma((GROUPS, 2)),
                dma((GROUPS, 2)),
                dma((GROUPS, 2)),
                dma((GROUPS, 2)),
                dma((GROUPS, 2)),
                dma((GROUPS, 2)),
                dma((GROUPS, 2)),
            ],
            compiler_params=pltpu.CompilerParams(
                collective_id=0, has_side_effects=True, vmem_limit_bytes=60 * 1024 * 1024
            ),
            cost_estimate=pl.CostEstimate(
                flops=12 * items * 192 * 128 * 128,
                bytes_accessed=8 * images * tokens * channels * 2,
                transcendentals=items * 192 * 128,
            ),
        )(
            block_lists.T,
            row_widths,
            queries.reshape(flat),
            key_states.reshape(flat),
            value_states.reshape(flat),
            out_grad.reshape(flat),
        )
        results = pl.pallas_call(
            split_kernel,
            out_shape=[jax.ShapeDtypeStruct(flat, bf16)] * 4,
            in_specs=[pl.BlockSpec(memory_space=pl.ANY)],
            out_specs=[hbm_spec] * 4,
            scratch_shapes=[dma((4,))],
            compiler_params=pltpu.CompilerParams(vmem_limit_bytes=8 * 1024 * 1024),
        )(stacked)
        return tuple(x.reshape(queries.shape) for x in results)

    split = P(None, "lat", "lon", None)
    return jax.shard_map(
        on_device,
        mesh=mesh,
        in_specs=(split, split, split, split, P(), P()),
        out_specs=(split, split, split, split),
        check_vma=False,
    )
```

```python
import functools
import math

import jax
import jax.numpy as jnp
from jax import lax
from jax.experimental import pallas as pl
from jax.experimental.pallas import tpu as pltpu
from jax.sharding import PartitionSpec as P

MESH = pl.DeviceIdType.MESH
HALO = 8
HDIM = 128
GROUPS = 8
LAG = 4
HIDDEN = -1e30
FLOOR = -1e29


def nt(a, b):
    return lax.dot_general(a, b, (((1,), (1,)), ((), ())), preferred_element_type=jnp.float32)


def nn(a, b):
    return jnp.dot(a, b, preferred_element_type=jnp.float32)


def window(x, old, new, size, rest):
    lane = lax.broadcasted_iota(jnp.int32, x.shape, 1)
    shifted = x if old == new else pltpu.roll(x, (new - old) % HDIM, 1)
    return jnp.where((lane >= new) & (lane < new + size), shifted, rest)


def kernel(
    lon_count,
    lat_count,
    lists_ref,
    widths_ref,
    q_hbm,
    k_hbm,
    v_hbm,
    g_hbm,
    outs,
    near,
    far,
    edge_out,
    bias,
    bias_t,
    exps,
    dps,
    stats,
    stats_out,
    stats_in,
    factors,
    columns,
    near_acc,
    part_out,
    part_in,
    far_acc,
    term_out,
    term_in,
    relay,
    own_sem,
    kv_send,
    kv_recv,
    edge_send,
    edge_recv,
    stat_send,
    stat_recv,
    part_send,
    part_recv,
    term_send,
    term_recv,
    pass_send,
    pass_recv,
    relay_send,
):
    lon = lax.axis_index("lon")
    lat = lax.axis_index("lat")
    left = lax.rem(lon + lon_count - 1, lon_count)
    right = lax.rem(lon + 1, lon_count)
    has_above = lat > 0
    has_below = lat < lat_count - 1
    middle = lat_count // 2
    beside = lon + 1 - 2 * lax.rem(lon, 2)
    is_middle = (lat == middle - 1) | (lat == middle)
    is_end = (lat == 0) | (lat == lat_count - 1)
    routes = ((middle, 0, middle - 1), (middle - 1, lat_count - 1, middle))
    images, tokens, channels = q_hbm.shape
    heads = channels // HDIM
    group_heads = heads // GROUPS
    group_items = images * group_heads
    group_lanes = group_heads * HDIM
    scale = HDIM ** -0.5
    half = images // 2
    whole, direct, passing = slice(0, images), slice(0, half), slice(half, images)

    sides = ({"lon": left}, {"lon": right})
    tiles = ({"lat": lat - 1}, {"lat": lat + 1})
    exists = (has_above, has_below)

    own_copies = [
        pltpu.make_async_copy(k_hbm, far.at[0, :, tokens : 2 * tokens, :], own_sem.at[0]),
        pltpu.make_async_copy(v_hbm, far.at[1, :, tokens : 2 * tokens, :], own_sem.at[1]),
        pltpu.make_async_copy(q_hbm, near.at[0, :, 0:tokens, :], own_sem.at[2]),
        pltpu.make_async_copy(g_hbm, near.at[1, :, 0:tokens, :], own_sem.at[3]),
    ]
    for copy in own_copies:
        copy.start()

    barrier = pltpu.get_barrier_semaphore()
    for side in sides:
        pl.semaphore_signal(barrier, inc=1, device_id=side, device_id_type=MESH)
    for there, tile in zip(exists, tiles):
        @pl.when(there)
        def _():
            pl.semaphore_signal(barrier, inc=1, device_id=tile, device_id_type=MESH)
    for here, far_lats in ((is_middle, (0, lat_count - 1)), (is_end, (middle - 1, middle))):
        @pl.when(here)
        def _():
            for far_lat in far_lats:
                pl.semaphore_signal(barrier, inc=1, device_id={"lat": far_lat, "lon": beside}, device_id_type=MESH)
    pl.semaphore_wait(
        barrier,
        2
        + jnp.where(has_above, 1, 0)
        + jnp.where(has_below, 1, 0)
        + jnp.where(is_middle | is_end, 2, 0),
    )

    def lanes(group):
        start = group * group_lanes
        return pl.ds(start if isinstance(group, int) else pl.multiple_of(start, HDIM), group_lanes)

    def remote(source, target, send, recv, device):
        return pltpu.make_async_remote_copy(
            src_ref=source, dst_ref=target, send_sem=send, recv_sem=recv, device_id=device, device_id_type=MESH
        )

    def kv_copy(group, way, some):
        start = 2 * tokens if way == 0 else 0
        return remote(
            far.at[:, some, tokens : 2 * tokens, lanes(group)],
            far.at[:, some, start : start + tokens, lanes(group)],
            kv_send.at[group, way],
            kv_recv.at[group, 1 - way],
            tiles[way],
        )

    def edge_copy(group, way):
        start = tokens + 2 * HALO if way == 0 else tokens
        return remote(
            edge_out.at[way, :, :, :, lanes(group)],
            near.at[:, :, start : start + 2 * HALO, lanes(group)],
            edge_send.at[group, way],
            edge_recv.at[group, 1 - way],
            sides[way],
        )

    def stat_copy(group, way):
        return remote(
            stats_out.at[way, group],
            stats_in.at[1 - way, group],
            stat_send.at[group, way],
            stat_recv.at[group, 1 - way],
            sides[way],
        )

    def part_copy(group, way):
        return remote(
            part_out.at[way, :, :, :, lanes(group)],
            part_in.at[1 - way, :, :, :, lanes(group)],
            part_send.at[group, way],
            part_recv.at[group, 1 - way],
            sides[way],
        )

    def term_copy(group, way, some):
        return remote(
            term_out.at[way, :, some, :, lanes(group)],
            term_in.at[1 - way, :, some, :, lanes(group)],
            term_send.at[group, way],
            term_recv.at[group, 1 - way],
            tiles[way],
        )

    def pass_copy(group, way, kind):
        return remote(
            far.at[:, passing, tokens : 2 * tokens, lanes(group)]
            if kind == 0
            else term_out.at[way, :, passing, :, lanes(group)],
            relay.at[kind, :, :, :, lanes(group)],
            pass_send.at[group, kind],
            pass_recv.at[group, kind],
            {"lat": routes[way][1], "lon": beside},
        )

    def relay_copy(group, way, kind):
        start = 2 * tokens if way == 0 else 0
        return remote(
            relay.at[kind, :, :, :, lanes(group)],
            far.at[:, passing, start : start + tokens, lanes(group)]
            if kind == 0
            else term_in.at[1 - way, :, passing, :, lanes(group)],
            relay_send.at[group, kind],
            (kv_recv if kind == 0 else term_recv).at[group, 1 - way],
            {"lat": routes[way][2], "lon": beside},
        )

    def relayed(group, kind):
        return True if kind == 0 else group < GROUPS - 1

    def to_tiles(group, kind, act):
        copy = (kv_copy, term_copy)[kind]
        for way in range(2):
            crossing = (lat == routes[way][0]) & relayed(group, kind)

            @pl.when(exists[way] & jnp.logical_not(crossing))
            def _():
                act(copy(group, way, whole))

            @pl.when(crossing)
            def _():
                act(copy(group, way, direct))
                act(pass_copy(group, way, kind))

    def from_tiles(group, kind):
        copy = (kv_copy, term_copy)[kind]
        for origin in range(2):
            @pl.when(exists[origin])
            def _():
                copy(group, 1 - origin, whole).wait_recv()

    def forward(group, kind):
        for way in range(2):
            @pl.when((lat == routes[way][1]) & relayed(group, kind))
            def _():
                pass_copy(group, way, kind).wait_recv()
                relay_copy(group, way, kind).start()

    def start(copy):
        copy.start()

    def wait_send(copy):
        copy.wait_send()

    def send_edges(group):
        for which in range(2):
            for image in range(images):
                def half(start, low):
                    block = near[which, image, start : start + 16, lanes(group)].astype(jnp.float32)
                    return block[low : low + HALO]

                edge_out[0, which, image, :, lanes(group)] = jnp.concatenate(
                    [half(0, 0), half(32, 0)], axis=0
                ).astype(jnp.bfloat16)
                edge_out[1, which, image, :, lanes(group)] = jnp.concatenate(
                    [half(16, HALO), half(48, HALO)], axis=0
                ).astype(jnp.bfloat16)
        for way in range(2):
            edge_copy(group, way).start()

    own_copies[0].wait()
    own_copies[1].wait()
    to_tiles(0, 0, start)
    own_copies[2].wait()
    own_copies[3].wait()
    send_edges(0)

    def send_group(group, carry):
        to_tiles(group, 0, start)
        send_edges(group)
        return carry

    lax.fori_loop(1, GROUPS, send_group, 0)

    near[:, :, tokens + 4 * HALO :, :] = jnp.zeros(
        (2, images, near.shape[2] - tokens - 4 * HALO, channels), jnp.bfloat16
    )
    for way in range(2):
        @pl.when(jnp.logical_not(exists[way]))
        def _():
            start = 0 if way == 0 else 2 * tokens
            far[:, :, start : start + tokens, :] = jnp.zeros((2, images, tokens, channels), jnp.bfloat16)
            term_in[way] = jnp.zeros((2, images, tokens, channels), jnp.bfloat16)

    def listed(target):
        found = (
            (lists_ref[0, lat] == target)
            | (lists_ref[1, lat] == target)
            | (lists_ref[2, lat] == target)
        ) & (target >= 0)
        return jnp.where(found, 1, 0)

    def mask(shape, key_axis):
        key = lax.broadcasted_iota(jnp.int32, shape, key_axis)
        query = lax.broadcasted_iota(jnp.int32, shape, 1 - key_axis)
        key_tile = key >> 6
        key_col = key & 31
        edge = query - tokens
        is_own = query < tokens
        from_left = edge < 2 * HALO
        query_col = jnp.where(
            is_own, query & 31, jnp.where(from_left, (edge & 7) - HALO, 32 + (edge & 7))
        )
        query_row = jnp.where(is_own, query >> 5, (edge >> 3) & 1)
        width = jnp.where(query_row == 0, widths_ref[2 * lat], widths_ref[2 * lat + 1])
        active = jnp.where(
            key_tile == 0, listed(lat - 1), jnp.where(key_tile == 1, listed(lat), listed(lat + 1))
        )
        seen = (jnp.abs(query_col - key_col) <= width) & (active == 1) & (edge < 4 * HALO)
        return jnp.where(seen, 0.0, HIDDEN)

    bias[...] = mask(bias.shape, 0)
    bias_t[...] = mask(bias_t.shape, 1)

    places = [(image, head) for image in range(images) for head in range(group_heads)]

    def cols(group, head):
        return pl.ds(pl.multiple_of(group * group_lanes + head * HDIM, HDIM), HDIM)

    to_log2 = scale * math.log2(math.e)

    def scores(group):
        tops, sums, balances = [], [], []
        for item, (image, head) in enumerate(places):
            at = cols(group, head)
            raw = nt(far[0, image, :, at], near[0, image, :, at]) * to_log2 + bias[...]
            dp = nt(far[1, image, :, at], near[1, image, :, at])
            top = jnp.maximum(jnp.max(raw, axis=0, keepdims=True), FLOOR)
            e = jnp.exp2(raw - top)
            slot = group * group_items + item
            exps[slot] = e
            dps[slot] = dp
            tops.append(top)
            sums.append(jnp.sum(e, axis=0, keepdims=True))
            balances.append(jnp.sum(e * dp, axis=0, keepdims=True))
        for kind, found in enumerate((tops, sums, balances)):
            rows = found + [jnp.zeros_like(found[0])] * (8 - len(found))
            stats[group, kind] = jnp.concatenate(rows, axis=0)
        for way, moves in enumerate((((0, 0, 8), (32, 8, 8), (64, 16, 16)), ((24, 0, 8), (56, 8, 8), (80, 16, 16)))):
            packed = jnp.zeros((8, HDIM), jnp.float32)
            for kind in range(3):
                for old, new, size in moves:
                    packed = window(stats[group, kind], old, 32 * kind + new, size, packed)
            stats_out[way, group] = packed
        for way in range(2):
            stat_copy(group, way).start()

    def combine(group):
        for way in range(2):
            stat_copy(group, way).wait_recv()
        others = []
        for kind in range(3):
            other = jnp.full((8, HDIM), FLOOR if kind == 0 else 0.0, jnp.float32)
            for origin, moves in enumerate((((0, 64, 16), (16, 0, 8), (24, 32, 8)), ((0, 80, 16), (16, 24, 8), (24, 56, 8)))):
                for old, new, size in moves:
                    other = window(stats_in[origin, group], 32 * kind + old, new, size, other)
            others.append(other)
        top, total, balance = (stats[group, kind] for kind in range(3))
        top2, total2, balance2 = others
        high = jnp.maximum(top, top2)
        part = jnp.exp2(top - high)
        part2 = jnp.exp2(top2 - high)
        whole_sum = jnp.maximum(part * total + part2 * total2, 0.5)
        inverse = 1.0 / whole_sum
        balance = (part * balance + part2 * balance2) * inverse
        factors[group, 0] = part * inverse
        factors[group, 1] = balance
        columns[group, 0] = jnp.transpose(high + jnp.log2(whole_sum))
        columns[group, 1] = jnp.transpose(balance)

    def gradients(group):
        seen = tokens + 4 * HALO
        for item, (image, head) in enumerate(places):
            at = cols(group, head)
            slot = group * group_items + item
            keys, values = far[0, image, :, at], far[1, image, :, at]
            queries, grads = near[0, image, :, at], near[1, image, :, at]
            w = exps[slot] * factors[group, 0, item : item + 1, :]
            ds = w * (dps[slot] - factors[group, 1, item : item + 1, :])
            dk = nn(ds.astype(jnp.bfloat16), queries) * scale
            dv = nn(w.astype(jnp.bfloat16), grads)
            for which, x in enumerate((dk, dv)):
                far_acc[which, image, :, at] = x[tokens : 2 * tokens]
                term_out[0, which, image, :, at] = x[0:tokens].astype(jnp.bfloat16)
                term_out[1, which, image, :, at] = x[2 * tokens :].astype(jnp.bfloat16)
            raw = nt(queries[0:seen], keys) * to_log2 + bias_t[...]
            dp = nt(grads[0:seen], values)
            w = jnp.exp2(raw - columns[group, 0, 0:seen, item : item + 1])
            ds = w * (dp - columns[group, 1, 0:seen, item : item + 1])
            att = nn(w.astype(jnp.bfloat16), values)
            dq = nn(ds.astype(jnp.bfloat16), keys) * scale
            for which, x in enumerate((att, dq)):
                near_acc[which, image, :, at] = x[0:tokens]
                for way in range(2):
                    low = tokens + 2 * HALO * way
                    part_out[way, which, image, :, at] = x[low : low + 2 * HALO].astype(jnp.bfloat16)
        to_tiles(group, 1, start)
        for way in range(2):
            part_copy(group, way).start()

    def finish(group):
        for way in range(2):
            part_copy(group, way).wait_recv()
        from_tiles(group, 1)
        at = lanes(group)
        for image in range(images):
            for which in range(2):
                acc = near_acc[which, image, :, at]
                add_l = part_in[0, which, image, :, at].astype(jnp.float32)
                add_r = part_in[1, which, image, :, at].astype(jnp.float32)
                rows = []
                for r in range(2):
                    here = acc[32 * r : 32 * r + 32]
                    rows.append(here[0:8] + add_l[8 * r : 8 * r + 8])
                    rows.append(here[8:24])
                    rows.append(here[24:32] + add_r[8 * r : 8 * r + 8])
                outs[which, image, :, at] = jnp.concatenate(rows, axis=0).astype(jnp.bfloat16)
            for which in range(2):
                total = far_acc[which, image, :, at]
                for way in range(2):
                    total = total + term_in[way, which, image, :, at].astype(jnp.float32)
                outs[2 + which, image, :, at] = total.astype(jnp.bfloat16)

    def step(index, carry):
        @pl.when(index < GROUPS)
        def _():
            from_tiles(index, 0)
            for origin in range(2):
                edge_copy(index, 1 - origin).wait_recv()

            forward(index, 0)
            scores(index)

        @pl.when((index >= 3) & (index <= GROUPS + 1))
        def _():
            forward(index - 3, 1)

        @pl.when((index >= 2) & (index <= GROUPS + 1))
        def _():
            combine(index - 2)
            gradients(index - 2)

        @pl.when(index >= LAG)
        def _():
            finish(index - LAG)

        return carry

    lax.fori_loop(0, GROUPS + LAG, step, 0)

    def drain(group, carry):
        for way in range(2):
            edge_copy(group, way).wait_send()
            stat_copy(group, way).wait_send()
            part_copy(group, way).wait_send()
        for kind in range(2):
            to_tiles(group, kind, wait_send)
            for way in range(2):
                @pl.when((lat == routes[way][1]) & relayed(group, kind))
                def _():
                    relay_copy(group, way, kind).wait_send()
        return carry

    lax.fori_loop(0, GROUPS, drain, 0)


def split_kernel(stacked, *refs):
    outs, sem = refs[:4], refs[4]
    copies = [pltpu.make_async_copy(stacked.at[i], outs[i], sem.at[i]) for i in range(4)]
    for copy in copies:
        copy.start()
    for copy in copies:
        copy.wait()


def solution(mesh):
    lon_count = mesh.shape["lon"]
    lat_count = mesh.shape["lat"]

    def on_device(queries, key_states, value_states, out_grad, block_lists, row_widths):
        images, rows, columns, channels = queries.shape
        tokens = rows * columns
        flat = (images, tokens, channels)
        items = images * channels // HDIM
        bf16, f32 = jnp.bfloat16, jnp.float32
        hbm_spec = pl.BlockSpec(memory_space=pltpu.HBM)
        vmem_spec = pl.BlockSpec(memory_space=pltpu.VMEM)
        smem_spec = pl.BlockSpec(memory_space=pltpu.SMEM)
        dma = pltpu.SemaphoreType.DMA
        stacked = pl.pallas_call(
            functools.partial(kernel, lon_count, lat_count),
            out_shape=pltpu.VMEM((4,) + flat, bf16),
            in_specs=[smem_spec, smem_spec] + [hbm_spec] * 4,
            out_specs=vmem_spec,
            scratch_shapes=[
                pltpu.VMEM((2, images, 2 * tokens, channels), bf16),
                pltpu.VMEM((2, images, 3 * tokens, channels), bf16),
                pltpu.VMEM((2, 2, images, 2 * HALO, channels), bf16),
                pltpu.VMEM((3 * tokens, 2 * tokens), f32),
                pltpu.VMEM((tokens + 4 * HALO, 3 * tokens), f32),
                pltpu.VMEM((items, 3 * tokens, 2 * tokens), f32),
                pltpu.VMEM((items, 3 * tokens, 2 * tokens), f32),
                pltpu.VMEM((GROUPS, 3, 8, 2 * tokens), f32),
                pltpu.VMEM((2, GROUPS, 8, 2 * tokens), f32),
                pltpu.VMEM((2, GROUPS, 8, 2 * tokens), f32),
                pltpu.VMEM((GROUPS, 2, 8, 2 * tokens), f32),
                pltpu.VMEM((GROUPS, 2, 2 * tokens, 8), f32),
                pltpu.VMEM((2, images, tokens, channels), f32),
                pltpu.VMEM((2, 2, images, 2 * HALO, channels), bf16),
                pltpu.VMEM((2, 2, images, 2 * HALO, channels), bf16),
                pltpu.VMEM((2, images, tokens, channels), f32),
                pltpu.VMEM((2, 2, images, tokens, channels), bf16),
                pltpu.VMEM((2, 2, images, tokens, channels), bf16),
                pltpu.VMEM((2, 2, images - images // 2, tokens, channels), bf16),
                dma((4,)),
                dma((GROUPS, 2)),
                dma((GROUPS, 2)),
                dma((GROUPS, 2)),
                dma((GROUPS, 2)),
                dma((GROUPS, 2)),
                dma((GROUPS, 2)),
                dma((GROUPS, 2)),
                dma((GROUPS, 2)),
                dma((GROUPS, 2)),
                dma((GROUPS, 2)),
                dma((GROUPS, 2)),
                dma((GROUPS, 2)),
                dma((GROUPS, 2)),
            ],
            compiler_params=pltpu.CompilerParams(
                collective_id=0, has_side_effects=True, vmem_limit_bytes=60 * 1024 * 1024
            ),
            cost_estimate=pl.CostEstimate(
                flops=12 * items * 192 * 128 * 128,
                bytes_accessed=8 * images * tokens * channels * 2,
                transcendentals=items * 192 * 128,
            ),
        )(
            block_lists.T,
            row_widths,
            queries.reshape(flat),
            key_states.reshape(flat),
            value_states.reshape(flat),
            out_grad.reshape(flat),
        )
        results = pl.pallas_call(
            split_kernel,
            out_shape=[jax.ShapeDtypeStruct(flat, bf16)] * 4,
            in_specs=[pl.BlockSpec(memory_space=pl.ANY)],
            out_specs=[hbm_spec] * 4,
            scratch_shapes=[dma((4,))],
            compiler_params=pltpu.CompilerParams(vmem_limit_bytes=8 * 1024 * 1024),
        )(stacked)
        return tuple(x.reshape(queries.shape) for x in results)

    split = P(None, "lat", "lon", None)
    return jax.shard_map(
        on_device,
        mesh=mesh,
        in_specs=(split, split, split, split, P(), P()),
        out_specs=(split, split, split, split),
        check_vma=False,
    )
```

```python
import functools
import math

import jax
import jax.numpy as jnp
from jax import lax
from jax.experimental import pallas as pl
from jax.experimental.pallas import tpu as pltpu
from jax.sharding import PartitionSpec as P

MESH = pl.DeviceIdType.MESH
HALO = 8
HDIM = 128
GROUPS = 8
BEHIND = 6
LAG = 11
HIDDEN = -1e30
FLOOR = -1e29


def nt(a, b):
    return lax.dot_general(a, b, (((1,), (1,)), ((), ())), preferred_element_type=jnp.float32)


def nn(a, b):
    return jnp.dot(a, b, preferred_element_type=jnp.float32)


def window(x, old, new, size, rest):
    lane = lax.broadcasted_iota(jnp.int32, x.shape, 1)
    shifted = x if old == new else pltpu.roll(x, (new - old) % HDIM, 1)
    return jnp.where((lane >= new) & (lane < new + size), shifted, rest)


def kernel(
    lon_count,
    lat_count,
    lists_ref,
    widths_ref,
    q_hbm,
    k_hbm,
    v_hbm,
    g_hbm,
    outs,
    near,
    far,
    edge_out,
    bias,
    bias_t,
    exps,
    dps,
    stats,
    stats_out,
    stats_in,
    factors,
    columns,
    near_acc,
    part_out,
    part_in,
    far_acc,
    term_out,
    term_in,
    relay,
    own_sem,
    kv_send,
    kv_recv,
    edge_send,
    edge_recv,
    stat_send,
    stat_recv,
    part_send,
    part_recv,
    term_send,
    term_recv,
    pass_send,
    pass_recv,
    relay_send,
):
    lon = lax.axis_index("lon")
    lat = lax.axis_index("lat")
    left = lax.rem(lon + lon_count - 1, lon_count)
    right = lax.rem(lon + 1, lon_count)
    has_above = lat > 0
    has_below = lat < lat_count - 1
    middle = lat_count // 2
    beside = lon + 1 - 2 * lax.rem(lon, 2)
    is_middle = (lat == middle - 1) | (lat == middle)
    is_end = (lat == 0) | (lat == lat_count - 1)
    routes = ((middle, 0, middle - 1), (middle - 1, lat_count - 1, middle))
    images, tokens, channels = q_hbm.shape
    heads = channels // HDIM
    group_heads = heads // GROUPS
    group_items = images * group_heads
    group_lanes = group_heads * HDIM
    scale = HDIM ** -0.5
    half = images // 2
    whole, direct, passing = slice(0, images), slice(0, half), slice(half, images)

    sides = ({"lon": left}, {"lon": right})
    tiles = ({"lat": lat - 1}, {"lat": lat + 1})
    exists = (has_above, has_below)

    own_copies = [
        pltpu.make_async_copy(k_hbm, far.at[0, :, tokens : 2 * tokens, :], own_sem.at[0]),
        pltpu.make_async_copy(v_hbm, far.at[1, :, tokens : 2 * tokens, :], own_sem.at[1]),
        pltpu.make_async_copy(q_hbm, near.at[0, :, 0:tokens, :], own_sem.at[2]),
        pltpu.make_async_copy(g_hbm, near.at[1, :, 0:tokens, :], own_sem.at[3]),
    ]
    for copy in own_copies:
        copy.start()

    barrier = pltpu.get_barrier_semaphore()
    for side in sides:
        pl.semaphore_signal(barrier, inc=1, device_id=side, device_id_type=MESH)
    for there, tile in zip(exists, tiles):
        @pl.when(there)
        def _():
            pl.semaphore_signal(barrier, inc=1, device_id=tile, device_id_type=MESH)
    for here, far_lats in ((is_middle, (0, lat_count - 1)), (is_end, (middle - 1, middle))):
        @pl.when(here)
        def _():
            for far_lat in far_lats:
                pl.semaphore_signal(barrier, inc=1, device_id={"lat": far_lat, "lon": beside}, device_id_type=MESH)
    pl.semaphore_wait(
        barrier,
        2
        + jnp.where(has_above, 1, 0)
        + jnp.where(has_below, 1, 0)
        + jnp.where(is_middle | is_end, 2, 0),
    )

    def lanes(group):
        start = group * group_lanes
        return pl.ds(start if isinstance(group, int) else pl.multiple_of(start, HDIM), group_lanes)

    def remote(source, target, send, recv, device):
        return pltpu.make_async_remote_copy(
            src_ref=source, dst_ref=target, send_sem=send, recv_sem=recv, device_id=device, device_id_type=MESH
        )

    def kv_copy(group, way, some):
        start = 2 * tokens if way == 0 else 0
        return remote(
            far.at[:, some, tokens : 2 * tokens, lanes(group)],
            far.at[:, some, start : start + tokens, lanes(group)],
            kv_send.at[group, way],
            kv_recv.at[group, 1 - way],
            tiles[way],
        )

    def edge_copy(group, way):
        start = tokens + 2 * HALO if way == 0 else tokens
        return remote(
            edge_out.at[way, :, :, :, lanes(group)],
            near.at[:, :, start : start + 2 * HALO, lanes(group)],
            edge_send.at[group, way],
            edge_recv.at[group, 1 - way],
            sides[way],
        )

    def stat_copy(group, way):
        return remote(
            stats_out.at[way, group],
            stats_in.at[1 - way, group],
            stat_send.at[group, way],
            stat_recv.at[group, 1 - way],
            sides[way],
        )

    def part_copy(group, way):
        return remote(
            part_out.at[way, :, :, :, lanes(group)],
            part_in.at[1 - way, :, :, :, lanes(group)],
            part_send.at[group, way],
            part_recv.at[group, 1 - way],
            sides[way],
        )

    def term_copy(group, way, some):
        return remote(
            term_out.at[way, :, some, :, lanes(group)],
            term_in.at[1 - way, :, some, :, lanes(group)],
            term_send.at[group, way],
            term_recv.at[group, 1 - way],
            tiles[way],
        )

    def pass_copy(group, way, kind):
        return remote(
            far.at[:, passing, tokens : 2 * tokens, lanes(group)]
            if kind == 0
            else term_out.at[way, :, passing, :, lanes(group)],
            relay.at[kind, :, :, :, lanes(group)],
            pass_send.at[group, kind],
            pass_recv.at[group, kind],
            {"lat": routes[way][1], "lon": beside},
        )

    def relay_copy(group, way, kind):
        start = 2 * tokens if way == 0 else 0
        return remote(
            relay.at[kind, :, :, :, lanes(group)],
            far.at[:, passing, start : start + tokens, lanes(group)]
            if kind == 0
            else term_in.at[1 - way, :, passing, :, lanes(group)],
            relay_send.at[group, kind],
            (kv_recv if kind == 0 else term_recv).at[group, 1 - way],
            {"lat": routes[way][2], "lon": beside},
        )

    def relayed(group, kind):
        return True if kind == 0 else group < GROUPS - 2

    def to_tiles(group, kind, act):
        copy = (kv_copy, term_copy)[kind]
        for way in range(2):
            crossing = (lat == routes[way][0]) & relayed(group, kind)

            @pl.when(exists[way] & jnp.logical_not(crossing))
            def _():
                act(copy(group, way, whole))

            @pl.when(crossing)
            def _():
                act(copy(group, way, direct))
                act(pass_copy(group, way, kind))

    def from_tiles(group, kind):
        copy = (kv_copy, term_copy)[kind]
        for origin in range(2):
            @pl.when(exists[origin])
            def _():
                copy(group, 1 - origin, whole).wait_recv()

    def forward(group, kind):
        for way in range(2):
            @pl.when((lat == routes[way][1]) & relayed(group, kind))
            def _():
                pass_copy(group, way, kind).wait_recv()
                relay_copy(group, way, kind).start()

    def start(copy):
        copy.start()

    def wait_send(copy):
        copy.wait_send()

    def send_edges(group):
        for which in range(2):
            for image in range(images):
                def half(start, low):
                    block = near[which, image, start : start + 16, lanes(group)].astype(jnp.float32)
                    return block[low : low + HALO]

                edge_out[0, which, image, :, lanes(group)] = jnp.concatenate(
                    [half(0, 0), half(32, 0)], axis=0
                ).astype(jnp.bfloat16)
                edge_out[1, which, image, :, lanes(group)] = jnp.concatenate(
                    [half(16, HALO), half(48, HALO)], axis=0
                ).astype(jnp.bfloat16)
        for way in range(2):
            edge_copy(group, way).start()

    own_copies[0].wait()
    own_copies[1].wait()
    to_tiles(0, 0, start)
    own_copies[2].wait()
    own_copies[3].wait()
    send_edges(0)

    def send_group(group, carry):
        to_tiles(group, 0, start)
        send_edges(group)
        return carry

    lax.fori_loop(1, GROUPS, send_group, 0)

    near[:, :, tokens + 4 * HALO :, :] = jnp.zeros(
        (2, images, near.shape[2] - tokens - 4 * HALO, channels), jnp.bfloat16
    )
    for way in range(2):
        @pl.when(jnp.logical_not(exists[way]))
        def _():
            start = 0 if way == 0 else 2 * tokens
            far[:, :, start : start + tokens, :] = jnp.zeros((2, images, tokens, channels), jnp.bfloat16)
            term_in[way] = jnp.zeros((2, images, tokens, channels), jnp.bfloat16)

    def listed(target):
        found = (
            (lists_ref[0, lat] == target)
            | (lists_ref[1, lat] == target)
            | (lists_ref[2, lat] == target)
        ) & (target >= 0)
        return jnp.where(found, 1, 0)

    def mask(shape, key_axis):
        key = lax.broadcasted_iota(jnp.int32, shape, key_axis)
        query = lax.broadcasted_iota(jnp.int32, shape, 1 - key_axis)
        key_tile = key >> 6
        key_col = key & 31
        edge = query - tokens
        is_own = query < tokens
        from_left = edge < 2 * HALO
        query_col = jnp.where(
            is_own, query & 31, jnp.where(from_left, (edge & 7) - HALO, 32 + (edge & 7))
        )
        query_row = jnp.where(is_own, query >> 5, (edge >> 3) & 1)
        width = jnp.where(query_row == 0, widths_ref[2 * lat], widths_ref[2 * lat + 1])
        active = jnp.where(
            key_tile == 0, listed(lat - 1), jnp.where(key_tile == 1, listed(lat), listed(lat + 1))
        )
        seen = (jnp.abs(query_col - key_col) <= width) & (active == 1) & (edge < 4 * HALO)
        return jnp.where(seen, 0.0, HIDDEN)

    bias[...] = mask(bias.shape, 0)
    bias_t[...] = mask(bias_t.shape, 1)

    places = [(image, head) for image in range(images) for head in range(group_heads)]

    def cols(group, head):
        return pl.ds(pl.multiple_of(group * group_lanes + head * HDIM, HDIM), HDIM)

    to_log2 = scale * math.log2(math.e)

    def scores(group):
        tops, sums, balances = [], [], []
        for item, (image, head) in enumerate(places):
            at = cols(group, head)
            raw = nt(far[0, image, :, at], near[0, image, :, at]) * to_log2 + bias[...]
            dp = nt(far[1, image, :, at], near[1, image, :, at])
            top = jnp.maximum(jnp.max(raw, axis=0, keepdims=True), FLOOR)
            e = jnp.exp2(raw - top)
            slot = group * group_items + item
            exps[slot] = e
            dps[slot] = dp
            tops.append(top)
            sums.append(jnp.sum(e, axis=0, keepdims=True))
            balances.append(jnp.sum(e * dp, axis=0, keepdims=True))
        for kind, found in enumerate((tops, sums, balances)):
            rows = found + [jnp.zeros_like(found[0])] * (8 - len(found))
            stats[group, kind] = jnp.concatenate(rows, axis=0)
        for way, moves in enumerate((((0, 0, 8), (32, 8, 8), (64, 16, 16)), ((24, 0, 8), (56, 8, 8), (80, 16, 16)))):
            packed = jnp.zeros((8, HDIM), jnp.float32)
            for kind in range(3):
                for old, new, size in moves:
                    packed = window(stats[group, kind], old, 32 * kind + new, size, packed)
            stats_out[way, group] = packed
        for way in range(2):
            stat_copy(group, way).start()

    def combine(group):
        for way in range(2):
            stat_copy(group, way).wait_recv()
        others = []
        for kind in range(3):
            other = jnp.full((8, HDIM), FLOOR if kind == 0 else 0.0, jnp.float32)
            for origin, moves in enumerate((((0, 64, 16), (16, 0, 8), (24, 32, 8)), ((0, 80, 16), (16, 24, 8), (24, 56, 8)))):
                for old, new, size in moves:
                    other = window(stats_in[origin, group], 32 * kind + old, new, size, other)
            others.append(other)
        top, total, balance = (stats[group, kind] for kind in range(3))
        top2, total2, balance2 = others
        high = jnp.maximum(top, top2)
        part = jnp.exp2(top - high)
        part2 = jnp.exp2(top2 - high)
        whole_sum = jnp.maximum(part * total + part2 * total2, 0.5)
        inverse = 1.0 / whole_sum
        balance = (part * balance + part2 * balance2) * inverse
        factors[group, 0] = part * inverse
        factors[group, 1] = balance
        columns[group, 0] = jnp.transpose(high + jnp.log2(whole_sum))
        columns[group, 1] = jnp.transpose(balance)

    def gradients(group):
        seen = tokens + 4 * HALO
        for item, (image, head) in enumerate(places):
            at = cols(group, head)
            slot = group * group_items + item
            keys, values = far[0, image, :, at], far[1, image, :, at]
            queries, grads = near[0, image, :, at], near[1, image, :, at]
            w = exps[slot] * factors[group, 0, item : item + 1, :]
            ds = w * (dps[slot] - factors[group, 1, item : item + 1, :])
            dk = nn(ds.astype(jnp.bfloat16), queries) * scale
            dv = nn(w.astype(jnp.bfloat16), grads)
            for which, x in enumerate((dk, dv)):
                far_acc[which, image, :, at] = x[tokens : 2 * tokens]
                term_out[0, which, image, :, at] = x[0:tokens].astype(jnp.bfloat16)
                term_out[1, which, image, :, at] = x[2 * tokens :].astype(jnp.bfloat16)
            raw = nt(queries[0:seen], keys) * to_log2 + bias_t[...]
            dp = nt(grads[0:seen], values)
            w = jnp.exp2(raw - columns[group, 0, 0:seen, item : item + 1])
            ds = w * (dp - columns[group, 1, 0:seen, item : item + 1])
            att = nn(w.astype(jnp.bfloat16), values)
            dq = nn(ds.astype(jnp.bfloat16), keys) * scale
            for which, x in enumerate((att, dq)):
                near_acc[which, image, :, at] = x[0:tokens]
                for way in range(2):
                    low = tokens + 2 * HALO * way
                    part_out[way, which, image, :, at] = x[low : low + 2 * HALO].astype(jnp.bfloat16)
        to_tiles(group, 1, start)
        for way in range(2):
            part_copy(group, way).start()

    def finish(group):
        for way in range(2):
            part_copy(group, way).wait_recv()
        from_tiles(group, 1)
        at = lanes(group)
        for image in range(images):
            for which in range(2):
                acc = near_acc[which, image, :, at]
                add_l = part_in[0, which, image, :, at].astype(jnp.float32)
                add_r = part_in[1, which, image, :, at].astype(jnp.float32)
                rows = []
                for r in range(2):
                    here = acc[32 * r : 32 * r + 32]
                    rows.append(here[0:8] + add_l[8 * r : 8 * r + 8])
                    rows.append(here[8:24])
                    rows.append(here[24:32] + add_r[8 * r : 8 * r + 8])
                outs[which, image, :, at] = jnp.concatenate(rows, axis=0).astype(jnp.bfloat16)
            for which in range(2):
                total = far_acc[which, image, :, at]
                for way in range(2):
                    total = total + term_in[way, which, image, :, at].astype(jnp.float32)
                outs[2 + which, image, :, at] = total.astype(jnp.bfloat16)

    def step(index, carry):
        @pl.when(index < GROUPS)
        def _():
            from_tiles(index, 0)
            for origin in range(2):
                edge_copy(index, 1 - origin).wait_recv()

            forward(index, 0)
            scores(index)

        @pl.when((index >= BEHIND + 2) & (index < GROUPS + BEHIND))
        def _():
            forward(index - BEHIND - 2, 1)

        @pl.when((index >= BEHIND) & (index < GROUPS + BEHIND))
        def _():
            combine(index - BEHIND)
            gradients(index - BEHIND)

        @pl.when(index >= LAG)
        def _():
            finish(index - LAG)

        return carry

    lax.fori_loop(0, GROUPS + LAG, step, 0)

    def drain(group, carry):
        for way in range(2):
            edge_copy(group, way).wait_send()
            stat_copy(group, way).wait_send()
            part_copy(group, way).wait_send()
        for kind in range(2):
            to_tiles(group, kind, wait_send)
            for way in range(2):
                @pl.when((lat == routes[way][1]) & relayed(group, kind))
                def _():
                    relay_copy(group, way, kind).wait_send()
        return carry

    lax.fori_loop(0, GROUPS, drain, 0)


def split_kernel(stacked, *refs):
    outs, sem = refs[:4], refs[4]
    copies = [pltpu.make_async_copy(stacked.at[i], outs[i], sem.at[i]) for i in range(4)]
    for copy in copies:
        copy.start()
    for copy in copies:
        copy.wait()


def solution(mesh):
    lon_count = mesh.shape["lon"]
    lat_count = mesh.shape["lat"]

    def on_device(queries, key_states, value_states, out_grad, block_lists, row_widths):
        images, rows, columns, channels = queries.shape
        tokens = rows * columns
        flat = (images, tokens, channels)
        items = images * channels // HDIM
        bf16, f32 = jnp.bfloat16, jnp.float32
        hbm_spec = pl.BlockSpec(memory_space=pltpu.HBM)
        vmem_spec = pl.BlockSpec(memory_space=pltpu.VMEM)
        smem_spec = pl.BlockSpec(memory_space=pltpu.SMEM)
        dma = pltpu.SemaphoreType.DMA
        stacked = pl.pallas_call(
            functools.partial(kernel, lon_count, lat_count),
            out_shape=pltpu.VMEM((4,) + flat, bf16),
            in_specs=[smem_spec, smem_spec] + [hbm_spec] * 4,
            out_specs=vmem_spec,
            scratch_shapes=[
                pltpu.VMEM((2, images, 2 * tokens, channels), bf16),
                pltpu.VMEM((2, images, 3 * tokens, channels), bf16),
                pltpu.VMEM((2, 2, images, 2 * HALO, channels), bf16),
                pltpu.VMEM((3 * tokens, 2 * tokens), f32),
                pltpu.VMEM((tokens + 4 * HALO, 3 * tokens), f32),
                pltpu.VMEM((items, 3 * tokens, 2 * tokens), f32),
                pltpu.VMEM((items, 3 * tokens, 2 * tokens), f32),
                pltpu.VMEM((GROUPS, 3, 8, 2 * tokens), f32),
                pltpu.VMEM((2, GROUPS, 8, 2 * tokens), f32),
                pltpu.VMEM((2, GROUPS, 8, 2 * tokens), f32),
                pltpu.VMEM((GROUPS, 2, 8, 2 * tokens), f32),
                pltpu.VMEM((GROUPS, 2, 2 * tokens, 8), f32),
                pltpu.VMEM((2, images, tokens, channels), f32),
                pltpu.VMEM((2, 2, images, 2 * HALO, channels), bf16),
                pltpu.VMEM((2, 2, images, 2 * HALO, channels), bf16),
                pltpu.VMEM((2, images, tokens, channels), f32),
                pltpu.VMEM((2, 2, images, tokens, channels), bf16),
                pltpu.VMEM((2, 2, images, tokens, channels), bf16),
                pltpu.VMEM((2, 2, images - images // 2, tokens, channels), bf16),
                dma((4,)),
                dma((GROUPS, 2)),
                dma((GROUPS, 2)),
                dma((GROUPS, 2)),
                dma((GROUPS, 2)),
                dma((GROUPS, 2)),
                dma((GROUPS, 2)),
                dma((GROUPS, 2)),
                dma((GROUPS, 2)),
                dma((GROUPS, 2)),
                dma((GROUPS, 2)),
                dma((GROUPS, 2)),
                dma((GROUPS, 2)),
                dma((GROUPS, 2)),
            ],
            compiler_params=pltpu.CompilerParams(
                collective_id=0, has_side_effects=True, vmem_limit_bytes=60 * 1024 * 1024
            ),
            cost_estimate=pl.CostEstimate(
                flops=12 * items * 192 * 128 * 128,
                bytes_accessed=8 * images * tokens * channels * 2,
                transcendentals=items * 192 * 128,
            ),
        )(
            block_lists.T,
            row_widths,
            queries.reshape(flat),
            key_states.reshape(flat),
            value_states.reshape(flat),
            out_grad.reshape(flat),
        )
        results = pl.pallas_call(
            split_kernel,
            out_shape=[jax.ShapeDtypeStruct(flat, bf16)] * 4,
            in_specs=[pl.BlockSpec(memory_space=pl.ANY)],
            out_specs=[hbm_spec] * 4,
            scratch_shapes=[dma((4,))],
            compiler_params=pltpu.CompilerParams(vmem_limit_bytes=8 * 1024 * 1024),
        )(stacked)
        return tuple(x.reshape(queries.shape) for x in results)

    split = P(None, "lat", "lon", None)
    return jax.shard_map(
        on_device,
        mesh=mesh,
        in_specs=(split, split, split, split, P(), P()),
        out_specs=(split, split, split, split),
        check_vma=False,
    )
```

```python
import functools
import math

import jax
import jax.numpy as jnp
from jax import lax
from jax.experimental import pallas as pl
from jax.experimental.pallas import tpu as pltpu
from jax.sharding import PartitionSpec as P

MESH = pl.DeviceIdType.MESH
HALO = 8
HDIM = 128
GROUPS = 8
BEHIND = 6
LAG = 11
HIDDEN = -1e30
FLOOR = -1e29


def nt(a, b):
    return lax.dot_general(a, b, (((1,), (1,)), ((), ())), preferred_element_type=jnp.float32)


def nn(a, b):
    return jnp.dot(a, b, preferred_element_type=jnp.float32)


def window(x, old, new, size, rest):
    lane = lax.broadcasted_iota(jnp.int32, x.shape, 1)
    shifted = x if old == new else pltpu.roll(x, (new - old) % HDIM, 1)
    return jnp.where((lane >= new) & (lane < new + size), shifted, rest)


def kernel(
    lon_count,
    lat_count,
    lists_ref,
    widths_ref,
    q_hbm,
    k_hbm,
    v_hbm,
    g_hbm,
    outs,
    near,
    far,
    edge_out,
    bias,
    bias_t,
    exps,
    dps,
    stats,
    stats_out,
    stats_in,
    factors,
    columns,
    near_acc,
    part_out,
    part_in,
    far_acc,
    term_out,
    term_in,
    relay,
    own_sem,
    kv_send,
    kv_recv,
    edge_send,
    edge_recv,
    stat_send,
    stat_recv,
    part_send,
    part_recv,
    term_send,
    term_recv,
    pass_send,
    pass_recv,
    relay_send,
):
    lon = lax.axis_index("lon")
    lat = lax.axis_index("lat")
    left = lax.rem(lon + lon_count - 1, lon_count)
    right = lax.rem(lon + 1, lon_count)
    has_above = lat > 0
    has_below = lat < lat_count - 1
    middle = lat_count // 2
    beside = lon + 1 - 2 * lax.rem(lon, 2)
    is_middle = (lat == middle - 1) | (lat == middle)
    routes = ((middle, 0, middle - 1), (middle - 1, lat_count - 1, middle))
    images, tokens, channels = q_hbm.shape
    heads = channels // HDIM
    group_heads = heads // GROUPS
    group_items = images * group_heads
    group_lanes = group_heads * HDIM
    scale = HDIM ** -0.5
    half = images // 2
    whole, direct, passing = slice(0, images), slice(0, half), slice(half, images)

    sides = ({"lon": left}, {"lon": right})
    tiles = ({"lat": lat - 1}, {"lat": lat + 1})
    exists = (has_above, has_below)

    own_copies = [
        pltpu.make_async_copy(k_hbm, far.at[0, :, tokens : 2 * tokens, :], own_sem.at[0]),
        pltpu.make_async_copy(v_hbm, far.at[1, :, tokens : 2 * tokens, :], own_sem.at[1]),
        pltpu.make_async_copy(q_hbm, near.at[0, :, 0:tokens, :], own_sem.at[2]),
        pltpu.make_async_copy(g_hbm, near.at[1, :, 0:tokens, :], own_sem.at[3]),
    ]
    for copy in own_copies:
        copy.start()

    barrier = pltpu.get_barrier_semaphore()
    for side in sides:
        pl.semaphore_signal(barrier, inc=1, device_id=side, device_id_type=MESH)
    for there, tile in zip(exists, tiles):
        @pl.when(there)
        def _():
            pl.semaphore_signal(barrier, inc=1, device_id=tile, device_id_type=MESH)
    for route in routes:
        @pl.when(lat == route[1])
        def _():
            pl.semaphore_signal(barrier, inc=1, device_id={"lat": route[0], "lon": beside}, device_id_type=MESH)
    pl.semaphore_wait(
        barrier,
        2 + jnp.where(has_above, 1, 0) + jnp.where(has_below, 1, 0) + jnp.where(is_middle, 1, 0),
    )

    def lanes(group):
        start = group * group_lanes
        return pl.ds(start if isinstance(group, int) else pl.multiple_of(start, HDIM), group_lanes)

    def remote(source, target, send, recv, device):
        return pltpu.make_async_remote_copy(
            src_ref=source, dst_ref=target, send_sem=send, recv_sem=recv, device_id=device, device_id_type=MESH
        )

    def kv_copy(group, way, some):
        start = 2 * tokens if way == 0 else 0
        return remote(
            far.at[:, some, tokens : 2 * tokens, lanes(group)],
            far.at[:, some, start : start + tokens, lanes(group)],
            kv_send.at[group, way],
            kv_recv.at[group, 1 - way],
            tiles[way],
        )

    def edge_copy(group, way):
        start = tokens + 2 * HALO if way == 0 else tokens
        return remote(
            edge_out.at[way, :, :, :, lanes(group)],
            near.at[:, :, start : start + 2 * HALO, lanes(group)],
            edge_send.at[group, way],
            edge_recv.at[group, 1 - way],
            sides[way],
        )

    def stat_copy(group, way):
        return remote(
            stats_out.at[way, group],
            stats_in.at[1 - way, group],
            stat_send.at[group, way],
            stat_recv.at[group, 1 - way],
            sides[way],
        )

    def part_copy(group, way):
        return remote(
            part_out.at[way, :, :, :, lanes(group)],
            part_in.at[1 - way, :, :, :, lanes(group)],
            part_send.at[group, way],
            part_recv.at[group, 1 - way],
            sides[way],
        )

    def term_copy(group, way, some):
        return remote(
            term_out.at[way, :, some, :, lanes(group)],
            term_in.at[1 - way, :, some, :, lanes(group)],
            term_send.at[group, way],
            term_recv.at[group, 1 - way],
            tiles[way],
        )

    def pass_copy(group, way, kind):
        return remote(
            far.at[:, passing, tokens : 2 * tokens, lanes(group)]
            if kind == 0
            else term_out.at[way, :, passing, :, lanes(group)],
            relay.at[kind, :, :, :, lanes(group)],
            pass_send.at[group, kind],
            pass_recv.at[group, kind],
            {"lat": routes[way][1], "lon": beside},
        )

    def relay_copy(group, way, kind):
        start = 2 * tokens if way == 0 else 0
        return remote(
            relay.at[kind, :, :, :, lanes(group)],
            far.at[:, passing, start : start + tokens, lanes(group)]
            if kind == 0
            else term_in.at[1 - way, :, passing, :, lanes(group)],
            relay_send.at[group, kind],
            (kv_recv if kind == 0 else term_recv).at[group, 1 - way],
            {"lat": routes[way][2], "lon": beside},
        )

    def relayed(group, kind):
        return True if kind == 0 else group < GROUPS - 2

    def to_tiles(group, kind, act):
        copy = (kv_copy, term_copy)[kind]
        for way in range(2):
            crossing = (lat == routes[way][0]) & relayed(group, kind)

            @pl.when(exists[way] & jnp.logical_not(crossing))
            def _():
                act(copy(group, way, whole))

            @pl.when(crossing)
            def _():
                act(copy(group, way, direct))
                act(pass_copy(group, way, kind))

    def from_tiles(group, kind):
        copy = (kv_copy, term_copy)[kind]
        for origin in range(2):
            @pl.when(exists[origin])
            def _():
                copy(group, 1 - origin, whole).wait_recv()

    def forward(group, kind):
        for way in range(2):
            @pl.when((lat == routes[way][1]) & relayed(group, kind))
            def _():
                pass_copy(group, way, kind).wait_recv()
                relay_copy(group, way, kind).start()

    def start(copy):
        copy.start()

    def wait_send(copy):
        copy.wait_send()

    def send_edges(group):
        for which in range(2):
            for image in range(images):
                def half(start, low):
                    block = near[which, image, start : start + 16, lanes(group)].astype(jnp.float32)
                    return block[low : low + HALO]

                edge_out[0, which, image, :, lanes(group)] = jnp.concatenate(
                    [half(0, 0), half(32, 0)], axis=0
                ).astype(jnp.bfloat16)
                edge_out[1, which, image, :, lanes(group)] = jnp.concatenate(
                    [half(16, HALO), half(48, HALO)], axis=0
                ).astype(jnp.bfloat16)
        for way in range(2):
            edge_copy(group, way).start()

    own_copies[0].wait()
    own_copies[1].wait()
    to_tiles(0, 0, start)
    own_copies[2].wait()
    own_copies[3].wait()
    send_edges(0)

    def send_group(group, carry):
        to_tiles(group, 0, start)
        send_edges(group)
        return carry

    lax.fori_loop(1, GROUPS, send_group, 0)

    near[:, :, tokens + 4 * HALO :, :] = jnp.zeros(
        (2, images, near.shape[2] - tokens - 4 * HALO, channels), jnp.bfloat16
    )
    for way in range(2):
        @pl.when(jnp.logical_not(exists[way]))
        def _():
            start = 0 if way == 0 else 2 * tokens
            far[:, :, start : start + tokens, :] = jnp.zeros((2, images, tokens, channels), jnp.bfloat16)
            term_in[way] = jnp.zeros((2, images, tokens, channels), jnp.bfloat16)

    def listed(target):
        found = (
            (lists_ref[0, lat] == target)
            | (lists_ref[1, lat] == target)
            | (lists_ref[2, lat] == target)
        ) & (target >= 0)
        return jnp.where(found, 1, 0)

    def mask(shape, key_axis):
        key = lax.broadcasted_iota(jnp.int32, shape, key_axis)
        query = lax.broadcasted_iota(jnp.int32, shape, 1 - key_axis)
        key_tile = key >> 6
        key_col = key & 31
        edge = query - tokens
        is_own = query < tokens
        from_left = edge < 2 * HALO
        query_col = jnp.where(
            is_own, query & 31, jnp.where(from_left, (edge & 7) - HALO, 32 + (edge & 7))
        )
        query_row = jnp.where(is_own, query >> 5, (edge >> 3) & 1)
        width = jnp.where(query_row == 0, widths_ref[2 * lat], widths_ref[2 * lat + 1])
        active = jnp.where(
            key_tile == 0, listed(lat - 1), jnp.where(key_tile == 1, listed(lat), listed(lat + 1))
        )
        seen = (jnp.abs(query_col - key_col) <= width) & (active == 1) & (edge < 4 * HALO)
        return jnp.where(seen, 0.0, HIDDEN)

    bias[...] = mask(bias.shape, 0)
    bias_t[...] = mask(bias_t.shape, 1)

    places = [(image, head) for image in range(images) for head in range(group_heads)]

    def cols(group, head):
        return pl.ds(pl.multiple_of(group * group_lanes + head * HDIM, HDIM), HDIM)

    to_log2 = scale * math.log2(math.e)

    def scores(group):
        tops, sums, balances = [], [], []
        for item, (image, head) in enumerate(places):
            at = cols(group, head)
            raw = nt(far[0, image, :, at], near[0, image, :, at]) * to_log2 + bias[...]
            dp = nt(far[1, image, :, at], near[1, image, :, at])
            top = jnp.maximum(jnp.max(raw, axis=0, keepdims=True), FLOOR)
            e = jnp.exp2(raw - top)
            slot = group * group_items + item
            exps[slot] = e
            dps[slot] = dp
            tops.append(top)
            sums.append(jnp.sum(e, axis=0, keepdims=True))
            balances.append(jnp.sum(e * dp, axis=0, keepdims=True))
        for kind, found in enumerate((tops, sums, balances)):
            rows = found + [jnp.zeros_like(found[0])] * (8 - len(found))
            stats[group, kind] = jnp.concatenate(rows, axis=0)
        for way, moves in enumerate((((0, 0, 8), (32, 8, 8), (64, 16, 16)), ((24, 0, 8), (56, 8, 8), (80, 16, 16)))):
            packed = jnp.zeros((8, HDIM), jnp.float32)
            for kind in range(3):
                for old, new, size in moves:
                    packed = window(stats[group, kind], old, 32 * kind + new, size, packed)
            stats_out[way, group] = packed
        for way in range(2):
            stat_copy(group, way).start()

    def combine(group):
        for way in range(2):
            stat_copy(group, way).wait_recv()
        others = []
        for kind in range(3):
            other = jnp.full((8, HDIM), FLOOR if kind == 0 else 0.0, jnp.float32)
            for origin, moves in enumerate((((0, 64, 16), (16, 0, 8), (24, 32, 8)), ((0, 80, 16), (16, 24, 8), (24, 56, 8)))):
                for old, new, size in moves:
                    other = window(stats_in[origin, group], 32 * kind + old, new, size, other)
            others.append(other)
        top, total, balance = (stats[group, kind] for kind in range(3))
        top2, total2, balance2 = others
        high = jnp.maximum(top, top2)
        part = jnp.exp2(top - high)
        part2 = jnp.exp2(top2 - high)
        whole_sum = jnp.maximum(part * total + part2 * total2, 0.5)
        inverse = 1.0 / whole_sum
        balance = (part * balance + part2 * balance2) * inverse
        factors[group, 0] = part * inverse
        factors[group, 1] = balance
        columns[group, 0] = jnp.transpose(high + jnp.log2(whole_sum))
        columns[group, 1] = jnp.transpose(balance)

    def gradients(group):
        seen = tokens + 4 * HALO
        for item, (image, head) in enumerate(places):
            at = cols(group, head)
            slot = group * group_items + item
            keys, values = far[0, image, :, at], far[1, image, :, at]
            queries, grads = near[0, image, :, at], near[1, image, :, at]
            w = exps[slot] * factors[group, 0, item : item + 1, :]
            ds = w * (dps[slot] - factors[group, 1, item : item + 1, :])
            dk = nn(ds.astype(jnp.bfloat16), queries) * scale
            dv = nn(w.astype(jnp.bfloat16), grads)
            for which, x in enumerate((dk, dv)):
                far_acc[which, image, :, at] = x[tokens : 2 * tokens]
                term_out[0, which, image, :, at] = x[0:tokens].astype(jnp.bfloat16)
                term_out[1, which, image, :, at] = x[2 * tokens :].astype(jnp.bfloat16)
            raw = nt(queries[0:seen], keys) * to_log2 + bias_t[...]
            dp = nt(grads[0:seen], values)
            w = jnp.exp2(raw - columns[group, 0, 0:seen, item : item + 1])
            ds = w * (dp - columns[group, 1, 0:seen, item : item + 1])
            att = nn(w.astype(jnp.bfloat16), values)
            dq = nn(ds.astype(jnp.bfloat16), keys) * scale
            for which, x in enumerate((att, dq)):
                near_acc[which, image, :, at] = x[0:tokens]
                for way in range(2):
                    low = tokens + 2 * HALO * way
                    part_out[way, which, image, :, at] = x[low : low + 2 * HALO].astype(jnp.bfloat16)
        to_tiles(group, 1, start)
        for way in range(2):
            part_copy(group, way).start()

    def finish(group):
        for way in range(2):
            part_copy(group, way).wait_recv()
        from_tiles(group, 1)
        at = lanes(group)
        for image in range(images):
            for which in range(2):
                acc = near_acc[which, image, :, at]
                add_l = part_in[0, which, image, :, at].astype(jnp.float32)
                add_r = part_in[1, which, image, :, at].astype(jnp.float32)
                rows = []
                for r in range(2):
                    here = acc[32 * r : 32 * r + 32]
                    rows.append(here[0:8] + add_l[8 * r : 8 * r + 8])
                    rows.append(here[8:24])
                    rows.append(here[24:32] + add_r[8 * r : 8 * r + 8])
                outs[which, image, :, at] = jnp.concatenate(rows, axis=0).astype(jnp.bfloat16)
            for which in range(2):
                total = far_acc[which, image, :, at]
                for way in range(2):
                    total = total + term_in[way, which, image, :, at].astype(jnp.float32)
                outs[2 + which, image, :, at] = total.astype(jnp.bfloat16)

    def step(index, carry):
        @pl.when(index < GROUPS // 2)
        def _():
            forward(2 * index, 0)
            forward(2 * index + 1, 0)

        @pl.when(index < GROUPS)
        def _():
            from_tiles(index, 0)
            for origin in range(2):
                edge_copy(index, 1 - origin).wait_recv()

            scores(index)

        @pl.when((index >= BEHIND + 2) & (index < GROUPS + BEHIND))
        def _():
            forward(index - BEHIND - 2, 1)

        @pl.when((index >= BEHIND) & (index < GROUPS + BEHIND))
        def _():
            combine(index - BEHIND)
            gradients(index - BEHIND)

        @pl.when(index >= LAG)
        def _():
            finish(index - LAG)

        return carry

    lax.fori_loop(0, GROUPS + LAG, step, 0)

    def drain(group, carry):
        for way in range(2):
            edge_copy(group, way).wait_send()
            stat_copy(group, way).wait_send()
            part_copy(group, way).wait_send()
        for kind in range(2):
            to_tiles(group, kind, wait_send)
            for way in range(2):
                @pl.when((lat == routes[way][1]) & relayed(group, kind))
                def _():
                    relay_copy(group, way, kind).wait_send()
        return carry

    lax.fori_loop(0, GROUPS, drain, 0)


def split_kernel(stacked, *refs):
    outs, sem = refs[:4], refs[4]
    copies = [pltpu.make_async_copy(stacked.at[i], outs[i], sem.at[i]) for i in range(4)]
    for copy in copies:
        copy.start()
    for copy in copies:
        copy.wait()


def solution(mesh):
    lon_count = mesh.shape["lon"]
    lat_count = mesh.shape["lat"]

    def on_device(queries, key_states, value_states, out_grad, block_lists, row_widths):
        images, rows, columns, channels = queries.shape
        tokens = rows * columns
        flat = (images, tokens, channels)
        items = images * channels // HDIM
        bf16, f32 = jnp.bfloat16, jnp.float32
        hbm_spec = pl.BlockSpec(memory_space=pltpu.HBM)
        vmem_spec = pl.BlockSpec(memory_space=pltpu.VMEM)
        smem_spec = pl.BlockSpec(memory_space=pltpu.SMEM)
        dma = pltpu.SemaphoreType.DMA
        stacked = pl.pallas_call(
            functools.partial(kernel, lon_count, lat_count),
            out_shape=pltpu.VMEM((4,) + flat, bf16),
            in_specs=[smem_spec, smem_spec] + [hbm_spec] * 4,
            out_specs=vmem_spec,
            scratch_shapes=[
                pltpu.VMEM((2, images, 2 * tokens, channels), bf16),
                pltpu.VMEM((2, images, 3 * tokens, channels), bf16),
                pltpu.VMEM((2, 2, images, 2 * HALO, channels), bf16),
                pltpu.VMEM((3 * tokens, 2 * tokens), f32),
                pltpu.VMEM((tokens + 4 * HALO, 3 * tokens), f32),
                pltpu.VMEM((items, 3 * tokens, 2 * tokens), f32),
                pltpu.VMEM((items, 3 * tokens, 2 * tokens), f32),
                pltpu.VMEM((GROUPS, 3, 8, 2 * tokens), f32),
                pltpu.VMEM((2, GROUPS, 8, 2 * tokens), f32),
                pltpu.VMEM((2, GROUPS, 8, 2 * tokens), f32),
                pltpu.VMEM((GROUPS, 2, 8, 2 * tokens), f32),
                pltpu.VMEM((GROUPS, 2, 2 * tokens, 8), f32),
                pltpu.VMEM((2, images, tokens, channels), f32),
                pltpu.VMEM((2, 2, images, 2 * HALO, channels), bf16),
                pltpu.VMEM((2, 2, images, 2 * HALO, channels), bf16),
                pltpu.VMEM((2, images, tokens, channels), f32),
                pltpu.VMEM((2, 2, images, tokens, channels), bf16),
                pltpu.VMEM((2, 2, images, tokens, channels), bf16),
                pltpu.VMEM((2, 2, images - images // 2, tokens, channels), bf16),
                dma((4,)),
                dma((GROUPS, 2)),
                dma((GROUPS, 2)),
                dma((GROUPS, 2)),
                dma((GROUPS, 2)),
                dma((GROUPS, 2)),
                dma((GROUPS, 2)),
                dma((GROUPS, 2)),
                dma((GROUPS, 2)),
                dma((GROUPS, 2)),
                dma((GROUPS, 2)),
                dma((GROUPS, 2)),
                dma((GROUPS, 2)),
                dma((GROUPS, 2)),
            ],
            compiler_params=pltpu.CompilerParams(
                collective_id=0, has_side_effects=True, vmem_limit_bytes=60 * 1024 * 1024
            ),
            cost_estimate=pl.CostEstimate(
                flops=12 * items * 192 * 128 * 128,
                bytes_accessed=8 * images * tokens * channels * 2,
                transcendentals=items * 192 * 128,
            ),
        )(
            block_lists.T,
            row_widths,
            queries.reshape(flat),
            key_states.reshape(flat),
            value_states.reshape(flat),
            out_grad.reshape(flat),
        )
        results = pl.pallas_call(
            split_kernel,
            out_shape=[jax.ShapeDtypeStruct(flat, bf16)] * 4,
            in_specs=[pl.BlockSpec(memory_space=pl.ANY)],
            out_specs=[hbm_spec] * 4,
            scratch_shapes=[dma((4,))],
            compiler_params=pltpu.CompilerParams(vmem_limit_bytes=8 * 1024 * 1024),
        )(stacked)
        return tuple(x.reshape(queries.shape) for x in results)

    split = P(None, "lat", "lon", None)
    return jax.shard_map(
        on_device,
        mesh=mesh,
        in_specs=(split, split, split, split, P(), P()),
        out_specs=(split, split, split, split),
        check_vma=False,
    )
```

```python
import functools
import math

import jax
import jax.numpy as jnp
from jax import lax
from jax.experimental import pallas as pl
from jax.experimental.pallas import tpu as pltpu
from jax.sharding import PartitionSpec as P

MESH = pl.DeviceIdType.MESH
HALO = 8
HDIM = 128
GROUPS = 8
AHEAD = 4
BEHIND = 4
LAG = 9
HIDDEN = -1e30
FLOOR = -1e29


def nt(a, b):
    return lax.dot_general(a, b, (((1,), (1,)), ((), ())), preferred_element_type=jnp.float32)


def nn(a, b):
    return jnp.dot(a, b, preferred_element_type=jnp.float32)


def window(x, old, new, size, rest):
    lane = lax.broadcasted_iota(jnp.int32, x.shape, 1)
    shifted = x if old == new else pltpu.roll(x, (new - old) % HDIM, 1)
    return jnp.where((lane >= new) & (lane < new + size), shifted, rest)


def kernel(
    lon_count,
    lat_count,
    lists_ref,
    widths_ref,
    q_hbm,
    k_hbm,
    v_hbm,
    g_hbm,
    outs,
    near,
    far,
    edge_out,
    bias,
    bias_t,
    exps,
    dps,
    stats,
    stats_out,
    stats_in,
    factors,
    columns,
    near_acc,
    part_out,
    part_in,
    far_acc,
    term_out,
    term_in,
    relay,
    own_sem,
    kv_send,
    kv_recv,
    edge_send,
    edge_recv,
    stat_send,
    stat_recv,
    part_send,
    part_recv,
    term_send,
    term_recv,
    pass_send,
    pass_recv,
    relay_send,
):
    lon = lax.axis_index("lon")
    lat = lax.axis_index("lat")
    left = lax.rem(lon + lon_count - 1, lon_count)
    right = lax.rem(lon + 1, lon_count)
    has_above = lat > 0
    has_below = lat < lat_count - 1
    middle = lat_count // 2
    beside = lon + 1 - 2 * lax.rem(lon, 2)
    is_middle = (lat == middle - 1) | (lat == middle)
    routes = ((middle, 0, middle - 1), (middle - 1, lat_count - 1, middle))
    images, tokens, channels = q_hbm.shape
    heads = channels // HDIM
    group_heads = heads // GROUPS
    group_items = images * group_heads
    group_lanes = group_heads * HDIM
    scale = HDIM ** -0.5
    half = images // 2
    whole, direct, passing = slice(0, images), slice(0, half), slice(half, images)

    sides = ({"lon": left}, {"lon": right})
    tiles = ({"lat": lat - 1}, {"lat": lat + 1})
    exists = (has_above, has_below)

    own_copies = [
        pltpu.make_async_copy(k_hbm, far.at[0, :, tokens : 2 * tokens, :], own_sem.at[0]),
        pltpu.make_async_copy(v_hbm, far.at[1, :, tokens : 2 * tokens, :], own_sem.at[1]),
        pltpu.make_async_copy(q_hbm, near.at[0, :, 0:tokens, :], own_sem.at[2]),
        pltpu.make_async_copy(g_hbm, near.at[1, :, 0:tokens, :], own_sem.at[3]),
    ]
    for copy in own_copies:
        copy.start()

    barrier = pltpu.get_barrier_semaphore()
    for side in sides:
        pl.semaphore_signal(barrier, inc=1, device_id=side, device_id_type=MESH)
    for there, tile in zip(exists, tiles):
        @pl.when(there)
        def _():
            pl.semaphore_signal(barrier, inc=1, device_id=tile, device_id_type=MESH)
    for route in routes:
        @pl.when(lat == route[1])
        def _():
            pl.semaphore_signal(barrier, inc=1, device_id={"lat": route[0], "lon": beside}, device_id_type=MESH)
    pl.semaphore_wait(
        barrier,
        2 + jnp.where(has_above, 1, 0) + jnp.where(has_below, 1, 0) + jnp.where(is_middle, 1, 0),
    )

    def lanes(group):
        start = group * group_lanes
        return pl.ds(start if isinstance(group, int) else pl.multiple_of(start, HDIM), group_lanes)

    def remote(source, target, send, recv, device):
        return pltpu.make_async_remote_copy(
            src_ref=source, dst_ref=target, send_sem=send, recv_sem=recv, device_id=device, device_id_type=MESH
        )

    def kv_copy(group, way, some):
        start = 2 * tokens if way == 0 else 0
        return remote(
            far.at[:, some, tokens : 2 * tokens, lanes(group)],
            far.at[:, some, start : start + tokens, lanes(group)],
            kv_send.at[way],
            kv_recv.at[group, 1 - way],
            tiles[way],
        )

    def edge_copy(group, way):
        start = tokens + 2 * HALO if way == 0 else tokens
        return remote(
            edge_out.at[way, :, :, :, lanes(group)],
            near.at[:, :, start : start + 2 * HALO, lanes(group)],
            edge_send.at[way],
            edge_recv.at[group, 1 - way],
            sides[way],
        )

    def stat_copy(group, way):
        return remote(
            stats_out.at[way, group],
            stats_in.at[1 - way, group],
            stat_send.at[way],
            stat_recv.at[group, 1 - way],
            sides[way],
        )

    def part_copy(group, way):
        return remote(
            part_out.at[way, :, :, :, lanes(group)],
            part_in.at[1 - way, :, :, :, lanes(group)],
            part_send.at[way],
            part_recv.at[group, 1 - way],
            sides[way],
        )

    def term_copy(group, way, some):
        return remote(
            term_out.at[way, :, some, :, lanes(group)],
            term_in.at[1 - way, :, some, :, lanes(group)],
            term_send.at[group, way],
            term_recv.at[group, 1 - way],
            tiles[way],
        )

    def pass_copy(group, way, kind):
        return remote(
            far.at[:, passing, tokens : 2 * tokens, lanes(group)]
            if kind == 0
            else term_out.at[way, :, passing, :, lanes(group)],
            relay.at[kind, :, :, :, lanes(group)],
            pass_send.at[group, kind],
            pass_recv.at[group, kind],
            {"lat": routes[way][1], "lon": beside},
        )

    def relay_copy(group, way, kind):
        start = 2 * tokens if way == 0 else 0
        return remote(
            relay.at[kind, :, :, :, lanes(group)],
            far.at[:, passing, start : start + tokens, lanes(group)]
            if kind == 0
            else term_in.at[1 - way, :, passing, :, lanes(group)],
            relay_send.at[group, kind],
            (kv_recv if kind == 0 else term_recv).at[group, 1 - way],
            {"lat": routes[way][2], "lon": beside},
        )

    def relayed(group, kind):
        return True if kind == 0 else group < GROUPS - 2

    def to_tiles(group, kind, act):
        copy = (kv_copy, term_copy)[kind]
        for way in range(2):
            crossing = (lat == routes[way][0]) & relayed(group, kind)

            @pl.when(exists[way] & jnp.logical_not(crossing))
            def _():
                act(copy(group, way, whole))

            @pl.when(crossing)
            def _():
                act(copy(group, way, direct))
                act(pass_copy(group, way, kind))

    def from_tiles(group, kind):
        copy = (kv_copy, term_copy)[kind]
        for origin in range(2):
            @pl.when(exists[origin])
            def _():
                copy(group, 1 - origin, whole).wait_recv()

    def forward(group, kind):
        for way in range(2):
            @pl.when((lat == routes[way][1]) & relayed(group, kind))
            def _():
                pass_copy(group, way, kind).wait_recv()
                relay_copy(group, way, kind).start()

    def start(copy):
        copy.start()

    def wait_send(copy):
        copy.wait_send()

    def send_edges(group):
        for which in range(2):
            for image in range(images):
                def half(start, low):
                    block = near[which, image, start : start + 16, lanes(group)].astype(jnp.float32)
                    return block[low : low + HALO]

                edge_out[0, which, image, :, lanes(group)] = jnp.concatenate(
                    [half(0, 0), half(32, 0)], axis=0
                ).astype(jnp.bfloat16)
                edge_out[1, which, image, :, lanes(group)] = jnp.concatenate(
                    [half(16, HALO), half(48, HALO)], axis=0
                ).astype(jnp.bfloat16)
        for way in range(2):
            edge_copy(group, way).start()

    own_copies[0].wait()
    own_copies[1].wait()
    to_tiles(0, 0, start)
    own_copies[2].wait()
    own_copies[3].wait()
    send_edges(0)

    def send_group(group, carry):
        to_tiles(group, 0, start)

        @pl.when(group < AHEAD)
        def _():
            send_edges(group)

        return carry

    lax.fori_loop(1, GROUPS, send_group, 0)

    near[:, :, tokens + 4 * HALO :, :] = jnp.zeros(
        (2, images, near.shape[2] - tokens - 4 * HALO, channels), jnp.bfloat16
    )
    for way in range(2):
        @pl.when(jnp.logical_not(exists[way]))
        def _():
            start = 0 if way == 0 else 2 * tokens
            far[:, :, start : start + tokens, :] = jnp.zeros((2, images, tokens, channels), jnp.bfloat16)
            term_in[way] = jnp.zeros((2, images, tokens, channels), jnp.bfloat16)

    def listed(target):
        found = (
            (lists_ref[0, lat] == target)
            | (lists_ref[1, lat] == target)
            | (lists_ref[2, lat] == target)
        ) & (target >= 0)
        return jnp.where(found, 1, 0)

    def mask(shape, key_axis):
        key = lax.broadcasted_iota(jnp.int32, shape, key_axis)
        query = lax.broadcasted_iota(jnp.int32, shape, 1 - key_axis)
        key_tile = key >> 6
        key_col = key & 31
        edge = query - tokens
        is_own = query < tokens
        from_left = edge < 2 * HALO
        query_col = jnp.where(
            is_own, query & 31, jnp.where(from_left, (edge & 7) - HALO, 32 + (edge & 7))
        )
        query_row = jnp.where(is_own, query >> 5, (edge >> 3) & 1)
        width = jnp.where(query_row == 0, widths_ref[2 * lat], widths_ref[2 * lat + 1])
        active = jnp.where(
            key_tile == 0, listed(lat - 1), jnp.where(key_tile == 1, listed(lat), listed(lat + 1))
        )
        seen = (jnp.abs(query_col - key_col) <= width) & (active == 1) & (edge < 4 * HALO)
        return jnp.where(seen, 0.0, HIDDEN)

    bias[...] = mask(bias.shape, 0)
    bias_t[...] = mask(bias_t.shape, 1)

    places = [(image, head) for image in range(images) for head in range(group_heads)]

    def cols(group, head):
        return pl.ds(pl.multiple_of(group * group_lanes + head * HDIM, HDIM), HDIM)

    to_log2 = scale * math.log2(math.e)

    def scores(group):
        tops, sums, balances = [], [], []
        for item, (image, head) in enumerate(places):
            at = cols(group, head)
            raw = nt(far[0, image, :, at], near[0, image, :, at]) * to_log2 + bias[...]
            dp = nt(far[1, image, :, at], near[1, image, :, at])
            top = jnp.maximum(jnp.max(raw, axis=0, keepdims=True), FLOOR)
            e = jnp.exp2(raw - top)
            slot = group * group_items + item
            exps[slot] = e
            dps[slot] = dp
            tops.append(top)
            sums.append(jnp.sum(e, axis=0, keepdims=True))
            balances.append(jnp.sum(e * dp, axis=0, keepdims=True))
        for kind, found in enumerate((tops, sums, balances)):
            rows = found + [jnp.zeros_like(found[0])] * (8 - len(found))
            stats[group, kind] = jnp.concatenate(rows, axis=0)
        for way, moves in enumerate((((0, 0, 8), (32, 8, 8), (64, 16, 16)), ((24, 0, 8), (56, 8, 8), (80, 16, 16)))):
            packed = jnp.zeros((8, HDIM), jnp.float32)
            for kind in range(3):
                for old, new, size in moves:
                    packed = window(stats[group, kind], old, 32 * kind + new, size, packed)
            stats_out[way, group] = packed
        for way in range(2):
            stat_copy(group, way).start()

    def combine(group):
        for way in range(2):
            stat_copy(group, way).wait_recv()
        others = []
        for kind in range(3):
            other = jnp.full((8, HDIM), FLOOR if kind == 0 else 0.0, jnp.float32)
            for origin, moves in enumerate((((0, 64, 16), (16, 0, 8), (24, 32, 8)), ((0, 80, 16), (16, 24, 8), (24, 56, 8)))):
                for old, new, size in moves:
                    other = window(stats_in[origin, group], 32 * kind + old, new, size, other)
            others.append(other)
        top, total, balance = (stats[group, kind] for kind in range(3))
        top2, total2, balance2 = others
        high = jnp.maximum(top, top2)
        part = jnp.exp2(top - high)
        part2 = jnp.exp2(top2 - high)
        whole_sum = jnp.maximum(part * total + part2 * total2, 0.5)
        inverse = 1.0 / whole_sum
        balance = (part * balance + part2 * balance2) * inverse
        factors[group, 0] = part * inverse
        factors[group, 1] = balance
        columns[group, 0] = jnp.transpose(high + jnp.log2(whole_sum))
        columns[group, 1] = jnp.transpose(balance)

    def gradients(group):
        seen = tokens + 4 * HALO
        for item, (image, head) in enumerate(places):
            at = cols(group, head)
            slot = group * group_items + item
            keys, values = far[0, image, :, at], far[1, image, :, at]
            queries, grads = near[0, image, :, at], near[1, image, :, at]
            w = exps[slot] * factors[group, 0, item : item + 1, :]
            ds = w * (dps[slot] - factors[group, 1, item : item + 1, :])
            dk = nn(ds.astype(jnp.bfloat16), queries) * scale
            dv = nn(w.astype(jnp.bfloat16), grads)
            for which, x in enumerate((dk, dv)):
                far_acc[which, image, :, at] = x[tokens : 2 * tokens]
                term_out[0, which, image, :, at] = x[0:tokens].astype(jnp.bfloat16)
                term_out[1, which, image, :, at] = x[2 * tokens :].astype(jnp.bfloat16)
            raw = nt(queries[0:seen], keys) * to_log2 + bias_t[...]
            dp = nt(grads[0:seen], values)
            w = jnp.exp2(raw - columns[group, 0, 0:seen, item : item + 1])
            ds = w * (dp - columns[group, 1, 0:seen, item : item + 1])
            att = nn(w.astype(jnp.bfloat16), values)
            dq = nn(ds.astype(jnp.bfloat16), keys) * scale
            for which, x in enumerate((att, dq)):
                near_acc[which, image, :, at] = x[0:tokens]
                for way in range(2):
                    low = tokens + 2 * HALO * way
                    part_out[way, which, image, :, at] = x[low : low + 2 * HALO].astype(jnp.bfloat16)
        to_tiles(group, 1, start)
        for way in range(2):
            part_copy(group, way).start()

    def finish(group):
        for way in range(2):
            part_copy(group, way).wait_recv()
        from_tiles(group, 1)
        at = lanes(group)
        for image in range(images):
            for which in range(2):
                acc = near_acc[which, image, :, at]
                add_l = part_in[0, which, image, :, at].astype(jnp.float32)
                add_r = part_in[1, which, image, :, at].astype(jnp.float32)
                rows = []
                for r in range(2):
                    here = acc[32 * r : 32 * r + 32]
                    rows.append(here[0:8] + add_l[8 * r : 8 * r + 8])
                    rows.append(here[8:24])
                    rows.append(here[24:32] + add_r[8 * r : 8 * r + 8])
                outs[which, image, :, at] = jnp.concatenate(rows, axis=0).astype(jnp.bfloat16)
            for which in range(2):
                total = far_acc[which, image, :, at]
                for way in range(2):
                    total = total + term_in[way, which, image, :, at].astype(jnp.float32)
                outs[2 + which, image, :, at] = total.astype(jnp.bfloat16)

    def step(index, carry):
        @pl.when(index < GROUPS // 2)
        def _():
            forward(2 * index, 0)
            forward(2 * index + 1, 0)

        @pl.when(index < GROUPS)
        def _():
            from_tiles(index, 0)
            for origin in range(2):
                edge_copy(index, 1 - origin).wait_recv()

            scores(index)

            @pl.when(index + AHEAD < GROUPS)
            def _():
                send_edges(index + AHEAD)

        @pl.when((index >= BEHIND + 2) & (index < GROUPS + BEHIND))
        def _():
            forward(index - BEHIND - 2, 1)

        @pl.when((index >= BEHIND) & (index < GROUPS + BEHIND))
        def _():
            combine(index - BEHIND)
            gradients(index - BEHIND)

        @pl.when(index >= LAG)
        def _():
            finish(index - LAG)

        return carry

    lax.fori_loop(0, GROUPS + LAG, step, 0)

    def drain(group, carry):
        to_tiles(group, 1, wait_send)
        for way in range(2):
            @pl.when(lat == routes[way][0])
            def _():
                pass_copy(group, way, 0).wait_send()

        for kind in range(2):
            for way in range(2):
                @pl.when((lat == routes[way][1]) & relayed(group, kind))
                def _():
                    relay_copy(group, way, kind).wait_send()
        return carry

    lax.fori_loop(0, GROUPS, drain, 0)
    for way in range(2):
        for source, sem in (
            (edge_out.at[way], edge_send.at[way]),
            (part_out.at[way], part_send.at[way]),
            (stats_out.at[way], stat_send.at[way]),
        ):
            remote(source, source, sem, sem, sides[way]).wait_send()
        crossing = lat == routes[way][0]
        for some, here in ((whole, jnp.logical_not(crossing)), (direct, crossing)):
            @pl.when(exists[way] & here)
            def _():
                sent = far.at[:, some, tokens : 2 * tokens, :]
                remote(sent, sent, kv_send.at[way], kv_send.at[way], tiles[way]).wait_send()


def split_kernel(stacked, *refs):
    outs, sem = refs[:4], refs[4]
    copies = [pltpu.make_async_copy(stacked.at[i], outs[i], sem.at[i]) for i in range(4)]
    for copy in copies:
        copy.start()
    for copy in copies:
        copy.wait()


def solution(mesh):
    lon_count = mesh.shape["lon"]
    lat_count = mesh.shape["lat"]

    def on_device(queries, key_states, value_states, out_grad, block_lists, row_widths):
        images, rows, columns, channels = queries.shape
        tokens = rows * columns
        flat = (images, tokens, channels)
        items = images * channels // HDIM
        bf16, f32 = jnp.bfloat16, jnp.float32
        hbm_spec = pl.BlockSpec(memory_space=pltpu.HBM)
        vmem_spec = pl.BlockSpec(memory_space=pltpu.VMEM)
        smem_spec = pl.BlockSpec(memory_space=pltpu.SMEM)
        dma = pltpu.SemaphoreType.DMA
        stacked = pl.pallas_call(
            functools.partial(kernel, lon_count, lat_count),
            out_shape=pltpu.VMEM((4,) + flat, bf16),
            in_specs=[smem_spec, smem_spec] + [hbm_spec] * 4,
            out_specs=vmem_spec,
            scratch_shapes=[
                pltpu.VMEM((2, images, 2 * tokens, channels), bf16),
                pltpu.VMEM((2, images, 3 * tokens, channels), bf16),
                pltpu.VMEM((2, 2, images, 2 * HALO, channels), bf16),
                pltpu.VMEM((3 * tokens, 2 * tokens), f32),
                pltpu.VMEM((tokens + 4 * HALO, 3 * tokens), f32),
                pltpu.VMEM((items, 3 * tokens, 2 * tokens), f32),
                pltpu.VMEM((items, 3 * tokens, 2 * tokens), f32),
                pltpu.VMEM((GROUPS, 3, 8, 2 * tokens), f32),
                pltpu.VMEM((2, GROUPS, 8, 2 * tokens), f32),
                pltpu.VMEM((2, GROUPS, 8, 2 * tokens), f32),
                pltpu.VMEM((GROUPS, 2, 8, 2 * tokens), f32),
                pltpu.VMEM((GROUPS, 2, 2 * tokens, 8), f32),
                pltpu.VMEM((2, images, tokens, channels), f32),
                pltpu.VMEM((2, 2, images, 2 * HALO, channels), bf16),
                pltpu.VMEM((2, 2, images, 2 * HALO, channels), bf16),
                pltpu.VMEM((2, images, tokens, channels), f32),
                pltpu.VMEM((2, 2, images, tokens, channels), bf16),
                pltpu.VMEM((2, 2, images, tokens, channels), bf16),
                pltpu.VMEM((2, 2, images - images // 2, tokens, channels), bf16),
                dma((4,)),
                dma((2,)),
                dma((GROUPS, 2)),
                dma((2,)),
                dma((GROUPS, 2)),
                dma((2,)),
                dma((GROUPS, 2)),
                dma((2,)),
                dma((GROUPS, 2)),
                dma((GROUPS, 2)),
                dma((GROUPS, 2)),
                dma((GROUPS, 2)),
                dma((GROUPS, 2)),
                dma((GROUPS, 2)),
            ],
            compiler_params=pltpu.CompilerParams(
                collective_id=0, has_side_effects=True, vmem_limit_bytes=60 * 1024 * 1024
            ),
            cost_estimate=pl.CostEstimate(
                flops=12 * items * 192 * 128 * 128,
                bytes_accessed=8 * images * tokens * channels * 2,
                transcendentals=items * 192 * 128,
            ),
        )(
            block_lists.T,
            row_widths,
            queries.reshape(flat),
            key_states.reshape(flat),
            value_states.reshape(flat),
            out_grad.reshape(flat),
        )
        results = pl.pallas_call(
            split_kernel,
            out_shape=[jax.ShapeDtypeStruct(flat, bf16)] * 4,
            in_specs=[pl.BlockSpec(memory_space=pl.ANY)],
            out_specs=[hbm_spec] * 4,
            scratch_shapes=[dma((4,))],
            compiler_params=pltpu.CompilerParams(vmem_limit_bytes=8 * 1024 * 1024),
        )(stacked)
        return tuple(x.reshape(queries.shape) for x in results)

    split = P(None, "lat", "lon", None)
    return jax.shard_map(
        on_device,
        mesh=mesh,
        in_specs=(split, split, split, split, P(), P()),
        out_specs=(split, split, split, split),
        check_vma=False,
    )
```

```python
import functools
import math

import jax
import jax.numpy as jnp
from jax import lax
from jax.experimental import pallas as pl
from jax.experimental.pallas import tpu as pltpu
from jax.sharding import PartitionSpec as P

MESH = pl.DeviceIdType.MESH
HALO = 8
HDIM = 128
GROUPS = 8
BEHIND = 6
LAG = 11
DETOURS = 2
HIDDEN = -1e30
FLOOR = -1e29


def nt(a, b):
    return lax.dot_general(a, b, (((1,), (1,)), ((), ())), preferred_element_type=jnp.float32)


def nn(a, b):
    return jnp.dot(a, b, preferred_element_type=jnp.float32)


def window(x, old, new, size, rest):
    lane = lax.broadcasted_iota(jnp.int32, x.shape, 1)
    shifted = x if old == new else pltpu.roll(x, (new - old) % HDIM, 1)
    return jnp.where((lane >= new) & (lane < new + size), shifted, rest)


def kernel(
    lon_count,
    lat_count,
    lists_ref,
    widths_ref,
    q_hbm,
    k_hbm,
    v_hbm,
    g_hbm,
    outs,
    near,
    far,
    edge_out,
    bias,
    bias_t,
    exps,
    dps,
    stats,
    stats_out,
    stats_in,
    factors,
    columns,
    near_acc,
    part_out,
    part_in,
    far_acc,
    term_out,
    term_in,
    relay,
    detour,
    own_sem,
    kv_send,
    kv_recv,
    edge_send,
    edge_recv,
    stat_send,
    stat_recv,
    part_send,
    part_recv,
    term_send,
    term_recv,
    pass_send,
    pass_recv,
    relay_send,
    detour_send,
    detour_recv,
):
    lon = lax.axis_index("lon")
    lat = lax.axis_index("lat")
    left = lax.rem(lon + lon_count - 1, lon_count)
    right = lax.rem(lon + 1, lon_count)
    has_above = lat > 0
    has_below = lat < lat_count - 1
    middle = lat_count // 2
    beside = lon + 1 - 2 * lax.rem(lon, 2)
    is_middle = (lat == middle - 1) | (lat == middle)
    routes = ((middle, 0, middle - 1), (middle - 1, lat_count - 1, middle))
    planes = middle // 2
    plane = lax.rem(lat // 2, planes)
    is_hot = (plane == 0) | (plane == planes - 1)
    is_detour = (plane == 1) | (plane == planes - 2)
    inward = jnp.where(plane < planes // 2, 2, -2)
    images, tokens, channels = q_hbm.shape
    heads = channels // HDIM
    group_heads = heads // GROUPS
    group_items = images * group_heads
    group_lanes = group_heads * HDIM
    scale = HDIM ** -0.5
    half = images // 2
    whole, direct, passing = slice(0, images), slice(0, half), slice(half, images)

    sides = ({"lon": left}, {"lon": right})
    tiles = ({"lat": lat - 1}, {"lat": lat + 1})
    exists = (has_above, has_below)

    own_copies = [
        pltpu.make_async_copy(k_hbm, far.at[0, :, tokens : 2 * tokens, :], own_sem.at[0]),
        pltpu.make_async_copy(v_hbm, far.at[1, :, tokens : 2 * tokens, :], own_sem.at[1]),
        pltpu.make_async_copy(q_hbm, near.at[0, :, 0:tokens, :], own_sem.at[2]),
        pltpu.make_async_copy(g_hbm, near.at[1, :, 0:tokens, :], own_sem.at[3]),
    ]
    for copy in own_copies:
        copy.start()

    barrier = pltpu.get_barrier_semaphore()
    for side in sides:
        pl.semaphore_signal(barrier, inc=1, device_id=side, device_id_type=MESH)
    for there, tile in zip(exists, tiles):
        @pl.when(there)
        def _():
            pl.semaphore_signal(barrier, inc=1, device_id=tile, device_id_type=MESH)
    for route in routes:
        @pl.when(lat == route[1])
        def _():
            pl.semaphore_signal(barrier, inc=1, device_id={"lat": route[0], "lon": beside}, device_id_type=MESH)
    @pl.when(is_detour)
    def _():
        for side in (left, right):
            pl.semaphore_signal(
                barrier, inc=1, device_id={"lat": lat - inward, "lon": side}, device_id_type=MESH
            )

    pl.semaphore_wait(
        barrier,
        2 + jnp.where(has_above, 1, 0) + jnp.where(has_below, 1, 0) + jnp.where(is_middle, 1, 0)
        + jnp.where(is_hot, 2, 0),
    )

    def lanes(group):
        start = group * group_lanes
        return pl.ds(start if isinstance(group, int) else pl.multiple_of(start, HDIM), group_lanes)

    def remote(source, target, send, recv, device):
        return pltpu.make_async_remote_copy(
            src_ref=source, dst_ref=target, send_sem=send, recv_sem=recv, device_id=device, device_id_type=MESH
        )

    def kv_copy(group, way, some):
        start = 2 * tokens if way == 0 else 0
        return remote(
            far.at[:, some, tokens : 2 * tokens, lanes(group)],
            far.at[:, some, start : start + tokens, lanes(group)],
            kv_send.at[way],
            kv_recv.at[group, 1 - way],
            tiles[way],
        )

    def edge_copy(group, way):
        start = tokens + 2 * HALO if way == 0 else tokens
        return remote(
            edge_out.at[way, :, :, :, lanes(group)],
            near.at[:, :, start : start + 2 * HALO, lanes(group)],
            edge_send.at[way],
            edge_recv.at[group, 1 - way],
            sides[way],
        )

    def stat_copy(group, way):
        return remote(
            stats_out.at[way, group],
            stats_in.at[1 - way, group],
            stat_send.at[way],
            stat_recv.at[group, 1 - way],
            sides[way],
        )

    def part_copy(group, way):
        return remote(
            part_out.at[way, :, :, :, lanes(group)],
            part_in.at[1 - way, :, :, :, lanes(group)],
            part_send.at[way],
            part_recv.at[group, 1 - way],
            sides[way],
        )

    def term_copy(group, way, some):
        return remote(
            term_out.at[way, :, some, :, lanes(group)],
            term_in.at[1 - way, :, some, :, lanes(group)],
            term_send.at[group, way],
            term_recv.at[group, 1 - way],
            tiles[way],
        )

    def pass_copy(group, way, kind):
        return remote(
            far.at[:, passing, tokens : 2 * tokens, lanes(group)]
            if kind == 0
            else term_out.at[way, :, passing, :, lanes(group)],
            relay.at[kind, :, :, :, lanes(group)],
            pass_send.at[group, kind],
            pass_recv.at[group, kind],
            {"lat": routes[way][1], "lon": beside},
        )

    def relay_copy(group, way, kind):
        start = 2 * tokens if way == 0 else 0
        return remote(
            relay.at[kind, :, :, :, lanes(group)],
            far.at[:, passing, start : start + tokens, lanes(group)]
            if kind == 0
            else term_in.at[1 - way, :, passing, :, lanes(group)],
            relay_send.at[group, kind],
            (kv_recv if kind == 0 else term_recv).at[group, 1 - way],
            {"lat": routes[way][2], "lon": beside},
        )

    def detour_in(group, way, kind):
        which = group // 2 - 1
        return remote(
            (edge_out, part_out)[kind].at[way, :, :, :, lanes(group)],
            detour.at[kind, which, 1 - way],
            (edge_send, part_send)[kind].at[way],
            detour_recv.at[kind, which, 1 - way],
            {"lat": lat + inward, "lon": (left, right)[way]},
        )

    def detour_out(group, origin, kind):
        which = group // 2 - 1
        low = tokens + 2 * HALO * origin
        return remote(
            detour.at[kind, which, origin],
            near.at[:, :, low : low + 2 * HALO, lanes(group)]
            if kind == 0
            else part_in.at[origin, :, :, :, lanes(group)],
            detour_send.at[kind, which, origin],
            (edge_recv, part_recv)[kind].at[group, origin],
            {"lat": lat - inward},
        )

    def to_sides(group, kind):
        aside = is_hot & ((group == 2) | (group == 4))
        for way in range(2):
            @pl.when(jnp.logical_not(aside))
            def _():
                (edge_copy, part_copy)[kind](group, way).start()

            @pl.when(aside)
            def _():
                detour_in(group, way, kind).start()

    def pass_aside(group, kind):
        for origin in range(2):
            detour_in(group, 1 - origin, kind).wait_recv()
            detour_out(group, origin, kind).start()

    def relayed(group, kind):
        return True if kind == 0 else group < GROUPS - 2

    def to_tiles(group, kind, act):
        copy = (kv_copy, term_copy)[kind]
        for way in range(2):
            crossing = (lat == routes[way][0]) & relayed(group, kind)

            @pl.when(exists[way] & jnp.logical_not(crossing))
            def _():
                act(copy(group, way, whole))

            @pl.when(crossing)
            def _():
                act(copy(group, way, direct))
                act(pass_copy(group, way, kind))

    def from_tiles(group, kind):
        copy = (kv_copy, term_copy)[kind]
        for origin in range(2):
            @pl.when(exists[origin])
            def _():
                copy(group, 1 - origin, whole).wait_recv()

    def forward(group, kind):
        for way in range(2):
            @pl.when((lat == routes[way][1]) & relayed(group, kind))
            def _():
                pass_copy(group, way, kind).wait_recv()
                relay_copy(group, way, kind).start()

    def start(copy):
        copy.start()

    def wait_send(copy):
        copy.wait_send()

    def send_edges(group):
        for which in range(2):
            for image in range(images):
                def half(start, low):
                    block = near[which, image, start : start + 16, lanes(group)].astype(jnp.float32)
                    return block[low : low + HALO]

                edge_out[0, which, image, :, lanes(group)] = jnp.concatenate(
                    [half(0, 0), half(32, 0)], axis=0
                ).astype(jnp.bfloat16)
                edge_out[1, which, image, :, lanes(group)] = jnp.concatenate(
                    [half(16, HALO), half(48, HALO)], axis=0
                ).astype(jnp.bfloat16)
        to_sides(group, 0)

    own_copies[0].wait()
    own_copies[1].wait()
    to_tiles(0, 0, start)
    own_copies[2].wait()
    own_copies[3].wait()
    send_edges(0)

    def send_group(group, carry):
        to_tiles(group, 0, start)
        send_edges(group)
        return carry

    lax.fori_loop(1, GROUPS, send_group, 0)

    near[:, :, tokens + 4 * HALO :, :] = jnp.zeros(
        (2, images, near.shape[2] - tokens - 4 * HALO, channels), jnp.bfloat16
    )
    for way in range(2):
        @pl.when(jnp.logical_not(exists[way]))
        def _():
            start = 0 if way == 0 else 2 * tokens
            far[:, :, start : start + tokens, :] = jnp.zeros((2, images, tokens, channels), jnp.bfloat16)
            term_in[way] = jnp.zeros((2, images, tokens, channels), jnp.bfloat16)

    def listed(target):
        found = (
            (lists_ref[0, lat] == target)
            | (lists_ref[1, lat] == target)
            | (lists_ref[2, lat] == target)
        ) & (target >= 0)
        return jnp.where(found, 1, 0)

    def mask(shape, key_axis):
        key = lax.broadcasted_iota(jnp.int32, shape, key_axis)
        query = lax.broadcasted_iota(jnp.int32, shape, 1 - key_axis)
        key_tile = key >> 6
        key_col = key & 31
        edge = query - tokens
        is_own = query < tokens
        from_left = edge < 2 * HALO
        query_col = jnp.where(
            is_own, query & 31, jnp.where(from_left, (edge & 7) - HALO, 32 + (edge & 7))
        )
        query_row = jnp.where(is_own, query >> 5, (edge >> 3) & 1)
        width = jnp.where(query_row == 0, widths_ref[2 * lat], widths_ref[2 * lat + 1])
        active = jnp.where(
            key_tile == 0, listed(lat - 1), jnp.where(key_tile == 1, listed(lat), listed(lat + 1))
        )
        seen = (jnp.abs(query_col - key_col) <= width) & (active == 1) & (edge < 4 * HALO)
        return jnp.where(seen, 0.0, HIDDEN)

    bias[...] = mask(bias.shape, 0)
    bias_t[...] = mask(bias_t.shape, 1)

    places = [(image, head) for image in range(images) for head in range(group_heads)]

    def cols(group, head):
        return pl.ds(pl.multiple_of(group * group_lanes + head * HDIM, HDIM), HDIM)

    to_log2 = scale * math.log2(math.e)

    def scores(group):
        tops, sums, balances = [], [], []
        for item, (image, head) in enumerate(places):
            at = cols(group, head)
            raw = nt(far[0, image, :, at], near[0, image, :, at]) * to_log2 + bias[...]
            dp = nt(far[1, image, :, at], near[1, image, :, at])
            top = jnp.maximum(jnp.max(raw, axis=0, keepdims=True), FLOOR)
            e = jnp.exp2(raw - top)
            slot = group * group_items + item
            exps[slot] = e
            dps[slot] = dp
            tops.append(top)
            sums.append(jnp.sum(e, axis=0, keepdims=True))
            balances.append(jnp.sum(e * dp, axis=0, keepdims=True))
        for kind, found in enumerate((tops, sums, balances)):
            rows = found + [jnp.zeros_like(found[0])] * (8 - len(found))
            stats[group, kind] = jnp.concatenate(rows, axis=0)
        for way, moves in enumerate((((0, 0, 8), (32, 8, 8), (64, 16, 16)), ((24, 0, 8), (56, 8, 8), (80, 16, 16)))):
            packed = jnp.zeros((8, HDIM), jnp.float32)
            for kind in range(3):
                for old, new, size in moves:
                    packed = window(stats[group, kind], old, 32 * kind + new, size, packed)
            stats_out[way, group] = packed
        for way in range(2):
            stat_copy(group, way).start()

    def combine(group):
        for way in range(2):
            stat_copy(group, way).wait_recv()
        others = []
        for kind in range(3):
            other = jnp.full((8, HDIM), FLOOR if kind == 0 else 0.0, jnp.float32)
            for origin, moves in enumerate((((0, 64, 16), (16, 0, 8), (24, 32, 8)), ((0, 80, 16), (16, 24, 8), (24, 56, 8)))):
                for old, new, size in moves:
                    other = window(stats_in[origin, group], 32 * kind + old, new, size, other)
            others.append(other)
        top, total, balance = (stats[group, kind] for kind in range(3))
        top2, total2, balance2 = others
        high = jnp.maximum(top, top2)
        part = jnp.exp2(top - high)
        part2 = jnp.exp2(top2 - high)
        whole_sum = jnp.maximum(part * total + part2 * total2, 0.5)
        inverse = 1.0 / whole_sum
        balance = (part * balance + part2 * balance2) * inverse
        factors[group, 0] = part * inverse
        factors[group, 1] = balance
        columns[group, 0] = jnp.transpose(high + jnp.log2(whole_sum))
        columns[group, 1] = jnp.transpose(balance)

    def gradients(group):
        seen = tokens + 4 * HALO
        for item, (image, head) in enumerate(places):
            at = cols(group, head)
            slot = group * group_items + item
            keys, values = far[0, image, :, at], far[1, image, :, at]
            queries, grads = near[0, image, :, at], near[1, image, :, at]
            w = exps[slot] * factors[group, 0, item : item + 1, :]
            ds = w * (dps[slot] - factors[group, 1, item : item + 1, :])
            dk = nn(ds.astype(jnp.bfloat16), queries) * scale
            dv = nn(w.astype(jnp.bfloat16), grads)
            for which, x in enumerate((dk, dv)):
                far_acc[which, image, :, at] = x[tokens : 2 * tokens]
                term_out[0, which, image, :, at] = x[0:tokens].astype(jnp.bfloat16)
                term_out[1, which, image, :, at] = x[2 * tokens :].astype(jnp.bfloat16)
            raw = nt(queries[0:seen], keys) * to_log2 + bias_t[...]
            dp = nt(grads[0:seen], values)
            w = jnp.exp2(raw - columns[group, 0, 0:seen, item : item + 1])
            ds = w * (dp - columns[group, 1, 0:seen, item : item + 1])
            att = nn(w.astype(jnp.bfloat16), values)
            dq = nn(ds.astype(jnp.bfloat16), keys) * scale
            for which, x in enumerate((att, dq)):
                near_acc[which, image, :, at] = x[0:tokens]
                for way in range(2):
                    low = tokens + 2 * HALO * way
                    part_out[way, which, image, :, at] = x[low : low + 2 * HALO].astype(jnp.bfloat16)
        to_tiles(group, 1, start)
        to_sides(group, 1)

    def finish(group):
        for way in range(2):
            part_copy(group, way).wait_recv()
        from_tiles(group, 1)
        at = lanes(group)
        for image in range(images):
            for which in range(2):
                acc = near_acc[which, image, :, at]
                add_l = part_in[0, which, image, :, at].astype(jnp.float32)
                add_r = part_in[1, which, image, :, at].astype(jnp.float32)
                rows = []
                for r in range(2):
                    here = acc[32 * r : 32 * r + 32]
                    rows.append(here[0:8] + add_l[8 * r : 8 * r + 8])
                    rows.append(here[8:24])
                    rows.append(here[24:32] + add_r[8 * r : 8 * r + 8])
                outs[which, image, :, at] = jnp.concatenate(rows, axis=0).astype(jnp.bfloat16)
            for which in range(2):
                total = far_acc[which, image, :, at]
                for way in range(2):
                    total = total + term_in[way, which, image, :, at].astype(jnp.float32)
                outs[2 + which, image, :, at] = total.astype(jnp.bfloat16)

    def step(index, carry):
        @pl.when(index < GROUPS // 2)
        def _():
            forward(2 * index, 0)
            forward(2 * index + 1, 0)

        for group in (2, 4):
            for kind, after in enumerate((1, BEHIND + 3)):
                @pl.when(is_detour & (index == group + after))
                def _():
                    pass_aside(group, kind)

        @pl.when(index < GROUPS)
        def _():
            from_tiles(index, 0)
            for origin in range(2):
                edge_copy(index, 1 - origin).wait_recv()

            scores(index)

        @pl.when((index >= BEHIND + 2) & (index < GROUPS + BEHIND))
        def _():
            forward(index - BEHIND - 2, 1)

        @pl.when((index >= BEHIND) & (index < GROUPS + BEHIND))
        def _():
            combine(index - BEHIND)
            gradients(index - BEHIND)

        @pl.when(index >= LAG)
        def _():
            finish(index - LAG)

        return carry

    lax.fori_loop(0, GROUPS + LAG, step, 0)

    def drain(group, carry):
        to_tiles(group, 1, wait_send)
        for way in range(2):
            @pl.when(lat == routes[way][0])
            def _():
                pass_copy(group, way, 0).wait_send()

        for kind in range(2):
            for way in range(2):
                @pl.when((lat == routes[way][1]) & relayed(group, kind))
                def _():
                    relay_copy(group, way, kind).wait_send()
        return carry

    lax.fori_loop(0, GROUPS, drain, 0)
    @pl.when(is_detour)
    def _():
        for kind in range(2):
            for group in (2, 4):
                for origin in range(2):
                    detour_out(group, origin, kind).wait_send()

    for way in range(2):
        for source, sem in (
            (edge_out.at[way], edge_send.at[way]),
            (part_out.at[way], part_send.at[way]),
            (stats_out.at[way], stat_send.at[way]),
        ):
            remote(source, source, sem, sem, sides[way]).wait_send()
        crossing = lat == routes[way][0]
        for some, here in ((whole, jnp.logical_not(crossing)), (direct, crossing)):
            @pl.when(exists[way] & here)
            def _():
                sent = far.at[:, some, tokens : 2 * tokens, :]
                remote(sent, sent, kv_send.at[way], kv_send.at[way], tiles[way]).wait_send()


def split_kernel(stacked, *refs):
    outs, sem = refs[:4], refs[4]
    copies = [pltpu.make_async_copy(stacked.at[i], outs[i], sem.at[i]) for i in range(4)]
    for copy in copies:
        copy.start()
    for copy in copies:
        copy.wait()


def solution(mesh):
    lon_count = mesh.shape["lon"]
    lat_count = mesh.shape["lat"]

    def on_device(queries, key_states, value_states, out_grad, block_lists, row_widths):
        images, rows, columns, channels = queries.shape
        tokens = rows * columns
        flat = (images, tokens, channels)
        items = images * channels // HDIM
        bf16, f32 = jnp.bfloat16, jnp.float32
        hbm_spec = pl.BlockSpec(memory_space=pltpu.HBM)
        vmem_spec = pl.BlockSpec(memory_space=pltpu.VMEM)
        smem_spec = pl.BlockSpec(memory_space=pltpu.SMEM)
        dma = pltpu.SemaphoreType.DMA
        stacked = pl.pallas_call(
            functools.partial(kernel, lon_count, lat_count),
            out_shape=pltpu.VMEM((4,) + flat, bf16),
            in_specs=[smem_spec, smem_spec] + [hbm_spec] * 4,
            out_specs=vmem_spec,
            scratch_shapes=[
                pltpu.VMEM((2, images, 2 * tokens, channels), bf16),
                pltpu.VMEM((2, images, 3 * tokens, channels), bf16),
                pltpu.VMEM((2, 2, images, 2 * HALO, channels), bf16),
                pltpu.VMEM((3 * tokens, 2 * tokens), f32),
                pltpu.VMEM((tokens + 4 * HALO, 3 * tokens), f32),
                pltpu.VMEM((items, 3 * tokens, 2 * tokens), f32),
                pltpu.VMEM((items, 3 * tokens, 2 * tokens), f32),
                pltpu.VMEM((GROUPS, 3, 8, 2 * tokens), f32),
                pltpu.VMEM((2, GROUPS, 8, 2 * tokens), f32),
                pltpu.VMEM((2, GROUPS, 8, 2 * tokens), f32),
                pltpu.VMEM((GROUPS, 2, 8, 2 * tokens), f32),
                pltpu.VMEM((GROUPS, 2, 2 * tokens, 8), f32),
                pltpu.VMEM((2, images, tokens, channels), f32),
                pltpu.VMEM((2, 2, images, 2 * HALO, channels), bf16),
                pltpu.VMEM((2, 2, images, 2 * HALO, channels), bf16),
                pltpu.VMEM((2, images, tokens, channels), f32),
                pltpu.VMEM((2, 2, images, tokens, channels), bf16),
                pltpu.VMEM((2, 2, images, tokens, channels), bf16),
                pltpu.VMEM((2, 2, images - images // 2, tokens, channels), bf16),
                pltpu.VMEM((2, DETOURS, 2, 2, images, 2 * HALO, channels // GROUPS), bf16),
                dma((4,)),
                dma((2,)),
                dma((GROUPS, 2)),
                dma((2,)),
                dma((GROUPS, 2)),
                dma((2,)),
                dma((GROUPS, 2)),
                dma((2,)),
                dma((GROUPS, 2)),
                dma((GROUPS, 2)),
                dma((GROUPS, 2)),
                dma((GROUPS, 2)),
                dma((GROUPS, 2)),
                dma((GROUPS, 2)),
                dma((2, DETOURS, 2)),
                dma((2, DETOURS, 2)),
            ],
            compiler_params=pltpu.CompilerParams(
                collective_id=0, has_side_effects=True, vmem_limit_bytes=60 * 1024 * 1024
            ),
            cost_estimate=pl.CostEstimate(
                flops=12 * items * 192 * 128 * 128,
                bytes_accessed=8 * images * tokens * channels * 2,
                transcendentals=items * 192 * 128,
            ),
        )(
            block_lists.T,
            row_widths,
            queries.reshape(flat),
            key_states.reshape(flat),
            value_states.reshape(flat),
            out_grad.reshape(flat),
        )
        results = pl.pallas_call(
            split_kernel,
            out_shape=[jax.ShapeDtypeStruct(flat, bf16)] * 4,
            in_specs=[pl.BlockSpec(memory_space=pl.ANY)],
            out_specs=[hbm_spec] * 4,
            scratch_shapes=[dma((4,))],
            compiler_params=pltpu.CompilerParams(vmem_limit_bytes=8 * 1024 * 1024),
        )(stacked)
        return tuple(x.reshape(queries.shape) for x in results)

    split = P(None, "lat", "lon", None)
    return jax.shard_map(
        on_device,
        mesh=mesh,
        in_specs=(split, split, split, split, P(), P()),
        out_specs=(split, split, split, split),
        check_vma=False,
    )
```

```python
import functools
import math

import jax
import jax.numpy as jnp
from jax import lax
from jax.experimental import pallas as pl
from jax.experimental.pallas import tpu as pltpu
from jax.sharding import PartitionSpec as P

MESH = pl.DeviceIdType.MESH
HALO = 8
HDIM = 128
GROUPS = 8
BEHIND = 6
LAG = 11
DETOURS = 2
HIDDEN = -1e30
FLOOR = -1e29


def nt(a, b):
    return lax.dot_general(a, b, (((1,), (1,)), ((), ())), preferred_element_type=jnp.float32)


def tn(a, b):
    return lax.dot_general(a, b, (((0,), (0,)), ((), ())), preferred_element_type=jnp.float32)


def nn(a, b):
    return jnp.dot(a, b, preferred_element_type=jnp.float32)


def window(x, old, new, size, rest):
    lane = lax.broadcasted_iota(jnp.int32, x.shape, 1)
    shifted = x if old == new else pltpu.roll(x, (new - old) % HDIM, 1)
    return jnp.where((lane >= new) & (lane < new + size), shifted, rest)


def kernel(
    lon_count,
    lat_count,
    lists_ref,
    widths_ref,
    q_hbm,
    k_hbm,
    v_hbm,
    g_hbm,
    outs,
    near,
    far,
    edge_out,
    bias,
    bias_t,
    exps,
    dps,
    stats,
    stats_out,
    stats_in,
    factors,
    columns,
    near_acc,
    part_out,
    part_in,
    far_acc,
    term_out,
    term_in,
    relay,
    detour,
    own_sem,
    kv_send,
    kv_recv,
    edge_send,
    edge_recv,
    stat_send,
    stat_recv,
    part_send,
    part_recv,
    term_send,
    term_recv,
    pass_send,
    pass_recv,
    relay_send,
    detour_send,
    detour_recv,
):
    lon = lax.axis_index("lon")
    lat = lax.axis_index("lat")
    left = lax.rem(lon + lon_count - 1, lon_count)
    right = lax.rem(lon + 1, lon_count)
    has_above = lat > 0
    has_below = lat < lat_count - 1
    middle = lat_count // 2
    beside = lon + 1 - 2 * lax.rem(lon, 2)
    is_middle = (lat == middle - 1) | (lat == middle)
    routes = ((middle, 0, middle - 1), (middle - 1, lat_count - 1, middle))
    planes = middle // 2
    plane = lax.rem(lat // 2, planes)
    is_hot = (plane == 0) | (plane == planes - 1)
    is_detour = (plane == 1) | (plane == planes - 2)
    inward = jnp.where(plane < planes // 2, 2, -2)
    images, tokens, channels = q_hbm.shape
    heads = channels // HDIM
    group_heads = heads // GROUPS
    group_items = images * group_heads
    group_lanes = group_heads * HDIM
    scale = HDIM ** -0.5
    half = images // 2
    whole, direct, passing = slice(0, images), slice(0, half), slice(half, images)

    sides = ({"lon": left}, {"lon": right})
    tiles = ({"lat": lat - 1}, {"lat": lat + 1})
    exists = (has_above, has_below)

    own_copies = [
        pltpu.make_async_copy(k_hbm, far.at[0, :, tokens : 2 * tokens, :], own_sem.at[0]),
        pltpu.make_async_copy(v_hbm, far.at[1, :, tokens : 2 * tokens, :], own_sem.at[1]),
        pltpu.make_async_copy(q_hbm, near.at[0, :, 0:tokens, :], own_sem.at[2]),
        pltpu.make_async_copy(g_hbm, near.at[1, :, 0:tokens, :], own_sem.at[3]),
    ]
    for copy in own_copies:
        copy.start()

    barrier = pltpu.get_barrier_semaphore()
    for side in sides:
        pl.semaphore_signal(barrier, inc=1, device_id=side, device_id_type=MESH)
    for there, tile in zip(exists, tiles):
        @pl.when(there)
        def _():
            pl.semaphore_signal(barrier, inc=1, device_id=tile, device_id_type=MESH)
    for route in routes:
        @pl.when(lat == route[1])
        def _():
            pl.semaphore_signal(barrier, inc=1, device_id={"lat": route[0], "lon": beside}, device_id_type=MESH)
    @pl.when(is_detour)
    def _():
        for side in (left, right):
            pl.semaphore_signal(
                barrier, inc=1, device_id={"lat": lat - inward, "lon": side}, device_id_type=MESH
            )

    pl.semaphore_wait(
        barrier,
        2 + jnp.where(has_above, 1, 0) + jnp.where(has_below, 1, 0) + jnp.where(is_middle, 1, 0)
        + jnp.where(is_hot, 2, 0),
    )

    def lanes(group):
        start = group * group_lanes
        return pl.ds(start if isinstance(group, int) else pl.multiple_of(start, HDIM), group_lanes)

    def remote(source, target, send, recv, device):
        return pltpu.make_async_remote_copy(
            src_ref=source, dst_ref=target, send_sem=send, recv_sem=recv, device_id=device, device_id_type=MESH
        )

    def kv_copy(group, way, some):
        start = 2 * tokens if way == 0 else 0
        return remote(
            far.at[:, some, tokens : 2 * tokens, lanes(group)],
            far.at[:, some, start : start + tokens, lanes(group)],
            kv_send.at[way],
            kv_recv.at[group, 1 - way],
            tiles[way],
        )

    def edge_copy(group, way):
        start = tokens + 2 * HALO if way == 0 else tokens
        return remote(
            edge_out.at[way, :, :, :, lanes(group)],
            near.at[:, :, start : start + 2 * HALO, lanes(group)],
            edge_send.at[way],
            edge_recv.at[group, 1 - way],
            sides[way],
        )

    def stat_copy(group, way):
        return remote(
            stats_out.at[way, group],
            stats_in.at[1 - way, group],
            stat_send.at[way],
            stat_recv.at[group, 1 - way],
            sides[way],
        )

    def part_copy(group, way):
        return remote(
            part_out.at[way, :, :, :, lanes(group)],
            part_in.at[1 - way, :, :, :, lanes(group)],
            part_send.at[way],
            part_recv.at[group, 1 - way],
            sides[way],
        )

    def term_copy(group, way, some):
        return remote(
            term_out.at[way, :, some, :, lanes(group)],
            term_in.at[1 - way, :, some, :, lanes(group)],
            term_send.at[group, way],
            term_recv.at[group, 1 - way],
            tiles[way],
        )

    def pass_copy(group, way, kind):
        return remote(
            far.at[:, passing, tokens : 2 * tokens, lanes(group)]
            if kind == 0
            else term_out.at[way, :, passing, :, lanes(group)],
            relay.at[kind, :, :, :, lanes(group)],
            pass_send.at[group, kind],
            pass_recv.at[group, kind],
            {"lat": routes[way][1], "lon": beside},
        )

    def relay_copy(group, way, kind):
        start = 2 * tokens if way == 0 else 0
        return remote(
            relay.at[kind, :, :, :, lanes(group)],
            far.at[:, passing, start : start + tokens, lanes(group)]
            if kind == 0
            else term_in.at[1 - way, :, passing, :, lanes(group)],
            relay_send.at[group, kind],
            (kv_recv if kind == 0 else term_recv).at[group, 1 - way],
            {"lat": routes[way][2], "lon": beside},
        )

    def detour_in(group, way, kind):
        which = group // 2 - 1
        return remote(
            (edge_out, part_out)[kind].at[way, :, :, :, lanes(group)],
            detour.at[kind, which, 1 - way],
            (edge_send, part_send)[kind].at[way],
            detour_recv.at[kind, which, 1 - way],
            {"lat": lat + inward, "lon": (left, right)[way]},
        )

    def detour_out(group, origin, kind):
        which = group // 2 - 1
        low = tokens + 2 * HALO * origin
        return remote(
            detour.at[kind, which, origin],
            near.at[:, :, low : low + 2 * HALO, lanes(group)]
            if kind == 0
            else part_in.at[origin, :, :, :, lanes(group)],
            detour_send.at[kind, which, origin],
            (edge_recv, part_recv)[kind].at[group, origin],
            {"lat": lat - inward},
        )

    def to_sides(group, kind):
        aside = is_hot & ((group == 2) | (group == 4))
        for way in range(2):
            @pl.when(jnp.logical_not(aside))
            def _():
                (edge_copy, part_copy)[kind](group, way).start()

            @pl.when(aside)
            def _():
                detour_in(group, way, kind).start()

    def pass_aside(group, kind):
        for origin in range(2):
            detour_in(group, 1 - origin, kind).wait_recv()
            detour_out(group, origin, kind).start()

    def relayed(group, kind):
        return True if kind == 0 else group < GROUPS - 2

    def to_tiles(group, kind, act):
        copy = (kv_copy, term_copy)[kind]
        for way in range(2):
            crossing = (lat == routes[way][0]) & relayed(group, kind)

            @pl.when(exists[way] & jnp.logical_not(crossing))
            def _():
                act(copy(group, way, whole))

            @pl.when(crossing)
            def _():
                act(copy(group, way, direct))
                act(pass_copy(group, way, kind))

    def from_tiles(group, kind):
        copy = (kv_copy, term_copy)[kind]
        for origin in range(2):
            @pl.when(exists[origin])
            def _():
                copy(group, 1 - origin, whole).wait_recv()

    def forward(group, kind):
        for way in range(2):
            @pl.when((lat == routes[way][1]) & relayed(group, kind))
            def _():
                pass_copy(group, way, kind).wait_recv()
                relay_copy(group, way, kind).start()

    def start(copy):
        copy.start()

    def wait_send(copy):
        copy.wait_send()

    def send_edges(group):
        for which in range(2):
            for image in range(images):
                def half(start, low):
                    block = near[which, image, start : start + 16, lanes(group)].astype(jnp.float32)
                    return block[low : low + HALO]

                edge_out[0, which, image, :, lanes(group)] = jnp.concatenate(
                    [half(0, 0), half(32, 0)], axis=0
                ).astype(jnp.bfloat16)
                edge_out[1, which, image, :, lanes(group)] = jnp.concatenate(
                    [half(16, HALO), half(48, HALO)], axis=0
                ).astype(jnp.bfloat16)
        to_sides(group, 0)

    own_copies[0].wait()
    own_copies[1].wait()
    to_tiles(0, 0, start)
    own_copies[2].wait()
    own_copies[3].wait()
    send_edges(0)

    def send_group(group, carry):
        to_tiles(group, 0, start)
        send_edges(group)
        return carry

    lax.fori_loop(1, GROUPS, send_group, 0)

    near[:, :, tokens + 4 * HALO :, :] = jnp.zeros(
        (2, images, near.shape[2] - tokens - 4 * HALO, channels), jnp.bfloat16
    )
    for way in range(2):
        @pl.when(jnp.logical_not(exists[way]))
        def _():
            start = 0 if way == 0 else 2 * tokens
            far[:, :, start : start + tokens, :] = jnp.zeros((2, images, tokens, channels), jnp.bfloat16)
            term_in[way] = jnp.zeros((2, images, tokens, channels), jnp.bfloat16)

    def listed(target):
        found = (
            (lists_ref[0, lat] == target)
            | (lists_ref[1, lat] == target)
            | (lists_ref[2, lat] == target)
        ) & (target >= 0)
        return jnp.where(found, 1, 0)

    def mask(shape, key_axis):
        key = lax.broadcasted_iota(jnp.int32, shape, key_axis)
        query = lax.broadcasted_iota(jnp.int32, shape, 1 - key_axis)
        key_tile = key >> 6
        key_col = key & 31
        edge = query - tokens
        is_own = query < tokens
        from_left = edge < 2 * HALO
        query_col = jnp.where(
            is_own, query & 31, jnp.where(from_left, (edge & 7) - HALO, 32 + (edge & 7))
        )
        query_row = jnp.where(is_own, query >> 5, (edge >> 3) & 1)
        width = jnp.where(query_row == 0, widths_ref[2 * lat], widths_ref[2 * lat + 1])
        active = jnp.where(
            key_tile == 0, listed(lat - 1), jnp.where(key_tile == 1, listed(lat), listed(lat + 1))
        )
        seen = (jnp.abs(query_col - key_col) <= width) & (active == 1) & (edge < 4 * HALO)
        return jnp.where(seen, 0.0, HIDDEN)

    bias[...] = mask(bias.shape, 0)
    bias_t[...] = mask(bias_t.shape, 1)

    places = [(image, head) for image in range(images) for head in range(group_heads)]

    def cols(group, head):
        return pl.ds(pl.multiple_of(group * group_lanes + head * HDIM, HDIM), HDIM)

    to_log2 = scale * math.log2(math.e)

    def scores(group):
        tops, sums, balances = [], [], []
        for item, (image, head) in enumerate(places):
            at = cols(group, head)
            raw = nt(far[0, image, :, at], near[0, image, :, at]) * to_log2 + bias[...]
            dp = nt(far[1, image, :, at], near[1, image, :, at])
            top = jnp.maximum(jnp.max(raw, axis=0, keepdims=True), FLOOR)
            e = jnp.exp2(raw - top)
            slot = group * group_items + item
            exps[slot] = e
            dps[slot] = dp
            tops.append(top)
            sums.append(jnp.sum(e, axis=0, keepdims=True))
            balances.append(jnp.sum(e * dp, axis=0, keepdims=True))
        for kind, found in enumerate((tops, sums, balances)):
            rows = found + [jnp.zeros_like(found[0])] * (8 - len(found))
            stats[group, kind] = jnp.concatenate(rows, axis=0)
        for way, moves in enumerate((((0, 0, 8), (32, 8, 8), (64, 16, 16)), ((24, 0, 8), (56, 8, 8), (80, 16, 16)))):
            packed = jnp.zeros((8, HDIM), jnp.float32)
            for kind in range(3):
                for old, new, size in moves:
                    packed = window(stats[group, kind], old, 32 * kind + new, size, packed)
            stats_out[way, group] = packed
        for way in range(2):
            stat_copy(group, way).start()

    def combine(group):
        for way in range(2):
            stat_copy(group, way).wait_recv()
        others = []
        for kind in range(3):
            other = jnp.full((8, HDIM), FLOOR if kind == 0 else 0.0, jnp.float32)
            for origin, moves in enumerate((((0, 64, 16), (16, 0, 8), (24, 32, 8)), ((0, 80, 16), (16, 24, 8), (24, 56, 8)))):
                for old, new, size in moves:
                    other = window(stats_in[origin, group], 32 * kind + old, new, size, other)
            others.append(other)
        top, total, balance = (stats[group, kind] for kind in range(3))
        top2, total2, balance2 = others
        high = jnp.maximum(top, top2)
        part = jnp.exp2(top - high)
        part2 = jnp.exp2(top2 - high)
        whole_sum = jnp.maximum(part * total + part2 * total2, 0.5)
        inverse = 1.0 / whole_sum
        balance = (part * balance + part2 * balance2) * inverse
        factors[group, 0] = part * inverse
        factors[group, 1] = balance
        columns[group, 0] = jnp.transpose(high + jnp.log2(whole_sum))
        columns[group, 1] = jnp.transpose(balance)

    def gradients(group):
        for item, (image, head) in enumerate(places):
            at = cols(group, head)
            slot = group * group_items + item
            keys, values = far[0, image, :, at], far[1, image, :, at]
            queries, grads = near[0, image, :, at], near[1, image, :, at]
            w = exps[slot] * factors[group, 0, item : item + 1, :]
            ds = w * (dps[slot] - factors[group, 1, item : item + 1, :])
            w = w.astype(jnp.bfloat16)
            ds = ds.astype(jnp.bfloat16)
            dk = nn(ds, queries) * scale
            dv = nn(w, grads)
            att = tn(w, values)
            dq = tn(ds, keys) * scale
            for which, x in enumerate((dk, dv)):
                far_acc[which, image, :, at] = x[tokens : 2 * tokens]
                term_out[0, which, image, :, at] = x[0:tokens].astype(jnp.bfloat16)
                term_out[1, which, image, :, at] = x[2 * tokens :].astype(jnp.bfloat16)
            for which, x in enumerate((att, dq)):
                near_acc[which, image, :, at] = x[0:tokens]
                for way in range(2):
                    low = tokens + 2 * HALO * way
                    part_out[way, which, image, :, at] = x[low : low + 2 * HALO].astype(jnp.bfloat16)
        to_tiles(group, 1, start)
        to_sides(group, 1)

    def finish(group):
        for way in range(2):
            part_copy(group, way).wait_recv()
        from_tiles(group, 1)
        at = lanes(group)
        for image in range(images):
            for which in range(2):
                acc = near_acc[which, image, :, at]
                add_l = part_in[0, which, image, :, at].astype(jnp.float32)
                add_r = part_in[1, which, image, :, at].astype(jnp.float32)
                rows = []
                for r in range(2):
                    here = acc[32 * r : 32 * r + 32]
                    rows.append(here[0:8] + add_l[8 * r : 8 * r + 8])
                    rows.append(here[8:24])
                    rows.append(here[24:32] + add_r[8 * r : 8 * r + 8])
                outs[which, image, :, at] = jnp.concatenate(rows, axis=0).astype(jnp.bfloat16)
            for which in range(2):
                total = far_acc[which, image, :, at]
                for way in range(2):
                    total = total + term_in[way, which, image, :, at].astype(jnp.float32)
                outs[2 + which, image, :, at] = total.astype(jnp.bfloat16)

    def step(index, carry):
        @pl.when(index < GROUPS // 2)
        def _():
            forward(2 * index, 0)
            forward(2 * index + 1, 0)

        for group in (2, 4):
            for kind, after in enumerate((1, BEHIND + 3)):
                @pl.when(is_detour & (index == group + after))
                def _():
                    pass_aside(group, kind)

        @pl.when(index < GROUPS)
        def _():
            from_tiles(index, 0)
            for origin in range(2):
                edge_copy(index, 1 - origin).wait_recv()

            scores(index)

        @pl.when((index >= BEHIND + 2) & (index < GROUPS + BEHIND))
        def _():
            forward(index - BEHIND - 2, 1)

        @pl.when((index >= BEHIND) & (index < GROUPS + BEHIND))
        def _():
            combine(index - BEHIND)
            gradients(index - BEHIND)

        @pl.when(index >= LAG)
        def _():
            finish(index - LAG)

        return carry

    lax.fori_loop(0, GROUPS + LAG, step, 0)

    def drain(group, carry):
        to_tiles(group, 1, wait_send)
        for way in range(2):
            @pl.when(lat == routes[way][0])
            def _():
                pass_copy(group, way, 0).wait_send()

        for kind in range(2):
            for way in range(2):
                @pl.when((lat == routes[way][1]) & relayed(group, kind))
                def _():
                    relay_copy(group, way, kind).wait_send()
        return carry

    lax.fori_loop(0, GROUPS, drain, 0)
    @pl.when(is_detour)
    def _():
        for kind in range(2):
            for group in (2, 4):
                for origin in range(2):
                    detour_out(group, origin, kind).wait_send()

    for way in range(2):
        for source, sem in (
            (edge_out.at[way], edge_send.at[way]),
            (part_out.at[way], part_send.at[way]),
            (stats_out.at[way], stat_send.at[way]),
        ):
            remote(source, source, sem, sem, sides[way]).wait_send()
        crossing = lat == routes[way][0]
        for some, here in ((whole, jnp.logical_not(crossing)), (direct, crossing)):
            @pl.when(exists[way] & here)
            def _():
                sent = far.at[:, some, tokens : 2 * tokens, :]
                remote(sent, sent, kv_send.at[way], kv_send.at[way], tiles[way]).wait_send()


def split_kernel(stacked, *refs):
    outs, sem = refs[:4], refs[4]
    copies = [pltpu.make_async_copy(stacked.at[i], outs[i], sem.at[i]) for i in range(4)]
    for copy in copies:
        copy.start()
    for copy in copies:
        copy.wait()


def solution(mesh):
    lon_count = mesh.shape["lon"]
    lat_count = mesh.shape["lat"]

    def on_device(queries, key_states, value_states, out_grad, block_lists, row_widths):
        images, rows, columns, channels = queries.shape
        tokens = rows * columns
        flat = (images, tokens, channels)
        items = images * channels // HDIM
        bf16, f32 = jnp.bfloat16, jnp.float32
        hbm_spec = pl.BlockSpec(memory_space=pltpu.HBM)
        vmem_spec = pl.BlockSpec(memory_space=pltpu.VMEM)
        smem_spec = pl.BlockSpec(memory_space=pltpu.SMEM)
        dma = pltpu.SemaphoreType.DMA
        stacked = pl.pallas_call(
            functools.partial(kernel, lon_count, lat_count),
            out_shape=pltpu.VMEM((4,) + flat, bf16),
            in_specs=[smem_spec, smem_spec] + [hbm_spec] * 4,
            out_specs=vmem_spec,
            scratch_shapes=[
                pltpu.VMEM((2, images, 2 * tokens, channels), bf16),
                pltpu.VMEM((2, images, 3 * tokens, channels), bf16),
                pltpu.VMEM((2, 2, images, 2 * HALO, channels), bf16),
                pltpu.VMEM((3 * tokens, 2 * tokens), f32),
                pltpu.VMEM((tokens + 4 * HALO, 3 * tokens), f32),
                pltpu.VMEM((items, 3 * tokens, 2 * tokens), f32),
                pltpu.VMEM((items, 3 * tokens, 2 * tokens), f32),
                pltpu.VMEM((GROUPS, 3, 8, 2 * tokens), f32),
                pltpu.VMEM((2, GROUPS, 8, 2 * tokens), f32),
                pltpu.VMEM((2, GROUPS, 8, 2 * tokens), f32),
                pltpu.VMEM((GROUPS, 2, 8, 2 * tokens), f32),
                pltpu.VMEM((GROUPS, 2, 2 * tokens, 8), f32),
                pltpu.VMEM((2, images, tokens, channels), f32),
                pltpu.VMEM((2, 2, images, 2 * HALO, channels), bf16),
                pltpu.VMEM((2, 2, images, 2 * HALO, channels), bf16),
                pltpu.VMEM((2, images, tokens, channels), f32),
                pltpu.VMEM((2, 2, images, tokens, channels), bf16),
                pltpu.VMEM((2, 2, images, tokens, channels), bf16),
                pltpu.VMEM((2, 2, images - images // 2, tokens, channels), bf16),
                pltpu.VMEM((2, DETOURS, 2, 2, images, 2 * HALO, channels // GROUPS), bf16),
                dma((4,)),
                dma((2,)),
                dma((GROUPS, 2)),
                dma((2,)),
                dma((GROUPS, 2)),
                dma((2,)),
                dma((GROUPS, 2)),
                dma((2,)),
                dma((GROUPS, 2)),
                dma((GROUPS, 2)),
                dma((GROUPS, 2)),
                dma((GROUPS, 2)),
                dma((GROUPS, 2)),
                dma((GROUPS, 2)),
                dma((2, DETOURS, 2)),
                dma((2, DETOURS, 2)),
            ],
            compiler_params=pltpu.CompilerParams(
                collective_id=0, has_side_effects=True, vmem_limit_bytes=60 * 1024 * 1024
            ),
            cost_estimate=pl.CostEstimate(
                flops=12 * items * 192 * 128 * 128,
                bytes_accessed=8 * images * tokens * channels * 2,
                transcendentals=items * 192 * 128,
            ),
        )(
            block_lists.T,
            row_widths,
            queries.reshape(flat),
            key_states.reshape(flat),
            value_states.reshape(flat),
            out_grad.reshape(flat),
        )
        results = pl.pallas_call(
            split_kernel,
            out_shape=[jax.ShapeDtypeStruct(flat, bf16)] * 4,
            in_specs=[pl.BlockSpec(memory_space=pl.ANY)],
            out_specs=[hbm_spec] * 4,
            scratch_shapes=[dma((4,))],
            compiler_params=pltpu.CompilerParams(vmem_limit_bytes=8 * 1024 * 1024),
        )(stacked)
        return tuple(x.reshape(queries.shape) for x in results)

    split = P(None, "lat", "lon", None)
    return jax.shard_map(
        on_device,
        mesh=mesh,
        in_specs=(split, split, split, split, P(), P()),
        out_specs=(split, split, split, split),
        check_vma=False,
    )
```

```python
import functools
import math

import jax
import jax.numpy as jnp
from jax import lax
from jax.experimental import pallas as pl
from jax.experimental.pallas import tpu as pltpu
from jax.sharding import PartitionSpec as P

MESH = pl.DeviceIdType.MESH
HALO = 8
HDIM = 128
GROUPS = 8
BEHIND = 6
LAG = 11
DETOURS = 2
HIDDEN = -1e30
FLOOR = -1e29


def nt(a, b):
    return lax.dot_general(a, b, (((1,), (1,)), ((), ())), preferred_element_type=jnp.float32)


def nn(a, b):
    return jnp.dot(a, b, preferred_element_type=jnp.float32)


def window(x, old, new, size, rest):
    lane = lax.broadcasted_iota(jnp.int32, x.shape, 1)
    shifted = x if old == new else pltpu.roll(x, (new - old) % HDIM, 1)
    return jnp.where((lane >= new) & (lane < new + size), shifted, rest)


def kernel(
    lon_count,
    lat_count,
    lists_hbm,
    widths_hbm,
    q_hbm,
    k_hbm,
    v_hbm,
    g_hbm,
    outs,
    near,
    far,
    edge_out,
    bias,
    exps,
    dps,
    stats,
    stats_out,
    stats_in,
    factors,
    columns,
    mixed,
    near_acc,
    part_out,
    part_in,
    far_acc,
    term_out,
    term_in,
    relay,
    detour,
    lists_ref,
    widths_ref,
    small_sem,
    own_sem,
    kv_send,
    kv_recv,
    edge_send,
    edge_recv,
    stat_send,
    stat_recv,
    part_send,
    part_recv,
    term_send,
    term_recv,
    pass_send,
    pass_recv,
    relay_send,
    detour_send,
    detour_recv,
):
    lon = lax.axis_index("lon")
    lat = lax.axis_index("lat")
    left = lax.rem(lon + lon_count - 1, lon_count)
    right = lax.rem(lon + 1, lon_count)
    has_above = lat > 0
    has_below = lat < lat_count - 1
    middle = lat_count // 2
    beside = lon + 1 - 2 * lax.rem(lon, 2)
    is_middle = (lat == middle - 1) | (lat == middle)
    routes = ((middle, 0, middle - 1), (middle - 1, lat_count - 1, middle))
    planes = middle // 2
    plane = lax.rem(lat // 2, planes)
    is_hot = (plane == 0) | (plane == planes - 1)
    is_detour = (plane == 1) | (plane == planes - 2)
    inward = jnp.where(plane < planes // 2, 2, -2)
    images, tokens, channels = q_hbm.shape
    heads = channels // HDIM
    group_heads = heads // GROUPS
    group_items = images * group_heads
    group_lanes = group_heads * HDIM
    scale = HDIM ** -0.5
    half = images // 2
    whole, direct, passing = slice(0, images), slice(0, half), slice(half, images)

    sides = ({"lon": left}, {"lon": right})
    tiles = ({"lat": lat - 1}, {"lat": lat + 1})
    exists = (has_above, has_below)

    own_copies = [
        pltpu.make_async_copy(k_hbm, far.at[0, :, tokens : 2 * tokens, :], own_sem.at[0]),
        pltpu.make_async_copy(v_hbm, far.at[1, :, tokens : 2 * tokens, :], own_sem.at[1]),
        pltpu.make_async_copy(q_hbm, near.at[0, :, 0:tokens, :], own_sem.at[2]),
        pltpu.make_async_copy(g_hbm, near.at[1, :, 0:tokens, :], own_sem.at[3]),
    ]
    for copy in own_copies:
        copy.start()
    small_copies = [
        pltpu.make_async_copy(lists_hbm, lists_ref, small_sem.at[0]),
        pltpu.make_async_copy(widths_hbm, widths_ref, small_sem.at[1]),
    ]
    for copy in small_copies:
        copy.start()

    barrier = pltpu.get_barrier_semaphore()
    for side in sides:
        pl.semaphore_signal(barrier, inc=1, device_id=side, device_id_type=MESH)
    for there, tile in zip(exists, tiles):
        @pl.when(there)
        def _():
            pl.semaphore_signal(barrier, inc=1, device_id=tile, device_id_type=MESH)
    for route in routes:
        @pl.when(lat == route[1])
        def _():
            pl.semaphore_signal(barrier, inc=1, device_id={"lat": route[0], "lon": beside}, device_id_type=MESH)
    @pl.when(is_detour)
    def _():
        for side in (left, right):
            pl.semaphore_signal(
                barrier, inc=1, device_id={"lat": lat - inward, "lon": side}, device_id_type=MESH
            )

    pl.semaphore_wait(
        barrier,
        2 + jnp.where(has_above, 1, 0) + jnp.where(has_below, 1, 0) + jnp.where(is_middle, 1, 0)
        + jnp.where(is_hot, 2, 0),
    )

    def lanes(group):
        start = group * group_lanes
        return pl.ds(start if isinstance(group, int) else pl.multiple_of(start, HDIM), group_lanes)

    def remote(source, target, send, recv, device):
        return pltpu.make_async_remote_copy(
            src_ref=source, dst_ref=target, send_sem=send, recv_sem=recv, device_id=device, device_id_type=MESH
        )

    def kv_copy(group, way, some):
        start = 2 * tokens if way == 0 else 0
        return remote(
            far.at[:, some, tokens : 2 * tokens, lanes(group)],
            far.at[:, some, start : start + tokens, lanes(group)],
            kv_send.at[way],
            kv_recv.at[group, 1 - way],
            tiles[way],
        )

    def edge_copy(group, way):
        start = tokens + 2 * HALO if way == 0 else tokens
        return remote(
            edge_out.at[way, :, :, :, lanes(group)],
            near.at[:, :, start : start + 2 * HALO, lanes(group)],
            edge_send.at[way],
            edge_recv.at[group, 1 - way],
            sides[way],
        )

    def stat_copy(group, way):
        return remote(
            stats_out.at[way, group],
            stats_in.at[1 - way, group],
            stat_send.at[way],
            stat_recv.at[group, 1 - way],
            sides[way],
        )

    def part_copy(group, way):
        return remote(
            part_out.at[way, :, :, :, lanes(group)],
            part_in.at[1 - way, :, :, :, lanes(group)],
            part_send.at[way],
            part_recv.at[group, 1 - way],
            sides[way],
        )

    def term_copy(group, way, some):
        return remote(
            term_out.at[way, :, some, :, lanes(group)],
            term_in.at[1 - way, :, some, :, lanes(group)],
            term_send.at[group, way],
            term_recv.at[group, 1 - way],
            tiles[way],
        )

    def pass_copy(group, way, kind):
        return remote(
            far.at[:, passing, tokens : 2 * tokens, lanes(group)]
            if kind == 0
            else term_out.at[way, :, passing, :, lanes(group)],
            relay.at[kind, :, :, :, lanes(group)],
            pass_send.at[group, kind],
            pass_recv.at[group, kind],
            {"lat": routes[way][1], "lon": beside},
        )

    def relay_copy(group, way, kind):
        start = 2 * tokens if way == 0 else 0
        return remote(
            relay.at[kind, :, :, :, lanes(group)],
            far.at[:, passing, start : start + tokens, lanes(group)]
            if kind == 0
            else term_in.at[1 - way, :, passing, :, lanes(group)],
            relay_send.at[group, kind],
            (kv_recv if kind == 0 else term_recv).at[group, 1 - way],
            {"lat": routes[way][2], "lon": beside},
        )

    def detour_in(group, way, kind):
        which = group // 2 - 1
        return remote(
            (edge_out, part_out)[kind].at[way, :, :, :, lanes(group)],
            detour.at[kind, which, 1 - way],
            (edge_send, part_send)[kind].at[way],
            detour_recv.at[kind, which, 1 - way],
            {"lat": lat + inward, "lon": (left, right)[way]},
        )

    def detour_out(group, origin, kind):
        which = group // 2 - 1
        low = tokens + 2 * HALO * origin
        return remote(
            detour.at[kind, which, origin],
            near.at[:, :, low : low + 2 * HALO, lanes(group)]
            if kind == 0
            else part_in.at[origin, :, :, :, lanes(group)],
            detour_send.at[kind, which, origin],
            (edge_recv, part_recv)[kind].at[group, origin],
            {"lat": lat - inward},
        )

    def to_sides(group, kind):
        aside = is_hot & ((group == 2) | (group == 4))
        for way in range(2):
            @pl.when(jnp.logical_not(aside))
            def _():
                (edge_copy, part_copy)[kind](group, way).start()

            @pl.when(aside)
            def _():
                detour_in(group, way, kind).start()

    def pass_aside(group, kind):
        for origin in range(2):
            detour_in(group, 1 - origin, kind).wait_recv()
            detour_out(group, origin, kind).start()

    def relayed(group, kind):
        return True if kind == 0 else group < GROUPS - 2

    def to_tiles(group, kind, act):
        copy = (kv_copy, term_copy)[kind]
        for way in range(2):
            crossing = (lat == routes[way][0]) & relayed(group, kind)

            @pl.when(exists[way] & jnp.logical_not(crossing))
            def _():
                act(copy(group, way, whole))

            @pl.when(crossing)
            def _():
                act(copy(group, way, direct))
                act(pass_copy(group, way, kind))

    def from_tiles(group, kind):
        copy = (kv_copy, term_copy)[kind]
        for origin in range(2):
            @pl.when(exists[origin])
            def _():
                copy(group, 1 - origin, whole).wait_recv()

    def forward(group, kind):
        for way in range(2):
            @pl.when((lat == routes[way][1]) & relayed(group, kind))
            def _():
                pass_copy(group, way, kind).wait_recv()
                relay_copy(group, way, kind).start()

    def start(copy):
        copy.start()

    def wait_send(copy):
        copy.wait_send()

    def send_edges(group):
        for which in range(2):
            for image in range(images):
                def half(start, low):
                    block = near[which, image, start : start + 16, lanes(group)].astype(jnp.float32)
                    return block[low : low + HALO]

                edge_out[0, which, image, :, lanes(group)] = jnp.concatenate(
                    [half(0, 0), half(32, 0)], axis=0
                ).astype(jnp.bfloat16)
                edge_out[1, which, image, :, lanes(group)] = jnp.concatenate(
                    [half(16, HALO), half(48, HALO)], axis=0
                ).astype(jnp.bfloat16)
        to_sides(group, 0)

    own_copies[0].wait()
    own_copies[1].wait()
    to_tiles(0, 0, start)
    own_copies[2].wait()
    own_copies[3].wait()
    send_edges(0)

    def send_group(group, carry):
        to_tiles(group, 0, start)
        send_edges(group)
        return carry

    lax.fori_loop(1, GROUPS, send_group, 0)

    near[:, :, tokens + 4 * HALO :, :] = jnp.zeros(
        (2, images, near.shape[2] - tokens - 4 * HALO, channels), jnp.bfloat16
    )
    for way in range(2):
        @pl.when(jnp.logical_not(exists[way]))
        def _():
            start = 0 if way == 0 else 2 * tokens
            far[:, :, start : start + tokens, :] = jnp.zeros((2, images, tokens, channels), jnp.bfloat16)
            term_in[way] = jnp.zeros((2, images, tokens, channels), jnp.bfloat16)

    def listed(target):
        found = (
            (lists_ref[0, lat] == target)
            | (lists_ref[1, lat] == target)
            | (lists_ref[2, lat] == target)
        ) & (target >= 0)
        return jnp.where(found, 1, 0)

    def mask(shape, key_axis):
        key = lax.broadcasted_iota(jnp.int32, shape, key_axis)
        query = lax.broadcasted_iota(jnp.int32, shape, 1 - key_axis)
        key_tile = key >> 6
        key_col = key & 31
        edge = query - tokens
        is_own = query < tokens
        from_left = edge < 2 * HALO
        query_col = jnp.where(
            is_own, query & 31, jnp.where(from_left, (edge & 7) - HALO, 32 + (edge & 7))
        )
        query_row = jnp.where(is_own, query >> 5, (edge >> 3) & 1)
        width = jnp.where(query_row == 0, widths_ref[2 * lat], widths_ref[2 * lat + 1])
        active = jnp.where(
            key_tile == 0, listed(lat - 1), jnp.where(key_tile == 1, listed(lat), listed(lat + 1))
        )
        visible = (jnp.abs(query_col - key_col) <= width) & (active == 1) & (edge < 4 * HALO)
        return jnp.where(visible, 0.0, HIDDEN)

    for copy in small_copies:
        copy.wait()
    bias[...] = mask(bias.shape, 0)

    places = [(image, head) for image in range(images) for head in range(group_heads)]

    def cols(group, head):
        return pl.ds(pl.multiple_of(group * group_lanes + head * HDIM, HDIM), HDIM)

    to_log2 = scale * math.log2(math.e)
    seen = tokens + 4 * HALO

    def scores(group):
        tops, sums, balances = [], [], []
        for item, (image, head) in enumerate(places):
            at = cols(group, head)
            raw = nt(far[0, image, :, at], near[0, image, :, at]) * to_log2 + bias[...]
            dp = nt(far[1, image, :, at], near[1, image, :, at])
            top = jnp.maximum(jnp.max(raw, axis=0, keepdims=True), FLOOR)
            e = jnp.exp2(raw - top)
            slot = group * group_items + item
            exps[slot] = e
            dps[slot] = dp
            mixed[slot] = nn(jnp.transpose(e.astype(jnp.bfloat16))[0:seen], far[1, image, :, at])
            tops.append(top)
            sums.append(jnp.sum(e, axis=0, keepdims=True))
            balances.append(jnp.sum(e * dp, axis=0, keepdims=True))
        for kind, found in enumerate((tops, sums, balances)):
            rows = found + [jnp.zeros_like(found[0])] * (8 - len(found))
            stats[group, kind] = jnp.concatenate(rows, axis=0)
        for way, moves in enumerate((((0, 0, 8), (32, 8, 8), (64, 16, 16)), ((24, 0, 8), (56, 8, 8), (80, 16, 16)))):
            packed = jnp.zeros((8, HDIM), jnp.float32)
            for kind in range(3):
                for old, new, size in moves:
                    packed = window(stats[group, kind], old, 32 * kind + new, size, packed)
            stats_out[way, group] = packed
        for way in range(2):
            stat_copy(group, way).start()

    def combine(group):
        for way in range(2):
            stat_copy(group, way).wait_recv()
        others = []
        for kind in range(3):
            other = jnp.full((8, HDIM), FLOOR if kind == 0 else 0.0, jnp.float32)
            for origin, moves in enumerate((((0, 64, 16), (16, 0, 8), (24, 32, 8)), ((0, 80, 16), (16, 24, 8), (24, 56, 8)))):
                for old, new, size in moves:
                    other = window(stats_in[origin, group], 32 * kind + old, new, size, other)
            others.append(other)
        top, total, balance = (stats[group, kind] for kind in range(3))
        top2, total2, balance2 = others
        high = jnp.maximum(top, top2)
        part = jnp.exp2(top - high)
        part2 = jnp.exp2(top2 - high)
        inverse = 1.0 / jnp.maximum(part * total + part2 * total2, 0.5)
        factor = part * inverse
        factors[group, 0] = factor
        factors[group, 1] = (part * balance + part2 * balance2) * inverse
        columns[group] = jnp.transpose(factor)

    def gradients(group):
        for item, (image, head) in enumerate(places):
            at = cols(group, head)
            slot = group * group_items + item
            keys = far[0, image, :, at]
            queries, grads = near[0, image, :, at], near[1, image, :, at]
            w = exps[slot] * factors[group, 0, item : item + 1, :]
            ds = w * (dps[slot] - factors[group, 1, item : item + 1, :])
            w = w.astype(jnp.bfloat16)
            ds = ds.astype(jnp.bfloat16)
            dk = nn(ds, queries) * scale
            dv = nn(w, grads)
            att = mixed[slot] * columns[group, 0:seen, item : item + 1]
            dq = nn(jnp.transpose(ds)[0:seen], keys) * scale
            for which, x in enumerate((dk, dv)):
                far_acc[which, image, :, at] = x[tokens : 2 * tokens]
                term_out[0, which, image, :, at] = x[0:tokens].astype(jnp.bfloat16)
                term_out[1, which, image, :, at] = x[2 * tokens :].astype(jnp.bfloat16)
            for which, x in enumerate((att, dq)):
                near_acc[which, image, :, at] = x[0:tokens]
                for way in range(2):
                    low = tokens + 2 * HALO * way
                    part_out[way, which, image, :, at] = x[low : low + 2 * HALO].astype(jnp.bfloat16)
        to_tiles(group, 1, start)
        to_sides(group, 1)

    def finish(group):
        for way in range(2):
            part_copy(group, way).wait_recv()
        from_tiles(group, 1)
        at = lanes(group)
        for image in range(images):
            for which in range(2):
                acc = near_acc[which, image, :, at]
                add_l = part_in[0, which, image, :, at].astype(jnp.float32)
                add_r = part_in[1, which, image, :, at].astype(jnp.float32)
                rows = []
                for r in range(2):
                    here = acc[32 * r : 32 * r + 32]
                    rows.append(here[0:8] + add_l[8 * r : 8 * r + 8])
                    rows.append(here[8:24])
                    rows.append(here[24:32] + add_r[8 * r : 8 * r + 8])
                outs[which, image, :, at] = jnp.concatenate(rows, axis=0).astype(jnp.bfloat16)
            for which in range(2):
                total = far_acc[which, image, :, at]
                for way in range(2):
                    total = total + term_in[way, which, image, :, at].astype(jnp.float32)
                outs[2 + which, image, :, at] = total.astype(jnp.bfloat16)

    def step(index, carry):
        @pl.when(index < GROUPS // 2)
        def _():
            forward(2 * index, 0)
            forward(2 * index + 1, 0)

        for group in (2, 4):
            for kind, after in enumerate((1, BEHIND + 3)):
                @pl.when(is_detour & (index == group + after))
                def _():
                    pass_aside(group, kind)

        @pl.when(index < GROUPS)
        def _():
            from_tiles(index, 0)
            for origin in range(2):
                edge_copy(index, 1 - origin).wait_recv()

            scores(index)

        @pl.when((index >= BEHIND + 2) & (index < GROUPS + BEHIND))
        def _():
            forward(index - BEHIND - 2, 1)

        @pl.when((index >= BEHIND) & (index < GROUPS + BEHIND))
        def _():
            combine(index - BEHIND)
            gradients(index - BEHIND)

        @pl.when(index >= LAG)
        def _():
            finish(index - LAG)

        return carry

    lax.fori_loop(0, GROUPS + LAG, step, 0)

    def drain(group, carry):
        to_tiles(group, 1, wait_send)
        for way in range(2):
            @pl.when(lat == routes[way][0])
            def _():
                pass_copy(group, way, 0).wait_send()

        for kind in range(2):
            for way in range(2):
                @pl.when((lat == routes[way][1]) & relayed(group, kind))
                def _():
                    relay_copy(group, way, kind).wait_send()
        return carry

    lax.fori_loop(0, GROUPS, drain, 0)
    @pl.when(is_detour)
    def _():
        for kind in range(2):
            for group in (2, 4):
                for origin in range(2):
                    detour_out(group, origin, kind).wait_send()

    for way in range(2):
        for source, sem in (
            (edge_out.at[way], edge_send.at[way]),
            (part_out.at[way], part_send.at[way]),
            (stats_out.at[way], stat_send.at[way]),
        ):
            remote(source, source, sem, sem, sides[way]).wait_send()
        crossing = lat == routes[way][0]
        for some, here in ((whole, jnp.logical_not(crossing)), (direct, crossing)):
            @pl.when(exists[way] & here)
            def _():
                sent = far.at[:, some, tokens : 2 * tokens, :]
                remote(sent, sent, kv_send.at[way], kv_send.at[way], tiles[way]).wait_send()


def split_kernel(stacked, *refs):
    outs, sem = refs[:4], refs[4]
    copies = [pltpu.make_async_copy(stacked.at[i], outs[i], sem.at[i]) for i in range(4)]
    for copy in copies:
        copy.start()
    for copy in copies:
        copy.wait()


def solution(mesh):
    lon_count = mesh.shape["lon"]
    lat_count = mesh.shape["lat"]

    def on_device(queries, key_states, value_states, out_grad, block_lists, row_widths):
        images, rows, columns, channels = queries.shape
        tokens = rows * columns
        flat = (images, tokens, channels)
        items = images * channels // HDIM
        bf16, f32 = jnp.bfloat16, jnp.float32
        hbm_spec = pl.BlockSpec(memory_space=pltpu.HBM)
        vmem_spec = pl.BlockSpec(memory_space=pltpu.VMEM)
        dma = pltpu.SemaphoreType.DMA
        stacked = pl.pallas_call(
            functools.partial(kernel, lon_count, lat_count),
            out_shape=pltpu.VMEM((4,) + flat, bf16),
            in_specs=[hbm_spec] * 6,
            out_specs=vmem_spec,
            scratch_shapes=[
                pltpu.VMEM((2, images, 2 * tokens, channels), bf16),
                pltpu.VMEM((2, images, 3 * tokens, channels), bf16),
                pltpu.VMEM((2, 2, images, 2 * HALO, channels), bf16),
                pltpu.VMEM((3 * tokens, 2 * tokens), f32),
                pltpu.VMEM((items, 3 * tokens, 2 * tokens), f32),
                pltpu.VMEM((items, 3 * tokens, 2 * tokens), f32),
                pltpu.VMEM((GROUPS, 3, 8, 2 * tokens), f32),
                pltpu.VMEM((2, GROUPS, 8, 2 * tokens), f32),
                pltpu.VMEM((2, GROUPS, 8, 2 * tokens), f32),
                pltpu.VMEM((GROUPS, 2, 8, 2 * tokens), f32),
                pltpu.VMEM((GROUPS, 2 * tokens, 8), f32),
                pltpu.VMEM((items, tokens + 4 * HALO, HDIM), f32),
                pltpu.VMEM((2, images, tokens, channels), f32),
                pltpu.VMEM((2, 2, images, 2 * HALO, channels), bf16),
                pltpu.VMEM((2, 2, images, 2 * HALO, channels), bf16),
                pltpu.VMEM((2, images, tokens, channels), f32),
                pltpu.VMEM((2, 2, images, tokens, channels), bf16),
                pltpu.VMEM((2, 2, images, tokens, channels), bf16),
                pltpu.VMEM((2, 2, images - images // 2, tokens, channels), bf16),
                pltpu.VMEM((2, DETOURS, 2, 2, images, 2 * HALO, channels // GROUPS), bf16),
                pltpu.SMEM(block_lists.shape[::-1], jnp.int32),
                pltpu.SMEM(row_widths.shape, jnp.int32),
                dma((2,)),
                dma((4,)),
                dma((2,)),
                dma((GROUPS, 2)),
                dma((2,)),
                dma((GROUPS, 2)),
                dma((2,)),
                dma((GROUPS, 2)),
                dma((2,)),
                dma((GROUPS, 2)),
                dma((GROUPS, 2)),
                dma((GROUPS, 2)),
                dma((GROUPS, 2)),
                dma((GROUPS, 2)),
                dma((GROUPS, 2)),
                dma((2, DETOURS, 2)),
                dma((2, DETOURS, 2)),
            ],
            compiler_params=pltpu.CompilerParams(
                collective_id=0, has_side_effects=True, vmem_limit_bytes=60 * 1024 * 1024
            ),
            cost_estimate=pl.CostEstimate(
                flops=12 * items * 192 * 128 * 128,
                bytes_accessed=8 * images * tokens * channels * 2,
                transcendentals=items * 192 * 128,
            ),
        )(
            block_lists.T,
            row_widths,
            queries.reshape(flat),
            key_states.reshape(flat),
            value_states.reshape(flat),
            out_grad.reshape(flat),
        )
        results = pl.pallas_call(
            split_kernel,
            out_shape=[jax.ShapeDtypeStruct(flat, bf16)] * 4,
            in_specs=[pl.BlockSpec(memory_space=pl.ANY)],
            out_specs=[hbm_spec] * 4,
            scratch_shapes=[dma((4,))],
            compiler_params=pltpu.CompilerParams(vmem_limit_bytes=8 * 1024 * 1024),
        )(stacked)
        return tuple(x.reshape(queries.shape) for x in results)

    split = P(None, "lat", "lon", None)
    return jax.shard_map(
        on_device,
        mesh=mesh,
        in_specs=(split, split, split, split, P(), P()),
        out_specs=(split, split, split, split),
        check_vma=False,
    )
```

```python
import functools
import math

import jax
import jax.numpy as jnp
from jax import lax
from jax.experimental import pallas as pl
from jax.experimental.pallas import tpu as pltpu
from jax.sharding import PartitionSpec as P

MESH = pl.DeviceIdType.MESH
HALO = 8
HDIM = 128
GROUPS = 8
AHEAD = 5
BEHIND = 5
LAG = 10
DETOURS = 2
HIDDEN = -1e30
FLOOR = -1e29


def nt(a, b):
    return lax.dot_general(a, b, (((1,), (1,)), ((), ())), preferred_element_type=jnp.float32)


def nn(a, b):
    return jnp.dot(a, b, preferred_element_type=jnp.float32)


def window(x, old, new, size, rest):
    lane = lax.broadcasted_iota(jnp.int32, x.shape, 1)
    shifted = x if old == new else pltpu.roll(x, (new - old) % HDIM, 1)
    return jnp.where((lane >= new) & (lane < new + size), shifted, rest)


def kernel(
    lon_count,
    lat_count,
    lists_hbm,
    widths_hbm,
    q_hbm,
    k_hbm,
    v_hbm,
    g_hbm,
    outs,
    near,
    far,
    edge_out,
    bias,
    exps,
    dps,
    stats,
    stats_out,
    stats_in,
    factors,
    columns,
    mixed,
    near_acc,
    part_out,
    part_in,
    far_acc,
    term_out,
    term_in,
    relay,
    detour,
    lists_ref,
    widths_ref,
    small_sem,
    own_sem,
    kv_send,
    kv_recv,
    edge_send,
    edge_recv,
    stat_send,
    stat_recv,
    part_send,
    part_recv,
    term_send,
    term_recv,
    pass_send,
    pass_recv,
    relay_send,
    detour_send,
    detour_recv,
):
    lon = lax.axis_index("lon")
    lat = lax.axis_index("lat")
    left = lax.rem(lon + lon_count - 1, lon_count)
    right = lax.rem(lon + 1, lon_count)
    has_above = lat > 0
    has_below = lat < lat_count - 1
    middle = lat_count // 2
    beside = lon + 1 - 2 * lax.rem(lon, 2)
    is_middle = (lat == middle - 1) | (lat == middle)
    routes = ((middle, 0, middle - 1), (middle - 1, lat_count - 1, middle))
    planes = middle // 2
    plane = lax.rem(lat // 2, planes)
    is_hot = (plane == 0) | (plane == planes - 1)
    is_detour = (plane == 1) | (plane == planes - 2)
    inward = jnp.where(plane < planes // 2, 2, -2)
    images, tokens, channels = q_hbm.shape
    heads = channels // HDIM
    group_heads = heads // GROUPS
    group_items = images * group_heads
    group_lanes = group_heads * HDIM
    scale = HDIM ** -0.5
    half = images // 2
    whole, direct, passing = slice(0, images), slice(0, half), slice(half, images)

    sides = ({"lon": left}, {"lon": right})
    tiles = ({"lat": lat - 1}, {"lat": lat + 1})
    exists = (has_above, has_below)

    own_copies = [
        pltpu.make_async_copy(k_hbm, far.at[0, :, tokens : 2 * tokens, :], own_sem.at[0]),
        pltpu.make_async_copy(v_hbm, far.at[1, :, tokens : 2 * tokens, :], own_sem.at[1]),
        pltpu.make_async_copy(q_hbm, near.at[0, :, 0:tokens, :], own_sem.at[2]),
        pltpu.make_async_copy(g_hbm, near.at[1, :, 0:tokens, :], own_sem.at[3]),
    ]
    for copy in own_copies:
        copy.start()
    small_copies = [
        pltpu.make_async_copy(lists_hbm, lists_ref, small_sem.at[0]),
        pltpu.make_async_copy(widths_hbm, widths_ref, small_sem.at[1]),
    ]
    for copy in small_copies:
        copy.start()

    barrier = pltpu.get_barrier_semaphore()
    for side in sides:
        pl.semaphore_signal(barrier, inc=1, device_id=side, device_id_type=MESH)
    for there, tile in zip(exists, tiles):
        @pl.when(there)
        def _():
            pl.semaphore_signal(barrier, inc=1, device_id=tile, device_id_type=MESH)
    for route in routes:
        @pl.when(lat == route[1])
        def _():
            pl.semaphore_signal(barrier, inc=1, device_id={"lat": route[0], "lon": beside}, device_id_type=MESH)
    @pl.when(is_detour)
    def _():
        for side in (left, right):
            pl.semaphore_signal(
                barrier, inc=1, device_id={"lat": lat - inward, "lon": side}, device_id_type=MESH
            )

    pl.semaphore_wait(
        barrier,
        2 + jnp.where(has_above, 1, 0) + jnp.where(has_below, 1, 0) + jnp.where(is_middle, 1, 0)
        + jnp.where(is_hot, 2, 0),
    )

    def lanes(group):
        start = group * group_lanes
        return pl.ds(start if isinstance(group, int) else pl.multiple_of(start, HDIM), group_lanes)

    def remote(source, target, send, recv, device):
        return pltpu.make_async_remote_copy(
            src_ref=source, dst_ref=target, send_sem=send, recv_sem=recv, device_id=device, device_id_type=MESH
        )

    def kv_copy(group, way, some):
        start = 2 * tokens if way == 0 else 0
        return remote(
            far.at[:, some, tokens : 2 * tokens, lanes(group)],
            far.at[:, some, start : start + tokens, lanes(group)],
            kv_send.at[way],
            kv_recv.at[group, 1 - way],
            tiles[way],
        )

    def edge_copy(group, way):
        start = tokens + 2 * HALO if way == 0 else tokens
        return remote(
            edge_out.at[way, :, :, :, lanes(group)],
            near.at[:, :, start : start + 2 * HALO, lanes(group)],
            edge_send.at[way],
            edge_recv.at[group, 1 - way],
            sides[way],
        )

    def stat_copy(group, way):
        return remote(
            stats_out.at[way, group],
            stats_in.at[1 - way, group],
            stat_send.at[way],
            stat_recv.at[group, 1 - way],
            sides[way],
        )

    def part_copy(group, way):
        return remote(
            part_out.at[way, :, :, :, lanes(group)],
            part_in.at[1 - way, :, :, :, lanes(group)],
            part_send.at[way],
            part_recv.at[group, 1 - way],
            sides[way],
        )

    def term_copy(group, way, some):
        return remote(
            term_out.at[way, :, some, :, lanes(group)],
            term_in.at[1 - way, :, some, :, lanes(group)],
            term_send.at[group, way],
            term_recv.at[group, 1 - way],
            tiles[way],
        )

    def pass_copy(group, way, kind):
        return remote(
            far.at[:, passing, tokens : 2 * tokens, lanes(group)]
            if kind == 0
            else term_out.at[way, :, passing, :, lanes(group)],
            relay.at[kind, :, :, :, lanes(group)],
            pass_send.at[group, kind],
            pass_recv.at[group, kind],
            {"lat": routes[way][1], "lon": beside},
        )

    def relay_copy(group, way, kind):
        start = 2 * tokens if way == 0 else 0
        return remote(
            relay.at[kind, :, :, :, lanes(group)],
            far.at[:, passing, start : start + tokens, lanes(group)]
            if kind == 0
            else term_in.at[1 - way, :, passing, :, lanes(group)],
            relay_send.at[group, kind],
            (kv_recv if kind == 0 else term_recv).at[group, 1 - way],
            {"lat": routes[way][2], "lon": beside},
        )

    def detour_in(group, way, kind):
        which = group // 2 - 1
        return remote(
            (edge_out, part_out)[kind].at[way, :, :, :, lanes(group)],
            detour.at[kind, which, 1 - way],
            (edge_send, part_send)[kind].at[way],
            detour_recv.at[kind, which, 1 - way],
            {"lat": lat + inward, "lon": (left, right)[way]},
        )

    def detour_out(group, origin, kind):
        which = group // 2 - 1
        low = tokens + 2 * HALO * origin
        return remote(
            detour.at[kind, which, origin],
            near.at[:, :, low : low + 2 * HALO, lanes(group)]
            if kind == 0
            else part_in.at[origin, :, :, :, lanes(group)],
            detour_send.at[kind, which, origin],
            (edge_recv, part_recv)[kind].at[group, origin],
            {"lat": lat - inward},
        )

    def to_sides(group, kind):
        aside = is_hot & ((group == 2) | (group == 4))
        for way in range(2):
            @pl.when(jnp.logical_not(aside))
            def _():
                (edge_copy, part_copy)[kind](group, way).start()

            @pl.when(aside)
            def _():
                detour_in(group, way, kind).start()

    def pass_aside(group, kind):
        for origin in range(2):
            detour_in(group, 1 - origin, kind).wait_recv()
            detour_out(group, origin, kind).start()

    def relayed(group, kind):
        return True if kind == 0 else group < GROUPS - 2

    def to_tiles(group, kind, act):
        copy = (kv_copy, term_copy)[kind]
        for way in range(2):
            crossing = (lat == routes[way][0]) & relayed(group, kind)

            @pl.when(exists[way] & jnp.logical_not(crossing))
            def _():
                act(copy(group, way, whole))

            @pl.when(crossing)
            def _():
                act(copy(group, way, direct))
                act(pass_copy(group, way, kind))

    def from_tiles(group, kind):
        copy = (kv_copy, term_copy)[kind]
        for origin in range(2):
            @pl.when(exists[origin])
            def _():
                copy(group, 1 - origin, whole).wait_recv()

    def forward(group, kind):
        for way in range(2):
            @pl.when((lat == routes[way][1]) & relayed(group, kind))
            def _():
                pass_copy(group, way, kind).wait_recv()
                relay_copy(group, way, kind).start()

    def start(copy):
        copy.start()

    def wait_send(copy):
        copy.wait_send()

    def send_edges(group):
        for which in range(2):
            for image in range(images):
                def half(start, low):
                    block = near[which, image, start : start + 16, lanes(group)].astype(jnp.float32)
                    return block[low : low + HALO]

                edge_out[0, which, image, :, lanes(group)] = jnp.concatenate(
                    [half(0, 0), half(32, 0)], axis=0
                ).astype(jnp.bfloat16)
                edge_out[1, which, image, :, lanes(group)] = jnp.concatenate(
                    [half(16, HALO), half(48, HALO)], axis=0
                ).astype(jnp.bfloat16)
        to_sides(group, 0)

    own_copies[0].wait()
    own_copies[1].wait()
    to_tiles(0, 0, start)
    own_copies[2].wait()
    own_copies[3].wait()
    send_edges(0)

    def send_group(group, carry):
        to_tiles(group, 0, start)

        @pl.when(group < AHEAD)
        def _():
            send_edges(group)

        return carry

    lax.fori_loop(1, GROUPS, send_group, 0)

    near[:, :, tokens + 4 * HALO :, :] = jnp.zeros(
        (2, images, near.shape[2] - tokens - 4 * HALO, channels), jnp.bfloat16
    )
    for way in range(2):
        @pl.when(jnp.logical_not(exists[way]))
        def _():
            start = 0 if way == 0 else 2 * tokens
            far[:, :, start : start + tokens, :] = jnp.zeros((2, images, tokens, channels), jnp.bfloat16)
            term_in[way] = jnp.zeros((2, images, tokens, channels), jnp.bfloat16)

    def listed(target):
        found = (
            (lists_ref[0, lat] == target)
            | (lists_ref[1, lat] == target)
            | (lists_ref[2, lat] == target)
        ) & (target >= 0)
        return jnp.where(found, 1, 0)

    def mask(shape, key_axis):
        key = lax.broadcasted_iota(jnp.int32, shape, key_axis)
        query = lax.broadcasted_iota(jnp.int32, shape, 1 - key_axis)
        key_tile = key >> 6
        key_col = key & 31
        edge = query - tokens
        is_own = query < tokens
        from_left = edge < 2 * HALO
        query_col = jnp.where(
            is_own, query & 31, jnp.where(from_left, (edge & 7) - HALO, 32 + (edge & 7))
        )
        query_row = jnp.where(is_own, query >> 5, (edge >> 3) & 1)
        width = jnp.where(query_row == 0, widths_ref[2 * lat], widths_ref[2 * lat + 1])
        active = jnp.where(
            key_tile == 0, listed(lat - 1), jnp.where(key_tile == 1, listed(lat), listed(lat + 1))
        )
        visible = (jnp.abs(query_col - key_col) <= width) & (active == 1) & (edge < 4 * HALO)
        return jnp.where(visible, 0.0, HIDDEN)

    for copy in small_copies:
        copy.wait()
    bias[...] = mask(bias.shape, 0)

    places = [(image, head) for image in range(images) for head in range(group_heads)]

    def cols(group, head):
        return pl.ds(pl.multiple_of(group * group_lanes + head * HDIM, HDIM), HDIM)

    to_log2 = scale * math.log2(math.e)
    seen = tokens + 4 * HALO

    def scores(group):
        tops, sums, balances = [], [], []
        for item, (image, head) in enumerate(places):
            at = cols(group, head)
            raw = nt(far[0, image, :, at], near[0, image, :, at]) * to_log2 + bias[...]
            dp = nt(far[1, image, :, at], near[1, image, :, at])
            top = jnp.maximum(jnp.max(raw, axis=0, keepdims=True), FLOOR)
            e = jnp.exp2(raw - top)
            slot = group * group_items + item
            exps[slot] = e
            dps[slot] = dp
            mixed[slot] = nn(jnp.transpose(e.astype(jnp.bfloat16))[0:seen], far[1, image, :, at])
            tops.append(top)
            sums.append(jnp.sum(e, axis=0, keepdims=True))
            balances.append(jnp.sum(e * dp, axis=0, keepdims=True))
        for kind, found in enumerate((tops, sums, balances)):
            rows = found + [jnp.zeros_like(found[0])] * (8 - len(found))
            stats[group, kind] = jnp.concatenate(rows, axis=0)
        for way, moves in enumerate((((0, 0, 8), (32, 8, 8), (64, 16, 16)), ((24, 0, 8), (56, 8, 8), (80, 16, 16)))):
            packed = jnp.zeros((8, HDIM), jnp.float32)
            for kind in range(3):
                for old, new, size in moves:
                    packed = window(stats[group, kind], old, 32 * kind + new, size, packed)
            stats_out[way, group] = packed
        for way in range(2):
            stat_copy(group, way).start()

    def combine(group):
        for way in range(2):
            stat_copy(group, way).wait_recv()
        others = []
        for kind in range(3):
            other = jnp.full((8, HDIM), FLOOR if kind == 0 else 0.0, jnp.float32)
            for origin, moves in enumerate((((0, 64, 16), (16, 0, 8), (24, 32, 8)), ((0, 80, 16), (16, 24, 8), (24, 56, 8)))):
                for old, new, size in moves:
                    other = window(stats_in[origin, group], 32 * kind + old, new, size, other)
            others.append(other)
        top, total, balance = (stats[group, kind] for kind in range(3))
        top2, total2, balance2 = others
        high = jnp.maximum(top, top2)
        part = jnp.exp2(top - high)
        part2 = jnp.exp2(top2 - high)
        inverse = 1.0 / jnp.maximum(part * total + part2 * total2, 0.5)
        factor = part * inverse
        factors[group, 0] = factor
        factors[group, 1] = (part * balance + part2 * balance2) * inverse
        columns[group] = jnp.transpose(factor)

    def gradients(group):
        for item, (image, head) in enumerate(places):
            at = cols(group, head)
            slot = group * group_items + item
            keys = far[0, image, :, at]
            queries, grads = near[0, image, :, at], near[1, image, :, at]
            w = exps[slot] * factors[group, 0, item : item + 1, :]
            ds = w * (dps[slot] - factors[group, 1, item : item + 1, :])
            w = w.astype(jnp.bfloat16)
            ds = ds.astype(jnp.bfloat16)
            dk = nn(ds, queries) * scale
            dv = nn(w, grads)
            att = mixed[slot] * columns[group, 0:seen, item : item + 1]
            dq = nn(jnp.transpose(ds)[0:seen], keys) * scale
            for which, x in enumerate((dk, dv)):
                far_acc[which, image, :, at] = x[tokens : 2 * tokens]
                term_out[0, which, image, :, at] = x[0:tokens].astype(jnp.bfloat16)
                term_out[1, which, image, :, at] = x[2 * tokens :].astype(jnp.bfloat16)
            for which, x in enumerate((att, dq)):
                near_acc[which, image, :, at] = x[0:tokens]
                for way in range(2):
                    low = tokens + 2 * HALO * way
                    part_out[way, which, image, :, at] = x[low : low + 2 * HALO].astype(jnp.bfloat16)
        to_tiles(group, 1, start)
        to_sides(group, 1)

    def finish(group):
        for way in range(2):
            part_copy(group, way).wait_recv()
        from_tiles(group, 1)
        at = lanes(group)
        for image in range(images):
            for which in range(2):
                acc = near_acc[which, image, :, at]
                add_l = part_in[0, which, image, :, at].astype(jnp.float32)
                add_r = part_in[1, which, image, :, at].astype(jnp.float32)
                rows = []
                for r in range(2):
                    here = acc[32 * r : 32 * r + 32]
                    rows.append(here[0:8] + add_l[8 * r : 8 * r + 8])
                    rows.append(here[8:24])
                    rows.append(here[24:32] + add_r[8 * r : 8 * r + 8])
                outs[which, image, :, at] = jnp.concatenate(rows, axis=0).astype(jnp.bfloat16)
            for which in range(2):
                total = far_acc[which, image, :, at]
                for way in range(2):
                    total = total + term_in[way, which, image, :, at].astype(jnp.float32)
                outs[2 + which, image, :, at] = total.astype(jnp.bfloat16)

    def step(index, carry):
        @pl.when(index < GROUPS // 2)
        def _():
            forward(2 * index, 0)
            forward(2 * index + 1, 0)

        for group in (2, 4):
            for kind, after in enumerate((1, BEHIND + 3)):
                @pl.when(is_detour & (index == group + after))
                def _():
                    pass_aside(group, kind)

        @pl.when(index < GROUPS)
        def _():
            from_tiles(index, 0)
            for origin in range(2):
                edge_copy(index, 1 - origin).wait_recv()

            scores(index)

            @pl.when(index + AHEAD < GROUPS)
            def _():
                send_edges(index + AHEAD)

        @pl.when((index >= BEHIND + 2) & (index < GROUPS + BEHIND))
        def _():
            forward(index - BEHIND - 2, 1)

        @pl.when((index >= BEHIND) & (index < GROUPS + BEHIND))
        def _():
            combine(index - BEHIND)
            gradients(index - BEHIND)

        @pl.when(index >= LAG)
        def _():
            finish(index - LAG)

        return carry

    lax.fori_loop(0, GROUPS + LAG, step, 0)

    def drain(group, carry):
        to_tiles(group, 1, wait_send)
        for way in range(2):
            @pl.when(lat == routes[way][0])
            def _():
                pass_copy(group, way, 0).wait_send()

        for kind in range(2):
            for way in range(2):
                @pl.when((lat == routes[way][1]) & relayed(group, kind))
                def _():
                    relay_copy(group, way, kind).wait_send()
        return carry

    lax.fori_loop(0, GROUPS, drain, 0)
    @pl.when(is_detour)
    def _():
        for kind in range(2):
            for group in (2, 4):
                for origin in range(2):
                    detour_out(group, origin, kind).wait_send()

    for way in range(2):
        for source, sem in (
            (edge_out.at[way], edge_send.at[way]),
            (part_out.at[way], part_send.at[way]),
            (stats_out.at[way], stat_send.at[way]),
        ):
            remote(source, source, sem, sem, sides[way]).wait_send()
        crossing = lat == routes[way][0]
        for some, here in ((whole, jnp.logical_not(crossing)), (direct, crossing)):
            @pl.when(exists[way] & here)
            def _():
                sent = far.at[:, some, tokens : 2 * tokens, :]
                remote(sent, sent, kv_send.at[way], kv_send.at[way], tiles[way]).wait_send()


def split_kernel(stacked, *refs):
    outs, sem = refs[:4], refs[4]
    copies = [pltpu.make_async_copy(stacked.at[i], outs[i], sem.at[i]) for i in range(4)]
    for copy in copies:
        copy.start()
    for copy in copies:
        copy.wait()


def solution(mesh):
    lon_count = mesh.shape["lon"]
    lat_count = mesh.shape["lat"]

    def on_device(queries, key_states, value_states, out_grad, block_lists, row_widths):
        images, rows, columns, channels = queries.shape
        tokens = rows * columns
        flat = (images, tokens, channels)
        items = images * channels // HDIM
        bf16, f32 = jnp.bfloat16, jnp.float32
        hbm_spec = pl.BlockSpec(memory_space=pltpu.HBM)
        vmem_spec = pl.BlockSpec(memory_space=pltpu.VMEM)
        dma = pltpu.SemaphoreType.DMA
        stacked = pl.pallas_call(
            functools.partial(kernel, lon_count, lat_count),
            out_shape=pltpu.VMEM((4,) + flat, bf16),
            in_specs=[hbm_spec] * 6,
            out_specs=vmem_spec,
            scratch_shapes=[
                pltpu.VMEM((2, images, 2 * tokens, channels), bf16),
                pltpu.VMEM((2, images, 3 * tokens, channels), bf16),
                pltpu.VMEM((2, 2, images, 2 * HALO, channels), bf16),
                pltpu.VMEM((3 * tokens, 2 * tokens), f32),
                pltpu.VMEM((items, 3 * tokens, 2 * tokens), f32),
                pltpu.VMEM((items, 3 * tokens, 2 * tokens), f32),
                pltpu.VMEM((GROUPS, 3, 8, 2 * tokens), f32),
                pltpu.VMEM((2, GROUPS, 8, 2 * tokens), f32),
                pltpu.VMEM((2, GROUPS, 8, 2 * tokens), f32),
                pltpu.VMEM((GROUPS, 2, 8, 2 * tokens), f32),
                pltpu.VMEM((GROUPS, 2 * tokens, 8), f32),
                pltpu.VMEM((items, tokens + 4 * HALO, HDIM), f32),
                pltpu.VMEM((2, images, tokens, channels), f32),
                pltpu.VMEM((2, 2, images, 2 * HALO, channels), bf16),
                pltpu.VMEM((2, 2, images, 2 * HALO, channels), bf16),
                pltpu.VMEM((2, images, tokens, channels), f32),
                pltpu.VMEM((2, 2, images, tokens, channels), bf16),
                pltpu.VMEM((2, 2, images, tokens, channels), bf16),
                pltpu.VMEM((2, 2, images - images // 2, tokens, channels), bf16),
                pltpu.VMEM((2, DETOURS, 2, 2, images, 2 * HALO, channels // GROUPS), bf16),
                pltpu.SMEM(block_lists.shape[::-1], jnp.int32),
                pltpu.SMEM(row_widths.shape, jnp.int32),
                dma((2,)),
                dma((4,)),
                dma((2,)),
                dma((GROUPS, 2)),
                dma((2,)),
                dma((GROUPS, 2)),
                dma((2,)),
                dma((GROUPS, 2)),
                dma((2,)),
                dma((GROUPS, 2)),
                dma((GROUPS, 2)),
                dma((GROUPS, 2)),
                dma((GROUPS, 2)),
                dma((GROUPS, 2)),
                dma((GROUPS, 2)),
                dma((2, DETOURS, 2)),
                dma((2, DETOURS, 2)),
            ],
            compiler_params=pltpu.CompilerParams(
                collective_id=0, has_side_effects=True, vmem_limit_bytes=60 * 1024 * 1024
            ),
            cost_estimate=pl.CostEstimate(
                flops=12 * items * 192 * 128 * 128,
                bytes_accessed=8 * images * tokens * channels * 2,
                transcendentals=items * 192 * 128,
            ),
        )(
            block_lists.T,
            row_widths,
            queries.reshape(flat),
            key_states.reshape(flat),
            value_states.reshape(flat),
            out_grad.reshape(flat),
        )
        results = pl.pallas_call(
            split_kernel,
            out_shape=[jax.ShapeDtypeStruct(flat, bf16)] * 4,
            in_specs=[pl.BlockSpec(memory_space=pl.ANY)],
            out_specs=[hbm_spec] * 4,
            scratch_shapes=[dma((4,))],
            compiler_params=pltpu.CompilerParams(vmem_limit_bytes=8 * 1024 * 1024),
        )(stacked)
        return tuple(x.reshape(queries.shape) for x in results)

    split = P(None, "lat", "lon", None)
    return jax.shard_map(
        on_device,
        mesh=mesh,
        in_specs=(split, split, split, split, P(), P()),
        out_specs=(split, split, split, split),
        check_vma=False,
    )
```

```python
import functools
import math

import jax
import jax.numpy as jnp
from jax import lax
from jax.experimental import pallas as pl
from jax.experimental.pallas import tpu as pltpu
from jax.sharding import PartitionSpec as P

MESH = pl.DeviceIdType.MESH
HALO = 8
HDIM = 128
GROUPS = 8
AHEAD = 5
BEHIND = 5
LAG = 10
DETOURS = 2
HIDDEN = -1e30
FLOOR = -1e29


def nt(a, b):
    return lax.dot_general(a, b, (((1,), (1,)), ((), ())), preferred_element_type=jnp.float32)


def nn(a, b):
    return jnp.dot(a, b, preferred_element_type=jnp.float32)


def window(x, old, new, size, rest):
    lane = lax.broadcasted_iota(jnp.int32, x.shape, 1)
    shifted = x if old == new else pltpu.roll(x, (new - old) % HDIM, 1)
    return jnp.where((lane >= new) & (lane < new + size), shifted, rest)


def kernel(
    lon_count,
    lat_count,
    lists_hbm,
    widths_hbm,
    q_hbm,
    k_hbm,
    v_hbm,
    g_hbm,
    outs,
    near,
    edge_in,
    far,
    edge_out,
    bias,
    exps,
    dps,
    stats,
    stats_out,
    stats_in,
    factors,
    columns,
    mixed,
    near_acc,
    part_out,
    part_in,
    far_acc,
    term_out,
    term_in,
    relay,
    detour,
    lists_ref,
    widths_ref,
    small_sem,
    own_sem,
    kv_send,
    kv_recv,
    edge_send,
    edge_recv,
    stat_send,
    stat_recv,
    part_send,
    part_recv,
    term_send,
    term_recv,
    pass_send,
    pass_recv,
    relay_send,
    detour_send,
    detour_recv,
):
    lon = lax.axis_index("lon")
    lat = lax.axis_index("lat")
    left = lax.rem(lon + lon_count - 1, lon_count)
    right = lax.rem(lon + 1, lon_count)
    has_above = lat > 0
    has_below = lat < lat_count - 1
    middle = lat_count // 2
    beside = lon + 1 - 2 * lax.rem(lon, 2)
    is_middle = (lat == middle - 1) | (lat == middle)
    routes = ((middle, 0, middle - 1), (middle - 1, lat_count - 1, middle))
    planes = middle // 2
    plane = lax.rem(lat // 2, planes)
    is_hot = (plane == 0) | (plane == planes - 1)
    is_detour = (plane == 1) | (plane == planes - 2)
    inward = jnp.where(plane < planes // 2, 2, -2)
    images, tokens, channels = q_hbm.shape
    heads = channels // HDIM
    group_heads = heads // GROUPS
    group_items = images * group_heads
    group_lanes = group_heads * HDIM
    scale = HDIM ** -0.5
    half = images // 2
    whole, direct, passing = slice(0, images), slice(0, half), slice(half, images)

    sides = ({"lon": left}, {"lon": right})
    tiles = ({"lat": lat - 1}, {"lat": lat + 1})
    exists = (has_above, has_below)

    def lanes(group):
        start = group * group_lanes
        return pl.ds(start if isinstance(group, int) else pl.multiple_of(start, HDIM), group_lanes)

    def own_copies(group):
        targets = (far.at[group, 1, 0], far.at[group, 1, 1], near.at[group, 0], near.at[group, 1])
        return [
            pltpu.make_async_copy(source.at[:, :, lanes(group)], target, own_sem.at[group, which])
            for which, (source, target) in enumerate(zip((k_hbm, v_hbm, q_hbm, g_hbm), targets))
        ]

    def fetch(group, carry):
        for copy in own_copies(group):
            copy.start()
        return carry

    fetch(0, 0)
    small_copies = [
        pltpu.make_async_copy(lists_hbm, lists_ref, small_sem.at[0]),
        pltpu.make_async_copy(widths_hbm, widths_ref, small_sem.at[1]),
    ]
    for copy in small_copies:
        copy.start()

    lax.fori_loop(1, GROUPS, fetch, 0)

    barrier = pltpu.get_barrier_semaphore()
    for side in sides:
        pl.semaphore_signal(barrier, inc=1, device_id=side, device_id_type=MESH)
    for there, tile in zip(exists, tiles):
        @pl.when(there)
        def _():
            pl.semaphore_signal(barrier, inc=1, device_id=tile, device_id_type=MESH)
    for route in routes:
        @pl.when(lat == route[1])
        def _():
            pl.semaphore_signal(barrier, inc=1, device_id={"lat": route[0], "lon": beside}, device_id_type=MESH)
    @pl.when(is_detour)
    def _():
        for side in (left, right):
            pl.semaphore_signal(
                barrier, inc=1, device_id={"lat": lat - inward, "lon": side}, device_id_type=MESH
            )

    pl.semaphore_wait(
        barrier,
        2 + jnp.where(has_above, 1, 0) + jnp.where(has_below, 1, 0) + jnp.where(is_middle, 1, 0)
        + jnp.where(is_hot, 2, 0),
    )

    def remote(source, target, send, recv, device):
        return pltpu.make_async_remote_copy(
            src_ref=source, dst_ref=target, send_sem=send, recv_sem=recv, device_id=device, device_id_type=MESH
        )

    def kv_copy(group, way, some):
        return remote(
            far.at[group, 1, :, some],
            far.at[group, 2 - 2 * way, :, some],
            kv_send.at[way],
            kv_recv.at[group, 1 - way],
            tiles[way],
        )

    def edge_copy(group, way):
        return remote(
            edge_out.at[group, way],
            edge_in.at[group, 1 - way],
            edge_send.at[way],
            edge_recv.at[group, 1 - way],
            sides[way],
        )

    def stat_copy(group, way):
        return remote(
            stats_out.at[way, group],
            stats_in.at[1 - way, group],
            stat_send.at[way],
            stat_recv.at[group, 1 - way],
            sides[way],
        )

    def part_copy(group, way):
        return remote(
            part_out.at[group, way],
            part_in.at[group, 1 - way],
            part_send.at[way],
            part_recv.at[group, 1 - way],
            sides[way],
        )

    def term_copy(group, way, some):
        return remote(
            term_out.at[group, way, :, some],
            term_in.at[group, 1 - way, :, some],
            term_send.at[group, way],
            term_recv.at[group, 1 - way],
            tiles[way],
        )

    def pass_copy(group, way, kind):
        return remote(
            far.at[group, 1, :, passing] if kind == 0 else term_out.at[group, way, :, passing],
            relay.at[kind, group],
            pass_send.at[group, kind],
            pass_recv.at[group, kind],
            {"lat": routes[way][1], "lon": beside},
        )

    def relay_copy(group, way, kind):
        return remote(
            relay.at[kind, group],
            far.at[group, 2 - 2 * way, :, passing]
            if kind == 0
            else term_in.at[group, 1 - way, :, passing],
            relay_send.at[group, kind],
            (kv_recv if kind == 0 else term_recv).at[group, 1 - way],
            {"lat": routes[way][2], "lon": beside},
        )

    def detour_in(group, way, kind):
        which = group // 2 - 1
        return remote(
            (edge_out, part_out)[kind].at[group, way],
            detour.at[kind, which, 1 - way],
            (edge_send, part_send)[kind].at[way],
            detour_recv.at[kind, which, 1 - way],
            {"lat": lat + inward, "lon": (left, right)[way]},
        )

    def detour_out(group, origin, kind):
        which = group // 2 - 1
        return remote(
            detour.at[kind, which, origin],
            (edge_in, part_in)[kind].at[group, origin],
            detour_send.at[kind, which, origin],
            (edge_recv, part_recv)[kind].at[group, origin],
            {"lat": lat - inward},
        )

    def to_sides(group, kind):
        aside = is_hot & ((group == 2) | (group == 4))
        for way in range(2):
            @pl.when(jnp.logical_not(aside))
            def _():
                (edge_copy, part_copy)[kind](group, way).start()

            @pl.when(aside)
            def _():
                detour_in(group, way, kind).start()

    def pass_aside(group, kind):
        for origin in range(2):
            detour_in(group, 1 - origin, kind).wait_recv()
            detour_out(group, origin, kind).start()

    def relayed(group, kind):
        return True if kind == 0 else group < GROUPS - 2

    def to_tiles(group, kind, act):
        copy = (kv_copy, term_copy)[kind]
        for way in range(2):
            crossing = (lat == routes[way][0]) & relayed(group, kind)

            @pl.when(exists[way] & jnp.logical_not(crossing))
            def _():
                act(copy(group, way, whole))

            @pl.when(crossing)
            def _():
                act(copy(group, way, direct))
                act(pass_copy(group, way, kind))

    def from_tiles(group, kind):
        copy = (kv_copy, term_copy)[kind]
        for origin in range(2):
            @pl.when(exists[origin])
            def _():
                copy(group, 1 - origin, whole).wait_recv()

    def forward(group, kind):
        for way in range(2):
            @pl.when((lat == routes[way][1]) & relayed(group, kind))
            def _():
                pass_copy(group, way, kind).wait_recv()
                relay_copy(group, way, kind).start()

    def start(copy):
        copy.start()

    def wait_send(copy):
        copy.wait_send()

    def send_edges(group):
        for which in range(2):
            for image in range(images):
                def half(start, low):
                    block = near[group, which, image, start : start + 16].astype(jnp.float32)
                    return block[low : low + HALO]

                edge_out[group, 0, which, image] = jnp.concatenate(
                    [half(0, 0), half(32, 0)], axis=0
                ).astype(jnp.bfloat16)
                edge_out[group, 1, which, image] = jnp.concatenate(
                    [half(16, HALO), half(48, HALO)], axis=0
                ).astype(jnp.bfloat16)
        to_sides(group, 0)

    def send_group(group, carry):
        copies = own_copies(group)
        copies[0].wait()
        copies[1].wait()
        to_tiles(group, 0, start)
        copies[2].wait()
        copies[3].wait()

        @pl.when(group < AHEAD)
        def _():
            send_edges(group)

        return carry

    lax.fori_loop(0, GROUPS, send_group, 0)

    for way in range(2):
        @pl.when(jnp.logical_not(exists[way]))
        def _():
            far[:, 2 * way] = jnp.zeros((GROUPS, 2, images, tokens, group_lanes), jnp.bfloat16)
            term_in[:, way] = jnp.zeros((GROUPS, 2, images, tokens, group_lanes), jnp.bfloat16)

    def listed(target):
        found = (
            (lists_ref[0, lat] == target)
            | (lists_ref[1, lat] == target)
            | (lists_ref[2, lat] == target)
        ) & (target >= 0)
        return jnp.where(found, 1, 0)

    def mask(shape, key_axis):
        key = lax.broadcasted_iota(jnp.int32, shape, key_axis)
        query = lax.broadcasted_iota(jnp.int32, shape, 1 - key_axis)
        key_tile = key >> 6
        key_col = key & 31
        edge = query - tokens
        is_own = query < tokens
        from_left = edge < 2 * HALO
        query_col = jnp.where(
            is_own, query & 31, jnp.where(from_left, (edge & 7) - HALO, 32 + (edge & 7))
        )
        query_row = jnp.where(is_own, query >> 5, (edge >> 3) & 1)
        width = jnp.where(query_row == 0, widths_ref[2 * lat], widths_ref[2 * lat + 1])
        active = jnp.where(
            key_tile == 0, listed(lat - 1), jnp.where(key_tile == 1, listed(lat), listed(lat + 1))
        )
        visible = (jnp.abs(query_col - key_col) <= width) & (active == 1) & (edge < 4 * HALO)
        return jnp.where(visible, 0.0, HIDDEN)

    for copy in small_copies:
        copy.wait()
    bias[...] = mask(bias.shape, 0)

    places = [(image, head) for image in range(images) for head in range(group_heads)]

    def from_near(group, which, image, head):
        at = pl.ds(head * HDIM, HDIM)
        edges = [edge_in[group, origin, which, image, :, at] for origin in range(2)]
        rest = jnp.zeros((2 * tokens - seen, HDIM), jnp.bfloat16)
        return jnp.concatenate([near[group, which, image, :, at]] + edges + [rest], axis=0)

    def from_far(group, which, image, head):
        at = pl.ds(head * HDIM, HDIM)
        return jnp.concatenate([far[group, slot, which, image, :, at] for slot in range(3)], axis=0)

    to_log2 = scale * math.log2(math.e)
    seen = tokens + 4 * HALO

    def scores(group):
        tops, sums, balances = [], [], []
        for item, (image, head) in enumerate(places):
            values = from_far(group, 1, image, head)
            raw = nt(from_far(group, 0, image, head), from_near(group, 0, image, head))
            raw = raw * to_log2 + bias[...]
            dp = nt(values, from_near(group, 1, image, head))
            top = jnp.maximum(jnp.max(raw, axis=0, keepdims=True), FLOOR)
            e = jnp.exp2(raw - top)
            slot = group * group_items + item
            exps[slot] = e
            dps[slot] = dp
            mixed[slot] = nn(jnp.transpose(e.astype(jnp.bfloat16))[0:seen], values)
            tops.append(top)
            sums.append(jnp.sum(e, axis=0, keepdims=True))
            balances.append(jnp.sum(e * dp, axis=0, keepdims=True))
        for kind, found in enumerate((tops, sums, balances)):
            rows = found + [jnp.zeros_like(found[0])] * (8 - len(found))
            stats[group, kind] = jnp.concatenate(rows, axis=0)
        for way, moves in enumerate((((0, 0, 8), (32, 8, 8), (64, 16, 16)), ((24, 0, 8), (56, 8, 8), (80, 16, 16)))):
            packed = jnp.zeros((8, HDIM), jnp.float32)
            for kind in range(3):
                for old, new, size in moves:
                    packed = window(stats[group, kind], old, 32 * kind + new, size, packed)
            stats_out[way, group] = packed
        for way in range(2):
            stat_copy(group, way).start()

    def combine(group):
        for way in range(2):
            stat_copy(group, way).wait_recv()
        others = []
        for kind in range(3):
            other = jnp.full((8, HDIM), FLOOR if kind == 0 else 0.0, jnp.float32)
            for origin, moves in enumerate((((0, 64, 16), (16, 0, 8), (24, 32, 8)), ((0, 80, 16), (16, 24, 8), (24, 56, 8)))):
                for old, new, size in moves:
                    other = window(stats_in[origin, group], 32 * kind + old, new, size, other)
            others.append(other)
        top, total, balance = (stats[group, kind] for kind in range(3))
        top2, total2, balance2 = others
        high = jnp.maximum(top, top2)
        part = jnp.exp2(top - high)
        part2 = jnp.exp2(top2 - high)
        inverse = 1.0 / jnp.maximum(part * total + part2 * total2, 0.5)
        factor = part * inverse
        factors[group, 0] = factor
        factors[group, 1] = (part * balance + part2 * balance2) * inverse
        columns[group] = jnp.transpose(factor)

    def gradients(group):
        for item, (image, head) in enumerate(places):
            at = pl.ds(head * HDIM, HDIM)
            slot = group * group_items + item
            keys = from_far(group, 0, image, head)
            queries, grads = (from_near(group, which, image, head) for which in range(2))
            w = exps[slot] * factors[group, 0, item : item + 1, :]
            ds = w * (dps[slot] - factors[group, 1, item : item + 1, :])
            w = w.astype(jnp.bfloat16)
            ds = ds.astype(jnp.bfloat16)
            dk = nn(ds, queries) * scale
            dv = nn(w, grads)
            att = mixed[slot] * columns[group, 0:seen, item : item + 1]
            dq = nn(jnp.transpose(ds)[0:seen], keys) * scale
            for which, x in enumerate((dk, dv)):
                far_acc[group, which, image, :, at] = x[tokens : 2 * tokens]
                term_out[group, 0, which, image, :, at] = x[0:tokens].astype(jnp.bfloat16)
                term_out[group, 1, which, image, :, at] = x[2 * tokens :].astype(jnp.bfloat16)
            for which, x in enumerate((att, dq)):
                near_acc[group, which, image, :, at] = x[0:tokens]
                for way in range(2):
                    low = tokens + 2 * HALO * way
                    part_out[group, way, which, image, :, at] = x[low : low + 2 * HALO].astype(jnp.bfloat16)
        to_tiles(group, 1, start)
        to_sides(group, 1)

    def finish(group):
        for way in range(2):
            part_copy(group, way).wait_recv()
        from_tiles(group, 1)
        at = lanes(group)
        for image in range(images):
            for which in range(2):
                acc = near_acc[group, which, image]
                add_l = part_in[group, 0, which, image].astype(jnp.float32)
                add_r = part_in[group, 1, which, image].astype(jnp.float32)
                rows = []
                for r in range(2):
                    here = acc[32 * r : 32 * r + 32]
                    rows.append(here[0:8] + add_l[8 * r : 8 * r + 8])
                    rows.append(here[8:24])
                    rows.append(here[24:32] + add_r[8 * r : 8 * r + 8])
                outs[which, image, :, at] = jnp.concatenate(rows, axis=0).astype(jnp.bfloat16)
            for which in range(2):
                total = far_acc[group, which, image]
                for way in range(2):
                    total = total + term_in[group, way, which, image].astype(jnp.float32)
                outs[2 + which, image, :, at] = total.astype(jnp.bfloat16)

    def step(index, carry):
        @pl.when(index < GROUPS // 2)
        def _():
            forward(2 * index, 0)
            forward(2 * index + 1, 0)

        for group in (2, 4):
            for kind, after in enumerate((1, BEHIND + 3)):
                @pl.when(is_detour & (index == group + after))
                def _():
                    pass_aside(group, kind)

        @pl.when(index < GROUPS)
        def _():
            from_tiles(index, 0)
            for origin in range(2):
                edge_copy(index, 1 - origin).wait_recv()

            scores(index)

            @pl.when(index + AHEAD < GROUPS)
            def _():
                send_edges(index + AHEAD)

        @pl.when((index >= BEHIND + 2) & (index < GROUPS + BEHIND))
        def _():
            forward(index - BEHIND - 2, 1)

        @pl.when((index >= BEHIND) & (index < GROUPS + BEHIND))
        def _():
            combine(index - BEHIND)
            gradients(index - BEHIND)

        @pl.when(index >= LAG)
        def _():
            finish(index - LAG)

        return carry

    lax.fori_loop(0, GROUPS + LAG, step, 0)

    def drain(group, carry):
        to_tiles(group, 1, wait_send)
        for way in range(2):
            @pl.when(lat == routes[way][0])
            def _():
                pass_copy(group, way, 0).wait_send()

        for kind in range(2):
            for way in range(2):
                @pl.when((lat == routes[way][1]) & relayed(group, kind))
                def _():
                    relay_copy(group, way, kind).wait_send()
        return carry

    lax.fori_loop(0, GROUPS, drain, 0)
    @pl.when(is_detour)
    def _():
        for kind in range(2):
            for group in (2, 4):
                for origin in range(2):
                    detour_out(group, origin, kind).wait_send()

    for way in range(2):
        for source, sem in (
            (edge_out.at[:, way], edge_send.at[way]),
            (part_out.at[:, way], part_send.at[way]),
            (stats_out.at[way], stat_send.at[way]),
        ):
            remote(source, source, sem, sem, sides[way]).wait_send()
        crossing = lat == routes[way][0]
        for some, here in ((whole, jnp.logical_not(crossing)), (direct, crossing)):
            @pl.when(exists[way] & here)
            def _():
                sent = far.at[:, 1, :, some]
                remote(sent, sent, kv_send.at[way], kv_send.at[way], tiles[way]).wait_send()


def split_kernel(stacked, *refs):
    outs, sem = refs[:4], refs[4]
    copies = [pltpu.make_async_copy(stacked.at[i], outs[i], sem.at[i]) for i in range(4)]
    for copy in copies:
        copy.start()
    for copy in copies:
        copy.wait()


def solution(mesh):
    lon_count = mesh.shape["lon"]
    lat_count = mesh.shape["lat"]

    def on_device(queries, key_states, value_states, out_grad, block_lists, row_widths):
        images, rows, columns, channels = queries.shape
        tokens = rows * columns
        flat = (images, tokens, channels)
        items = images * channels // HDIM
        lanes = channels // GROUPS
        bf16, f32 = jnp.bfloat16, jnp.float32
        hbm_spec = pl.BlockSpec(memory_space=pltpu.HBM)
        vmem_spec = pl.BlockSpec(memory_space=pltpu.VMEM)
        dma = pltpu.SemaphoreType.DMA
        stacked = pl.pallas_call(
            functools.partial(kernel, lon_count, lat_count),
            out_shape=pltpu.VMEM((4,) + flat, bf16),
            in_specs=[hbm_spec] * 6,
            out_specs=vmem_spec,
            scratch_shapes=[
                pltpu.VMEM((GROUPS, 2, images, tokens, lanes), bf16),
                pltpu.VMEM((GROUPS, 2, 2, images, 2 * HALO, lanes), bf16),
                pltpu.VMEM((GROUPS, 3, 2, images, tokens, lanes), bf16),
                pltpu.VMEM((GROUPS, 2, 2, images, 2 * HALO, lanes), bf16),
                pltpu.VMEM((3 * tokens, 2 * tokens), f32),
                pltpu.VMEM((items, 3 * tokens, 2 * tokens), f32),
                pltpu.VMEM((items, 3 * tokens, 2 * tokens), f32),
                pltpu.VMEM((GROUPS, 3, 8, 2 * tokens), f32),
                pltpu.VMEM((2, GROUPS, 8, 2 * tokens), f32),
                pltpu.VMEM((2, GROUPS, 8, 2 * tokens), f32),
                pltpu.VMEM((GROUPS, 2, 8, 2 * tokens), f32),
                pltpu.VMEM((GROUPS, 2 * tokens, 8), f32),
                pltpu.VMEM((items, tokens + 4 * HALO, HDIM), f32),
                pltpu.VMEM((GROUPS, 2, images, tokens, lanes), f32),
                pltpu.VMEM((GROUPS, 2, 2, images, 2 * HALO, lanes), bf16),
                pltpu.VMEM((GROUPS, 2, 2, images, 2 * HALO, lanes), bf16),
                pltpu.VMEM((GROUPS, 2, images, tokens, lanes), f32),
                pltpu.VMEM((GROUPS, 2, 2, images, tokens, lanes), bf16),
                pltpu.VMEM((GROUPS, 2, 2, images, tokens, lanes), bf16),
                pltpu.VMEM((2, GROUPS, 2, images - images // 2, tokens, lanes), bf16),
                pltpu.VMEM((2, DETOURS, 2, 2, images, 2 * HALO, lanes), bf16),
                pltpu.SMEM(block_lists.shape[::-1], jnp.int32),
                pltpu.SMEM(row_widths.shape, jnp.int32),
                dma((2,)),
                dma((GROUPS, 4)),
                dma((2,)),
                dma((GROUPS, 2)),
                dma((2,)),
                dma((GROUPS, 2)),
                dma((2,)),
                dma((GROUPS, 2)),
                dma((2,)),
                dma((GROUPS, 2)),
                dma((GROUPS, 2)),
                dma((GROUPS, 2)),
                dma((GROUPS, 2)),
                dma((GROUPS, 2)),
                dma((GROUPS, 2)),
                dma((2, DETOURS, 2)),
                dma((2, DETOURS, 2)),
            ],
            compiler_params=pltpu.CompilerParams(
                collective_id=0, has_side_effects=True, vmem_limit_bytes=60 * 1024 * 1024
            ),
            cost_estimate=pl.CostEstimate(
                flops=12 * items * 192 * 128 * 128,
                bytes_accessed=8 * images * tokens * channels * 2,
                transcendentals=items * 192 * 128,
            ),
        )(
            block_lists.T,
            row_widths,
            queries.reshape(flat),
            key_states.reshape(flat),
            value_states.reshape(flat),
            out_grad.reshape(flat),
        )
        results = pl.pallas_call(
            split_kernel,
            out_shape=[jax.ShapeDtypeStruct(flat, bf16)] * 4,
            in_specs=[pl.BlockSpec(memory_space=pl.ANY)],
            out_specs=[hbm_spec] * 4,
            scratch_shapes=[dma((4,))],
            compiler_params=pltpu.CompilerParams(vmem_limit_bytes=8 * 1024 * 1024),
        )(stacked)
        return tuple(x.reshape(queries.shape) for x in results)

    split = P(None, "lat", "lon", None)
    return jax.shard_map(
        on_device,
        mesh=mesh,
        in_specs=(split, split, split, split, P(), P()),
        out_specs=(split, split, split, split),
        check_vma=False,
    )
```

```python
import functools
import math

import jax
import jax.numpy as jnp
from jax import lax
from jax.experimental import pallas as pl
from jax.experimental.pallas import tpu as pltpu
from jax.sharding import PartitionSpec as P

MESH = pl.DeviceIdType.MESH
HALO = 8
HDIM = 128
GROUPS = 8
AHEAD = 4
BEHIND = 5
DETOURS = 2
HIDDEN = -1e30
FLOOR = -1e29


def nt(a, b):
    return lax.dot_general(a, b, (((1,), (1,)), ((), ())), preferred_element_type=jnp.float32)


def nn(a, b):
    return jnp.dot(a, b, preferred_element_type=jnp.float32)


def window(x, old, new, size, rest):
    lane = lax.broadcasted_iota(jnp.int32, x.shape, 1)
    shifted = x if old == new else pltpu.roll(x, (new - old) % HDIM, 1)
    return jnp.where((lane >= new) & (lane < new + size), shifted, rest)


def kernel(
    lon_count,
    lat_count,
    lists_hbm,
    widths_hbm,
    q_hbm,
    k_hbm,
    v_hbm,
    g_hbm,
    outs,
    near,
    edge_in,
    far,
    edge_out,
    bias,
    exps,
    dps,
    stats,
    stats_out,
    stats_in,
    factors,
    columns,
    mixed,
    near_acc,
    part_out,
    part_in,
    far_acc,
    term_out,
    term_in,
    relay,
    detour,
    lists_ref,
    widths_ref,
    small_sem,
    own_sem,
    kv_send,
    kv_recv,
    edge_send,
    edge_recv,
    stat_send,
    stat_recv,
    part_send,
    part_recv,
    term_send,
    term_recv,
    pass_send,
    pass_recv,
    relay_send,
    detour_send,
    detour_recv,
):
    lon = lax.axis_index("lon")
    lat = lax.axis_index("lat")
    left = lax.rem(lon + lon_count - 1, lon_count)
    right = lax.rem(lon + 1, lon_count)
    has_above = lat > 0
    has_below = lat < lat_count - 1
    middle = lat_count // 2
    beside = lon + 1 - 2 * lax.rem(lon, 2)
    is_middle = (lat == middle - 1) | (lat == middle)
    routes = ((middle, 0, middle - 1), (middle - 1, lat_count - 1, middle))
    planes = middle // 2
    plane = lax.rem(lat // 2, planes)
    is_hot = (plane == 0) | (plane == planes - 1)
    is_detour = (plane == 1) | (plane == planes - 2)
    inward = jnp.where(plane < planes // 2, 2, -2)
    images, tokens, channels = q_hbm.shape
    heads = channels // HDIM
    group_heads = heads // GROUPS
    group_items = images * group_heads
    group_lanes = group_heads * HDIM
    scale = HDIM ** -0.5
    half = images // 2
    whole, direct, passing = slice(0, images), slice(0, half), slice(half, images)

    sides = ({"lon": left}, {"lon": right})
    tiles = ({"lat": lat - 1}, {"lat": lat + 1})
    exists = (has_above, has_below)

    def lanes(group):
        start = group * group_lanes
        return pl.ds(start if isinstance(group, int) else pl.multiple_of(start, HDIM), group_lanes)

    def own_copies(group):
        targets = (far.at[group, 1, 0], far.at[group, 1, 1], near.at[group, 0], near.at[group, 1])
        return [
            pltpu.make_async_copy(source.at[:, :, lanes(group)], target, own_sem.at[group, which])
            for which, (source, target) in enumerate(zip((k_hbm, v_hbm, q_hbm, g_hbm), targets))
        ]

    def fetch(group, carry):
        for copy in own_copies(group):
            copy.start()
        return carry

    fetch(0, 0)
    small_copies = [
        pltpu.make_async_copy(lists_hbm, lists_ref, small_sem.at[0]),
        pltpu.make_async_copy(widths_hbm, widths_ref, small_sem.at[1]),
    ]
    for copy in small_copies:
        copy.start()

    lax.fori_loop(1, GROUPS, fetch, 0)

    barrier = pltpu.get_barrier_semaphore()
    for side in sides:
        pl.semaphore_signal(barrier, inc=1, device_id=side, device_id_type=MESH)
    for there, tile in zip(exists, tiles):
        @pl.when(there)
        def _():
            pl.semaphore_signal(barrier, inc=1, device_id=tile, device_id_type=MESH)
    for route in routes:
        @pl.when(lat == route[1])
        def _():
            pl.semaphore_signal(barrier, inc=1, device_id={"lat": route[0], "lon": beside}, device_id_type=MESH)
    @pl.when(is_detour)
    def _():
        for side in (left, right):
            pl.semaphore_signal(
                barrier, inc=1, device_id={"lat": lat - inward, "lon": side}, device_id_type=MESH
            )

    pl.semaphore_wait(
        barrier,
        2 + jnp.where(has_above, 1, 0) + jnp.where(has_below, 1, 0) + jnp.where(is_middle, 1, 0)
        + jnp.where(is_hot, 2, 0),
    )

    def remote(source, target, send, recv, device):
        return pltpu.make_async_remote_copy(
            src_ref=source, dst_ref=target, send_sem=send, recv_sem=recv, device_id=device, device_id_type=MESH
        )

    def kv_copy(group, way, some):
        return remote(
            far.at[group, 1, :, some],
            far.at[group, 2 - 2 * way, :, some],
            kv_send.at[way],
            kv_recv.at[group, 1 - way],
            tiles[way],
        )

    def edge_copy(group, way):
        return remote(
            edge_out.at[group, way],
            edge_in.at[group, 1 - way],
            edge_send.at[way],
            edge_recv.at[group, 1 - way],
            sides[way],
        )

    def stat_copy(group, way):
        return remote(
            stats_out.at[way, group],
            stats_in.at[1 - way, group],
            stat_send.at[way],
            stat_recv.at[group, 1 - way],
            sides[way],
        )

    def part_copy(group, way):
        return remote(
            part_out.at[group, way],
            part_in.at[group, 1 - way],
            part_send.at[way],
            part_recv.at[group, 1 - way],
            sides[way],
        )

    def term_copy(group, way, some):
        return remote(
            term_out.at[group, way, :, some],
            term_in.at[group, 1 - way, :, some],
            term_send.at[group, way],
            term_recv.at[group, 1 - way],
            tiles[way],
        )

    def pass_copy(group, way, kind):
        return remote(
            far.at[group, 1, :, passing] if kind == 0 else term_out.at[group, way, :, passing],
            relay.at[kind, group],
            pass_send.at[group, kind],
            pass_recv.at[group, kind],
            {"lat": routes[way][1], "lon": beside},
        )

    def relay_copy(group, way, kind):
        return remote(
            relay.at[kind, group],
            far.at[group, 2 - 2 * way, :, passing]
            if kind == 0
            else term_in.at[group, 1 - way, :, passing],
            relay_send.at[group, kind],
            (kv_recv if kind == 0 else term_recv).at[group, 1 - way],
            {"lat": routes[way][2], "lon": beside},
        )

    def detour_in(group, way, kind):
        which = group // 2 - 1
        return remote(
            (edge_out, part_out)[kind].at[group, way],
            detour.at[kind, which, 1 - way],
            (edge_send, part_send)[kind].at[way],
            detour_recv.at[kind, which, 1 - way],
            {"lat": lat + inward, "lon": (left, right)[way]},
        )

    def detour_out(group, origin, kind):
        which = group // 2 - 1
        return remote(
            detour.at[kind, which, origin],
            (edge_in, part_in)[kind].at[group, origin],
            detour_send.at[kind, which, origin],
            (edge_recv, part_recv)[kind].at[group, origin],
            {"lat": lat - inward},
        )

    def to_sides(group, kind):
        aside = is_hot & ((group == 2) | (group == 4))
        for way in range(2):
            @pl.when(jnp.logical_not(aside))
            def _():
                (edge_copy, part_copy)[kind](group, way).start()

            @pl.when(aside)
            def _():
                detour_in(group, way, kind).start()

    def pass_aside(group, kind):
        for origin in range(2):
            detour_in(group, 1 - origin, kind).wait_recv()
            detour_out(group, origin, kind).start()

    def relayed(group, kind):
        return True if kind == 0 else group < GROUPS - 1

    def to_tiles(group, kind, act):
        copy = (kv_copy, term_copy)[kind]
        for way in range(2):
            crossing = (lat == routes[way][0]) & relayed(group, kind)

            @pl.when(exists[way] & jnp.logical_not(crossing))
            def _():
                act(copy(group, way, whole))

            @pl.when(crossing)
            def _():
                act(copy(group, way, direct))
                act(pass_copy(group, way, kind))

    def from_tiles(group, kind):
        copy = (kv_copy, term_copy)[kind]
        for origin in range(2):
            @pl.when(exists[origin])
            def _():
                copy(group, 1 - origin, whole).wait_recv()

    def forward(group, kind):
        for way in range(2):
            @pl.when((lat == routes[way][1]) & relayed(group, kind))
            def _():
                pass_copy(group, way, kind).wait_recv()
                relay_copy(group, way, kind).start()

    def start(copy):
        copy.start()

    def wait_send(copy):
        copy.wait_send()

    def send_edges(group):
        for which in range(2):
            for image in range(images):
                def half(start, low):
                    block = near[group, which, image, start : start + 16].astype(jnp.float32)
                    return block[low : low + HALO]

                edge_out[group, 0, which, image] = jnp.concatenate(
                    [half(0, 0), half(32, 0)], axis=0
                ).astype(jnp.bfloat16)
                edge_out[group, 1, which, image] = jnp.concatenate(
                    [half(16, HALO), half(48, HALO)], axis=0
                ).astype(jnp.bfloat16)
        to_sides(group, 0)

    def send_group(group, carry):
        copies = own_copies(group)
        copies[0].wait()
        copies[1].wait()
        to_tiles(group, 0, start)
        copies[2].wait()
        copies[3].wait()

        @pl.when(group < AHEAD)
        def _():
            send_edges(group)

        return carry

    lax.fori_loop(0, GROUPS, send_group, 0)

    for way in range(2):
        @pl.when(jnp.logical_not(exists[way]))
        def _():
            far[:, 2 * way] = jnp.zeros((GROUPS, 2, images, tokens, group_lanes), jnp.bfloat16)
            term_in[:, way] = jnp.zeros((GROUPS, 2, images, tokens, group_lanes), jnp.bfloat16)

    def listed(target):
        found = (
            (lists_ref[0, lat] == target)
            | (lists_ref[1, lat] == target)
            | (lists_ref[2, lat] == target)
        ) & (target >= 0)
        return jnp.where(found, 1, 0)

    def mask(shape, key_axis):
        key = lax.broadcasted_iota(jnp.int32, shape, key_axis)
        query = lax.broadcasted_iota(jnp.int32, shape, 1 - key_axis)
        key_tile = key >> 6
        key_col = key & 31
        edge = query - tokens
        is_own = query < tokens
        from_left = edge < 2 * HALO
        query_col = jnp.where(
            is_own, query & 31, jnp.where(from_left, (edge & 7) - HALO, 32 + (edge & 7))
        )
        query_row = jnp.where(is_own, query >> 5, (edge >> 3) & 1)
        width = jnp.where(query_row == 0, widths_ref[2 * lat], widths_ref[2 * lat + 1])
        active = jnp.where(
            key_tile == 0, listed(lat - 1), jnp.where(key_tile == 1, listed(lat), listed(lat + 1))
        )
        visible = (jnp.abs(query_col - key_col) <= width) & (active == 1) & (edge < 4 * HALO)
        return jnp.where(visible, 0.0, HIDDEN)

    for copy in small_copies:
        copy.wait()
    bias[...] = mask(bias.shape, 0)

    places = [(image, head) for image in range(images) for head in range(group_heads)]

    def from_near(group, which, image, head):
        at = pl.ds(head * HDIM, HDIM)
        edges = [edge_in[group, origin, which, image, :, at] for origin in range(2)]
        rest = jnp.zeros((2 * tokens - seen, HDIM), jnp.bfloat16)
        return jnp.concatenate([near[group, which, image, :, at]] + edges + [rest], axis=0)

    def from_far(group, which, image, head):
        at = pl.ds(head * HDIM, HDIM)
        return jnp.concatenate([far[group, slot, which, image, :, at] for slot in range(3)], axis=0)

    to_log2 = scale * math.log2(math.e)
    seen = tokens + 4 * HALO

    def scores(group):
        tops, sums, balances = [], [], []
        for item, (image, head) in enumerate(places):
            values = from_far(group, 1, image, head)
            raw = nt(from_far(group, 0, image, head), from_near(group, 0, image, head))
            raw = raw * to_log2 + bias[...]
            dp = nt(values, from_near(group, 1, image, head))
            top = jnp.maximum(jnp.max(raw, axis=0, keepdims=True), FLOOR)
            e = jnp.exp2(raw - top)
            slot = group * group_items + item
            exps[slot] = e
            dps[slot] = dp
            mixed[slot] = nn(jnp.transpose(e.astype(jnp.bfloat16))[0:seen], values)
            tops.append(top)
            sums.append(jnp.sum(e, axis=0, keepdims=True))
            balances.append(jnp.sum(e * dp, axis=0, keepdims=True))
        for kind, found in enumerate((tops, sums, balances)):
            rows = found + [jnp.zeros_like(found[0])] * (8 - len(found))
            stats[group, kind] = jnp.concatenate(rows, axis=0)
        for way, moves in enumerate((((0, 0, 8), (32, 8, 8), (64, 16, 16)), ((24, 0, 8), (56, 8, 8), (80, 16, 16)))):
            packed = jnp.zeros((8, HDIM), jnp.float32)
            for kind in range(3):
                for old, new, size in moves:
                    packed = window(stats[group, kind], old, 32 * kind + new, size, packed)
            stats_out[way, group] = packed
        for way in range(2):
            stat_copy(group, way).start()

    def wait_stats(group):
        for way in range(2):
            stat_copy(group, way).wait_recv()

    def combine(group):
        others = []
        for kind in range(3):
            other = jnp.full((8, HDIM), FLOOR if kind == 0 else 0.0, jnp.float32)
            for origin, moves in enumerate((((0, 64, 16), (16, 0, 8), (24, 32, 8)), ((0, 80, 16), (16, 24, 8), (24, 56, 8)))):
                for old, new, size in moves:
                    other = window(stats_in[origin, group], 32 * kind + old, new, size, other)
            others.append(other)
        top, total, balance = (stats[group, kind] for kind in range(3))
        top2, total2, balance2 = others
        high = jnp.maximum(top, top2)
        part = jnp.exp2(top - high)
        part2 = jnp.exp2(top2 - high)
        inverse = 1.0 / jnp.maximum(part * total + part2 * total2, 0.5)
        factor = part * inverse
        factors[group, 0] = factor
        factors[group, 1] = (part * balance + part2 * balance2) * inverse
        columns[group] = jnp.transpose(factor)

    def gradients(group, later):
        for item, (image, head) in enumerate(places):
            at = pl.ds(head * HDIM, HDIM)
            slot = group * group_items + item
            keys = from_far(group, 0, image, head)
            queries, grads = (from_near(group, which, image, head) for which in range(2))
            w = exps[slot] * factors[group, 0, item : item + 1, :]
            ds = w * (dps[slot] - factors[group, 1, item : item + 1, :])
            w = w.astype(jnp.bfloat16)
            ds = ds.astype(jnp.bfloat16)
            dk = nn(ds, queries) * scale
            dv = nn(w, grads)
            att = mixed[slot] * columns[group, 0:seen, item : item + 1]
            dq = nn(jnp.transpose(ds)[0:seen], keys) * scale
            for which, x in enumerate((dk, dv)):
                far_acc[group, which, image, :, at] = x[tokens : 2 * tokens]
                term_out[group, 0, which, image, :, at] = x[0:tokens].astype(jnp.bfloat16)
                term_out[group, 1, which, image, :, at] = x[2 * tokens :].astype(jnp.bfloat16)
            for which, x in enumerate((att, dq)):
                near_acc[group, which, image, :, at] = x[0:tokens]
                for way in range(2):
                    low = tokens + 2 * HALO * way
                    part_out[group, way, which, image, :, at] = x[low : low + 2 * HALO].astype(jnp.bfloat16)
        combine(later)
        to_tiles(group, 1, start)
        to_sides(group, 1)

    def finish(group):
        for way in range(2):
            part_copy(group, way).wait_recv()
        from_tiles(group, 1)
        at = lanes(group)
        for image in range(images):
            for which in range(2):
                acc = near_acc[group, which, image]
                add_l = part_in[group, 0, which, image].astype(jnp.float32)
                add_r = part_in[group, 1, which, image].astype(jnp.float32)
                rows = []
                for r in range(2):
                    here = acc[32 * r : 32 * r + 32]
                    rows.append(here[0:8] + add_l[8 * r : 8 * r + 8])
                    rows.append(here[8:24])
                    rows.append(here[24:32] + add_r[8 * r : 8 * r + 8])
                outs[which, image, :, at] = jnp.concatenate(rows, axis=0).astype(jnp.bfloat16)
            for which in range(2):
                total = far_acc[group, which, image]
                for way in range(2):
                    total = total + term_in[group, way, which, image].astype(jnp.float32)
                outs[2 + which, image, :, at] = total.astype(jnp.bfloat16)

    def step(index, carry):
        @pl.when(index < GROUPS // 2)
        def _():
            forward(2 * index, 0)
            forward(2 * index + 1, 0)

        for group in (2, 4):
            @pl.when(is_detour & (index == group + 1))
            def _():
                pass_aside(group, 0)

        @pl.when(index < GROUPS)
        def _():
            from_tiles(index, 0)
            for origin in range(2):
                edge_copy(index, 1 - origin).wait_recv()

            scores(index)

            @pl.when(index + AHEAD < GROUPS)
            def _():
                send_edges(index + AHEAD)

        @pl.when((index >= BEHIND + 2) & (index < GROUPS + BEHIND))
        def _():
            forward(index - BEHIND - 2, 1)

        @pl.when(index == BEHIND - 1)
        def _():
            wait_stats(0)
            combine(0)

        @pl.when(index >= BEHIND)
        def _():
            group = index - BEHIND
            later = jnp.minimum(group + 1, GROUPS - 1)

            @pl.when(group + 1 < GROUPS)
            def _():
                wait_stats(later)

            gradients(group, later)

        return carry

    lax.fori_loop(0, GROUPS + BEHIND, step, 0)

    @pl.when(is_detour)
    def _():
        for group in (2, 4):
            pass_aside(group, 1)

    def last(group, carry):
        @pl.when(group == 1)
        def _():
            forward(GROUPS - 2, 1)

        finish(group)
        return carry

    lax.fori_loop(0, GROUPS, last, 0)

    def drain(group, carry):
        to_tiles(group, 1, wait_send)
        for way in range(2):
            @pl.when(lat == routes[way][0])
            def _():
                pass_copy(group, way, 0).wait_send()

        for kind in range(2):
            for way in range(2):
                @pl.when((lat == routes[way][1]) & relayed(group, kind))
                def _():
                    relay_copy(group, way, kind).wait_send()
        return carry

    lax.fori_loop(0, GROUPS, drain, 0)
    @pl.when(is_detour)
    def _():
        for kind in range(2):
            for group in (2, 4):
                for origin in range(2):
                    detour_out(group, origin, kind).wait_send()

    for way in range(2):
        for source, sem in (
            (edge_out.at[:, way], edge_send.at[way]),
            (part_out.at[:, way], part_send.at[way]),
            (stats_out.at[way], stat_send.at[way]),
        ):
            remote(source, source, sem, sem, sides[way]).wait_send()
        crossing = lat == routes[way][0]
        for some, here in ((whole, jnp.logical_not(crossing)), (direct, crossing)):
            @pl.when(exists[way] & here)
            def _():
                sent = far.at[:, 1, :, some]
                remote(sent, sent, kv_send.at[way], kv_send.at[way], tiles[way]).wait_send()


def split_kernel(stacked, *refs):
    outs, sem = refs[:4], refs[4]
    copies = [pltpu.make_async_copy(stacked.at[i], outs[i], sem.at[i]) for i in range(4)]
    for copy in copies:
        copy.start()
    for copy in copies:
        copy.wait()


def solution(mesh):
    lon_count = mesh.shape["lon"]
    lat_count = mesh.shape["lat"]

    def on_device(queries, key_states, value_states, out_grad, block_lists, row_widths):
        images, rows, columns, channels = queries.shape
        tokens = rows * columns
        flat = (images, tokens, channels)
        items = images * channels // HDIM
        lanes = channels // GROUPS
        bf16, f32 = jnp.bfloat16, jnp.float32
        hbm_spec = pl.BlockSpec(memory_space=pltpu.HBM)
        vmem_spec = pl.BlockSpec(memory_space=pltpu.VMEM)
        dma = pltpu.SemaphoreType.DMA
        stacked = pl.pallas_call(
            functools.partial(kernel, lon_count, lat_count),
            out_shape=pltpu.VMEM((4,) + flat, bf16),
            in_specs=[hbm_spec] * 6,
            out_specs=vmem_spec,
            scratch_shapes=[
                pltpu.VMEM((GROUPS, 2, images, tokens, lanes), bf16),
                pltpu.VMEM((GROUPS, 2, 2, images, 2 * HALO, lanes), bf16),
                pltpu.VMEM((GROUPS, 3, 2, images, tokens, lanes), bf16),
                pltpu.VMEM((GROUPS, 2, 2, images, 2 * HALO, lanes), bf16),
                pltpu.VMEM((3 * tokens, 2 * tokens), f32),
                pltpu.VMEM((items, 3 * tokens, 2 * tokens), f32),
                pltpu.VMEM((items, 3 * tokens, 2 * tokens), f32),
                pltpu.VMEM((GROUPS, 3, 8, 2 * tokens), f32),
                pltpu.VMEM((2, GROUPS, 8, 2 * tokens), f32),
                pltpu.VMEM((2, GROUPS, 8, 2 * tokens), f32),
                pltpu.VMEM((GROUPS, 2, 8, 2 * tokens), f32),
                pltpu.VMEM((GROUPS, 2 * tokens, 8), f32),
                pltpu.VMEM((items, tokens + 4 * HALO, HDIM), f32),
                pltpu.VMEM((GROUPS, 2, images, tokens, lanes), f32),
                pltpu.VMEM((GROUPS, 2, 2, images, 2 * HALO, lanes), bf16),
                pltpu.VMEM((GROUPS, 2, 2, images, 2 * HALO, lanes), bf16),
                pltpu.VMEM((GROUPS, 2, images, tokens, lanes), f32),
                pltpu.VMEM((GROUPS, 2, 2, images, tokens, lanes), bf16),
                pltpu.VMEM((GROUPS, 2, 2, images, tokens, lanes), bf16),
                pltpu.VMEM((2, GROUPS, 2, images - images // 2, tokens, lanes), bf16),
                pltpu.VMEM((2, DETOURS, 2, 2, images, 2 * HALO, lanes), bf16),
                pltpu.SMEM(block_lists.shape[::-1], jnp.int32),
                pltpu.SMEM(row_widths.shape, jnp.int32),
                dma((2,)),
                dma((GROUPS, 4)),
                dma((2,)),
                dma((GROUPS, 2)),
                dma((2,)),
                dma((GROUPS, 2)),
                dma((2,)),
                dma((GROUPS, 2)),
                dma((2,)),
                dma((GROUPS, 2)),
                dma((GROUPS, 2)),
                dma((GROUPS, 2)),
                dma((GROUPS, 2)),
                dma((GROUPS, 2)),
                dma((GROUPS, 2)),
                dma((2, DETOURS, 2)),
                dma((2, DETOURS, 2)),
            ],
            compiler_params=pltpu.CompilerParams(
                collective_id=0, has_side_effects=True, vmem_limit_bytes=60 * 1024 * 1024
            ),
            cost_estimate=pl.CostEstimate(
                flops=12 * items * 192 * 128 * 128,
                bytes_accessed=8 * images * tokens * channels * 2,
                transcendentals=items * 192 * 128,
            ),
        )(
            block_lists.T,
            row_widths,
            queries.reshape(flat),
            key_states.reshape(flat),
            value_states.reshape(flat),
            out_grad.reshape(flat),
        )
        results = pl.pallas_call(
            split_kernel,
            out_shape=[jax.ShapeDtypeStruct(flat, bf16)] * 4,
            in_specs=[pl.BlockSpec(memory_space=pl.ANY)],
            out_specs=[hbm_spec] * 4,
            scratch_shapes=[dma((4,))],
            compiler_params=pltpu.CompilerParams(vmem_limit_bytes=8 * 1024 * 1024),
        )(stacked)
        return tuple(x.reshape(queries.shape) for x in results)

    split = P(None, "lat", "lon", None)
    return jax.shard_map(
        on_device,
        mesh=mesh,
        in_specs=(split, split, split, split, P(), P()),
        out_specs=(split, split, split, split),
        check_vma=False,
    )
```

```python
import functools
import math

import jax
import jax.numpy as jnp
from jax import lax
from jax.experimental import pallas as pl
from jax.experimental.pallas import tpu as pltpu
from jax.sharding import PartitionSpec as P

MESH = pl.DeviceIdType.MESH
HALO = 8
HDIM = 128
GROUPS = 8
AHEAD = 5
BEHIND = 5
DETOURS = 2
HIDDEN = -1e30
FLOOR = -1e29


def nt(a, b):
    return lax.dot_general(a, b, (((1,), (1,)), ((), ())), preferred_element_type=jnp.float32)


def nn(a, b):
    return jnp.dot(a, b, preferred_element_type=jnp.float32)


def window(x, old, new, size, rest):
    lane = lax.broadcasted_iota(jnp.int32, x.shape, 1)
    shifted = x if old == new else pltpu.roll(x, (new - old) % HDIM, 1)
    return jnp.where((lane >= new) & (lane < new + size), shifted, rest)


def kernel(
    lon_count,
    lat_count,
    lists_hbm,
    widths_hbm,
    q_hbm,
    k_hbm,
    v_hbm,
    g_hbm,
    outs,
    near,
    edge_in,
    far,
    edge_out,
    bias,
    exps,
    dps,
    stats,
    stats_out,
    stats_in,
    factors,
    columns,
    mixed,
    near_acc,
    part_out,
    part_in,
    far_acc,
    term_out,
    term_in,
    relay,
    detour,
    lists_ref,
    widths_ref,
    small_sem,
    own_sem,
    kv_send,
    kv_recv,
    edge_send,
    edge_recv,
    stat_send,
    stat_recv,
    part_send,
    part_recv,
    term_send,
    term_recv,
    pass_send,
    pass_recv,
    relay_send,
    detour_send,
    detour_recv,
):
    lon = lax.axis_index("lon")
    lat = lax.axis_index("lat")
    left = lax.rem(lon + lon_count - 1, lon_count)
    right = lax.rem(lon + 1, lon_count)
    has_above = lat > 0
    has_below = lat < lat_count - 1
    middle = lat_count // 2
    beside = lon + 1 - 2 * lax.rem(lon, 2)
    is_middle = (lat == middle - 1) | (lat == middle)
    routes = ((middle, 0, middle - 1), (middle - 1, lat_count - 1, middle))
    planes = middle // 2
    plane = lax.rem(lat // 2, planes)
    is_hot = (plane == 0) | (plane == planes - 1)
    is_detour = (plane == 1) | (plane == planes - 2)
    inward = jnp.where(plane < planes // 2, 2, -2)
    images, tokens, channels = q_hbm.shape
    heads = channels // HDIM
    group_heads = heads // GROUPS
    group_items = images * group_heads
    group_lanes = group_heads * HDIM
    scale = HDIM ** -0.5
    half = images // 2
    whole, direct, passing = slice(0, images), slice(0, half), slice(half, images)

    sides = ({"lon": left}, {"lon": right})
    tiles = ({"lat": lat - 1}, {"lat": lat + 1})
    exists = (has_above, has_below)

    def lanes(group):
        start = group * group_lanes
        return pl.ds(start if isinstance(group, int) else pl.multiple_of(start, HDIM), group_lanes)

    def own_copies(group):
        targets = (far.at[group, 1, 0], far.at[group, 1, 1], near.at[group, 0], near.at[group, 1])
        return [
            pltpu.make_async_copy(source.at[:, :, lanes(group)], target, own_sem.at[group, which])
            for which, (source, target) in enumerate(zip((k_hbm, v_hbm, q_hbm, g_hbm), targets))
        ]

    def fetch(group, carry):
        for copy in own_copies(group):
            copy.start()
        return carry

    fetch(0, 0)
    small_copies = [
        pltpu.make_async_copy(lists_hbm, lists_ref, small_sem.at[0]),
        pltpu.make_async_copy(widths_hbm, widths_ref, small_sem.at[1]),
    ]
    for copy in small_copies:
        copy.start()

    lax.fori_loop(1, GROUPS, fetch, 0)

    barrier = pltpu.get_barrier_semaphore()
    for side in sides:
        pl.semaphore_signal(barrier, inc=1, device_id=side, device_id_type=MESH)
    for there, tile in zip(exists, tiles):
        @pl.when(there)
        def _():
            pl.semaphore_signal(barrier, inc=1, device_id=tile, device_id_type=MESH)
    for route in routes:
        @pl.when(lat == route[1])
        def _():
            pl.semaphore_signal(barrier, inc=1, device_id={"lat": route[0], "lon": beside}, device_id_type=MESH)
    @pl.when(is_detour)
    def _():
        for side in (left, right):
            pl.semaphore_signal(
                barrier, inc=1, device_id={"lat": lat - inward, "lon": side}, device_id_type=MESH
            )

    pl.semaphore_wait(
        barrier,
        2 + jnp.where(has_above, 1, 0) + jnp.where(has_below, 1, 0) + jnp.where(is_middle, 1, 0)
        + jnp.where(is_hot, 2, 0),
    )

    def remote(source, target, send, recv, device):
        return pltpu.make_async_remote_copy(
            src_ref=source, dst_ref=target, send_sem=send, recv_sem=recv, device_id=device, device_id_type=MESH
        )

    def kv_copy(group, way, some):
        return remote(
            far.at[group, 1, :, some],
            far.at[group, 2 - 2 * way, :, some],
            kv_send.at[way],
            kv_recv.at[group, 1 - way],
            tiles[way],
        )

    def edge_copy(group, way):
        return remote(
            edge_out.at[group, way],
            edge_in.at[group, 1 - way],
            edge_send.at[way],
            edge_recv.at[group, 1 - way],
            sides[way],
        )

    def stat_copy(group, way):
        return remote(
            stats_out.at[way, group],
            stats_in.at[1 - way, group],
            stat_send.at[way],
            stat_recv.at[group, 1 - way],
            sides[way],
        )

    def part_copy(group, way):
        return remote(
            part_out.at[group, way],
            part_in.at[group, 1 - way],
            part_send.at[way],
            part_recv.at[group, 1 - way],
            sides[way],
        )

    def term_copy(group, way, some):
        return remote(
            term_out.at[group, way, :, some],
            term_in.at[group, 1 - way, :, some],
            term_send.at[group, way],
            term_recv.at[group, 1 - way],
            tiles[way],
        )

    def pass_copy(group, way, kind):
        return remote(
            far.at[group, 1, :, passing] if kind == 0 else term_out.at[group, way, :, passing],
            relay.at[kind, group],
            pass_send.at[group, kind],
            pass_recv.at[group, kind],
            {"lat": routes[way][1], "lon": beside},
        )

    def relay_copy(group, way, kind):
        return remote(
            relay.at[kind, group],
            far.at[group, 2 - 2 * way, :, passing]
            if kind == 0
            else term_in.at[group, 1 - way, :, passing],
            relay_send.at[group, kind],
            (kv_recv if kind == 0 else term_recv).at[group, 1 - way],
            {"lat": routes[way][2], "lon": beside},
        )

    def detour_in(group, way, kind):
        which = group // 2 - 1
        return remote(
            (edge_out, part_out)[kind].at[group, way],
            detour.at[kind, which, 1 - way],
            (edge_send, part_send)[kind].at[way],
            detour_recv.at[kind, which, 1 - way],
            {"lat": lat + inward, "lon": (left, right)[way]},
        )

    def detour_out(group, origin, kind):
        which = group // 2 - 1
        return remote(
            detour.at[kind, which, origin],
            (edge_in, part_in)[kind].at[group, origin],
            detour_send.at[kind, which, origin],
            (edge_recv, part_recv)[kind].at[group, origin],
            {"lat": lat - inward},
        )

    def to_sides(group, kind):
        aside = is_hot & ((group == 2) | (group == 4))
        for way in range(2):
            @pl.when(jnp.logical_not(aside))
            def _():
                (edge_copy, part_copy)[kind](group, way).start()

            @pl.when(aside)
            def _():
                detour_in(group, way, kind).start()

    def pass_aside(group, kind):
        for origin in range(2):
            detour_in(group, 1 - origin, kind).wait_recv()
            detour_out(group, origin, kind).start()

    def relayed(group, kind):
        return True if kind == 0 else group < GROUPS - 1

    def to_tiles(group, kind, act):
        copy = (kv_copy, term_copy)[kind]
        for way in range(2):
            crossing = (lat == routes[way][0]) & relayed(group, kind)

            @pl.when(exists[way] & jnp.logical_not(crossing))
            def _():
                act(copy(group, way, whole))

            @pl.when(crossing)
            def _():
                act(copy(group, way, direct))
                act(pass_copy(group, way, kind))

    def from_tiles(group, kind):
        copy = (kv_copy, term_copy)[kind]
        for origin in range(2):
            @pl.when(exists[origin])
            def _():
                copy(group, 1 - origin, whole).wait_recv()

    def forward(group, kind):
        for way in range(2):
            @pl.when((lat == routes[way][1]) & relayed(group, kind))
            def _():
                pass_copy(group, way, kind).wait_recv()
                relay_copy(group, way, kind).start()

    def start(copy):
        copy.start()

    def wait_send(copy):
        copy.wait_send()

    def send_edges(group):
        for which in range(2):
            for image in range(images):
                def half(start, low):
                    block = near[group, which, image, start : start + 16].astype(jnp.float32)
                    return block[low : low + HALO]

                edge_out[group, 0, which, image] = jnp.concatenate(
                    [half(0, 0), half(32, 0)], axis=0
                ).astype(jnp.bfloat16)
                edge_out[group, 1, which, image] = jnp.concatenate(
                    [half(16, HALO), half(48, HALO)], axis=0
                ).astype(jnp.bfloat16)
        to_sides(group, 0)

    def send_group(group, carry):
        copies = own_copies(group)
        copies[0].wait()
        copies[1].wait()
        to_tiles(group, 0, start)
        copies[2].wait()
        copies[3].wait()

        @pl.when(group < AHEAD)
        def _():
            send_edges(group)

        return carry

    lax.fori_loop(0, GROUPS, send_group, 0)

    for way in range(2):
        @pl.when(jnp.logical_not(exists[way]))
        def _():
            far[:, 2 * way] = jnp.zeros((GROUPS, 2, images, tokens, group_lanes), jnp.bfloat16)
            term_in[:, way] = jnp.zeros((GROUPS, 2, images, tokens, group_lanes), jnp.bfloat16)

    def listed(target):
        found = (
            (lists_ref[0, lat] == target)
            | (lists_ref[1, lat] == target)
            | (lists_ref[2, lat] == target)
        ) & (target >= 0)
        return jnp.where(found, 1, 0)

    def mask(shape, key_axis):
        key = lax.broadcasted_iota(jnp.int32, shape, key_axis)
        query = lax.broadcasted_iota(jnp.int32, shape, 1 - key_axis)
        key_tile = key >> 6
        key_col = key & 31
        edge = query - tokens
        is_own = query < tokens
        from_left = edge < 2 * HALO
        query_col = jnp.where(
            is_own, query & 31, jnp.where(from_left, (edge & 7) - HALO, 32 + (edge & 7))
        )
        query_row = jnp.where(is_own, query >> 5, (edge >> 3) & 1)
        width = jnp.where(query_row == 0, widths_ref[2 * lat], widths_ref[2 * lat + 1])
        active = jnp.where(
            key_tile == 0, listed(lat - 1), jnp.where(key_tile == 1, listed(lat), listed(lat + 1))
        )
        visible = (jnp.abs(query_col - key_col) <= width) & (active == 1) & (edge < 4 * HALO)
        return jnp.where(visible, 0.0, HIDDEN)

    for copy in small_copies:
        copy.wait()
    bias[...] = mask(bias.shape, 0)

    places = [(image, head) for image in range(images) for head in range(group_heads)]

    def from_near(group, which, image, head):
        at = pl.ds(head * HDIM, HDIM)
        edges = [edge_in[group, origin, which, image, :, at] for origin in range(2)]
        rest = jnp.zeros((2 * tokens - seen, HDIM), jnp.bfloat16)
        return jnp.concatenate([near[group, which, image, :, at]] + edges + [rest], axis=0)

    def from_far(group, which, image, head):
        at = pl.ds(head * HDIM, HDIM)
        return jnp.concatenate([far[group, slot, which, image, :, at] for slot in range(3)], axis=0)

    to_log2 = scale * math.log2(math.e)
    seen = tokens + 4 * HALO

    def scores(group):
        tops, sums, balances = [], [], []
        for item, (image, head) in enumerate(places):
            values = from_far(group, 1, image, head)
            raw = nt(from_far(group, 0, image, head), from_near(group, 0, image, head))
            raw = raw * to_log2 + bias[...]
            dp = nt(values, from_near(group, 1, image, head))
            top = jnp.maximum(jnp.max(raw, axis=0, keepdims=True), FLOOR)
            e = jnp.exp2(raw - top)
            slot = group * group_items + item
            exps[slot] = e
            dps[slot] = dp
            mixed[slot] = nn(jnp.transpose(e.astype(jnp.bfloat16))[0:seen], values)
            tops.append(top)
            sums.append(jnp.sum(e, axis=0, keepdims=True))
            balances.append(jnp.sum(e * dp, axis=0, keepdims=True))
        for kind, found in enumerate((tops, sums, balances)):
            rows = found + [jnp.zeros_like(found[0])] * (8 - len(found))
            stats[group, kind] = jnp.concatenate(rows, axis=0)
        for way, moves in enumerate((((0, 0, 8), (32, 8, 8), (64, 16, 16)), ((24, 0, 8), (56, 8, 8), (80, 16, 16)))):
            packed = jnp.zeros((8, HDIM), jnp.float32)
            for kind in range(3):
                for old, new, size in moves:
                    packed = window(stats[group, kind], old, 32 * kind + new, size, packed)
            stats_out[way, group] = packed
        for way in range(2):
            stat_copy(group, way).start()

    def wait_stats(group):
        for way in range(2):
            stat_copy(group, way).wait_recv()

    def combine(group):
        others = []
        for kind in range(3):
            other = jnp.full((8, HDIM), FLOOR if kind == 0 else 0.0, jnp.float32)
            for origin, moves in enumerate((((0, 64, 16), (16, 0, 8), (24, 32, 8)), ((0, 80, 16), (16, 24, 8), (24, 56, 8)))):
                for old, new, size in moves:
                    other = window(stats_in[origin, group], 32 * kind + old, new, size, other)
            others.append(other)
        top, total, balance = (stats[group, kind] for kind in range(3))
        top2, total2, balance2 = others
        high = jnp.maximum(top, top2)
        part = jnp.exp2(top - high)
        part2 = jnp.exp2(top2 - high)
        inverse = 1.0 / jnp.maximum(part * total + part2 * total2, 0.5)
        factor = part * inverse
        factors[group, 0] = factor
        factors[group, 1] = (part * balance + part2 * balance2) * inverse
        columns[group] = jnp.transpose(factor)

    def gradients(group):
        for item, (image, head) in enumerate(places):
            at = pl.ds(head * HDIM, HDIM)
            slot = group * group_items + item
            keys = from_far(group, 0, image, head)
            queries, grads = (from_near(group, which, image, head) for which in range(2))
            w = exps[slot] * factors[group, 0, item : item + 1, :]
            ds = w * (dps[slot] - factors[group, 1, item : item + 1, :])
            w = w.astype(jnp.bfloat16)
            ds = ds.astype(jnp.bfloat16)
            dk = nn(ds, queries) * scale
            dv = nn(w, grads)
            att = mixed[slot] * columns[group, 0:seen, item : item + 1]
            dq = nn(jnp.transpose(ds)[0:seen], keys) * scale
            for which, x in enumerate((dk, dv)):
                far_acc[group, which, image, :, at] = x[tokens : 2 * tokens]
                term_out[group, 0, which, image, :, at] = x[0:tokens].astype(jnp.bfloat16)
                term_out[group, 1, which, image, :, at] = x[2 * tokens :].astype(jnp.bfloat16)
            for which, x in enumerate((att, dq)):
                near_acc[group, which, image, :, at] = x[0:tokens]
                for way in range(2):
                    low = tokens + 2 * HALO * way
                    part_out[group, way, which, image, :, at] = x[low : low + 2 * HALO].astype(jnp.bfloat16)
        to_tiles(group, 1, start)
        to_sides(group, 1)

    def finish(group):
        for way in range(2):
            part_copy(group, way).wait_recv()
        from_tiles(group, 1)
        at = lanes(group)
        for image in range(images):
            for which in range(2):
                acc = near_acc[group, which, image]
                add_l = part_in[group, 0, which, image].astype(jnp.float32)
                add_r = part_in[group, 1, which, image].astype(jnp.float32)
                rows = []
                for r in range(2):
                    here = acc[32 * r : 32 * r + 32]
                    rows.append(here[0:8] + add_l[8 * r : 8 * r + 8])
                    rows.append(here[8:24])
                    rows.append(here[24:32] + add_r[8 * r : 8 * r + 8])
                outs[which, image, :, at] = jnp.concatenate(rows, axis=0).astype(jnp.bfloat16)
            for which in range(2):
                total = far_acc[group, which, image]
                for way in range(2):
                    total = total + term_in[group, way, which, image].astype(jnp.float32)
                outs[2 + which, image, :, at] = total.astype(jnp.bfloat16)

    def step(index, carry):
        @pl.when(index < GROUPS // 2)
        def _():
            forward(2 * index, 0)
            forward(2 * index + 1, 0)

        for group in (2, 4):
            @pl.when(is_detour & (index == group + 1))
            def _():
                pass_aside(group, 0)

        @pl.when(index < GROUPS)
        def _():
            from_tiles(index, 0)
            for origin in range(2):
                edge_copy(index, 1 - origin).wait_recv()

            scores(index)

            @pl.when(index + AHEAD < GROUPS)
            def _():
                send_edges(index + AHEAD)

        @pl.when((index >= BEHIND + 2) & (index < GROUPS + BEHIND))
        def _():
            forward(index - BEHIND - 2, 1)

        @pl.when(index >= BEHIND)
        def _():
            wait_stats(index - BEHIND)
            combine(index - BEHIND)
            gradients(index - BEHIND)

        return carry

    lax.fori_loop(0, GROUPS + BEHIND, step, 0)

    @pl.when(is_detour)
    def _():
        for group in (2, 4):
            pass_aside(group, 1)

    def last(group, carry):
        @pl.when(group == 1)
        def _():
            forward(GROUPS - 2, 1)

        finish(group)
        return carry

    lax.fori_loop(0, GROUPS, last, 0)

    def drain(group, carry):
        to_tiles(group, 1, wait_send)
        for way in range(2):
            @pl.when(lat == routes[way][0])
            def _():
                pass_copy(group, way, 0).wait_send()

        for kind in range(2):
            for way in range(2):
                @pl.when((lat == routes[way][1]) & relayed(group, kind))
                def _():
                    relay_copy(group, way, kind).wait_send()
        return carry

    lax.fori_loop(0, GROUPS, drain, 0)
    @pl.when(is_detour)
    def _():
        for kind in range(2):
            for group in (2, 4):
                for origin in range(2):
                    detour_out(group, origin, kind).wait_send()

    for way in range(2):
        for source, sem in (
            (edge_out.at[:, way], edge_send.at[way]),
            (part_out.at[:, way], part_send.at[way]),
            (stats_out.at[way], stat_send.at[way]),
        ):
            remote(source, source, sem, sem, sides[way]).wait_send()
        crossing = lat == routes[way][0]
        for some, here in ((whole, jnp.logical_not(crossing)), (direct, crossing)):
            @pl.when(exists[way] & here)
            def _():
                sent = far.at[:, 1, :, some]
                remote(sent, sent, kv_send.at[way], kv_send.at[way], tiles[way]).wait_send()


def split_kernel(stacked, *refs):
    outs, sem = refs[:4], refs[4]
    copies = [pltpu.make_async_copy(stacked.at[i], outs[i], sem.at[i]) for i in range(4)]
    for copy in copies:
        copy.start()
    for copy in copies:
        copy.wait()


def solution(mesh):
    lon_count = mesh.shape["lon"]
    lat_count = mesh.shape["lat"]

    def on_device(queries, key_states, value_states, out_grad, block_lists, row_widths):
        images, rows, columns, channels = queries.shape
        tokens = rows * columns
        flat = (images, tokens, channels)
        items = images * channels // HDIM
        lanes = channels // GROUPS
        bf16, f32 = jnp.bfloat16, jnp.float32
        hbm_spec = pl.BlockSpec(memory_space=pltpu.HBM)
        vmem_spec = pl.BlockSpec(memory_space=pltpu.VMEM)
        dma = pltpu.SemaphoreType.DMA
        stacked = pl.pallas_call(
            functools.partial(kernel, lon_count, lat_count),
            out_shape=pltpu.VMEM((4,) + flat, bf16),
            in_specs=[hbm_spec] * 6,
            out_specs=vmem_spec,
            scratch_shapes=[
                pltpu.VMEM((GROUPS, 2, images, tokens, lanes), bf16),
                pltpu.VMEM((GROUPS, 2, 2, images, 2 * HALO, lanes), bf16),
                pltpu.VMEM((GROUPS, 3, 2, images, tokens, lanes), bf16),
                pltpu.VMEM((GROUPS, 2, 2, images, 2 * HALO, lanes), bf16),
                pltpu.VMEM((3 * tokens, 2 * tokens), f32),
                pltpu.VMEM((items, 3 * tokens, 2 * tokens), f32),
                pltpu.VMEM((items, 3 * tokens, 2 * tokens), f32),
                pltpu.VMEM((GROUPS, 3, 8, 2 * tokens), f32),
                pltpu.VMEM((2, GROUPS, 8, 2 * tokens), f32),
                pltpu.VMEM((2, GROUPS, 8, 2 * tokens), f32),
                pltpu.VMEM((GROUPS, 2, 8, 2 * tokens), f32),
                pltpu.VMEM((GROUPS, 2 * tokens, 8), f32),
                pltpu.VMEM((items, tokens + 4 * HALO, HDIM), f32),
                pltpu.VMEM((GROUPS, 2, images, tokens, lanes), f32),
                pltpu.VMEM((GROUPS, 2, 2, images, 2 * HALO, lanes), bf16),
                pltpu.VMEM((GROUPS, 2, 2, images, 2 * HALO, lanes), bf16),
                pltpu.VMEM((GROUPS, 2, images, tokens, lanes), f32),
                pltpu.VMEM((GROUPS, 2, 2, images, tokens, lanes), bf16),
                pltpu.VMEM((GROUPS, 2, 2, images, tokens, lanes), bf16),
                pltpu.VMEM((2, GROUPS, 2, images - images // 2, tokens, lanes), bf16),
                pltpu.VMEM((2, DETOURS, 2, 2, images, 2 * HALO, lanes), bf16),
                pltpu.SMEM(block_lists.shape[::-1], jnp.int32),
                pltpu.SMEM(row_widths.shape, jnp.int32),
                dma((2,)),
                dma((GROUPS, 4)),
                dma((2,)),
                dma((GROUPS, 2)),
                dma((2,)),
                dma((GROUPS, 2)),
                dma((2,)),
                dma((GROUPS, 2)),
                dma((2,)),
                dma((GROUPS, 2)),
                dma((GROUPS, 2)),
                dma((GROUPS, 2)),
                dma((GROUPS, 2)),
                dma((GROUPS, 2)),
                dma((GROUPS, 2)),
                dma((2, DETOURS, 2)),
                dma((2, DETOURS, 2)),
            ],
            compiler_params=pltpu.CompilerParams(
                collective_id=0, has_side_effects=True, vmem_limit_bytes=60 * 1024 * 1024
            ),
            cost_estimate=pl.CostEstimate(
                flops=12 * items * 192 * 128 * 128,
                bytes_accessed=8 * images * tokens * channels * 2,
                transcendentals=items * 192 * 128,
            ),
        )(
            block_lists.T,
            row_widths,
            queries.reshape(flat),
            key_states.reshape(flat),
            value_states.reshape(flat),
            out_grad.reshape(flat),
        )
        results = pl.pallas_call(
            split_kernel,
            out_shape=[jax.ShapeDtypeStruct(flat, bf16)] * 4,
            in_specs=[pl.BlockSpec(memory_space=pl.ANY)],
            out_specs=[hbm_spec] * 4,
            scratch_shapes=[dma((4,))],
            compiler_params=pltpu.CompilerParams(vmem_limit_bytes=8 * 1024 * 1024),
        )(stacked)
        return tuple(x.reshape(queries.shape) for x in results)

    split = P(None, "lat", "lon", None)
    return jax.shard_map(
        on_device,
        mesh=mesh,
        in_specs=(split, split, split, split, P(), P()),
        out_specs=(split, split, split, split),
        check_vma=False,
    )
```

```python
import functools
import math

import jax
import jax.numpy as jnp
from jax import lax
from jax.experimental import pallas as pl
from jax.experimental.pallas import tpu as pltpu
from jax.sharding import PartitionSpec as P

MESH = pl.DeviceIdType.MESH
HALO = 8
HDIM = 128
GROUPS = 8
AHEAD = 5
BEHIND = 5
DETOURS = 2
HIDDEN = -1e30
FLOOR = -1e29


def nt(a, b):
    return lax.dot_general(a, b, (((1,), (1,)), ((), ())), preferred_element_type=jnp.float32)


def nn(a, b):
    return jnp.dot(a, b, preferred_element_type=jnp.float32)


def window(x, old, new, size, rest):
    lane = lax.broadcasted_iota(jnp.int32, x.shape, 1)
    shifted = x if old == new else pltpu.roll(x, (new - old) % HDIM, 1)
    return jnp.where((lane >= new) & (lane < new + size), shifted, rest)


def kernel(
    lon_count,
    lat_count,
    lists_hbm,
    widths_hbm,
    q_hbm,
    k_hbm,
    v_hbm,
    g_hbm,
    outs,
    near,
    edge_in,
    far,
    edge_out,
    bias,
    exps,
    dps,
    stats,
    stats_out,
    stats_in,
    factors,
    columns,
    mixed,
    near_acc,
    part_out,
    part_in,
    far_acc,
    term_out,
    term_in,
    relay,
    detour,
    lists_ref,
    widths_ref,
    small_sem,
    own_sem,
    kv_send,
    kv_recv,
    edge_send,
    edge_recv,
    stat_send,
    stat_recv,
    part_send,
    part_recv,
    term_send,
    term_recv,
    pass_send,
    pass_recv,
    relay_send,
    detour_send,
    detour_recv,
):
    lon = lax.axis_index("lon")
    lat = lax.axis_index("lat")
    left = lax.rem(lon + lon_count - 1, lon_count)
    right = lax.rem(lon + 1, lon_count)
    has_above = lat > 0
    has_below = lat < lat_count - 1
    middle = lat_count // 2
    beside = lon + 1 - 2 * lax.rem(lon, 2)
    is_middle = (lat == middle - 1) | (lat == middle)
    routes = ((middle, 0, middle - 1), (middle - 1, lat_count - 1, middle))
    planes = middle // 2
    plane = lax.rem(lat // 2, planes)
    is_hot = (plane == 0) | (plane == planes - 1)
    is_detour = (plane == 1) | (plane == planes - 2)
    inward = jnp.where(plane < planes // 2, 2, -2)
    images, tokens, channels = q_hbm.shape
    heads = channels // HDIM
    group_heads = heads // GROUPS
    group_items = images * group_heads
    group_lanes = group_heads * HDIM
    scale = HDIM ** -0.5
    half = images // 2
    whole, direct, passing = slice(0, images), slice(0, half), slice(half, images)

    sides = ({"lon": left}, {"lon": right})
    tiles = ({"lat": lat - 1}, {"lat": lat + 1})
    exists = (has_above, has_below)

    def lanes(group):
        start = group * group_lanes
        return pl.ds(start if isinstance(group, int) else pl.multiple_of(start, HDIM), group_lanes)

    def own_copies(group):
        targets = (far.at[group, 1, 0], far.at[group, 1, 1], near.at[group, 0], near.at[group, 1])
        return [
            pltpu.make_async_copy(source.at[:, :, lanes(group)], target, own_sem.at[group, which])
            for which, (source, target) in enumerate(zip((k_hbm, v_hbm, q_hbm, g_hbm), targets))
        ]

    def fetch(group, carry):
        for copy in own_copies(group):
            copy.start()
        return carry

    fetch(0, 0)
    small_copies = [
        pltpu.make_async_copy(lists_hbm, lists_ref, small_sem.at[0]),
        pltpu.make_async_copy(widths_hbm, widths_ref, small_sem.at[1]),
    ]
    for copy in small_copies:
        copy.start()

    lax.fori_loop(1, GROUPS, fetch, 0)

    barrier = pltpu.get_barrier_semaphore()
    for side in sides:
        pl.semaphore_signal(barrier, inc=1, device_id=side, device_id_type=MESH)
    for there, tile in zip(exists, tiles):
        @pl.when(there)
        def _():
            pl.semaphore_signal(barrier, inc=1, device_id=tile, device_id_type=MESH)
    for route in routes:
        @pl.when(lat == route[1])
        def _():
            pl.semaphore_signal(barrier, inc=1, device_id={"lat": route[0], "lon": beside}, device_id_type=MESH)
    @pl.when(is_detour)
    def _():
        for side in (left, right):
            pl.semaphore_signal(
                barrier, inc=1, device_id={"lat": lat - inward, "lon": side}, device_id_type=MESH
            )

    pl.semaphore_wait(
        barrier,
        2 + jnp.where(has_above, 1, 0) + jnp.where(has_below, 1, 0) + jnp.where(is_middle, 1, 0)
        + jnp.where(is_hot, 2, 0),
    )

    def remote(source, target, send, recv, device):
        return pltpu.make_async_remote_copy(
            src_ref=source, dst_ref=target, send_sem=send, recv_sem=recv, device_id=device, device_id_type=MESH
        )

    def kv_copy(group, way, some):
        return remote(
            far.at[group, 1, :, some],
            far.at[group, 2 - 2 * way, :, some],
            kv_send.at[way],
            kv_recv.at[group, 1 - way],
            tiles[way],
        )

    def edge_copy(group, way):
        return remote(
            edge_out.at[group, way],
            edge_in.at[group, 1 - way],
            edge_send.at[way],
            edge_recv.at[group, 1 - way],
            sides[way],
        )

    def stat_copy(group, way):
        return remote(
            stats_out.at[way, group],
            stats_in.at[1 - way, group],
            stat_send.at[way],
            stat_recv.at[group, 1 - way],
            sides[way],
        )

    def part_copy(group, way):
        return remote(
            part_out.at[group, way],
            part_in.at[group, 1 - way],
            part_send.at[way],
            part_recv.at[group, 1 - way],
            sides[way],
        )

    def term_copy(group, way, some):
        return remote(
            term_out.at[group, way, :, some],
            term_in.at[group, 1 - way, :, some],
            term_send.at[group, way],
            term_recv.at[group, 1 - way],
            tiles[way],
        )

    def pass_copy(group, way, kind):
        return remote(
            far.at[group, 1, :, passing] if kind == 0 else term_out.at[group, way, :, passing],
            relay.at[kind, group],
            pass_send.at[group, kind],
            pass_recv.at[group, kind],
            {"lat": routes[way][1], "lon": beside},
        )

    def relay_copy(group, way, kind):
        return remote(
            relay.at[kind, group],
            far.at[group, 2 - 2 * way, :, passing]
            if kind == 0
            else term_in.at[group, 1 - way, :, passing],
            relay_send.at[group, kind],
            (kv_recv if kind == 0 else term_recv).at[group, 1 - way],
            {"lat": routes[way][2], "lon": beside},
        )

    def detour_in(group, way, kind):
        which = group // 2 - 1
        return remote(
            (edge_out, part_out)[kind].at[group, way],
            detour.at[kind, which, 1 - way],
            (edge_send, part_send)[kind].at[way],
            detour_recv.at[kind, which, 1 - way],
            {"lat": lat + inward, "lon": (left, right)[way]},
        )

    def detour_out(group, origin, kind):
        which = group // 2 - 1
        return remote(
            detour.at[kind, which, origin],
            (edge_in, part_in)[kind].at[group, origin],
            detour_send.at[kind, which, origin],
            (edge_recv, part_recv)[kind].at[group, origin],
            {"lat": lat - inward},
        )

    def to_sides(group, kind):
        aside = is_hot & ((group == 2) | (group == 4))
        for way in range(2):
            @pl.when(jnp.logical_not(aside))
            def _():
                (edge_copy, part_copy)[kind](group, way).start()

            @pl.when(aside)
            def _():
                detour_in(group, way, kind).start()

    def pass_aside(group, kind):
        for origin in range(2):
            detour_in(group, 1 - origin, kind).wait_recv()
            detour_out(group, origin, kind).start()

    def relayed(group, kind):
        return True if kind == 0 else group < GROUPS - 1

    def to_tiles(group, kind, act):
        copy = (kv_copy, term_copy)[kind]
        for way in range(2):
            crossing = (lat == routes[way][0]) & relayed(group, kind)

            @pl.when(exists[way] & jnp.logical_not(crossing))
            def _():
                act(copy(group, way, whole))

            @pl.when(crossing)
            def _():
                act(copy(group, way, direct))
                act(pass_copy(group, way, kind))

    def from_tiles(group, kind):
        copy = (kv_copy, term_copy)[kind]
        for origin in range(2):
            @pl.when(exists[origin])
            def _():
                copy(group, 1 - origin, whole).wait_recv()

    def forward(group, kind):
        for way in range(2):
            @pl.when((lat == routes[way][1]) & relayed(group, kind))
            def _():
                pass_copy(group, way, kind).wait_recv()
                relay_copy(group, way, kind).start()

    def start(copy):
        copy.start()

    def wait_send(copy):
        copy.wait_send()

    def send_edges(group):
        for which in range(2):
            for image in range(images):
                def half(start, low):
                    block = near[group, which, image, start : start + 16].astype(jnp.float32)
                    return block[low : low + HALO]

                edge_out[group, 0, which, image] = jnp.concatenate(
                    [half(0, 0), half(32, 0)], axis=0
                ).astype(jnp.bfloat16)
                edge_out[group, 1, which, image] = jnp.concatenate(
                    [half(16, HALO), half(48, HALO)], axis=0
                ).astype(jnp.bfloat16)
        to_sides(group, 0)

    def send_group(group, carry):
        copies = own_copies(group)
        copies[0].wait()
        copies[1].wait()
        to_tiles(group, 0, start)
        copies[2].wait()
        copies[3].wait()

        @pl.when(group < AHEAD)
        def _():
            send_edges(group)

        return carry

    lax.fori_loop(0, GROUPS, send_group, 0)

    for way in range(2):
        @pl.when(jnp.logical_not(exists[way]))
        def _():
            far[:, 2 * way] = jnp.zeros((GROUPS, 2, images, tokens, group_lanes), jnp.bfloat16)
            term_in[:, way] = jnp.zeros((GROUPS, 2, images, tokens, group_lanes), jnp.bfloat16)

    def listed(target):
        found = (
            (lists_ref[0, lat] == target)
            | (lists_ref[1, lat] == target)
            | (lists_ref[2, lat] == target)
        ) & (target >= 0)
        return jnp.where(found, 1, 0)

    def mask(shape, key_axis):
        key = lax.broadcasted_iota(jnp.int32, shape, key_axis)
        query = lax.broadcasted_iota(jnp.int32, shape, 1 - key_axis)
        key_tile = key >> 6
        key_col = key & 31
        edge = query - tokens
        is_own = query < tokens
        from_left = edge < 2 * HALO
        query_col = jnp.where(
            is_own, query & 31, jnp.where(from_left, (edge & 7) - HALO, 32 + (edge & 7))
        )
        query_row = jnp.where(is_own, query >> 5, (edge >> 3) & 1)
        width = jnp.where(query_row == 0, widths_ref[2 * lat], widths_ref[2 * lat + 1])
        active = jnp.where(
            key_tile == 0, listed(lat - 1), jnp.where(key_tile == 1, listed(lat), listed(lat + 1))
        )
        visible = (jnp.abs(query_col - key_col) <= width) & (active == 1) & (edge < 4 * HALO)
        return jnp.where(visible, 0.0, HIDDEN)

    for copy in small_copies:
        copy.wait()
    bias[...] = mask(bias.shape, 0)

    places = [(image, head) for image in range(images) for head in range(group_heads)]

    def from_near(group, which, image, head):
        at = pl.ds(head * HDIM, HDIM)
        edges = [edge_in[group, origin, which, image, :, at] for origin in range(2)]
        rest = jnp.zeros((2 * tokens - seen, HDIM), jnp.bfloat16)
        return jnp.concatenate([near[group, which, image, :, at]] + edges + [rest], axis=0)

    def from_far(group, which, image, head):
        at = pl.ds(head * HDIM, HDIM)
        return jnp.concatenate([far[group, slot, which, image, :, at] for slot in range(3)], axis=0)

    to_log2 = scale * math.log2(math.e)
    seen = tokens + 4 * HALO

    def scores(group):
        tops, sums, balances = [], [], []
        for item, (image, head) in enumerate(places):
            values = from_far(group, 1, image, head)
            raw = nt(from_far(group, 0, image, head), from_near(group, 0, image, head))
            raw = raw * to_log2 + bias[...]
            dp = nt(values, from_near(group, 1, image, head))
            top = jnp.maximum(jnp.max(raw, axis=0, keepdims=True), FLOOR)
            e = jnp.exp2(raw - top)
            slot = group * group_items + item
            exps[slot] = e
            dps[slot] = dp
            mixed[slot] = nn(jnp.transpose(e.astype(jnp.bfloat16))[0:seen], values)
            tops.append(top)
            sums.append(jnp.sum(e, axis=0, keepdims=True))
            balances.append(jnp.sum(e * dp, axis=0, keepdims=True))
        for kind, found in enumerate((tops, sums, balances)):
            rows = found + [jnp.zeros_like(found[0])] * (8 - len(found))
            stats[group, kind] = jnp.concatenate(rows, axis=0)
        for way, moves in enumerate((((0, 0, 8), (32, 8, 8), (64, 16, 16)), ((24, 0, 8), (56, 8, 8), (80, 16, 16)))):
            packed = jnp.zeros((8, HDIM), jnp.float32)
            for kind in range(3):
                for old, new, size in moves:
                    packed = window(stats[group, kind], old, 32 * kind + new, size, packed)
            stats_out[way, group] = packed
        for way in range(2):
            stat_copy(group, way).start()

    def wait_stats(group):
        for way in range(2):
            stat_copy(group, way).wait_recv()

    def combine(group):
        others = []
        for kind in range(3):
            other = jnp.full((8, HDIM), FLOOR if kind == 0 else 0.0, jnp.float32)
            for origin, moves in enumerate((((0, 64, 16), (16, 0, 8), (24, 32, 8)), ((0, 80, 16), (16, 24, 8), (24, 56, 8)))):
                for old, new, size in moves:
                    other = window(stats_in[origin, group], 32 * kind + old, new, size, other)
            others.append(other)
        top, total, balance = (stats[group, kind] for kind in range(3))
        top2, total2, balance2 = others
        high = jnp.maximum(top, top2)
        part = jnp.exp2(top - high)
        part2 = jnp.exp2(top2 - high)
        inverse = 1.0 / jnp.maximum(part * total + part2 * total2, 0.5)
        factor = part * inverse
        factors[group, 0] = factor
        factors[group, 1] = (part * balance + part2 * balance2) * inverse
        columns[group] = jnp.transpose(factor)

    def gradients(group):
        for item, (image, head) in enumerate(places):
            at = pl.ds(head * HDIM, HDIM)
            slot = group * group_items + item
            keys = from_far(group, 0, image, head)
            queries, grads = (from_near(group, which, image, head) for which in range(2))
            w = exps[slot] * factors[group, 0, item : item + 1, :]
            ds = w * (dps[slot] - factors[group, 1, item : item + 1, :])
            w = w.astype(jnp.bfloat16)
            ds = ds.astype(jnp.bfloat16)
            dk = nn(ds, queries) * scale
            dv = nn(w, grads)
            att = mixed[slot] * columns[group, 0:seen, item : item + 1]
            dq = nn(jnp.transpose(ds)[0:seen], keys) * scale
            for which, x in enumerate((dk, dv)):
                far_acc[group, which, image, :, at] = x[tokens : 2 * tokens]
                term_out[group, 0, which, image, :, at] = x[0:tokens].astype(jnp.bfloat16)
                term_out[group, 1, which, image, :, at] = x[2 * tokens :].astype(jnp.bfloat16)
            for which, x in enumerate((att, dq)):
                near_acc[group, which, image, :, at] = x[0:tokens]
                for way in range(2):
                    low = tokens + 2 * HALO * way
                    part_out[group, way, which, image, :, at] = x[low : low + 2 * HALO].astype(jnp.bfloat16)
        to_tiles(group, 1, start)
        to_sides(group, 1)

    def finish(group):
        for way in range(2):
            part_copy(group, way).wait_recv()
        from_tiles(group, 1)
        at = lanes(group)
        for image in range(images):
            for which in range(2):
                acc = near_acc[group, which, image]
                add_l = part_in[group, 0, which, image].astype(jnp.float32)
                add_r = part_in[group, 1, which, image].astype(jnp.float32)
                rows = []
                for r in range(2):
                    here = acc[32 * r : 32 * r + 32]
                    rows.append(here[0:8] + add_l[8 * r : 8 * r + 8])
                    rows.append(here[8:24])
                    rows.append(here[24:32] + add_r[8 * r : 8 * r + 8])
                outs[which, image, :, at] = jnp.concatenate(rows, axis=0).astype(jnp.bfloat16)
            for which in range(2):
                total = far_acc[group, which, image]
                for way in range(2):
                    total = total + term_in[group, way, which, image].astype(jnp.float32)
                outs[2 + which, image, :, at] = total.astype(jnp.bfloat16)

    def step(index, carry):
        @pl.when((index >= 1) & (index <= GROUPS // 2))
        def _():
            forward(2 * index - 2, 0)
            forward(2 * index - 1, 0)

        for group in (2, 4):
            @pl.when(is_detour & (index == group + 1))
            def _():
                pass_aside(group, 0)

        @pl.when(index < GROUPS)
        def _():
            from_tiles(index, 0)
            for origin in range(2):
                edge_copy(index, 1 - origin).wait_recv()

            scores(index)

            @pl.when(index + AHEAD < GROUPS)
            def _():
                send_edges(index + AHEAD)

        @pl.when(index >= BEHIND + 3)
        def _():
            forward(index - BEHIND - 3, 1)

        @pl.when(index >= BEHIND)
        def _():
            wait_stats(index - BEHIND)
            combine(index - BEHIND)
            gradients(index - BEHIND)

        return carry

    lax.fori_loop(0, GROUPS + BEHIND, step, 0)

    @pl.when(is_detour)
    def _():
        for group in (2, 4):
            pass_aside(group, 1)

    def last(group, carry):
        @pl.when(group < 2)
        def _():
            forward(GROUPS - 3 + group, 1)

        finish(group)
        return carry

    lax.fori_loop(0, GROUPS, last, 0)

    def drain(group, carry):
        to_tiles(group, 1, wait_send)
        for way in range(2):
            @pl.when(lat == routes[way][0])
            def _():
                pass_copy(group, way, 0).wait_send()

        for kind in range(2):
            for way in range(2):
                @pl.when((lat == routes[way][1]) & relayed(group, kind))
                def _():
                    relay_copy(group, way, kind).wait_send()
        return carry

    lax.fori_loop(0, GROUPS, drain, 0)
    @pl.when(is_detour)
    def _():
        for kind in range(2):
            for group in (2, 4):
                for origin in range(2):
                    detour_out(group, origin, kind).wait_send()

    for way in range(2):
        for source, sem in (
            (edge_out.at[:, way], edge_send.at[way]),
            (part_out.at[:, way], part_send.at[way]),
            (stats_out.at[way], stat_send.at[way]),
        ):
            remote(source, source, sem, sem, sides[way]).wait_send()
        crossing = lat == routes[way][0]
        for some, here in ((whole, jnp.logical_not(crossing)), (direct, crossing)):
            @pl.when(exists[way] & here)
            def _():
                sent = far.at[:, 1, :, some]
                remote(sent, sent, kv_send.at[way], kv_send.at[way], tiles[way]).wait_send()


def split_kernel(stacked, *refs):
    outs, sem = refs[:4], refs[4]
    images = stacked.shape[1]
    copies = [
        pltpu.make_async_copy(stacked.at[i, j], outs[i].at[j], sem.at[i, j])
        for i in range(4)
        for j in range(images)
    ]
    for copy in copies:
        copy.start()
    for copy in copies:
        copy.wait()


def solution(mesh):
    lon_count = mesh.shape["lon"]
    lat_count = mesh.shape["lat"]

    def on_device(queries, key_states, value_states, out_grad, block_lists, row_widths):
        images, rows, columns, channels = queries.shape
        tokens = rows * columns
        flat = (images, tokens, channels)
        items = images * channels // HDIM
        lanes = channels // GROUPS
        bf16, f32 = jnp.bfloat16, jnp.float32
        hbm_spec = pl.BlockSpec(memory_space=pltpu.HBM)
        vmem_spec = pl.BlockSpec(memory_space=pltpu.VMEM)
        dma = pltpu.SemaphoreType.DMA
        stacked = pl.pallas_call(
            functools.partial(kernel, lon_count, lat_count),
            out_shape=pltpu.VMEM((4,) + flat, bf16),
            in_specs=[hbm_spec] * 6,
            out_specs=vmem_spec,
            scratch_shapes=[
                pltpu.VMEM((GROUPS, 2, images, tokens, lanes), bf16),
                pltpu.VMEM((GROUPS, 2, 2, images, 2 * HALO, lanes), bf16),
                pltpu.VMEM((GROUPS, 3, 2, images, tokens, lanes), bf16),
                pltpu.VMEM((GROUPS, 2, 2, images, 2 * HALO, lanes), bf16),
                pltpu.VMEM((3 * tokens, 2 * tokens), f32),
                pltpu.VMEM((items, 3 * tokens, 2 * tokens), f32),
                pltpu.VMEM((items, 3 * tokens, 2 * tokens), f32),
                pltpu.VMEM((GROUPS, 3, 8, 2 * tokens), f32),
                pltpu.VMEM((2, GROUPS, 8, 2 * tokens), f32),
                pltpu.VMEM((2, GROUPS, 8, 2 * tokens), f32),
                pltpu.VMEM((GROUPS, 2, 8, 2 * tokens), f32),
                pltpu.VMEM((GROUPS, 2 * tokens, 8), f32),
                pltpu.VMEM((items, tokens + 4 * HALO, HDIM), f32),
                pltpu.VMEM((GROUPS, 2, images, tokens, lanes), f32),
                pltpu.VMEM((GROUPS, 2, 2, images, 2 * HALO, lanes), bf16),
                pltpu.VMEM((GROUPS, 2, 2, images, 2 * HALO, lanes), bf16),
                pltpu.VMEM((GROUPS, 2, images, tokens, lanes), f32),
                pltpu.VMEM((GROUPS, 2, 2, images, tokens, lanes), bf16),
                pltpu.VMEM((GROUPS, 2, 2, images, tokens, lanes), bf16),
                pltpu.VMEM((2, GROUPS, 2, images - images // 2, tokens, lanes), bf16),
                pltpu.VMEM((2, DETOURS, 2, 2, images, 2 * HALO, lanes), bf16),
                pltpu.SMEM(block_lists.shape[::-1], jnp.int32),
                pltpu.SMEM(row_widths.shape, jnp.int32),
                dma((2,)),
                dma((GROUPS, 4)),
                dma((2,)),
                dma((GROUPS, 2)),
                dma((2,)),
                dma((GROUPS, 2)),
                dma((2,)),
                dma((GROUPS, 2)),
                dma((2,)),
                dma((GROUPS, 2)),
                dma((GROUPS, 2)),
                dma((GROUPS, 2)),
                dma((GROUPS, 2)),
                dma((GROUPS, 2)),
                dma((GROUPS, 2)),
                dma((2, DETOURS, 2)),
                dma((2, DETOURS, 2)),
            ],
            compiler_params=pltpu.CompilerParams(
                collective_id=0, has_side_effects=True, vmem_limit_bytes=60 * 1024 * 1024
            ),
            cost_estimate=pl.CostEstimate(
                flops=12 * items * 192 * 128 * 128,
                bytes_accessed=8 * images * tokens * channels * 2,
                transcendentals=items * 192 * 128,
            ),
        )(
            block_lists.T,
            row_widths,
            queries.reshape(flat),
            key_states.reshape(flat),
            value_states.reshape(flat),
            out_grad.reshape(flat),
        )
        results = pl.pallas_call(
            split_kernel,
            out_shape=[jax.ShapeDtypeStruct(flat, bf16)] * 4,
            in_specs=[pl.BlockSpec(memory_space=pl.ANY)],
            out_specs=[hbm_spec] * 4,
            scratch_shapes=[dma((4, images))],
            compiler_params=pltpu.CompilerParams(vmem_limit_bytes=8 * 1024 * 1024),
        )(stacked)
        return tuple(x.reshape(queries.shape) for x in results)

    split = P(None, "lat", "lon", None)
    return jax.shard_map(
        on_device,
        mesh=mesh,
        in_specs=(split, split, split, split, P(), P()),
        out_specs=(split, split, split, split),
        check_vma=False,
    )
```

```python
import functools
import math

import jax
import jax.numpy as jnp
from jax import lax
from jax.experimental import pallas as pl
from jax.experimental.pallas import tpu as pltpu
from jax.sharding import PartitionSpec as P

MESH = pl.DeviceIdType.MESH
HALO = 8
HDIM = 128
GROUPS = 8
AHEAD = 5
BEHIND = 5
DETOURS = 2
HIDDEN = -1e30
FLOOR = -1e29


def nt(a, b):
    return lax.dot_general(a, b, (((1,), (1,)), ((), ())), preferred_element_type=jnp.float32)


def nn(a, b):
    return jnp.dot(a, b, preferred_element_type=jnp.float32)


def window(x, old, new, size, rest):
    lane = lax.broadcasted_iota(jnp.int32, x.shape, 1)
    shifted = x if old == new else pltpu.roll(x, (new - old) % HDIM, 1)
    return jnp.where((lane >= new) & (lane < new + size), shifted, rest)


def kernel(
    lon_count,
    lat_count,
    lists_hbm,
    widths_hbm,
    q_hbm,
    k_hbm,
    v_hbm,
    g_hbm,
    outs,
    near,
    edge_in,
    far,
    edge_out,
    bias,
    exps,
    dps,
    stats,
    stats_out,
    stats_in,
    factors,
    columns,
    mixed,
    near_acc,
    part_out,
    part_in,
    far_acc,
    term_out,
    term_in,
    relay,
    detour,
    lists_ref,
    widths_ref,
    small_sem,
    own_sem,
    kv_send,
    kv_recv,
    edge_send,
    edge_recv,
    stat_send,
    stat_recv,
    part_send,
    part_recv,
    term_send,
    term_recv,
    pass_send,
    pass_recv,
    relay_send,
    detour_send,
    detour_recv,
    ready,
):
    lon = lax.axis_index("lon")
    lat = lax.axis_index("lat")
    left = lax.rem(lon + lon_count - 1, lon_count)
    right = lax.rem(lon + 1, lon_count)
    has_above = lat > 0
    has_below = lat < lat_count - 1
    middle = lat_count // 2
    beside = lon + 1 - 2 * lax.rem(lon, 2)
    is_middle = (lat == middle - 1) | (lat == middle)
    routes = ((middle, 0, middle - 1), (middle - 1, lat_count - 1, middle))
    planes = middle // 2
    plane = lax.rem(lat // 2, planes)
    is_hot = (plane == 0) | (plane == planes - 1)
    is_detour = (plane == 1) | (plane == planes - 2)
    inward = jnp.where(plane < planes // 2, 2, -2)
    images, tokens, channels = q_hbm.shape
    heads = channels // HDIM
    group_heads = heads // GROUPS
    group_items = images * group_heads
    group_lanes = group_heads * HDIM
    scale = HDIM ** -0.5
    half = images // 2
    whole, direct, passing = slice(0, images), slice(0, half), slice(half, images)

    sides = ({"lon": left}, {"lon": right})
    tiles = ({"lat": lat - 1}, {"lat": lat + 1})
    exists = (has_above, has_below)

    def lanes(group):
        start = group * group_lanes
        return pl.ds(start if isinstance(group, int) else pl.multiple_of(start, HDIM), group_lanes)

    def own_copies(group):
        targets = (far.at[group, 1, 0], far.at[group, 1, 1], near.at[group, 0], near.at[group, 1])
        return [
            pltpu.make_async_copy(source.at[:, :, lanes(group)], target, own_sem.at[group, which])
            for which, (source, target) in enumerate(zip((k_hbm, v_hbm, q_hbm, g_hbm), targets))
        ]

    def fetch(group, carry):
        for copy in own_copies(group):
            copy.start()
        return carry

    fetch(0, 0)
    small_copies = [
        pltpu.make_async_copy(lists_hbm, lists_ref, small_sem.at[0]),
        pltpu.make_async_copy(widths_hbm, widths_ref, small_sem.at[1]),
    ]
    for copy in small_copies:
        copy.start()

    lax.fori_loop(1, GROUPS, fetch, 0)

    barrier = pltpu.get_barrier_semaphore()
    for side in sides:
        pl.semaphore_signal(barrier, inc=1, device_id=side, device_id_type=MESH)
    below_middle = lat == middle
    teller = lat == middle - 2
    greets = (has_above, has_below & (lat != middle - 1))
    for there, tile in zip(greets, tiles):
        @pl.when(there)
        def _():
            pl.semaphore_signal(barrier, inc=1, device_id=tile, device_id_type=MESH)
    for here, place in ((below_middle, {"lat": middle - 2}), (lat == 0, {"lat": middle - 2, "lon": beside})):
        @pl.when(here)
        def _():
            pl.semaphore_signal(barrier, inc=1, device_id=place, device_id_type=MESH)
    for route in routes:
        @pl.when(lat == route[1])
        def _():
            pl.semaphore_signal(barrier, inc=1, device_id={"lat": route[0], "lon": beside}, device_id_type=MESH)
    @pl.when(is_detour)
    def _():
        for side in (left, right):
            pl.semaphore_signal(
                barrier, inc=1, device_id={"lat": lat - inward, "lon": side}, device_id_type=MESH
            )

    pl.semaphore_wait(
        barrier,
        2 + jnp.where(has_above & (lat != middle), 1, 0) + jnp.where(has_below, 1, 0) + jnp.where(is_middle, 1, 0)
        + jnp.where(is_hot, 2, 0)
        + jnp.where(teller, 2, 0),
    )

    @pl.when(teller)
    def _():
        pl.semaphore_signal(ready, inc=1, device_id={"lat": middle}, device_id_type=MESH)
        pl.semaphore_signal(ready, inc=1, device_id={"lat": 0, "lon": beside}, device_id_type=MESH)


    def remote(source, target, send, recv, device):
        return pltpu.make_async_remote_copy(
            src_ref=source, dst_ref=target, send_sem=send, recv_sem=recv, device_id=device, device_id_type=MESH
        )

    def kv_copy(group, way, some):
        return remote(
            far.at[group, 1, :, some],
            far.at[group, 2 - 2 * way, :, some],
            kv_send.at[way],
            kv_recv.at[group, 1 - way],
            tiles[way],
        )

    def edge_copy(group, way):
        return remote(
            edge_out.at[group, way],
            edge_in.at[group, 1 - way],
            edge_send.at[way],
            edge_recv.at[group, 1 - way],
            sides[way],
        )

    def stat_copy(group, way):
        return remote(
            stats_out.at[way, group],
            stats_in.at[1 - way, group],
            stat_send.at[way],
            stat_recv.at[group, 1 - way],
            sides[way],
        )

    def part_copy(group, way):
        return remote(
            part_out.at[group, way],
            part_in.at[group, 1 - way],
            part_send.at[way],
            part_recv.at[group, 1 - way],
            sides[way],
        )

    def term_copy(group, way, some):
        return remote(
            term_out.at[group, way, :, some],
            term_in.at[group, 1 - way, :, some],
            term_send.at[group, way],
            term_recv.at[group, 1 - way],
            tiles[way],
        )

    def pass_copy(group, way, kind):
        return remote(
            far.at[group, 1, :, passing] if kind == 0 else term_out.at[group, way, :, passing],
            relay.at[kind, group],
            pass_send.at[group, kind],
            pass_recv.at[group, kind],
            {"lat": routes[way][1], "lon": beside},
        )

    def relay_copy(group, way, kind):
        return remote(
            relay.at[kind, group],
            far.at[group, 2 - 2 * way, :, passing]
            if kind == 0
            else term_in.at[group, 1 - way, :, passing],
            relay_send.at[group, kind],
            (kv_recv if kind == 0 else term_recv).at[group, 1 - way],
            {"lat": routes[way][2], "lon": beside},
        )

    def detour_in(group, way, kind):
        which = group // 2 - 1
        return remote(
            (edge_out, part_out)[kind].at[group, way],
            detour.at[kind, which, 1 - way],
            (edge_send, part_send)[kind].at[way],
            detour_recv.at[kind, which, 1 - way],
            {"lat": lat + inward, "lon": (left, right)[way]},
        )

    def detour_out(group, origin, kind):
        which = group // 2 - 1
        return remote(
            detour.at[kind, which, origin],
            (edge_in, part_in)[kind].at[group, origin],
            detour_send.at[kind, which, origin],
            (edge_recv, part_recv)[kind].at[group, origin],
            {"lat": lat - inward},
        )

    def to_sides(group, kind):
        aside = is_hot & ((group == 2) | (group == 4))
        for way in range(2):
            @pl.when(jnp.logical_not(aside))
            def _():
                (edge_copy, part_copy)[kind](group, way).start()

            @pl.when(aside)
            def _():
                detour_in(group, way, kind).start()

    def pass_aside(group, kind):
        for origin in range(2):
            detour_in(group, 1 - origin, kind).wait_recv()
            detour_out(group, origin, kind).start()

    def relayed(group, kind):
        return True if kind == 0 else group < GROUPS - 1

    def to_tiles(group, kind, act):
        copy = (kv_copy, term_copy)[kind]
        for way in range(2):
            crossing = (lat == routes[way][0]) & relayed(group, kind)

            @pl.when(exists[way] & jnp.logical_not(crossing))
            def _():
                act(copy(group, way, whole))

            @pl.when(crossing)
            def _():
                if kind == 1 or way == 1:
                    act(copy(group, way, direct))
                act(pass_copy(group, way, kind))

    def from_tiles(group, kind):
        copy = (kv_copy, term_copy)[kind]
        for origin in range(2):
            @pl.when(exists[origin])
            def _():
                copy(group, 1 - origin, whole).wait_recv()

    def forward(group, kind):
        for way in range(2):
            @pl.when((lat == routes[way][1]) & relayed(group, kind))
            def _():
                pass_copy(group, way, kind).wait_recv()
                relay_copy(group, way, kind).start()

    def start(copy):
        copy.start()

    def wait_send(copy):
        copy.wait_send()

    def send_edges(group):
        for which in range(2):
            for image in range(images):
                def half(start, low):
                    block = near[group, which, image, start : start + 16].astype(jnp.float32)
                    return block[low : low + HALO]

                edge_out[group, 0, which, image] = jnp.concatenate(
                    [half(0, 0), half(32, 0)], axis=0
                ).astype(jnp.bfloat16)
                edge_out[group, 1, which, image] = jnp.concatenate(
                    [half(16, HALO), half(48, HALO)], axis=0
                ).astype(jnp.bfloat16)
        to_sides(group, 0)

    def send_group(group, carry):
        copies = own_copies(group)
        copies[0].wait()
        copies[1].wait()
        to_tiles(group, 0, start)
        copies[2].wait()
        copies[3].wait()

        @pl.when(group < AHEAD)
        def _():
            send_edges(group)

        return carry

    lax.fori_loop(0, GROUPS, send_group, 0)

    def send_above(group, carry):
        kv_copy(group, 0, direct).start()
        return carry

    for way in range(2):
        @pl.when(jnp.logical_not(exists[way]))
        def _():
            far[:, 2 * way] = jnp.zeros((GROUPS, 2, images, tokens, group_lanes), jnp.bfloat16)
            term_in[:, way] = jnp.zeros((GROUPS, 2, images, tokens, group_lanes), jnp.bfloat16)

    def listed(target):
        found = (
            (lists_ref[0, lat] == target)
            | (lists_ref[1, lat] == target)
            | (lists_ref[2, lat] == target)
        ) & (target >= 0)
        return jnp.where(found, 1, 0)

    def mask(shape, key_axis):
        key = lax.broadcasted_iota(jnp.int32, shape, key_axis)
        query = lax.broadcasted_iota(jnp.int32, shape, 1 - key_axis)
        key_tile = key >> 6
        key_col = key & 31
        edge = query - tokens
        is_own = query < tokens
        from_left = edge < 2 * HALO
        query_col = jnp.where(
            is_own, query & 31, jnp.where(from_left, (edge & 7) - HALO, 32 + (edge & 7))
        )
        query_row = jnp.where(is_own, query >> 5, (edge >> 3) & 1)
        width = jnp.where(query_row == 0, widths_ref[2 * lat], widths_ref[2 * lat + 1])
        active = jnp.where(
            key_tile == 0, listed(lat - 1), jnp.where(key_tile == 1, listed(lat), listed(lat + 1))
        )
        visible = (jnp.abs(query_col - key_col) <= width) & (active == 1) & (edge < 4 * HALO)
        return jnp.where(visible, 0.0, HIDDEN)

    for copy in small_copies:
        copy.wait()
    bias[...] = mask(bias.shape, 0)

    places = [(image, head) for image in range(images) for head in range(group_heads)]

    def from_near(group, which, image, head):
        at = pl.ds(head * HDIM, HDIM)
        edges = [edge_in[group, origin, which, image, :, at] for origin in range(2)]
        rest = jnp.zeros((2 * tokens - seen, HDIM), jnp.bfloat16)
        return jnp.concatenate([near[group, which, image, :, at]] + edges + [rest], axis=0)

    def from_far(group, which, image, head):
        at = pl.ds(head * HDIM, HDIM)
        return jnp.concatenate([far[group, slot, which, image, :, at] for slot in range(3)], axis=0)

    to_log2 = scale * math.log2(math.e)
    seen = tokens + 4 * HALO

    def scores(group):
        tops, sums, balances = [], [], []
        for item, (image, head) in enumerate(places):
            values = from_far(group, 1, image, head)
            raw = nt(from_far(group, 0, image, head), from_near(group, 0, image, head))
            raw = raw * to_log2 + bias[...]
            dp = nt(values, from_near(group, 1, image, head))
            top = jnp.maximum(jnp.max(raw, axis=0, keepdims=True), FLOOR)
            e = jnp.exp2(raw - top)
            slot = group * group_items + item
            exps[slot] = e
            dps[slot] = dp
            mixed[slot] = nn(jnp.transpose(e.astype(jnp.bfloat16))[0:seen], values)
            tops.append(top)
            sums.append(jnp.sum(e, axis=0, keepdims=True))
            balances.append(jnp.sum(e * dp, axis=0, keepdims=True))
        for kind, found in enumerate((tops, sums, balances)):
            rows = found + [jnp.zeros_like(found[0])] * (8 - len(found))
            stats[group, kind] = jnp.concatenate(rows, axis=0)
        for way, moves in enumerate((((0, 0, 8), (32, 8, 8), (64, 16, 16)), ((24, 0, 8), (56, 8, 8), (80, 16, 16)))):
            packed = jnp.zeros((8, HDIM), jnp.float32)
            for kind in range(3):
                for old, new, size in moves:
                    packed = window(stats[group, kind], old, 32 * kind + new, size, packed)
            stats_out[way, group] = packed
        for way in range(2):
            stat_copy(group, way).start()

    def wait_stats(group):
        for way in range(2):
            stat_copy(group, way).wait_recv()

    def combine(group):
        others = []
        for kind in range(3):
            other = jnp.full((8, HDIM), FLOOR if kind == 0 else 0.0, jnp.float32)
            for origin, moves in enumerate((((0, 64, 16), (16, 0, 8), (24, 32, 8)), ((0, 80, 16), (16, 24, 8), (24, 56, 8)))):
                for old, new, size in moves:
                    other = window(stats_in[origin, group], 32 * kind + old, new, size, other)
            others.append(other)
        top, total, balance = (stats[group, kind] for kind in range(3))
        top2, total2, balance2 = others
        high = jnp.maximum(top, top2)
        part = jnp.exp2(top - high)
        part2 = jnp.exp2(top2 - high)
        inverse = 1.0 / jnp.maximum(part * total + part2 * total2, 0.5)
        factor = part * inverse
        factors[group, 0] = factor
        factors[group, 1] = (part * balance + part2 * balance2) * inverse
        columns[group] = jnp.transpose(factor)

    def gradients(group):
        for item, (image, head) in enumerate(places):
            at = pl.ds(head * HDIM, HDIM)
            slot = group * group_items + item
            keys = from_far(group, 0, image, head)
            queries, grads = (from_near(group, which, image, head) for which in range(2))
            w = exps[slot] * factors[group, 0, item : item + 1, :]
            ds = w * (dps[slot] - factors[group, 1, item : item + 1, :])
            w = w.astype(jnp.bfloat16)
            ds = ds.astype(jnp.bfloat16)
            dk = nn(ds, queries) * scale
            dv = nn(w, grads)
            att = mixed[slot] * columns[group, 0:seen, item : item + 1]
            dq = nn(jnp.transpose(ds)[0:seen], keys) * scale
            for which, x in enumerate((dk, dv)):
                far_acc[group, which, image, :, at] = x[tokens : 2 * tokens]
                term_out[group, 0, which, image, :, at] = x[0:tokens].astype(jnp.bfloat16)
                term_out[group, 1, which, image, :, at] = x[2 * tokens :].astype(jnp.bfloat16)
            for which, x in enumerate((att, dq)):
                near_acc[group, which, image, :, at] = x[0:tokens]
                for way in range(2):
                    low = tokens + 2 * HALO * way
                    part_out[group, way, which, image, :, at] = x[low : low + 2 * HALO].astype(jnp.bfloat16)
        to_tiles(group, 1, start)
        to_sides(group, 1)

    def finish(group):
        for way in range(2):
            part_copy(group, way).wait_recv()
        from_tiles(group, 1)
        at = lanes(group)
        for image in range(images):
            for which in range(2):
                acc = near_acc[group, which, image]
                add_l = part_in[group, 0, which, image].astype(jnp.float32)
                add_r = part_in[group, 1, which, image].astype(jnp.float32)
                rows = []
                for r in range(2):
                    here = acc[32 * r : 32 * r + 32]
                    rows.append(here[0:8] + add_l[8 * r : 8 * r + 8])
                    rows.append(here[8:24])
                    rows.append(here[24:32] + add_r[8 * r : 8 * r + 8])
                outs[which, image, :, at] = jnp.concatenate(rows, axis=0).astype(jnp.bfloat16)
            for which in range(2):
                total = far_acc[group, which, image]
                for way in range(2):
                    total = total + term_in[group, way, which, image].astype(jnp.float32)
                outs[2 + which, image, :, at] = total.astype(jnp.bfloat16)

    def step(index, carry):
        @pl.when(index < GROUPS // 2)
        def _():
            forward(2 * index, 0)
            forward(2 * index + 1, 0)

        for group in (2, 4):
            @pl.when(is_detour & (index == group + 1))
            def _():
                pass_aside(group, 0)

        @pl.when(index < GROUPS)
        def _():
            from_tiles(index, 0)
            for origin in range(2):
                edge_copy(index, 1 - origin).wait_recv()

            scores(index)

            @pl.when(index + AHEAD < GROUPS)
            def _():
                send_edges(index + AHEAD)

        @pl.when((index >= BEHIND + 2) & (index < GROUPS + BEHIND))
        def _():
            forward(index - BEHIND - 2, 1)

        @pl.when(index >= BEHIND)
        def _():
            wait_stats(index - BEHIND)
            combine(index - BEHIND)
            gradients(index - BEHIND)

        return carry

    @pl.when(below_middle | (lat == 0))
    def _():
        pl.semaphore_wait(ready, 1)

    @pl.when(below_middle)
    def _():
        lax.fori_loop(0, GROUPS, send_above, 0)

    lax.fori_loop(0, GROUPS + BEHIND, step, 0)

    @pl.when(is_detour)
    def _():
        for group in (2, 4):
            pass_aside(group, 1)

    def last(group, carry):
        @pl.when(group == 1)
        def _():
            forward(GROUPS - 2, 1)

        finish(group)
        return carry

    lax.fori_loop(0, GROUPS, last, 0)

    def drain(group, carry):
        to_tiles(group, 1, wait_send)
        for way in range(2):
            @pl.when(lat == routes[way][0])
            def _():
                pass_copy(group, way, 0).wait_send()

        for kind in range(2):
            for way in range(2):
                @pl.when((lat == routes[way][1]) & relayed(group, kind))
                def _():
                    relay_copy(group, way, kind).wait_send()
        return carry

    lax.fori_loop(0, GROUPS, drain, 0)
    @pl.when(is_detour)
    def _():
        for kind in range(2):
            for group in (2, 4):
                for origin in range(2):
                    detour_out(group, origin, kind).wait_send()

    for way in range(2):
        for source, sem in (
            (edge_out.at[:, way], edge_send.at[way]),
            (part_out.at[:, way], part_send.at[way]),
            (stats_out.at[way], stat_send.at[way]),
        ):
            remote(source, source, sem, sem, sides[way]).wait_send()
        crossing = lat == routes[way][0]
        for some, here in ((whole, jnp.logical_not(crossing)), (direct, crossing)):
            @pl.when(exists[way] & here)
            def _():
                sent = far.at[:, 1, :, some]
                remote(sent, sent, kv_send.at[way], kv_send.at[way], tiles[way]).wait_send()


def split_kernel(stacked, *refs):
    outs, sem = refs[:4], refs[4]
    copies = [pltpu.make_async_copy(stacked.at[i], outs[i], sem.at[i]) for i in range(4)]
    for copy in copies:
        copy.start()
    for copy in copies:
        copy.wait()


def solution(mesh):
    lon_count = mesh.shape["lon"]
    lat_count = mesh.shape["lat"]

    def on_device(queries, key_states, value_states, out_grad, block_lists, row_widths):
        images, rows, columns, channels = queries.shape
        tokens = rows * columns
        flat = (images, tokens, channels)
        items = images * channels // HDIM
        lanes = channels // GROUPS
        bf16, f32 = jnp.bfloat16, jnp.float32
        hbm_spec = pl.BlockSpec(memory_space=pltpu.HBM)
        vmem_spec = pl.BlockSpec(memory_space=pltpu.VMEM)
        dma = pltpu.SemaphoreType.DMA
        stacked = pl.pallas_call(
            functools.partial(kernel, lon_count, lat_count),
            out_shape=pltpu.VMEM((4,) + flat, bf16),
            in_specs=[hbm_spec] * 6,
            out_specs=vmem_spec,
            scratch_shapes=[
                pltpu.VMEM((GROUPS, 2, images, tokens, lanes), bf16),
                pltpu.VMEM((GROUPS, 2, 2, images, 2 * HALO, lanes), bf16),
                pltpu.VMEM((GROUPS, 3, 2, images, tokens, lanes), bf16),
                pltpu.VMEM((GROUPS, 2, 2, images, 2 * HALO, lanes), bf16),
                pltpu.VMEM((3 * tokens, 2 * tokens), f32),
                pltpu.VMEM((items, 3 * tokens, 2 * tokens), f32),
                pltpu.VMEM((items, 3 * tokens, 2 * tokens), f32),
                pltpu.VMEM((GROUPS, 3, 8, 2 * tokens), f32),
                pltpu.VMEM((2, GROUPS, 8, 2 * tokens), f32),
                pltpu.VMEM((2, GROUPS, 8, 2 * tokens), f32),
                pltpu.VMEM((GROUPS, 2, 8, 2 * tokens), f32),
                pltpu.VMEM((GROUPS, 2 * tokens, 8), f32),
                pltpu.VMEM((items, tokens + 4 * HALO, HDIM), f32),
                pltpu.VMEM((GROUPS, 2, images, tokens, lanes), f32),
                pltpu.VMEM((GROUPS, 2, 2, images, 2 * HALO, lanes), bf16),
                pltpu.VMEM((GROUPS, 2, 2, images, 2 * HALO, lanes), bf16),
                pltpu.VMEM((GROUPS, 2, images, tokens, lanes), f32),
                pltpu.VMEM((GROUPS, 2, 2, images, tokens, lanes), bf16),
                pltpu.VMEM((GROUPS, 2, 2, images, tokens, lanes), bf16),
                pltpu.VMEM((2, GROUPS, 2, images - images // 2, tokens, lanes), bf16),
                pltpu.VMEM((2, DETOURS, 2, 2, images, 2 * HALO, lanes), bf16),
                pltpu.SMEM(block_lists.shape[::-1], jnp.int32),
                pltpu.SMEM(row_widths.shape, jnp.int32),
                dma((2,)),
                dma((GROUPS, 4)),
                dma((2,)),
                dma((GROUPS, 2)),
                dma((2,)),
                dma((GROUPS, 2)),
                dma((2,)),
                dma((GROUPS, 2)),
                dma((2,)),
                dma((GROUPS, 2)),
                dma((GROUPS, 2)),
                dma((GROUPS, 2)),
                dma((GROUPS, 2)),
                dma((GROUPS, 2)),
                dma((GROUPS, 2)),
                dma((2, DETOURS, 2)),
                dma((2, DETOURS, 2)),
                pltpu.SemaphoreType.REGULAR,
            ],
            compiler_params=pltpu.CompilerParams(
                collective_id=0, has_side_effects=True, vmem_limit_bytes=60 * 1024 * 1024
            ),
            cost_estimate=pl.CostEstimate(
                flops=12 * items * 192 * 128 * 128,
                bytes_accessed=8 * images * tokens * channels * 2,
                transcendentals=items * 192 * 128,
            ),
        )(
            block_lists.T,
            row_widths,
            queries.reshape(flat),
            key_states.reshape(flat),
            value_states.reshape(flat),
            out_grad.reshape(flat),
        )
        results = pl.pallas_call(
            split_kernel,
            out_shape=[jax.ShapeDtypeStruct(flat, bf16)] * 4,
            in_specs=[pl.BlockSpec(memory_space=pl.ANY)],
            out_specs=[hbm_spec] * 4,
            scratch_shapes=[dma((4,))],
            compiler_params=pltpu.CompilerParams(vmem_limit_bytes=8 * 1024 * 1024),
        )(stacked)
        return tuple(x.reshape(queries.shape) for x in results)

    split = P(None, "lat", "lon", None)
    return jax.shard_map(
        on_device,
        mesh=mesh,
        in_specs=(split, split, split, split, P(), P()),
        out_specs=(split, split, split, split),
        check_vma=False,
    )
```

```python
import functools
import math

import jax
import jax.numpy as jnp
from jax import lax
from jax.experimental import pallas as pl
from jax.experimental.pallas import tpu as pltpu
from jax.sharding import PartitionSpec as P

MESH = pl.DeviceIdType.MESH
HALO = 8
HDIM = 128
GROUPS = 8
AHEAD = 5
BEHIND = 5
DETOURS = 2
HIDDEN = -1e30
FLOOR = -1e29


def nt(a, b):
    return lax.dot_general(a, b, (((1,), (1,)), ((), ())), preferred_element_type=jnp.float32)


def nn(a, b):
    return jnp.dot(a, b, preferred_element_type=jnp.float32)


def window(x, old, new, size, rest):
    lane = lax.broadcasted_iota(jnp.int32, x.shape, 1)
    shifted = x if old == new else pltpu.roll(x, (new - old) % HDIM, 1)
    return jnp.where((lane >= new) & (lane < new + size), shifted, rest)


def kernel(
    lon_count,
    lat_count,
    lists_hbm,
    widths_hbm,
    q_hbm,
    k_hbm,
    v_hbm,
    g_hbm,
    outs,
    near,
    edge_in,
    far,
    edge_out,
    bias,
    exps,
    dps,
    stats,
    stats_out,
    stats_in,
    factors,
    columns,
    mixed,
    near_acc,
    part_out,
    part_in,
    far_acc,
    term_out,
    term_in,
    relay,
    detour,
    lists_ref,
    widths_ref,
    small_sem,
    own_sem,
    kv_send,
    kv_recv,
    edge_send,
    edge_recv,
    stat_send,
    stat_recv,
    part_send,
    part_recv,
    term_send,
    term_recv,
    pass_send,
    pass_recv,
    relay_send,
    detour_send,
    detour_recv,
    ready,
):
    lon = lax.axis_index("lon")
    lat = lax.axis_index("lat")
    left = lax.rem(lon + lon_count - 1, lon_count)
    right = lax.rem(lon + 1, lon_count)
    has_above = lat > 0
    has_below = lat < lat_count - 1
    middle = lat_count // 2
    beside = lon + 1 - 2 * lax.rem(lon, 2)
    is_middle = (lat == middle - 1) | (lat == middle)
    routes = ((middle, 0, middle - 1), (middle - 1, lat_count - 1, middle))
    planes = middle // 2
    plane = lax.rem(lat // 2, planes)
    is_hot = (plane == 0) | (plane == planes - 1)
    is_detour = (plane == 1) | (plane == planes - 2)
    inward = jnp.where(plane < planes // 2, 2, -2)
    images, tokens, channels = q_hbm.shape
    heads = channels // HDIM
    group_heads = heads // GROUPS
    group_items = images * group_heads
    group_lanes = group_heads * HDIM
    scale = HDIM ** -0.5
    half = images // 2
    whole, direct, passing = slice(0, images), slice(0, half), slice(half, images)

    sides = ({"lon": left}, {"lon": right})
    tiles = ({"lat": lat - 1}, {"lat": lat + 1})
    exists = (has_above, has_below)

    def lanes(group):
        start = group * group_lanes
        return pl.ds(start if isinstance(group, int) else pl.multiple_of(start, HDIM), group_lanes)

    def own_copies(group):
        targets = (far.at[group, 1, 0], far.at[group, 1, 1], near.at[group, 0], near.at[group, 1])
        return [
            pltpu.make_async_copy(source.at[:, :, lanes(group)], target, own_sem.at[group, which])
            for which, (source, target) in enumerate(zip((k_hbm, v_hbm, q_hbm, g_hbm), targets))
        ]

    def fetch(group, carry):
        for copy in own_copies(group):
            copy.start()
        return carry

    fetch(0, 0)
    small_copies = [
        pltpu.make_async_copy(lists_hbm, lists_ref, small_sem.at[0]),
        pltpu.make_async_copy(widths_hbm, widths_ref, small_sem.at[1]),
    ]
    for copy in small_copies:
        copy.start()

    lax.fori_loop(1, GROUPS, fetch, 0)

    barrier = pltpu.get_barrier_semaphore()
    for side in sides:
        pl.semaphore_signal(barrier, inc=1, device_id=side, device_id_type=MESH)
    below_middle = lat == middle
    teller = lat == middle - 2
    greets = (has_above, has_below & (lat != middle - 1))
    for there, tile in zip(greets, tiles):
        @pl.when(there)
        def _():
            pl.semaphore_signal(barrier, inc=1, device_id=tile, device_id_type=MESH)
    for here, place in ((below_middle, {"lat": middle - 2}), (lat == 0, {"lat": middle - 2, "lon": beside})):
        @pl.when(here)
        def _():
            pl.semaphore_signal(barrier, inc=1, device_id=place, device_id_type=MESH)
    for route in routes:
        @pl.when(lat == route[1])
        def _():
            pl.semaphore_signal(barrier, inc=1, device_id={"lat": route[0], "lon": beside}, device_id_type=MESH)
    @pl.when(is_detour)
    def _():
        for side in (left, right):
            pl.semaphore_signal(
                barrier, inc=1, device_id={"lat": lat - inward, "lon": side}, device_id_type=MESH
            )

    pl.semaphore_wait(
        barrier,
        2 + jnp.where(has_above & (lat != middle), 1, 0) + jnp.where(has_below, 1, 0) + jnp.where(is_middle, 1, 0)
        + jnp.where(is_hot, 2, 0)
        + jnp.where(teller, 2, 0),
    )

    @pl.when(teller)
    def _():
        pl.semaphore_signal(ready, inc=1, device_id={"lat": middle}, device_id_type=MESH)
        pl.semaphore_signal(ready, inc=1, device_id={"lat": 0, "lon": beside}, device_id_type=MESH)


    def remote(source, target, send, recv, device):
        return pltpu.make_async_remote_copy(
            src_ref=source, dst_ref=target, send_sem=send, recv_sem=recv, device_id=device, device_id_type=MESH
        )

    def kv_copy(group, way, some):
        return remote(
            far.at[group, 1, :, some],
            far.at[group, 2 - 2 * way, :, some],
            kv_send.at[way],
            kv_recv.at[group, 1 - way],
            tiles[way],
        )

    def edge_copy(group, way):
        return remote(
            edge_out.at[group, way],
            edge_in.at[group, 1 - way],
            edge_send.at[way],
            edge_recv.at[group, 1 - way],
            sides[way],
        )

    def stat_copy(group, way):
        return remote(
            stats_out.at[way, group],
            stats_in.at[1 - way, group],
            stat_send.at[way],
            stat_recv.at[group, 1 - way],
            sides[way],
        )

    def part_copy(group, way):
        return remote(
            part_out.at[group, way],
            part_in.at[group, 1 - way],
            part_send.at[way],
            part_recv.at[group, 1 - way],
            sides[way],
        )

    def term_copy(group, way, some):
        return remote(
            term_out.at[group, way, :, some],
            term_in.at[group, 1 - way, :, some],
            term_send.at[group, way],
            term_recv.at[group, 1 - way],
            tiles[way],
        )

    def pass_copy(group, way, kind):
        return remote(
            far.at[group, 1, :, passing] if kind == 0 else term_out.at[group, way, :, passing],
            relay.at[kind, group],
            pass_send.at[group, kind],
            pass_recv.at[group, kind],
            {"lat": routes[way][1], "lon": beside},
        )

    def relay_copy(group, way, kind):
        return remote(
            relay.at[kind, group],
            far.at[group, 2 - 2 * way, :, passing]
            if kind == 0
            else term_in.at[group, 1 - way, :, passing],
            relay_send.at[group, kind],
            (kv_recv if kind == 0 else term_recv).at[group, 1 - way],
            {"lat": routes[way][2], "lon": beside},
        )

    def detour_in(group, way, kind):
        which = group // 2 - 1
        return remote(
            (edge_out, part_out)[kind].at[group, way],
            detour.at[kind, which, 1 - way],
            (edge_send, part_send)[kind].at[way],
            detour_recv.at[kind, which, 1 - way],
            {"lat": lat + inward, "lon": (left, right)[way]},
        )

    def detour_out(group, origin, kind):
        which = group // 2 - 1
        return remote(
            detour.at[kind, which, origin],
            (edge_in, part_in)[kind].at[group, origin],
            detour_send.at[kind, which, origin],
            (edge_recv, part_recv)[kind].at[group, origin],
            {"lat": lat - inward},
        )

    def to_sides(group, kind):
        aside = is_hot & ((group == 2) | (group == 4))
        for way in range(2):
            @pl.when(jnp.logical_not(aside))
            def _():
                (edge_copy, part_copy)[kind](group, way).start()

            @pl.when(aside)
            def _():
                detour_in(group, way, kind).start()

    def pass_aside(group, kind):
        for origin in range(2):
            detour_in(group, 1 - origin, kind).wait_recv()
            detour_out(group, origin, kind).start()

    def relayed(group, kind):
        return True if kind == 0 else group < GROUPS - 2

    def to_tiles(group, kind, act):
        copy = (kv_copy, term_copy)[kind]
        for way in range(2):
            crossing = (lat == routes[way][0]) & relayed(group, kind)

            @pl.when(exists[way] & jnp.logical_not(crossing))
            def _():
                act(copy(group, way, whole))

            @pl.when(crossing)
            def _():
                if kind == 1 or way == 1:
                    act(copy(group, way, direct))
                act(pass_copy(group, way, kind))

    def from_tiles(group, kind):
        copy = (kv_copy, term_copy)[kind]
        for origin in range(2):
            @pl.when(exists[origin])
            def _():
                copy(group, 1 - origin, whole).wait_recv()

    def forward(group, kind):
        for way in range(2):
            @pl.when((lat == routes[way][1]) & relayed(group, kind))
            def _():
                pass_copy(group, way, kind).wait_recv()
                relay_copy(group, way, kind).start()

    def start(copy):
        copy.start()

    def wait_send(copy):
        copy.wait_send()

    def send_edges(group):
        for which in range(2):
            for image in range(images):
                def half(start, low):
                    block = near[group, which, image, start : start + 16].astype(jnp.float32)
                    return block[low : low + HALO]

                edge_out[group, 0, which, image] = jnp.concatenate(
                    [half(0, 0), half(32, 0)], axis=0
                ).astype(jnp.bfloat16)
                edge_out[group, 1, which, image] = jnp.concatenate(
                    [half(16, HALO), half(48, HALO)], axis=0
                ).astype(jnp.bfloat16)
        to_sides(group, 0)

    def send_group(group, carry):
        copies = own_copies(group)
        copies[0].wait()
        copies[1].wait()
        to_tiles(group, 0, start)
        copies[2].wait()
        copies[3].wait()

        @pl.when(group < AHEAD)
        def _():
            send_edges(group)

        return carry

    lax.fori_loop(0, GROUPS, send_group, 0)

    def send_above(group, carry):
        kv_copy(group, 0, direct).start()
        return carry

    for way in range(2):
        @pl.when(jnp.logical_not(exists[way]))
        def _():
            far[:, 2 * way] = jnp.zeros((GROUPS, 2, images, tokens, group_lanes), jnp.bfloat16)
            term_in[:, way] = jnp.zeros((GROUPS, 2, images, tokens, group_lanes), jnp.bfloat16)

    def listed(target):
        found = (
            (lists_ref[0, lat] == target)
            | (lists_ref[1, lat] == target)
            | (lists_ref[2, lat] == target)
        ) & (target >= 0)
        return jnp.where(found, 1, 0)

    def mask(shape, key_axis):
        key = lax.broadcasted_iota(jnp.int32, shape, key_axis)
        query = lax.broadcasted_iota(jnp.int32, shape, 1 - key_axis)
        key_tile = key >> 6
        key_col = key & 31
        edge = query - tokens
        is_own = query < tokens
        from_left = edge < 2 * HALO
        query_col = jnp.where(
            is_own, query & 31, jnp.where(from_left, (edge & 7) - HALO, 32 + (edge & 7))
        )
        query_row = jnp.where(is_own, query >> 5, (edge >> 3) & 1)
        width = jnp.where(query_row == 0, widths_ref[2 * lat], widths_ref[2 * lat + 1])
        active = jnp.where(
            key_tile == 0, listed(lat - 1), jnp.where(key_tile == 1, listed(lat), listed(lat + 1))
        )
        visible = (jnp.abs(query_col - key_col) <= width) & (active == 1) & (edge < 4 * HALO)
        return jnp.where(visible, 0.0, HIDDEN)

    for copy in small_copies:
        copy.wait()
    bias[...] = mask(bias.shape, 0)

    places = [(image, head) for image in range(images) for head in range(group_heads)]

    def from_near(group, which, image, head):
        at = pl.ds(head * HDIM, HDIM)
        edges = [edge_in[group, origin, which, image, :, at] for origin in range(2)]
        rest = jnp.zeros((2 * tokens - seen, HDIM), jnp.bfloat16)
        return jnp.concatenate([near[group, which, image, :, at]] + edges + [rest], axis=0)

    def from_far(group, which, image, head):
        at = pl.ds(head * HDIM, HDIM)
        return jnp.concatenate([far[group, slot, which, image, :, at] for slot in range(3)], axis=0)

    to_log2 = scale * math.log2(math.e)
    seen = tokens + 4 * HALO

    def scores(group):
        tops, sums, balances = [], [], []
        for item, (image, head) in enumerate(places):
            values = from_far(group, 1, image, head)
            raw = nt(from_far(group, 0, image, head), from_near(group, 0, image, head))
            raw = raw * to_log2 + bias[...]
            dp = nt(values, from_near(group, 1, image, head))
            top = jnp.maximum(jnp.max(raw, axis=0, keepdims=True), FLOOR)
            e = jnp.exp2(raw - top)
            slot = group * group_items + item
            exps[slot] = e
            dps[slot] = dp
            mixed[slot] = nn(jnp.transpose(e.astype(jnp.bfloat16))[0:seen], values)
            tops.append(top)
            sums.append(jnp.sum(e, axis=0, keepdims=True))
            balances.append(jnp.sum(e * dp, axis=0, keepdims=True))
        for kind, found in enumerate((tops, sums, balances)):
            rows = found + [jnp.zeros_like(found[0])] * (8 - len(found))
            stats[group, kind] = jnp.concatenate(rows, axis=0)
        for way, moves in enumerate((((0, 0, 8), (32, 8, 8), (64, 16, 16)), ((24, 0, 8), (56, 8, 8), (80, 16, 16)))):
            packed = jnp.zeros((8, HDIM), jnp.float32)
            for kind in range(3):
                for old, new, size in moves:
                    packed = window(stats[group, kind], old, 32 * kind + new, size, packed)
            stats_out[way, group] = packed
        for way in range(2):
            stat_copy(group, way).start()

    def wait_stats(group):
        for way in range(2):
            stat_copy(group, way).wait_recv()

    def combine(group):
        others = []
        for kind in range(3):
            other = jnp.full((8, HDIM), FLOOR if kind == 0 else 0.0, jnp.float32)
            for origin, moves in enumerate((((0, 64, 16), (16, 0, 8), (24, 32, 8)), ((0, 80, 16), (16, 24, 8), (24, 56, 8)))):
                for old, new, size in moves:
                    other = window(stats_in[origin, group], 32 * kind + old, new, size, other)
            others.append(other)
        top, total, balance = (stats[group, kind] for kind in range(3))
        top2, total2, balance2 = others
        high = jnp.maximum(top, top2)
        part = jnp.exp2(top - high)
        part2 = jnp.exp2(top2 - high)
        inverse = 1.0 / jnp.maximum(part * total + part2 * total2, 0.5)
        factor = part * inverse
        factors[group, 0] = factor
        factors[group, 1] = (part * balance + part2 * balance2) * inverse
        columns[group] = jnp.transpose(factor)

    def gradients(group):
        for item, (image, head) in enumerate(places):
            at = pl.ds(head * HDIM, HDIM)
            slot = group * group_items + item
            keys = from_far(group, 0, image, head)
            queries, grads = (from_near(group, which, image, head) for which in range(2))
            w = exps[slot] * factors[group, 0, item : item + 1, :]
            ds = w * (dps[slot] - factors[group, 1, item : item + 1, :])
            w = w.astype(jnp.bfloat16)
            ds = ds.astype(jnp.bfloat16)
            dk = nn(ds, queries) * scale
            dv = nn(w, grads)
            att = mixed[slot] * columns[group, 0:seen, item : item + 1]
            dq = nn(jnp.transpose(ds)[0:seen], keys) * scale
            for which, x in enumerate((dk, dv)):
                far_acc[group, which, image, :, at] = x[tokens : 2 * tokens]
                term_out[group, 0, which, image, :, at] = x[0:tokens].astype(jnp.bfloat16)
                term_out[group, 1, which, image, :, at] = x[2 * tokens :].astype(jnp.bfloat16)
            for which, x in enumerate((att, dq)):
                near_acc[group, which, image, :, at] = x[0:tokens]
                for way in range(2):
                    low = tokens + 2 * HALO * way
                    part_out[group, way, which, image, :, at] = x[low : low + 2 * HALO].astype(jnp.bfloat16)
        to_tiles(group, 1, start)
        to_sides(group, 1)

    def finish(group):
        for way in range(2):
            part_copy(group, way).wait_recv()
        from_tiles(group, 1)
        at = lanes(group)
        for image in range(images):
            for which in range(2):
                acc = near_acc[group, which, image]
                add_l = part_in[group, 0, which, image].astype(jnp.float32)
                add_r = part_in[group, 1, which, image].astype(jnp.float32)
                rows = []
                for r in range(2):
                    here = acc[32 * r : 32 * r + 32]
                    rows.append(here[0:8] + add_l[8 * r : 8 * r + 8])
                    rows.append(here[8:24])
                    rows.append(here[24:32] + add_r[8 * r : 8 * r + 8])
                outs[which, image, :, at] = jnp.concatenate(rows, axis=0).astype(jnp.bfloat16)
            for which in range(2):
                total = far_acc[group, which, image]
                for way in range(2):
                    total = total + term_in[group, way, which, image].astype(jnp.float32)
                outs[2 + which, image, :, at] = total.astype(jnp.bfloat16)

    def step(index, carry):
        @pl.when(index < GROUPS // 2)
        def _():
            forward(2 * index, 0)
            forward(2 * index + 1, 0)

        for group in (2, 4):
            @pl.when(is_detour & (index == group + 1))
            def _():
                pass_aside(group, 0)

        @pl.when(index < GROUPS)
        def _():
            from_tiles(index, 0)
            for origin in range(2):
                edge_copy(index, 1 - origin).wait_recv()

            scores(index)

            @pl.when(index + AHEAD < GROUPS)
            def _():
                send_edges(index + AHEAD)

        @pl.when((index >= BEHIND + 2) & (index < GROUPS + BEHIND))
        def _():
            forward(index - BEHIND - 2, 1)

        @pl.when(index >= BEHIND)
        def _():
            wait_stats(index - BEHIND)
            combine(index - BEHIND)
            gradients(index - BEHIND)

        return carry

    @pl.when(below_middle | (lat == 0))
    def _():
        pl.semaphore_wait(ready, 1)

    @pl.when(below_middle)
    def _():
        lax.fori_loop(0, GROUPS, send_above, 0)

    lax.fori_loop(0, GROUPS + BEHIND, step, 0)

    @pl.when(is_detour)
    def _():
        for group in (2, 4):
            pass_aside(group, 1)

    def last(group, carry):
        finish(group)
        return carry

    lax.fori_loop(0, GROUPS, last, 0)

    def drain(group, carry):
        to_tiles(group, 1, wait_send)
        for way in range(2):
            @pl.when(lat == routes[way][0])
            def _():
                pass_copy(group, way, 0).wait_send()

        for kind in range(2):
            for way in range(2):
                @pl.when((lat == routes[way][1]) & relayed(group, kind))
                def _():
                    relay_copy(group, way, kind).wait_send()
        return carry

    lax.fori_loop(0, GROUPS, drain, 0)
    @pl.when(is_detour)
    def _():
        for kind in range(2):
            for group in (2, 4):
                for origin in range(2):
                    detour_out(group, origin, kind).wait_send()

    for way in range(2):
        for source, sem in (
            (edge_out.at[:, way], edge_send.at[way]),
            (part_out.at[:, way], part_send.at[way]),
            (stats_out.at[way], stat_send.at[way]),
        ):
            remote(source, source, sem, sem, sides[way]).wait_send()
        crossing = lat == routes[way][0]
        for some, here in ((whole, jnp.logical_not(crossing)), (direct, crossing)):
            @pl.when(exists[way] & here)
            def _():
                sent = far.at[:, 1, :, some]
                remote(sent, sent, kv_send.at[way], kv_send.at[way], tiles[way]).wait_send()


def split_kernel(stacked, *refs):
    outs, sem = refs[:4], refs[4]
    copies = [pltpu.make_async_copy(stacked.at[i], outs[i], sem.at[i]) for i in range(4)]
    for copy in copies:
        copy.start()
    for copy in copies:
        copy.wait()


def solution(mesh):
    lon_count = mesh.shape["lon"]
    lat_count = mesh.shape["lat"]

    def on_device(queries, key_states, value_states, out_grad, block_lists, row_widths):
        images, rows, columns, channels = queries.shape
        tokens = rows * columns
        flat = (images, tokens, channels)
        items = images * channels // HDIM
        lanes = channels // GROUPS
        bf16, f32 = jnp.bfloat16, jnp.float32
        hbm_spec = pl.BlockSpec(memory_space=pltpu.HBM)
        vmem_spec = pl.BlockSpec(memory_space=pltpu.VMEM)
        dma = pltpu.SemaphoreType.DMA
        stacked = pl.pallas_call(
            functools.partial(kernel, lon_count, lat_count),
            out_shape=pltpu.VMEM((4,) + flat, bf16),
            in_specs=[hbm_spec] * 6,
            out_specs=vmem_spec,
            scratch_shapes=[
                pltpu.VMEM((GROUPS, 2, images, tokens, lanes), bf16),
                pltpu.VMEM((GROUPS, 2, 2, images, 2 * HALO, lanes), bf16),
                pltpu.VMEM((GROUPS, 3, 2, images, tokens, lanes), bf16),
                pltpu.VMEM((GROUPS, 2, 2, images, 2 * HALO, lanes), bf16),
                pltpu.VMEM((3 * tokens, 2 * tokens), f32),
                pltpu.VMEM((items, 3 * tokens, 2 * tokens), f32),
                pltpu.VMEM((items, 3 * tokens, 2 * tokens), f32),
                pltpu.VMEM((GROUPS, 3, 8, 2 * tokens), f32),
                pltpu.VMEM((2, GROUPS, 8, 2 * tokens), f32),
                pltpu.VMEM((2, GROUPS, 8, 2 * tokens), f32),
                pltpu.VMEM((GROUPS, 2, 8, 2 * tokens), f32),
                pltpu.VMEM((GROUPS, 2 * tokens, 8), f32),
                pltpu.VMEM((items, tokens + 4 * HALO, HDIM), f32),
                pltpu.VMEM((GROUPS, 2, images, tokens, lanes), f32),
                pltpu.VMEM((GROUPS, 2, 2, images, 2 * HALO, lanes), bf16),
                pltpu.VMEM((GROUPS, 2, 2, images, 2 * HALO, lanes), bf16),
                pltpu.VMEM((GROUPS, 2, images, tokens, lanes), f32),
                pltpu.VMEM((GROUPS, 2, 2, images, tokens, lanes), bf16),
                pltpu.VMEM((GROUPS, 2, 2, images, tokens, lanes), bf16),
                pltpu.VMEM((2, GROUPS, 2, images - images // 2, tokens, lanes), bf16),
                pltpu.VMEM((2, DETOURS, 2, 2, images, 2 * HALO, lanes), bf16),
                pltpu.SMEM(block_lists.shape[::-1], jnp.int32),
                pltpu.SMEM(row_widths.shape, jnp.int32),
                dma((2,)),
                dma((GROUPS, 4)),
                dma((2,)),
                dma((GROUPS, 2)),
                dma((2,)),
                dma((GROUPS, 2)),
                dma((2,)),
                dma((GROUPS, 2)),
                dma((2,)),
                dma((GROUPS, 2)),
                dma((GROUPS, 2)),
                dma((GROUPS, 2)),
                dma((GROUPS, 2)),
                dma((GROUPS, 2)),
                dma((GROUPS, 2)),
                dma((2, DETOURS, 2)),
                dma((2, DETOURS, 2)),
                pltpu.SemaphoreType.REGULAR,
            ],
            compiler_params=pltpu.CompilerParams(
                collective_id=0, has_side_effects=True, vmem_limit_bytes=60 * 1024 * 1024
            ),
            cost_estimate=pl.CostEstimate(
                flops=12 * items * 192 * 128 * 128,
                bytes_accessed=8 * images * tokens * channels * 2,
                transcendentals=items * 192 * 128,
            ),
        )(
            block_lists.T,
            row_widths,
            queries.reshape(flat),
            key_states.reshape(flat),
            value_states.reshape(flat),
            out_grad.reshape(flat),
        )
        results = pl.pallas_call(
            split_kernel,
            out_shape=[jax.ShapeDtypeStruct(flat, bf16)] * 4,
            in_specs=[pl.BlockSpec(memory_space=pl.ANY)],
            out_specs=[hbm_spec] * 4,
            scratch_shapes=[dma((4,))],
            compiler_params=pltpu.CompilerParams(vmem_limit_bytes=8 * 1024 * 1024),
        )(stacked)
        return tuple(x.reshape(queries.shape) for x in results)

    split = P(None, "lat", "lon", None)
    return jax.shard_map(
        on_device,
        mesh=mesh,
        in_specs=(split, split, split, split, P(), P()),
        out_specs=(split, split, split, split),
        check_vma=False,
    )
```

```python
import functools
import math

import jax
import jax.numpy as jnp
from jax import lax
from jax.experimental import pallas as pl
from jax.experimental.pallas import tpu as pltpu
from jax.sharding import PartitionSpec as P

MESH = pl.DeviceIdType.MESH
HALO = 8
HDIM = 128
GROUPS = 8
AHEAD = 5
BEHIND = 5
DETOURS = 2
HIDDEN = -1e30
FLOOR = -1e29


def nt(a, b):
    return lax.dot_general(a, b, (((1,), (1,)), ((), ())), preferred_element_type=jnp.float32)


def nn(a, b):
    return jnp.dot(a, b, preferred_element_type=jnp.float32)


def window(x, old, new, size, rest):
    lane = lax.broadcasted_iota(jnp.int32, x.shape, 1)
    shifted = x if old == new else pltpu.roll(x, (new - old) % HDIM, 1)
    return jnp.where((lane >= new) & (lane < new + size), shifted, rest)


def kernel(
    lon_count,
    lat_count,
    lists_hbm,
    widths_hbm,
    q_hbm,
    k_hbm,
    v_hbm,
    g_hbm,
    outs,
    near,
    edge_in,
    far,
    edge_out,
    bias,
    exps,
    dps,
    stats,
    stats_out,
    stats_in,
    factors,
    columns,
    mixed,
    near_acc,
    part_out,
    part_in,
    far_acc,
    term_out,
    term_in,
    relay,
    detour,
    lists_ref,
    widths_ref,
    small_sem,
    own_sem,
    kv_send,
    kv_recv,
    edge_send,
    edge_recv,
    stat_send,
    stat_recv,
    part_send,
    part_recv,
    term_send,
    term_recv,
    pass_send,
    pass_recv,
    relay_send,
    detour_send,
    detour_recv,
    ready,
):
    lon = lax.axis_index("lon")
    lat = lax.axis_index("lat")
    left = lax.rem(lon + lon_count - 1, lon_count)
    right = lax.rem(lon + 1, lon_count)
    has_above = lat > 0
    has_below = lat < lat_count - 1
    middle = lat_count // 2
    beside = lon + 1 - 2 * lax.rem(lon, 2)
    is_middle = (lat == middle - 1) | (lat == middle)
    routes = ((middle, 0, middle - 1), (middle - 1, lat_count - 1, middle))
    planes = middle // 2
    plane = lax.rem(lat // 2, planes)
    is_hot = (plane == 0) | (plane == planes - 1)
    is_detour = (plane == 1) | (plane == planes - 2)
    inward = jnp.where(plane < planes // 2, 2, -2)
    images, tokens, channels = q_hbm.shape
    heads = channels // HDIM
    group_heads = heads // GROUPS
    group_items = images * group_heads
    group_lanes = group_heads * HDIM
    scale = HDIM ** -0.5
    half = images // 2
    whole, direct, passing = slice(0, images), slice(0, half), slice(half, images)

    sides = ({"lon": left}, {"lon": right})
    tiles = ({"lat": lat - 1}, {"lat": lat + 1})
    exists = (has_above, has_below)

    barrier = pltpu.get_barrier_semaphore()
    for side in sides:
        pl.semaphore_signal(barrier, inc=1, device_id=side, device_id_type=MESH)
    below_middle = lat == middle
    teller = lat == middle - 2
    greets = (has_above, has_below & (lat != middle - 1))
    for there, tile in zip(greets, tiles):
        @pl.when(there)
        def _():
            pl.semaphore_signal(barrier, inc=1, device_id=tile, device_id_type=MESH)
    for here, place in ((below_middle, {"lat": middle - 2}), (lat == 0, {"lat": middle - 2, "lon": beside})):
        @pl.when(here)
        def _():
            pl.semaphore_signal(barrier, inc=1, device_id=place, device_id_type=MESH)
    for route in routes:
        @pl.when(lat == route[1])
        def _():
            pl.semaphore_signal(barrier, inc=1, device_id={"lat": route[0], "lon": beside}, device_id_type=MESH)
    @pl.when(is_detour)
    def _():
        for side in (left, right):
            pl.semaphore_signal(
                barrier, inc=1, device_id={"lat": lat - inward, "lon": side}, device_id_type=MESH
            )

    def lanes(group):
        start = group * group_lanes
        return pl.ds(start if isinstance(group, int) else pl.multiple_of(start, HDIM), group_lanes)

    def own_copies(group):
        targets = (far.at[group, 1, 0], far.at[group, 1, 1], near.at[group, 0], near.at[group, 1])
        return [
            pltpu.make_async_copy(source.at[:, :, lanes(group)], target, own_sem.at[group, which])
            for which, (source, target) in enumerate(zip((k_hbm, v_hbm, q_hbm, g_hbm), targets))
        ]

    def fetch(group, carry):
        for copy in own_copies(group):
            copy.start()
        return carry

    fetch(0, 0)
    small_copies = [
        pltpu.make_async_copy(lists_hbm, lists_ref, small_sem.at[0]),
        pltpu.make_async_copy(widths_hbm, widths_ref, small_sem.at[1]),
    ]
    for copy in small_copies:
        copy.start()

    lax.fori_loop(1, GROUPS, fetch, 0)

    pl.semaphore_wait(
        barrier,
        2 + jnp.where(has_above & (lat != middle), 1, 0) + jnp.where(has_below, 1, 0) + jnp.where(is_middle, 1, 0)
        + jnp.where(is_hot, 2, 0)
        + jnp.where(teller, 2, 0),
    )

    @pl.when(teller)
    def _():
        pl.semaphore_signal(ready, inc=1, device_id={"lat": middle}, device_id_type=MESH)
        pl.semaphore_signal(ready, inc=1, device_id={"lat": 0, "lon": beside}, device_id_type=MESH)


    def remote(source, target, send, recv, device):
        return pltpu.make_async_remote_copy(
            src_ref=source, dst_ref=target, send_sem=send, recv_sem=recv, device_id=device, device_id_type=MESH
        )

    def kv_copy(group, way, some):
        return remote(
            far.at[group, 1, :, some],
            far.at[group, 2 - 2 * way, :, some],
            kv_send.at[way],
            kv_recv.at[group, 1 - way],
            tiles[way],
        )

    def edge_copy(group, way):
        return remote(
            edge_out.at[group, way],
            edge_in.at[group, 1 - way],
            edge_send.at[way],
            edge_recv.at[group, 1 - way],
            sides[way],
        )

    def stat_copy(group, way):
        return remote(
            stats_out.at[way, group, 0:group_items],
            stats_in.at[1 - way, group, 0:group_items],
            stat_send.at[way],
            stat_recv.at[group, 1 - way],
            sides[way],
        )

    def part_copy(group, way):
        return remote(
            part_out.at[group, way],
            part_in.at[group, 1 - way],
            part_send.at[way],
            part_recv.at[group, 1 - way],
            sides[way],
        )

    def term_copy(group, way, some):
        return remote(
            term_out.at[group, way, :, some],
            term_in.at[group, 1 - way, :, some],
            term_send.at[group, way],
            term_recv.at[group, 1 - way],
            tiles[way],
        )

    def pass_copy(group, way, kind):
        return remote(
            far.at[group, 1, :, passing] if kind == 0 else term_out.at[group, way, :, passing],
            relay.at[kind, group],
            pass_send.at[group, kind],
            pass_recv.at[group, kind],
            {"lat": routes[way][1], "lon": beside},
        )

    def relay_copy(group, way, kind):
        return remote(
            relay.at[kind, group],
            far.at[group, 2 - 2 * way, :, passing]
            if kind == 0
            else term_in.at[group, 1 - way, :, passing],
            relay_send.at[group, kind],
            (kv_recv if kind == 0 else term_recv).at[group, 1 - way],
            {"lat": routes[way][2], "lon": beside},
        )

    def detour_in(group, way, kind):
        which = group // 2 - 1
        return remote(
            (edge_out, part_out)[kind].at[group, way],
            detour.at[kind, which, 1 - way],
            (edge_send, part_send)[kind].at[way],
            detour_recv.at[kind, which, 1 - way],
            {"lat": lat + inward, "lon": (left, right)[way]},
        )

    def detour_out(group, origin, kind):
        which = group // 2 - 1
        return remote(
            detour.at[kind, which, origin],
            (edge_in, part_in)[kind].at[group, origin],
            detour_send.at[kind, which, origin],
            (edge_recv, part_recv)[kind].at[group, origin],
            {"lat": lat - inward},
        )

    def to_sides(group, kind):
        aside = is_hot & ((group == 2) | (group == 4))
        for way in range(2):
            @pl.when(jnp.logical_not(aside))
            def _():
                (edge_copy, part_copy)[kind](group, way).start()

            @pl.when(aside)
            def _():
                detour_in(group, way, kind).start()

    def pass_aside(group, kind):
        for origin in range(2):
            detour_in(group, 1 - origin, kind).wait_recv()
            detour_out(group, origin, kind).start()

    def relayed(group, kind):
        return True if kind == 0 else group < GROUPS - 2

    def to_tiles(group, kind, act):
        copy = (kv_copy, term_copy)[kind]
        for way in range(2):
            crossing = (lat == routes[way][0]) & relayed(group, kind)

            @pl.when(exists[way] & jnp.logical_not(crossing))
            def _():
                act(copy(group, way, whole))

            @pl.when(crossing)
            def _():
                if kind == 1 or way == 1:
                    act(copy(group, way, direct))
                act(pass_copy(group, way, kind))

    def from_tiles(group, kind):
        copy = (kv_copy, term_copy)[kind]
        for origin in range(2):
            @pl.when(exists[origin])
            def _():
                copy(group, 1 - origin, whole).wait_recv()

    def forward(group, kind):
        for way in range(2):
            @pl.when((lat == routes[way][1]) & relayed(group, kind))
            def _():
                pass_copy(group, way, kind).wait_recv()
                relay_copy(group, way, kind).start()

    def start(copy):
        copy.start()

    def wait_send(copy):
        copy.wait_send()

    def send_edges(group):
        for which in range(2):
            for image in range(images):
                def half(start, low):
                    block = near[group, which, image, start : start + 16].astype(jnp.float32)
                    return block[low : low + HALO]

                edge_out[group, 0, which, image] = jnp.concatenate(
                    [half(0, 0), half(32, 0)], axis=0
                ).astype(jnp.bfloat16)
                edge_out[group, 1, which, image] = jnp.concatenate(
                    [half(16, HALO), half(48, HALO)], axis=0
                ).astype(jnp.bfloat16)
        to_sides(group, 0)

    def send_group(group, carry):
        copies = own_copies(group)
        copies[0].wait()
        copies[1].wait()
        to_tiles(group, 0, start)
        copies[2].wait()
        copies[3].wait()

        @pl.when(group < AHEAD)
        def _():
            send_edges(group)

        return carry

    lax.fori_loop(0, GROUPS, send_group, 0)

    def send_above(group, carry):
        kv_copy(group, 0, direct).start()
        return carry

    for way in range(2):
        @pl.when(jnp.logical_not(exists[way]))
        def _():
            far[:, 2 * way] = jnp.zeros((GROUPS, 2, images, tokens, group_lanes), jnp.bfloat16)
            term_in[:, way] = jnp.zeros((GROUPS, 2, images, tokens, group_lanes), jnp.bfloat16)

    def listed(target):
        found = (
            (lists_ref[0, lat] == target)
            | (lists_ref[1, lat] == target)
            | (lists_ref[2, lat] == target)
        ) & (target >= 0)
        return jnp.where(found, 1, 0)

    def mask(shape, key_axis):
        key = lax.broadcasted_iota(jnp.int32, shape, key_axis)
        query = lax.broadcasted_iota(jnp.int32, shape, 1 - key_axis)
        key_tile = key >> 6
        key_col = key & 31
        edge = query - tokens
        is_own = query < tokens
        from_left = edge < 2 * HALO
        query_col = jnp.where(
            is_own, query & 31, jnp.where(from_left, (edge & 7) - HALO, 32 + (edge & 7))
        )
        query_row = jnp.where(is_own, query >> 5, (edge >> 3) & 1)
        width = jnp.where(query_row == 0, widths_ref[2 * lat], widths_ref[2 * lat + 1])
        active = jnp.where(
            key_tile == 0, listed(lat - 1), jnp.where(key_tile == 1, listed(lat), listed(lat + 1))
        )
        visible = (jnp.abs(query_col - key_col) <= width) & (active == 1) & (edge < 4 * HALO)
        return jnp.where(visible, 0.0, HIDDEN)

    for copy in small_copies:
        copy.wait()
    bias[...] = mask(bias.shape, 0)

    places = [(image, head) for image in range(images) for head in range(group_heads)]

    def from_near(group, which, image, head):
        at = pl.ds(head * HDIM, HDIM)
        edges = [edge_in[group, origin, which, image, :, at] for origin in range(2)]
        rest = jnp.zeros((2 * tokens - seen, HDIM), jnp.bfloat16)
        return jnp.concatenate([near[group, which, image, :, at]] + edges + [rest], axis=0)

    def from_far(group, which, image, head):
        at = pl.ds(head * HDIM, HDIM)
        return jnp.concatenate([far[group, slot, which, image, :, at] for slot in range(3)], axis=0)

    to_log2 = scale * math.log2(math.e)
    seen = tokens + 4 * HALO

    def scores(group):
        tops, sums, balances = [], [], []
        for item, (image, head) in enumerate(places):
            values = from_far(group, 1, image, head)
            raw = nt(from_far(group, 0, image, head), from_near(group, 0, image, head))
            raw = raw * to_log2 + bias[...]
            dp = nt(values, from_near(group, 1, image, head))
            top = jnp.maximum(jnp.max(raw, axis=0, keepdims=True), FLOOR)
            e = jnp.exp2(raw - top)
            slot = group * group_items + item
            exps[slot] = e
            dps[slot] = dp
            mixed[slot] = nn(jnp.transpose(e.astype(jnp.bfloat16))[0:seen], values)
            tops.append(top)
            sums.append(jnp.sum(e, axis=0, keepdims=True))
            balances.append(jnp.sum(e * dp, axis=0, keepdims=True))
        for kind, found in enumerate((tops, sums, balances)):
            rows = found + [jnp.zeros_like(found[0])] * (8 - len(found))
            stats[group, kind] = jnp.concatenate(rows, axis=0)
        for way, moves in enumerate((((0, 0, 8), (32, 8, 8), (64, 16, 16)), ((24, 0, 8), (56, 8, 8), (80, 16, 16)))):
            packed = jnp.zeros((8, HDIM), jnp.float32)
            for kind in range(3):
                for old, new, size in moves:
                    packed = window(stats[group, kind], old, 32 * kind + new, size, packed)
            stats_out[way, group] = packed
        for way in range(2):
            stat_copy(group, way).start()

    def wait_stats(group):
        for way in range(2):
            stat_copy(group, way).wait_recv()

    def combine(group):
        others = []
        for kind in range(3):
            other = jnp.full((8, HDIM), FLOOR if kind == 0 else 0.0, jnp.float32)
            for origin, moves in enumerate((((0, 64, 16), (16, 0, 8), (24, 32, 8)), ((0, 80, 16), (16, 24, 8), (24, 56, 8)))):
                for old, new, size in moves:
                    other = window(stats_in[origin, group], 32 * kind + old, new, size, other)
            others.append(other)
        top, total, balance = (stats[group, kind] for kind in range(3))
        top2, total2, balance2 = others
        high = jnp.maximum(top, top2)
        part = jnp.exp2(top - high)
        part2 = jnp.exp2(top2 - high)
        inverse = 1.0 / jnp.maximum(part * total + part2 * total2, 0.5)
        factor = part * inverse
        factors[group, 0] = factor
        factors[group, 1] = (part * balance + part2 * balance2) * inverse
        columns[group] = jnp.transpose(factor)

    def gradients(group):
        for item, (image, head) in enumerate(places):
            at = pl.ds(head * HDIM, HDIM)
            slot = group * group_items + item
            keys = from_far(group, 0, image, head)
            queries, grads = (from_near(group, which, image, head) for which in range(2))
            w = exps[slot] * factors[group, 0, item : item + 1, :]
            ds = w * (dps[slot] - factors[group, 1, item : item + 1, :])
            w = w.astype(jnp.bfloat16)
            ds = ds.astype(jnp.bfloat16)
            dk = nn(ds, queries) * scale
            dv = nn(w, grads)
            att = mixed[slot] * columns[group, 0:seen, item : item + 1]
            dq = nn(jnp.transpose(ds)[0:seen], keys) * scale
            for which, x in enumerate((dk, dv)):
                far_acc[group, which, image, :, at] = x[tokens : 2 * tokens]
                term_out[group, 0, which, image, :, at] = x[0:tokens].astype(jnp.bfloat16)
                term_out[group, 1, which, image, :, at] = x[2 * tokens :].astype(jnp.bfloat16)
            for which, x in enumerate((att, dq)):
                near_acc[group, which, image, :, at] = x[0:tokens]
                for way in range(2):
                    low = tokens + 2 * HALO * way
                    part_out[group, way, which, image, :, at] = x[low : low + 2 * HALO].astype(jnp.bfloat16)
        to_tiles(group, 1, start)
        to_sides(group, 1)

    def finish(group):
        for way in range(2):
            part_copy(group, way).wait_recv()
        from_tiles(group, 1)
        at = lanes(group)
        for image in range(images):
            for which in range(2):
                acc = near_acc[group, which, image]
                add_l = part_in[group, 0, which, image].astype(jnp.float32)
                add_r = part_in[group, 1, which, image].astype(jnp.float32)
                rows = []
                for r in range(2):
                    here = acc[32 * r : 32 * r + 32]
                    rows.append(here[0:8] + add_l[8 * r : 8 * r + 8])
                    rows.append(here[8:24])
                    rows.append(here[24:32] + add_r[8 * r : 8 * r + 8])
                outs[which, image, :, at] = jnp.concatenate(rows, axis=0).astype(jnp.bfloat16)
            for which in range(2):
                total = far_acc[group, which, image]
                for way in range(2):
                    total = total + term_in[group, way, which, image].astype(jnp.float32)
                outs[2 + which, image, :, at] = total.astype(jnp.bfloat16)

    def step(index, carry):
        @pl.when(index < GROUPS // 2)
        def _():
            forward(2 * index, 0)
            forward(2 * index + 1, 0)

        for group in (2, 4):
            @pl.when(is_detour & (index == group + 1))
            def _():
                pass_aside(group, 0)

        @pl.when(index < GROUPS)
        def _():
            from_tiles(index, 0)
            for origin in range(2):
                edge_copy(index, 1 - origin).wait_recv()

            scores(index)

            @pl.when(index + AHEAD < GROUPS)
            def _():
                send_edges(index + AHEAD)

        @pl.when((index >= BEHIND + 2) & (index < GROUPS + BEHIND))
        def _():
            forward(index - BEHIND - 2, 1)

        @pl.when(index >= BEHIND)
        def _():
            wait_stats(index - BEHIND)
            combine(index - BEHIND)
            gradients(index - BEHIND)

        return carry

    @pl.when(below_middle | (lat == 0))
    def _():
        pl.semaphore_wait(ready, 1)

    @pl.when(below_middle)
    def _():
        lax.fori_loop(0, GROUPS, send_above, 0)

    lax.fori_loop(0, GROUPS + BEHIND, step, 0)

    @pl.when(is_detour)
    def _():
        for group in (2, 4):
            pass_aside(group, 1)

    def last(group, carry):
        finish(group)
        return carry

    lax.fori_loop(0, GROUPS, last, 0)

    def drain(group, carry):
        to_tiles(group, 1, wait_send)
        for way in range(2):
            @pl.when(lat == routes[way][0])
            def _():
                pass_copy(group, way, 0).wait_send()

        for kind in range(2):
            for way in range(2):
                @pl.when((lat == routes[way][1]) & relayed(group, kind))
                def _():
                    relay_copy(group, way, kind).wait_send()
        return carry

    lax.fori_loop(0, GROUPS, drain, 0)
    @pl.when(is_detour)
    def _():
        for kind in range(2):
            for group in (2, 4):
                for origin in range(2):
                    detour_out(group, origin, kind).wait_send()

    for way in range(2):
        for source, sem in (
            (edge_out.at[:, way], edge_send.at[way]),
            (part_out.at[:, way], part_send.at[way]),
            (stats_out.at[way, :, 0:group_items], stat_send.at[way]),
        ):
            remote(source, source, sem, sem, sides[way]).wait_send()
        crossing = lat == routes[way][0]
        for some, here in ((whole, jnp.logical_not(crossing)), (direct, crossing)):
            @pl.when(exists[way] & here)
            def _():
                sent = far.at[:, 1, :, some]
                remote(sent, sent, kv_send.at[way], kv_send.at[way], tiles[way]).wait_send()


def split_kernel(stacked, *refs):
    outs, sem = refs[:4], refs[4]
    copies = [pltpu.make_async_copy(stacked.at[i], outs[i], sem.at[i]) for i in range(4)]
    for copy in copies:
        copy.start()
    for copy in copies:
        copy.wait()


def solution(mesh):
    lon_count = mesh.shape["lon"]
    lat_count = mesh.shape["lat"]

    def on_device(queries, key_states, value_states, out_grad, block_lists, row_widths):
        images, rows, columns, channels = queries.shape
        tokens = rows * columns
        flat = (images, tokens, channels)
        items = images * channels // HDIM
        lanes = channels // GROUPS
        bf16, f32 = jnp.bfloat16, jnp.float32
        hbm_spec = pl.BlockSpec(memory_space=pltpu.HBM)
        vmem_spec = pl.BlockSpec(memory_space=pltpu.VMEM)
        dma = pltpu.SemaphoreType.DMA
        stacked = pl.pallas_call(
            functools.partial(kernel, lon_count, lat_count),
            out_shape=pltpu.VMEM((4,) + flat, bf16),
            in_specs=[hbm_spec] * 6,
            out_specs=vmem_spec,
            scratch_shapes=[
                pltpu.VMEM((GROUPS, 2, images, tokens, lanes), bf16),
                pltpu.VMEM((GROUPS, 2, 2, images, 2 * HALO, lanes), bf16),
                pltpu.VMEM((GROUPS, 3, 2, images, tokens, lanes), bf16),
                pltpu.VMEM((GROUPS, 2, 2, images, 2 * HALO, lanes), bf16),
                pltpu.VMEM((3 * tokens, 2 * tokens), f32),
                pltpu.VMEM((items, 3 * tokens, 2 * tokens), f32),
                pltpu.VMEM((items, 3 * tokens, 2 * tokens), f32),
                pltpu.VMEM((GROUPS, 3, 8, 2 * tokens), f32),
                pltpu.VMEM((2, GROUPS, 8, 2 * tokens), f32),
                pltpu.VMEM((2, GROUPS, 8, 2 * tokens), f32),
                pltpu.VMEM((GROUPS, 2, 8, 2 * tokens), f32),
                pltpu.VMEM((GROUPS, 2 * tokens, 8), f32),
                pltpu.VMEM((items, tokens + 4 * HALO, HDIM), f32),
                pltpu.VMEM((GROUPS, 2, images, tokens, lanes), f32),
                pltpu.VMEM((GROUPS, 2, 2, images, 2 * HALO, lanes), bf16),
                pltpu.VMEM((GROUPS, 2, 2, images, 2 * HALO, lanes), bf16),
                pltpu.VMEM((GROUPS, 2, images, tokens, lanes), f32),
                pltpu.VMEM((GROUPS, 2, 2, images, tokens, lanes), bf16),
                pltpu.VMEM((GROUPS, 2, 2, images, tokens, lanes), bf16),
                pltpu.VMEM((2, GROUPS, 2, images - images // 2, tokens, lanes), bf16),
                pltpu.VMEM((2, DETOURS, 2, 2, images, 2 * HALO, lanes), bf16),
                pltpu.SMEM(block_lists.shape[::-1], jnp.int32),
                pltpu.SMEM(row_widths.shape, jnp.int32),
                dma((2,)),
                dma((GROUPS, 4)),
                dma((2,)),
                dma((GROUPS, 2)),
                dma((2,)),
                dma((GROUPS, 2)),
                dma((2,)),
                dma((GROUPS, 2)),
                dma((2,)),
                dma((GROUPS, 2)),
                dma((GROUPS, 2)),
                dma((GROUPS, 2)),
                dma((GROUPS, 2)),
                dma((GROUPS, 2)),
                dma((GROUPS, 2)),
                dma((2, DETOURS, 2)),
                dma((2, DETOURS, 2)),
                pltpu.SemaphoreType.REGULAR,
            ],
            compiler_params=pltpu.CompilerParams(
                collective_id=0, has_side_effects=True, vmem_limit_bytes=60 * 1024 * 1024
            ),
            cost_estimate=pl.CostEstimate(
                flops=12 * items * 192 * 128 * 128,
                bytes_accessed=8 * images * tokens * channels * 2,
                transcendentals=items * 192 * 128,
            ),
        )(
            block_lists.T,
            row_widths,
            queries.reshape(flat),
            key_states.reshape(flat),
            value_states.reshape(flat),
            out_grad.reshape(flat),
        )
        results = pl.pallas_call(
            split_kernel,
            out_shape=[jax.ShapeDtypeStruct(flat, bf16)] * 4,
            in_specs=[pl.BlockSpec(memory_space=pl.ANY)],
            out_specs=[hbm_spec] * 4,
            scratch_shapes=[dma((4,))],
            compiler_params=pltpu.CompilerParams(vmem_limit_bytes=8 * 1024 * 1024),
        )(stacked)
        return tuple(x.reshape(queries.shape) for x in results)

    split = P(None, "lat", "lon", None)
    return jax.shard_map(
        on_device,
        mesh=mesh,
        in_specs=(split, split, split, split, P(), P()),
        out_specs=(split, split, split, split),
        check_vma=False,
    )
```

```python
import functools
import math

import jax
import jax.numpy as jnp
from jax import lax
from jax.experimental import pallas as pl
from jax.experimental.pallas import tpu as pltpu
from jax.sharding import PartitionSpec as P

MESH = pl.DeviceIdType.MESH
HALO = 8
HDIM = 128
GROUPS = 8
AHEAD = 5
BEHIND = 5
DETOURS = 2
HIDDEN = -1e30
FLOOR = -1e29


def nt(a, b):
    return lax.dot_general(a, b, (((1,), (1,)), ((), ())), preferred_element_type=jnp.float32)


def nn(a, b):
    return jnp.dot(a, b, preferred_element_type=jnp.float32)


def window(x, old, new, size, rest):
    lane = lax.broadcasted_iota(jnp.int32, x.shape, 1)
    shifted = x if old == new else pltpu.roll(x, (new - old) % HDIM, 1)
    return jnp.where((lane >= new) & (lane < new + size), shifted, rest)


def kernel(
    lon_count,
    lat_count,
    lists_hbm,
    widths_hbm,
    q_hbm,
    k_hbm,
    v_hbm,
    g_hbm,
    outs,
    near,
    edge_in,
    far,
    edge_out,
    bias,
    exps,
    dps,
    stats,
    stats_out,
    stats_in,
    factors,
    columns,
    mixed,
    near_acc,
    part_out,
    part_in,
    far_acc,
    term_out,
    term_in,
    relay,
    detour,
    lists_ref,
    widths_ref,
    small_sem,
    own_sem,
    kv_send,
    kv_recv,
    edge_send,
    edge_recv,
    stat_send,
    stat_recv,
    part_send,
    part_recv,
    term_send,
    half_send,
    term_recv,
    pass_send,
    pass_recv,
    relay_send,
    detour_send,
    detour_recv,
    ready,
):
    lon = lax.axis_index("lon")
    lat = lax.axis_index("lat")
    left = lax.rem(lon + lon_count - 1, lon_count)
    right = lax.rem(lon + 1, lon_count)
    has_above = lat > 0
    has_below = lat < lat_count - 1
    middle = lat_count // 2
    beside = lon + 1 - 2 * lax.rem(lon, 2)
    is_middle = (lat == middle - 1) | (lat == middle)
    routes = ((middle, 0, middle - 1), (middle - 1, lat_count - 1, middle))
    planes = middle // 2
    plane = lax.rem(lat // 2, planes)
    is_hot = (plane == 0) | (plane == planes - 1)
    is_detour = (plane == 1) | (plane == planes - 2)
    inward = jnp.where(plane < planes // 2, 2, -2)
    images, tokens, channels = q_hbm.shape
    heads = channels // HDIM
    group_heads = heads // GROUPS
    group_items = images * group_heads
    group_lanes = group_heads * HDIM
    scale = HDIM ** -0.5
    half = images // 2
    whole, direct, passing = slice(0, images), slice(0, half), slice(half, images)

    sides = ({"lon": left}, {"lon": right})
    tiles = ({"lat": lat - 1}, {"lat": lat + 1})
    exists = (has_above, has_below)

    barrier = pltpu.get_barrier_semaphore()
    for side in sides:
        pl.semaphore_signal(barrier, inc=1, device_id=side, device_id_type=MESH)
    below_middle = lat == middle
    teller = lat == middle - 2
    greets = (has_above, has_below & (lat != middle - 1))
    for there, tile in zip(greets, tiles):
        @pl.when(there)
        def _():
            pl.semaphore_signal(barrier, inc=1, device_id=tile, device_id_type=MESH)
    for here, place in ((below_middle, {"lat": middle - 2}), (lat == 0, {"lat": middle - 2, "lon": beside})):
        @pl.when(here)
        def _():
            pl.semaphore_signal(barrier, inc=1, device_id=place, device_id_type=MESH)
    for route in routes:
        @pl.when(lat == route[1])
        def _():
            pl.semaphore_signal(barrier, inc=1, device_id={"lat": route[0], "lon": beside}, device_id_type=MESH)
    @pl.when(is_detour)
    def _():
        for side in (left, right):
            pl.semaphore_signal(
                barrier, inc=1, device_id={"lat": lat - inward, "lon": side}, device_id_type=MESH
            )

    def lanes(group):
        start = group * group_lanes
        return pl.ds(start if isinstance(group, int) else pl.multiple_of(start, HDIM), group_lanes)

    def own_copies(group):
        targets = (far.at[group, 1, 0], far.at[group, 1, 1], near.at[group, 0], near.at[group, 1])
        return [
            pltpu.make_async_copy(source.at[:, :, lanes(group)], target, own_sem.at[group, which])
            for which, (source, target) in enumerate(zip((k_hbm, v_hbm, q_hbm, g_hbm), targets))
        ]

    def fetch(group, carry):
        for copy in own_copies(group):
            copy.start()
        return carry

    fetch(0, 0)
    small_copies = [
        pltpu.make_async_copy(lists_hbm, lists_ref, small_sem.at[0]),
        pltpu.make_async_copy(widths_hbm, widths_ref, small_sem.at[1]),
    ]
    for copy in small_copies:
        copy.start()

    lax.fori_loop(1, GROUPS, fetch, 0)

    pl.semaphore_wait(
        barrier,
        2 + jnp.where(has_above & (lat != middle), 1, 0) + jnp.where(has_below, 1, 0) + jnp.where(is_middle, 1, 0)
        + jnp.where(is_hot, 2, 0)
        + jnp.where(teller, 2, 0),
    )

    @pl.when(teller)
    def _():
        pl.semaphore_signal(ready, inc=1, device_id={"lat": middle}, device_id_type=MESH)
        pl.semaphore_signal(ready, inc=1, device_id={"lat": 0, "lon": beside}, device_id_type=MESH)


    def remote(source, target, send, recv, device):
        return pltpu.make_async_remote_copy(
            src_ref=source, dst_ref=target, send_sem=send, recv_sem=recv, device_id=device, device_id_type=MESH
        )

    def kv_copy(group, way, some):
        return remote(
            far.at[group, 1, :, some],
            far.at[group, 2 - 2 * way, :, some],
            kv_send.at[way],
            kv_recv.at[group, 1 - way],
            tiles[way],
        )

    def edge_copy(group, way):
        return remote(
            edge_out.at[group, way],
            edge_in.at[group, 1 - way],
            edge_send.at[way],
            edge_recv.at[group, 1 - way],
            sides[way],
        )

    def stat_copy(group, way):
        return remote(
            stats_out.at[way, group, 0:group_items],
            stats_in.at[1 - way, group, 0:group_items],
            stat_send.at[way],
            stat_recv.at[group, 1 - way],
            sides[way],
        )

    def part_copy(group, way):
        return remote(
            part_out.at[group, way],
            part_in.at[group, 1 - way],
            part_send.at[way],
            part_recv.at[group, 1 - way],
            sides[way],
        )

    def term_copy(group, way, some):
        return remote(
            term_out.at[group, way, :, some],
            term_in.at[group, 1 - way, :, some],
            (term_send if some is whole else half_send).at[way],
            term_recv.at[group, 1 - way],
            tiles[way],
        )

    def pass_copy(group, way, kind):
        return remote(
            far.at[group, 1, :, passing] if kind == 0 else term_out.at[group, way, :, passing],
            relay.at[kind, group],
            pass_send.at[kind],
            pass_recv.at[group, kind],
            {"lat": routes[way][1], "lon": beside},
        )

    def relay_copy(group, way, kind):
        return remote(
            relay.at[kind, group],
            far.at[group, 2 - 2 * way, :, passing]
            if kind == 0
            else term_in.at[group, 1 - way, :, passing],
            relay_send.at[kind],
            (kv_recv if kind == 0 else term_recv).at[group, 1 - way],
            {"lat": routes[way][2], "lon": beside},
        )

    def detour_in(group, way, kind):
        which = group // 2 - 1
        return remote(
            (edge_out, part_out)[kind].at[group, way],
            detour.at[kind, which, 1 - way],
            (edge_send, part_send)[kind].at[way],
            detour_recv.at[kind, which, 1 - way],
            {"lat": lat + inward, "lon": (left, right)[way]},
        )

    def detour_out(group, origin, kind):
        which = group // 2 - 1
        return remote(
            detour.at[kind, which, origin],
            (edge_in, part_in)[kind].at[group, origin],
            detour_send.at[kind, which, origin],
            (edge_recv, part_recv)[kind].at[group, origin],
            {"lat": lat - inward},
        )

    def to_sides(group, kind):
        aside = is_hot & ((group == 2) | (group == 4))
        for way in range(2):
            @pl.when(jnp.logical_not(aside))
            def _():
                (edge_copy, part_copy)[kind](group, way).start()

            @pl.when(aside)
            def _():
                detour_in(group, way, kind).start()

    def pass_aside(group, kind):
        for origin in range(2):
            detour_in(group, 1 - origin, kind).wait_recv()
            detour_out(group, origin, kind).start()

    def relayed(group, kind):
        return True if kind == 0 else group < GROUPS - 2

    def to_tiles(group, kind, act):
        copy = (kv_copy, term_copy)[kind]
        for way in range(2):
            crossing = (lat == routes[way][0]) & relayed(group, kind)

            @pl.when(exists[way] & jnp.logical_not(crossing))
            def _():
                act(copy(group, way, whole))

            @pl.when(crossing)
            def _():
                if kind == 1 or way == 1:
                    act(copy(group, way, direct))
                act(pass_copy(group, way, kind))

    def from_tiles(group, kind):
        copy = (kv_copy, term_copy)[kind]
        for origin in range(2):
            @pl.when(exists[origin])
            def _():
                copy(group, 1 - origin, whole).wait_recv()

    def forward(group, kind):
        for way in range(2):
            @pl.when((lat == routes[way][1]) & relayed(group, kind))
            def _():
                pass_copy(group, way, kind).wait_recv()
                relay_copy(group, way, kind).start()

    def start(copy):
        copy.start()

    def send_edges(group):
        for which in range(2):
            for image in range(images):
                def half(start, low):
                    block = near[group, which, image, start : start + 16].astype(jnp.float32)
                    return block[low : low + HALO]

                edge_out[group, 0, which, image] = jnp.concatenate(
                    [half(0, 0), half(32, 0)], axis=0
                ).astype(jnp.bfloat16)
                edge_out[group, 1, which, image] = jnp.concatenate(
                    [half(16, HALO), half(48, HALO)], axis=0
                ).astype(jnp.bfloat16)
        to_sides(group, 0)

    def send_group(group, carry):
        copies = own_copies(group)
        copies[0].wait()
        copies[1].wait()
        to_tiles(group, 0, start)
        copies[2].wait()
        copies[3].wait()

        @pl.when(group < AHEAD)
        def _():
            send_edges(group)

        return carry

    lax.fori_loop(0, GROUPS, send_group, 0)

    def send_above(group, carry):
        kv_copy(group, 0, direct).start()
        return carry

    for way in range(2):
        @pl.when(jnp.logical_not(exists[way]))
        def _():
            far[:, 2 * way] = jnp.zeros((GROUPS, 2, images, tokens, group_lanes), jnp.bfloat16)
            term_in[:, way] = jnp.zeros((GROUPS, 2, images, tokens, group_lanes), jnp.bfloat16)

    def listed(target):
        found = (
            (lists_ref[0, lat] == target)
            | (lists_ref[1, lat] == target)
            | (lists_ref[2, lat] == target)
        ) & (target >= 0)
        return jnp.where(found, 1, 0)

    def mask(shape, key_axis):
        key = lax.broadcasted_iota(jnp.int32, shape, key_axis)
        query = lax.broadcasted_iota(jnp.int32, shape, 1 - key_axis)
        key_tile = key >> 6
        key_col = key & 31
        edge = query - tokens
        is_own = query < tokens
        from_left = edge < 2 * HALO
        query_col = jnp.where(
            is_own, query & 31, jnp.where(from_left, (edge & 7) - HALO, 32 + (edge & 7))
        )
        query_row = jnp.where(is_own, query >> 5, (edge >> 3) & 1)
        width = jnp.where(query_row == 0, widths_ref[2 * lat], widths_ref[2 * lat + 1])
        active = jnp.where(
            key_tile == 0, listed(lat - 1), jnp.where(key_tile == 1, listed(lat), listed(lat + 1))
        )
        visible = (jnp.abs(query_col - key_col) <= width) & (active == 1) & (edge < 4 * HALO)
        return jnp.where(visible, 0.0, HIDDEN)

    for copy in small_copies:
        copy.wait()
    bias[...] = mask(bias.shape, 0)

    places = [(image, head) for image in range(images) for head in range(group_heads)]

    def from_near(group, which, image, head):
        at = pl.ds(head * HDIM, HDIM)
        edges = [edge_in[group, origin, which, image, :, at] for origin in range(2)]
        rest = jnp.zeros((2 * tokens - seen, HDIM), jnp.bfloat16)
        return jnp.concatenate([near[group, which, image, :, at]] + edges + [rest], axis=0)

    def from_far(group, which, image, head):
        at = pl.ds(head * HDIM, HDIM)
        return jnp.concatenate([far[group, slot, which, image, :, at] for slot in range(3)], axis=0)

    to_log2 = scale * math.log2(math.e)
    seen = tokens + 4 * HALO

    def scores(group):
        tops, sums, balances = [], [], []
        for item, (image, head) in enumerate(places):
            values = from_far(group, 1, image, head)
            raw = nt(from_far(group, 0, image, head), from_near(group, 0, image, head))
            raw = raw * to_log2 + bias[...]
            dp = nt(values, from_near(group, 1, image, head))
            top = jnp.maximum(jnp.max(raw, axis=0, keepdims=True), FLOOR)
            e = jnp.exp2(raw - top)
            slot = group * group_items + item
            exps[slot] = e
            dps[slot] = dp
            mixed[slot] = nn(jnp.transpose(e.astype(jnp.bfloat16))[0:seen], values)
            tops.append(top)
            sums.append(jnp.sum(e, axis=0, keepdims=True))
            balances.append(jnp.sum(e * dp, axis=0, keepdims=True))
        for kind, found in enumerate((tops, sums, balances)):
            rows = found + [jnp.zeros_like(found[0])] * (8 - len(found))
            stats[group, kind] = jnp.concatenate(rows, axis=0)
        for way, moves in enumerate((((0, 0, 8), (32, 8, 8), (64, 16, 16)), ((24, 0, 8), (56, 8, 8), (80, 16, 16)))):
            packed = jnp.zeros((8, HDIM), jnp.float32)
            for kind in range(3):
                for old, new, size in moves:
                    packed = window(stats[group, kind], old, 32 * kind + new, size, packed)
            stats_out[way, group] = packed
        for way in range(2):
            stat_copy(group, way).start()

    def wait_stats(group):
        for way in range(2):
            stat_copy(group, way).wait_recv()

    def combine(group):
        others = []
        for kind in range(3):
            other = jnp.full((8, HDIM), FLOOR if kind == 0 else 0.0, jnp.float32)
            for origin, moves in enumerate((((0, 64, 16), (16, 0, 8), (24, 32, 8)), ((0, 80, 16), (16, 24, 8), (24, 56, 8)))):
                for old, new, size in moves:
                    other = window(stats_in[origin, group], 32 * kind + old, new, size, other)
            others.append(other)
        top, total, balance = (stats[group, kind] for kind in range(3))
        top2, total2, balance2 = others
        high = jnp.maximum(top, top2)
        part = jnp.exp2(top - high)
        part2 = jnp.exp2(top2 - high)
        inverse = 1.0 / jnp.maximum(part * total + part2 * total2, 0.5)
        factor = part * inverse
        factors[group, 0] = factor
        factors[group, 1] = (part * balance + part2 * balance2) * inverse
        columns[group] = jnp.transpose(factor)

    def gradients(group):
        for item, (image, head) in enumerate(places):
            at = pl.ds(head * HDIM, HDIM)
            slot = group * group_items + item
            keys = from_far(group, 0, image, head)
            queries, grads = (from_near(group, which, image, head) for which in range(2))
            w = exps[slot] * factors[group, 0, item : item + 1, :]
            ds = w * (dps[slot] - factors[group, 1, item : item + 1, :])
            w = w.astype(jnp.bfloat16)
            ds = ds.astype(jnp.bfloat16)
            dk = nn(ds, queries) * scale
            dv = nn(w, grads)
            att = mixed[slot] * columns[group, 0:seen, item : item + 1]
            dq = nn(jnp.transpose(ds)[0:seen], keys) * scale
            for which, x in enumerate((dk, dv)):
                far_acc[group, which, image, :, at] = x[tokens : 2 * tokens]
                term_out[group, 0, which, image, :, at] = x[0:tokens].astype(jnp.bfloat16)
                term_out[group, 1, which, image, :, at] = x[2 * tokens :].astype(jnp.bfloat16)
            for which, x in enumerate((att, dq)):
                near_acc[group, which, image, :, at] = x[0:tokens]
                for way in range(2):
                    low = tokens + 2 * HALO * way
                    part_out[group, way, which, image, :, at] = x[low : low + 2 * HALO].astype(jnp.bfloat16)
        to_tiles(group, 1, start)
        to_sides(group, 1)

    def finish(group):
        for way in range(2):
            part_copy(group, way).wait_recv()
        from_tiles(group, 1)
        at = lanes(group)
        for image in range(images):
            for which in range(2):
                acc = near_acc[group, which, image]
                add_l = part_in[group, 0, which, image].astype(jnp.float32)
                add_r = part_in[group, 1, which, image].astype(jnp.float32)
                rows = []
                for r in range(2):
                    here = acc[32 * r : 32 * r + 32]
                    rows.append(here[0:8] + add_l[8 * r : 8 * r + 8])
                    rows.append(here[8:24])
                    rows.append(here[24:32] + add_r[8 * r : 8 * r + 8])
                outs[which, image, :, at] = jnp.concatenate(rows, axis=0).astype(jnp.bfloat16)
            for which in range(2):
                total = far_acc[group, which, image]
                for way in range(2):
                    total = total + term_in[group, way, which, image].astype(jnp.float32)
                outs[2 + which, image, :, at] = total.astype(jnp.bfloat16)

    def step(index, carry):
        @pl.when(index < GROUPS // 2)
        def _():
            forward(2 * index, 0)
            forward(2 * index + 1, 0)

        for group in (2, 4):
            @pl.when(is_detour & (index == group + 1))
            def _():
                pass_aside(group, 0)

        @pl.when(index < GROUPS)
        def _():
            from_tiles(index, 0)
            for origin in range(2):
                edge_copy(index, 1 - origin).wait_recv()

            scores(index)

            @pl.when(index + AHEAD < GROUPS)
            def _():
                send_edges(index + AHEAD)

        @pl.when((index >= BEHIND + 2) & (index < GROUPS + BEHIND))
        def _():
            forward(index - BEHIND - 2, 1)

        @pl.when(index >= BEHIND)
        def _():
            wait_stats(index - BEHIND)
            combine(index - BEHIND)
            gradients(index - BEHIND)

        return carry

    @pl.when(below_middle | (lat == 0))
    def _():
        pl.semaphore_wait(ready, 1)

    @pl.when(below_middle)
    def _():
        lax.fori_loop(0, GROUPS, send_above, 0)

    lax.fori_loop(0, GROUPS + BEHIND, step, 0)

    @pl.when(is_detour)
    def _():
        for group in (2, 4):
            pass_aside(group, 1)

    def last(group, carry):
        finish(group)
        return carry

    lax.fori_loop(0, GROUPS, last, 0)

    def sent(source, sem):
        remote(source, source, sem, sem, sides[0]).wait_send()

    @pl.when(is_detour)
    def _():
        for kind in range(2):
            for group in (2, 4):
                for origin in range(2):
                    detour_out(group, origin, kind).wait_send()

    for way in range(2):
        for source, sem in (
            (edge_out.at[:, way], edge_send.at[way]),
            (part_out.at[:, way], part_send.at[way]),
            (stats_out.at[way, :, 0:group_items], stat_send.at[way]),
        ):
            sent(source, sem)
        crossing = lat == routes[way][0]

        @pl.when(exists[way] & jnp.logical_not(crossing))
        def _():
            sent(far.at[:, 1], kv_send.at[way])
            sent(term_out.at[:, way], term_send.at[way])

        @pl.when(crossing)
        def _():
            sent(far.at[:, 1, :, direct], kv_send.at[way])
            sent(far.at[:, 1, :, passing], pass_send.at[0])
            sent(term_out.at[0 : GROUPS - 2, way, :, direct], half_send.at[way])
            sent(term_out.at[0 : GROUPS - 2, way, :, passing], pass_send.at[1])
            sent(term_out.at[GROUPS - 2 :, way], term_send.at[way])

        @pl.when(lat == routes[way][1])
        def _():
            sent(relay.at[0], relay_send.at[0])
            sent(relay.at[1, 0 : GROUPS - 2], relay_send.at[1])


def split_kernel(stacked, *refs):
    outs, sem = refs[:4], refs[4]
    copies = [pltpu.make_async_copy(stacked.at[i], outs[i], sem.at[i]) for i in range(4)]
    for copy in copies:
        copy.start()
    for copy in copies:
        copy.wait()


def solution(mesh):
    lon_count = mesh.shape["lon"]
    lat_count = mesh.shape["lat"]

    def on_device(queries, key_states, value_states, out_grad, block_lists, row_widths):
        images, rows, columns, channels = queries.shape
        tokens = rows * columns
        flat = (images, tokens, channels)
        items = images * channels // HDIM
        lanes = channels // GROUPS
        bf16, f32 = jnp.bfloat16, jnp.float32
        hbm_spec = pl.BlockSpec(memory_space=pltpu.HBM)
        vmem_spec = pl.BlockSpec(memory_space=pltpu.VMEM)
        dma = pltpu.SemaphoreType.DMA
        stacked = pl.pallas_call(
            functools.partial(kernel, lon_count, lat_count),
            out_shape=pltpu.VMEM((4,) + flat, bf16),
            in_specs=[hbm_spec] * 6,
            out_specs=vmem_spec,
            scratch_shapes=[
                pltpu.VMEM((GROUPS, 2, images, tokens, lanes), bf16),
                pltpu.VMEM((GROUPS, 2, 2, images, 2 * HALO, lanes), bf16),
                pltpu.VMEM((GROUPS, 3, 2, images, tokens, lanes), bf16),
                pltpu.VMEM((GROUPS, 2, 2, images, 2 * HALO, lanes), bf16),
                pltpu.VMEM((3 * tokens, 2 * tokens), f32),
                pltpu.VMEM((items, 3 * tokens, 2 * tokens), f32),
                pltpu.VMEM((items, 3 * tokens, 2 * tokens), f32),
                pltpu.VMEM((GROUPS, 3, 8, 2 * tokens), f32),
                pltpu.VMEM((2, GROUPS, 8, 2 * tokens), f32),
                pltpu.VMEM((2, GROUPS, 8, 2 * tokens), f32),
                pltpu.VMEM((GROUPS, 2, 8, 2 * tokens), f32),
                pltpu.VMEM((GROUPS, 2 * tokens, 8), f32),
                pltpu.VMEM((items, tokens + 4 * HALO, HDIM), f32),
                pltpu.VMEM((GROUPS, 2, images, tokens, lanes), f32),
                pltpu.VMEM((GROUPS, 2, 2, images, 2 * HALO, lanes), bf16),
                pltpu.VMEM((GROUPS, 2, 2, images, 2 * HALO, lanes), bf16),
                pltpu.VMEM((GROUPS, 2, images, tokens, lanes), f32),
                pltpu.VMEM((GROUPS, 2, 2, images, tokens, lanes), bf16),
                pltpu.VMEM((GROUPS, 2, 2, images, tokens, lanes), bf16),
                pltpu.VMEM((2, GROUPS, 2, images - images // 2, tokens, lanes), bf16),
                pltpu.VMEM((2, DETOURS, 2, 2, images, 2 * HALO, lanes), bf16),
                pltpu.SMEM(block_lists.shape[::-1], jnp.int32),
                pltpu.SMEM(row_widths.shape, jnp.int32),
                dma((2,)),
                dma((GROUPS, 4)),
                dma((2,)),
                dma((GROUPS, 2)),
                dma((2,)),
                dma((GROUPS, 2)),
                dma((2,)),
                dma((GROUPS, 2)),
                dma((2,)),
                dma((GROUPS, 2)),
                dma((2,)),
                dma((2,)),
                dma((GROUPS, 2)),
                dma((2,)),
                dma((GROUPS, 2)),
                dma((2,)),
                dma((2, DETOURS, 2)),
                dma((2, DETOURS, 2)),
                pltpu.SemaphoreType.REGULAR,
            ],
            compiler_params=pltpu.CompilerParams(
                collective_id=0, has_side_effects=True, vmem_limit_bytes=60 * 1024 * 1024
            ),
            cost_estimate=pl.CostEstimate(
                flops=12 * items * 192 * 128 * 128,
                bytes_accessed=8 * images * tokens * channels * 2,
                transcendentals=items * 192 * 128,
            ),
        )(
            block_lists.T,
            row_widths,
            queries.reshape(flat),
            key_states.reshape(flat),
            value_states.reshape(flat),
            out_grad.reshape(flat),
        )
        results = pl.pallas_call(
            split_kernel,
            out_shape=[jax.ShapeDtypeStruct(flat, bf16)] * 4,
            in_specs=[pl.BlockSpec(memory_space=pl.ANY)],
            out_specs=[hbm_spec] * 4,
            scratch_shapes=[dma((4,))],
            compiler_params=pltpu.CompilerParams(vmem_limit_bytes=8 * 1024 * 1024),
        )(stacked)
        return tuple(x.reshape(queries.shape) for x in results)

    split = P(None, "lat", "lon", None)
    return jax.shard_map(
        on_device,
        mesh=mesh,
        in_specs=(split, split, split, split, P(), P()),
        out_specs=(split, split, split, split),
        check_vma=False,
    )
```

```python
import functools
import math

import jax
import jax.numpy as jnp
from jax import lax
from jax.experimental import pallas as pl
from jax.experimental.pallas import tpu as pltpu
from jax.sharding import PartitionSpec as P

MESH = pl.DeviceIdType.MESH
HALO = 8
HDIM = 128
GROUPS = 8
AHEAD = 5
BEHIND = 5
DETOURS = 2
HIDDEN = -1e30
FLOOR = -1e29


def nt(a, b):
    return lax.dot_general(a, b, (((1,), (1,)), ((), ())), preferred_element_type=jnp.float32)


def nn(a, b):
    return jnp.dot(a, b, preferred_element_type=jnp.float32)


def window(x, old, new, size, rest):
    lane = lax.broadcasted_iota(jnp.int32, x.shape, 1)
    shifted = x if old == new else pltpu.roll(x, (new - old) % HDIM, 1)
    return jnp.where((lane >= new) & (lane < new + size), shifted, rest)


def kernel(
    lon_count,
    lat_count,
    lists_hbm,
    widths_hbm,
    q_hbm,
    k_hbm,
    v_hbm,
    g_hbm,
    outs,
    near,
    edge_in,
    far,
    edge_out,
    bias,
    exps,
    dps,
    stats,
    stats_out,
    stats_in,
    factors,
    columns,
    mixed,
    near_acc,
    part_out,
    part_in,
    far_acc,
    term_out,
    term_in,
    relay,
    detour,
    lists_ref,
    widths_ref,
    small_sem,
    own_sem,
    kv_send,
    kv_recv,
    edge_send,
    edge_recv,
    stat_send,
    stat_recv,
    part_send,
    part_recv,
    term_send,
    half_send,
    term_recv,
    pass_send,
    pass_recv,
    relay_send,
    detour_send,
    detour_recv,
    ready,
):
    lon = lax.axis_index("lon")
    lat = lax.axis_index("lat")
    left = lax.rem(lon + lon_count - 1, lon_count)
    right = lax.rem(lon + 1, lon_count)
    has_above = lat > 0
    has_below = lat < lat_count - 1
    middle = lat_count // 2
    beside = lon + 1 - 2 * lax.rem(lon, 2)
    is_middle = (lat == middle - 1) | (lat == middle)
    routes = ((middle, 0, middle - 1), (middle - 1, lat_count - 1, middle))
    planes = middle // 2
    plane = lax.rem(lat // 2, planes)
    is_hot = (plane == 0) | (plane == planes - 1)
    is_detour = (plane == 1) | (plane == planes - 2)
    inward = jnp.where(plane < planes // 2, 2, -2)
    images, tokens, channels = q_hbm.shape
    heads = channels // HDIM
    group_heads = heads // GROUPS
    group_items = images * group_heads
    group_lanes = group_heads * HDIM
    scale = HDIM ** -0.5
    half = images // 2
    whole, direct, passing = slice(0, images), slice(0, half), slice(half, images)

    sides = ({"lon": left}, {"lon": right})
    tiles = ({"lat": lat - 1}, {"lat": lat + 1})
    exists = (has_above, has_below)

    barrier = pltpu.get_barrier_semaphore()
    for side in sides:
        pl.semaphore_signal(barrier, inc=1, device_id=side, device_id_type=MESH)
    below_middle = lat == middle
    teller = lat == middle - 2
    greets = (has_above, has_below & (lat != middle - 1))
    for there, tile in zip(greets, tiles):
        @pl.when(there)
        def _():
            pl.semaphore_signal(barrier, inc=1, device_id=tile, device_id_type=MESH)
    for here, place in ((below_middle, {"lat": middle - 2}), (lat == 0, {"lat": middle - 2, "lon": beside})):
        @pl.when(here)
        def _():
            pl.semaphore_signal(barrier, inc=1, device_id=place, device_id_type=MESH)
    for route in routes:
        @pl.when(lat == route[1])
        def _():
            pl.semaphore_signal(barrier, inc=1, device_id={"lat": route[0], "lon": beside}, device_id_type=MESH)
    @pl.when(is_detour)
    def _():
        for side in (left, right):
            pl.semaphore_signal(
                barrier, inc=1, device_id={"lat": lat - inward, "lon": side}, device_id_type=MESH
            )

    def lanes(group):
        start = group * group_lanes
        return pl.ds(start if isinstance(group, int) else pl.multiple_of(start, HDIM), group_lanes)

    def own_copies(group):
        targets = (far.at[group, 1, 0], far.at[group, 1, 1], near.at[group, 0], near.at[group, 1])
        return [
            pltpu.make_async_copy(source.at[:, :, lanes(group)], target, own_sem.at[group, which])
            for which, (source, target) in enumerate(zip((k_hbm, v_hbm, q_hbm, g_hbm), targets))
        ]

    def fetch(group, carry):
        for copy in own_copies(group):
            copy.start()
        return carry

    fetch(0, 0)
    small_copies = [
        pltpu.make_async_copy(lists_hbm, lists_ref, small_sem.at[0]),
        pltpu.make_async_copy(widths_hbm, widths_ref, small_sem.at[1]),
    ]
    for copy in small_copies:
        copy.start()

    lax.fori_loop(1, GROUPS, fetch, 0)

    pl.semaphore_wait(
        barrier,
        2 + jnp.where(has_above & (lat != middle), 1, 0) + jnp.where(has_below, 1, 0) + jnp.where(is_middle, 1, 0)
        + jnp.where(is_hot, 2, 0)
        + jnp.where(teller, 2, 0),
    )

    @pl.when(teller)
    def _():
        pl.semaphore_signal(ready, inc=1, device_id={"lat": middle}, device_id_type=MESH)
        pl.semaphore_signal(ready, inc=1, device_id={"lat": 0, "lon": beside}, device_id_type=MESH)


    def remote(source, target, send, recv, device):
        return pltpu.make_async_remote_copy(
            src_ref=source, dst_ref=target, send_sem=send, recv_sem=recv, device_id=device, device_id_type=MESH
        )

    def kv_copy(group, way, some):
        return remote(
            far.at[group, 1, :, some],
            far.at[group, 2 - 2 * way, :, some],
            kv_send.at[way],
            kv_recv.at[group, 1 - way],
            tiles[way],
        )

    def edge_copy(group, way):
        return remote(
            edge_out.at[group, way],
            edge_in.at[group, 1 - way],
            edge_send.at[way],
            edge_recv.at[group, 1 - way],
            sides[way],
        )

    def stat_copy(group, way):
        return remote(
            stats_out.at[way, group, 0:group_items],
            stats_in.at[1 - way, group, 0:group_items],
            stat_send.at[way],
            stat_recv.at[group, 1 - way],
            sides[way],
        )

    def part_copy(group, way):
        return remote(
            part_out.at[group, way],
            part_in.at[group, 1 - way],
            part_send.at[way],
            part_recv.at[group, 1 - way],
            sides[way],
        )

    def term_copy(group, way, some):
        return remote(
            term_out.at[group, way, :, some],
            term_in.at[group, 1 - way, :, some],
            (term_send if some is whole else half_send).at[way],
            term_recv.at[group, 1 - way],
            tiles[way],
        )

    def pass_copy(group, way, kind):
        return remote(
            far.at[group, 1, :, passing] if kind == 0 else term_out.at[group, way, :, passing],
            relay.at[kind, group],
            pass_send.at[kind],
            pass_recv.at[group, kind],
            {"lat": routes[way][1], "lon": beside},
        )

    def relay_copy(group, way, kind):
        return remote(
            relay.at[kind, group],
            far.at[group, 2 - 2 * way, :, passing]
            if kind == 0
            else term_in.at[group, 1 - way, :, passing],
            relay_send.at[kind],
            (kv_recv if kind == 0 else term_recv).at[group, 1 - way],
            {"lat": routes[way][2], "lon": beside},
        )

    def detour_in(group, way, kind):
        which = group // 2 - 1
        return remote(
            (edge_out, part_out)[kind].at[group, way],
            detour.at[kind, which, 1 - way],
            (edge_send, part_send)[kind].at[way],
            detour_recv.at[kind, which, 1 - way],
            {"lat": lat + inward, "lon": (left, right)[way]},
        )

    def detour_out(group, origin, kind):
        which = group // 2 - 1
        return remote(
            detour.at[kind, which, origin],
            (edge_in, part_in)[kind].at[group, origin],
            detour_send.at[kind, which, origin],
            (edge_recv, part_recv)[kind].at[group, origin],
            {"lat": lat - inward},
        )

    def to_sides(group, kind):
        aside = is_hot & ((group == 2) | (group == 4))
        for way in range(2):
            @pl.when(jnp.logical_not(aside))
            def _():
                (edge_copy, part_copy)[kind](group, way).start()

            @pl.when(aside)
            def _():
                detour_in(group, way, kind).start()

    def pass_aside(group, kind):
        for origin in range(2):
            detour_in(group, 1 - origin, kind).wait_recv()
            detour_out(group, origin, kind).start()

    relayed_terms = (GROUPS - 2, GROUPS - 1)

    def relayed(group, kind, way):
        return True if kind == 0 else group < relayed_terms[way]

    def to_tiles(group, kind, act):
        copy = (kv_copy, term_copy)[kind]
        for way in range(2):
            crossing = (lat == routes[way][0]) & relayed(group, kind, way)

            @pl.when(exists[way] & jnp.logical_not(crossing))
            def _():
                act(copy(group, way, whole))

            @pl.when(crossing)
            def _():
                if kind == 1 or way == 1:
                    act(copy(group, way, direct))
                act(pass_copy(group, way, kind))

    def from_tiles(group, kind):
        copy = (kv_copy, term_copy)[kind]
        for origin in range(2):
            @pl.when(exists[origin])
            def _():
                copy(group, 1 - origin, whole).wait_recv()

    def forward(group, kind):
        for way in range(2):
            @pl.when((lat == routes[way][1]) & relayed(group, kind, way))
            def _():
                pass_copy(group, way, kind).wait_recv()
                relay_copy(group, way, kind).start()

    def start(copy):
        copy.start()

    def send_edges(group):
        for which in range(2):
            for image in range(images):
                def half(start, low):
                    block = near[group, which, image, start : start + 16].astype(jnp.float32)
                    return block[low : low + HALO]

                edge_out[group, 0, which, image] = jnp.concatenate(
                    [half(0, 0), half(32, 0)], axis=0
                ).astype(jnp.bfloat16)
                edge_out[group, 1, which, image] = jnp.concatenate(
                    [half(16, HALO), half(48, HALO)], axis=0
                ).astype(jnp.bfloat16)
        to_sides(group, 0)

    def send_group(group, carry):
        copies = own_copies(group)
        copies[0].wait()
        copies[1].wait()
        to_tiles(group, 0, start)
        copies[2].wait()
        copies[3].wait()

        @pl.when(group < AHEAD)
        def _():
            send_edges(group)

        return carry

    lax.fori_loop(0, GROUPS, send_group, 0)

    def send_above(group, carry):
        kv_copy(group, 0, direct).start()
        return carry

    for way in range(2):
        @pl.when(jnp.logical_not(exists[way]))
        def _():
            far[:, 2 * way] = jnp.zeros((GROUPS, 2, images, tokens, group_lanes), jnp.bfloat16)
            term_in[:, way] = jnp.zeros((GROUPS, 2, images, tokens, group_lanes), jnp.bfloat16)

    def listed(target):
        found = (
            (lists_ref[0, lat] == target)
            | (lists_ref[1, lat] == target)
            | (lists_ref[2, lat] == target)
        ) & (target >= 0)
        return jnp.where(found, 1, 0)

    def mask(shape, key_axis):
        key = lax.broadcasted_iota(jnp.int32, shape, key_axis)
        query = lax.broadcasted_iota(jnp.int32, shape, 1 - key_axis)
        key_tile = key >> 6
        key_col = key & 31
        edge = query - tokens
        is_own = query < tokens
        from_left = edge < 2 * HALO
        query_col = jnp.where(
            is_own, query & 31, jnp.where(from_left, (edge & 7) - HALO, 32 + (edge & 7))
        )
        query_row = jnp.where(is_own, query >> 5, (edge >> 3) & 1)
        width = jnp.where(query_row == 0, widths_ref[2 * lat], widths_ref[2 * lat + 1])
        active = jnp.where(
            key_tile == 0, listed(lat - 1), jnp.where(key_tile == 1, listed(lat), listed(lat + 1))
        )
        visible = (jnp.abs(query_col - key_col) <= width) & (active == 1) & (edge < 4 * HALO)
        return jnp.where(visible, 0.0, HIDDEN)

    for copy in small_copies:
        copy.wait()
    bias[...] = mask(bias.shape, 0)

    places = [(image, head) for image in range(images) for head in range(group_heads)]

    def from_near(group, which, image, head):
        at = pl.ds(head * HDIM, HDIM)
        edges = [edge_in[group, origin, which, image, :, at] for origin in range(2)]
        rest = jnp.zeros((2 * tokens - seen, HDIM), jnp.bfloat16)
        return jnp.concatenate([near[group, which, image, :, at]] + edges + [rest], axis=0)

    def from_far(group, which, image, head):
        at = pl.ds(head * HDIM, HDIM)
        return jnp.concatenate([far[group, slot, which, image, :, at] for slot in range(3)], axis=0)

    to_log2 = scale * math.log2(math.e)
    seen = tokens + 4 * HALO

    def scores(group):
        tops, sums, balances = [], [], []
        for item, (image, head) in enumerate(places):
            values = from_far(group, 1, image, head)
            raw = nt(from_far(group, 0, image, head), from_near(group, 0, image, head))
            raw = raw * to_log2 + bias[...]
            dp = nt(values, from_near(group, 1, image, head))
            top = jnp.maximum(jnp.max(raw, axis=0, keepdims=True), FLOOR)
            e = jnp.exp2(raw - top)
            slot = group * group_items + item
            exps[slot] = e
            dps[slot] = dp
            mixed[slot] = nn(jnp.transpose(e.astype(jnp.bfloat16))[0:seen], values)
            tops.append(top)
            sums.append(jnp.sum(e, axis=0, keepdims=True))
            balances.append(jnp.sum(e * dp, axis=0, keepdims=True))
        for kind, found in enumerate((tops, sums, balances)):
            rows = found + [jnp.zeros_like(found[0])] * (8 - len(found))
            stats[group, kind] = jnp.concatenate(rows, axis=0)
        for way, moves in enumerate((((0, 0, 8), (32, 8, 8), (64, 16, 16)), ((24, 0, 8), (56, 8, 8), (80, 16, 16)))):
            packed = jnp.zeros((8, HDIM), jnp.float32)
            for kind in range(3):
                for old, new, size in moves:
                    packed = window(stats[group, kind], old, 32 * kind + new, size, packed)
            stats_out[way, group] = packed
        for way in range(2):
            stat_copy(group, way).start()

    def wait_stats(group):
        for way in range(2):
            stat_copy(group, way).wait_recv()

    def combine(group):
        others = []
        for kind in range(3):
            other = jnp.full((8, HDIM), FLOOR if kind == 0 else 0.0, jnp.float32)
            for origin, moves in enumerate((((0, 64, 16), (16, 0, 8), (24, 32, 8)), ((0, 80, 16), (16, 24, 8), (24, 56, 8)))):
                for old, new, size in moves:
                    other = window(stats_in[origin, group], 32 * kind + old, new, size, other)
            others.append(other)
        top, total, balance = (stats[group, kind] for kind in range(3))
        top2, total2, balance2 = others
        high = jnp.maximum(top, top2)
        part = jnp.exp2(top - high)
        part2 = jnp.exp2(top2 - high)
        inverse = 1.0 / jnp.maximum(part * total + part2 * total2, 0.5)
        factor = part * inverse
        factors[group, 0] = factor
        factors[group, 1] = (part * balance + part2 * balance2) * inverse
        columns[group] = jnp.transpose(factor)

    def gradients(group):
        for item, (image, head) in enumerate(places):
            at = pl.ds(head * HDIM, HDIM)
            slot = group * group_items + item
            keys = from_far(group, 0, image, head)
            queries, grads = (from_near(group, which, image, head) for which in range(2))
            w = exps[slot] * factors[group, 0, item : item + 1, :]
            ds = w * (dps[slot] - factors[group, 1, item : item + 1, :])
            w = w.astype(jnp.bfloat16)
            ds = ds.astype(jnp.bfloat16)
            dk = nn(ds, queries) * scale
            dv = nn(w, grads)
            att = mixed[slot] * columns[group, 0:seen, item : item + 1]
            dq = nn(jnp.transpose(ds)[0:seen], keys) * scale
            for which, x in enumerate((dk, dv)):
                far_acc[group, which, image, :, at] = x[tokens : 2 * tokens]
                term_out[group, 0, which, image, :, at] = x[0:tokens].astype(jnp.bfloat16)
                term_out[group, 1, which, image, :, at] = x[2 * tokens :].astype(jnp.bfloat16)
            for which, x in enumerate((att, dq)):
                near_acc[group, which, image, :, at] = x[0:tokens]
                for way in range(2):
                    low = tokens + 2 * HALO * way
                    part_out[group, way, which, image, :, at] = x[low : low + 2 * HALO].astype(jnp.bfloat16)
        to_tiles(group, 1, start)
        to_sides(group, 1)

    def finish(group):
        for way in range(2):
            part_copy(group, way).wait_recv()
        from_tiles(group, 1)
        at = lanes(group)
        for image in range(images):
            for which in range(2):
                acc = near_acc[group, which, image]
                add_l = part_in[group, 0, which, image].astype(jnp.float32)
                add_r = part_in[group, 1, which, image].astype(jnp.float32)
                rows = []
                for r in range(2):
                    here = acc[32 * r : 32 * r + 32]
                    rows.append(here[0:8] + add_l[8 * r : 8 * r + 8])
                    rows.append(here[8:24])
                    rows.append(here[24:32] + add_r[8 * r : 8 * r + 8])
                outs[which, image, :, at] = jnp.concatenate(rows, axis=0).astype(jnp.bfloat16)
            for which in range(2):
                total = far_acc[group, which, image]
                for way in range(2):
                    total = total + term_in[group, way, which, image].astype(jnp.float32)
                outs[2 + which, image, :, at] = total.astype(jnp.bfloat16)

    def step(index, carry):
        @pl.when(index < GROUPS // 2)
        def _():
            forward(2 * index, 0)
            forward(2 * index + 1, 0)

        for group in (2, 4):
            @pl.when(is_detour & (index == group + 1))
            def _():
                pass_aside(group, 0)

        @pl.when(index < GROUPS)
        def _():
            from_tiles(index, 0)
            for origin in range(2):
                edge_copy(index, 1 - origin).wait_recv()

            scores(index)

            @pl.when(index + AHEAD < GROUPS)
            def _():
                send_edges(index + AHEAD)

        @pl.when((index >= BEHIND + 2) & (index < GROUPS + BEHIND))
        def _():
            forward(index - BEHIND - 2, 1)

        @pl.when(index >= BEHIND)
        def _():
            wait_stats(index - BEHIND)
            combine(index - BEHIND)
            gradients(index - BEHIND)

        return carry

    @pl.when(below_middle | (lat == 0))
    def _():
        pl.semaphore_wait(ready, 1)

    @pl.when(below_middle)
    def _():
        lax.fori_loop(0, GROUPS, send_above, 0)

    lax.fori_loop(0, GROUPS + BEHIND, step, 0)

    @pl.when(is_detour)
    def _():
        for group in (2, 4):
            pass_aside(group, 1)

    forward(GROUPS - 2, 1)

    def last(group, carry):
        finish(group)
        return carry

    lax.fori_loop(0, GROUPS, last, 0)

    def sent(source, sem):
        remote(source, source, sem, sem, sides[0]).wait_send()

    @pl.when(is_detour)
    def _():
        for kind in range(2):
            for group in (2, 4):
                for origin in range(2):
                    detour_out(group, origin, kind).wait_send()

    for way in range(2):
        for source, sem in (
            (edge_out.at[:, way], edge_send.at[way]),
            (part_out.at[:, way], part_send.at[way]),
            (stats_out.at[way, :, 0:group_items], stat_send.at[way]),
        ):
            sent(source, sem)
        crossing = lat == routes[way][0]

        @pl.when(exists[way] & jnp.logical_not(crossing))
        def _():
            sent(far.at[:, 1], kv_send.at[way])
            sent(term_out.at[:, way], term_send.at[way])

        @pl.when(crossing)
        def _():
            sent(far.at[:, 1, :, direct], kv_send.at[way])
            sent(far.at[:, 1, :, passing], pass_send.at[0])
            count = relayed_terms[way]
            sent(term_out.at[0:count, way, :, direct], half_send.at[way])
            sent(term_out.at[0:count, way, :, passing], pass_send.at[1])
            sent(term_out.at[count:, way], term_send.at[way])

        @pl.when(lat == routes[way][1])
        def _():
            sent(relay.at[0], relay_send.at[0])
            sent(relay.at[1, 0 : relayed_terms[way]], relay_send.at[1])


def split_kernel(stacked, *refs):
    outs, sem = refs[:4], refs[4]
    copies = [pltpu.make_async_copy(stacked.at[i], outs[i], sem.at[i]) for i in range(4)]
    for copy in copies:
        copy.start()
    for copy in copies:
        copy.wait()


def solution(mesh):
    lon_count = mesh.shape["lon"]
    lat_count = mesh.shape["lat"]

    def on_device(queries, key_states, value_states, out_grad, block_lists, row_widths):
        images, rows, columns, channels = queries.shape
        tokens = rows * columns
        flat = (images, tokens, channels)
        items = images * channels // HDIM
        lanes = channels // GROUPS
        bf16, f32 = jnp.bfloat16, jnp.float32
        hbm_spec = pl.BlockSpec(memory_space=pltpu.HBM)
        vmem_spec = pl.BlockSpec(memory_space=pltpu.VMEM)
        dma = pltpu.SemaphoreType.DMA
        stacked = pl.pallas_call(
            functools.partial(kernel, lon_count, lat_count),
            out_shape=pltpu.VMEM((4,) + flat, bf16),
            in_specs=[hbm_spec] * 6,
            out_specs=vmem_spec,
            scratch_shapes=[
                pltpu.VMEM((GROUPS, 2, images, tokens, lanes), bf16),
                pltpu.VMEM((GROUPS, 2, 2, images, 2 * HALO, lanes), bf16),
                pltpu.VMEM((GROUPS, 3, 2, images, tokens, lanes), bf16),
                pltpu.VMEM((GROUPS, 2, 2, images, 2 * HALO, lanes), bf16),
                pltpu.VMEM((3 * tokens, 2 * tokens), f32),
                pltpu.VMEM((items, 3 * tokens, 2 * tokens), f32),
                pltpu.VMEM((items, 3 * tokens, 2 * tokens), f32),
                pltpu.VMEM((GROUPS, 3, 8, 2 * tokens), f32),
                pltpu.VMEM((2, GROUPS, 8, 2 * tokens), f32),
                pltpu.VMEM((2, GROUPS, 8, 2 * tokens), f32),
                pltpu.VMEM((GROUPS, 2, 8, 2 * tokens), f32),
                pltpu.VMEM((GROUPS, 2 * tokens, 8), f32),
                pltpu.VMEM((items, tokens + 4 * HALO, HDIM), f32),
                pltpu.VMEM((GROUPS, 2, images, tokens, lanes), f32),
                pltpu.VMEM((GROUPS, 2, 2, images, 2 * HALO, lanes), bf16),
                pltpu.VMEM((GROUPS, 2, 2, images, 2 * HALO, lanes), bf16),
                pltpu.VMEM((GROUPS, 2, images, tokens, lanes), f32),
                pltpu.VMEM((GROUPS, 2, 2, images, tokens, lanes), bf16),
                pltpu.VMEM((GROUPS, 2, 2, images, tokens, lanes), bf16),
                pltpu.VMEM((2, GROUPS, 2, images - images // 2, tokens, lanes), bf16),
                pltpu.VMEM((2, DETOURS, 2, 2, images, 2 * HALO, lanes), bf16),
                pltpu.SMEM(block_lists.shape[::-1], jnp.int32),
                pltpu.SMEM(row_widths.shape, jnp.int32),
                dma((2,)),
                dma((GROUPS, 4)),
                dma((2,)),
                dma((GROUPS, 2)),
                dma((2,)),
                dma((GROUPS, 2)),
                dma((2,)),
                dma((GROUPS, 2)),
                dma((2,)),
                dma((GROUPS, 2)),
                dma((2,)),
                dma((2,)),
                dma((GROUPS, 2)),
                dma((2,)),
                dma((GROUPS, 2)),
                dma((2,)),
                dma((2, DETOURS, 2)),
                dma((2, DETOURS, 2)),
                pltpu.SemaphoreType.REGULAR,
            ],
            compiler_params=pltpu.CompilerParams(
                collective_id=0, has_side_effects=True, vmem_limit_bytes=60 * 1024 * 1024
            ),
            cost_estimate=pl.CostEstimate(
                flops=12 * items * 192 * 128 * 128,
                bytes_accessed=8 * images * tokens * channels * 2,
                transcendentals=items * 192 * 128,
            ),
        )(
            block_lists.T,
            row_widths,
            queries.reshape(flat),
            key_states.reshape(flat),
            value_states.reshape(flat),
            out_grad.reshape(flat),
        )
        results = pl.pallas_call(
            split_kernel,
            out_shape=[jax.ShapeDtypeStruct(flat, bf16)] * 4,
            in_specs=[pl.BlockSpec(memory_space=pl.ANY)],
            out_specs=[hbm_spec] * 4,
            scratch_shapes=[dma((4,))],
            compiler_params=pltpu.CompilerParams(vmem_limit_bytes=8 * 1024 * 1024),
        )(stacked)
        return tuple(x.reshape(queries.shape) for x in results)

    split = P(None, "lat", "lon", None)
    return jax.shard_map(
        on_device,
        mesh=mesh,
        in_specs=(split, split, split, split, P(), P()),
        out_specs=(split, split, split, split),
        check_vma=False,
    )
```

```python
import functools
import math

import jax
import jax.numpy as jnp
from jax import lax
from jax.experimental import pallas as pl
from jax.experimental.pallas import tpu as pltpu
from jax.sharding import PartitionSpec as P

MESH = pl.DeviceIdType.MESH
HALO = 8
HDIM = 128
GROUPS = 8
AHEAD = 6
BEHIND = 5
DETOURS = 2
HIDDEN = -1e30
FLOOR = -1e29


def nt(a, b):
    return lax.dot_general(a, b, (((1,), (1,)), ((), ())), preferred_element_type=jnp.float32)


def nn(a, b):
    return jnp.dot(a, b, preferred_element_type=jnp.float32)


def window(x, old, new, size, rest):
    lane = lax.broadcasted_iota(jnp.int32, x.shape, 1)
    shifted = x if old == new else pltpu.roll(x, (new - old) % HDIM, 1)
    return jnp.where((lane >= new) & (lane < new + size), shifted, rest)


def kernel(
    lon_count,
    lat_count,
    lists_hbm,
    widths_hbm,
    q_hbm,
    k_hbm,
    v_hbm,
    g_hbm,
    outs,
    near,
    edge_in,
    far,
    edge_out,
    bias,
    exps,
    dps,
    stats,
    stats_out,
    stats_in,
    factors,
    columns,
    mixed,
    near_acc,
    part_out,
    part_in,
    far_acc,
    term_out,
    term_in,
    relay,
    detour,
    lists_ref,
    widths_ref,
    small_sem,
    own_sem,
    kv_send,
    kv_recv,
    edge_send,
    edge_recv,
    stat_send,
    stat_recv,
    part_send,
    part_recv,
    term_send,
    half_send,
    term_recv,
    pass_send,
    pass_recv,
    relay_send,
    detour_send,
    detour_recv,
    ready,
):
    lon = lax.axis_index("lon")
    lat = lax.axis_index("lat")
    left = lax.rem(lon + lon_count - 1, lon_count)
    right = lax.rem(lon + 1, lon_count)
    has_above = lat > 0
    has_below = lat < lat_count - 1
    middle = lat_count // 2
    beside = lon + 1 - 2 * lax.rem(lon, 2)
    is_middle = (lat == middle - 1) | (lat == middle)
    routes = ((middle, 0, middle - 1), (middle - 1, lat_count - 1, middle))
    planes = middle // 2
    plane = lax.rem(lat // 2, planes)
    is_hot = (plane == 0) | (plane == planes - 1)
    is_detour = (plane == 1) | (plane == planes - 2)
    inward = jnp.where(plane < planes // 2, 2, -2)
    images, tokens, channels = q_hbm.shape
    heads = channels // HDIM
    group_heads = heads // GROUPS
    group_items = images * group_heads
    group_lanes = group_heads * HDIM
    scale = HDIM ** -0.5
    half = images // 2
    whole, direct, passing = slice(0, images), slice(0, half), slice(half, images)

    sides = ({"lon": left}, {"lon": right})
    tiles = ({"lat": lat - 1}, {"lat": lat + 1})
    exists = (has_above, has_below)

    barrier = pltpu.get_barrier_semaphore()
    for side in sides:
        pl.semaphore_signal(barrier, inc=1, device_id=side, device_id_type=MESH)
    below_middle = lat == middle
    teller = lat == middle - 2
    greets = (has_above, has_below & (lat != middle - 1))
    for there, tile in zip(greets, tiles):
        @pl.when(there)
        def _():
            pl.semaphore_signal(barrier, inc=1, device_id=tile, device_id_type=MESH)
    for here, place in ((below_middle, {"lat": middle - 2}), (lat == 0, {"lat": middle - 2, "lon": beside})):
        @pl.when(here)
        def _():
            pl.semaphore_signal(barrier, inc=1, device_id=place, device_id_type=MESH)
    for route in routes:
        @pl.when(lat == route[1])
        def _():
            pl.semaphore_signal(barrier, inc=1, device_id={"lat": route[0], "lon": beside}, device_id_type=MESH)
    @pl.when(is_detour)
    def _():
        for side in (left, right):
            pl.semaphore_signal(
                barrier, inc=1, device_id={"lat": lat - inward, "lon": side}, device_id_type=MESH
            )

    def lanes(group):
        start = group * group_lanes
        return pl.ds(start if isinstance(group, int) else pl.multiple_of(start, HDIM), group_lanes)

    def own_copies(group):
        targets = (far.at[group, 1, 0], far.at[group, 1, 1], near.at[group, 0], near.at[group, 1])
        return [
            pltpu.make_async_copy(source.at[:, :, lanes(group)], target, own_sem.at[group, which])
            for which, (source, target) in enumerate(zip((k_hbm, v_hbm, q_hbm, g_hbm), targets))
        ]

    def fetch(group, carry):
        for copy in own_copies(group):
            copy.start()
        return carry

    fetch(0, 0)
    small_copies = [
        pltpu.make_async_copy(lists_hbm, lists_ref, small_sem.at[0]),
        pltpu.make_async_copy(widths_hbm, widths_ref, small_sem.at[1]),
    ]
    for copy in small_copies:
        copy.start()

    lax.fori_loop(1, GROUPS, fetch, 0)

    pl.semaphore_wait(
        barrier,
        2 + jnp.where(has_above & (lat != middle), 1, 0) + jnp.where(has_below, 1, 0) + jnp.where(is_middle, 1, 0)
        + jnp.where(is_hot, 2, 0)
        + jnp.where(teller, 2, 0),
    )

    @pl.when(teller)
    def _():
        pl.semaphore_signal(ready, inc=1, device_id={"lat": middle}, device_id_type=MESH)
        pl.semaphore_signal(ready, inc=1, device_id={"lat": 0, "lon": beside}, device_id_type=MESH)


    def remote(source, target, send, recv, device):
        return pltpu.make_async_remote_copy(
            src_ref=source, dst_ref=target, send_sem=send, recv_sem=recv, device_id=device, device_id_type=MESH
        )

    def kv_copy(group, way, some):
        return remote(
            far.at[group, 1, :, some],
            far.at[group, 2 - 2 * way, :, some],
            kv_send.at[way],
            kv_recv.at[group, 1 - way],
            tiles[way],
        )

    def edge_copy(group, way):
        return remote(
            edge_out.at[group, way],
            edge_in.at[group, 1 - way],
            edge_send.at[way],
            edge_recv.at[group, 1 - way],
            sides[way],
        )

    def stat_copy(group, way):
        return remote(
            stats_out.at[way, group, 0:group_items],
            stats_in.at[1 - way, group, 0:group_items],
            stat_send.at[way],
            stat_recv.at[group, 1 - way],
            sides[way],
        )

    def part_copy(group, way):
        return remote(
            part_out.at[group, way],
            part_in.at[group, 1 - way],
            part_send.at[way],
            part_recv.at[group, 1 - way],
            sides[way],
        )

    def term_copy(group, way, some):
        return remote(
            term_out.at[group, way, :, some],
            term_in.at[group, 1 - way, :, some],
            (term_send if some is whole else half_send).at[way],
            term_recv.at[group, 1 - way],
            tiles[way],
        )

    def pass_copy(group, way, kind):
        return remote(
            far.at[group, 1, :, passing] if kind == 0 else term_out.at[group, way, :, passing],
            relay.at[kind, group],
            pass_send.at[kind],
            pass_recv.at[group, kind],
            {"lat": routes[way][1], "lon": beside},
        )

    def relay_copy(group, way, kind):
        return remote(
            relay.at[kind, group],
            far.at[group, 2 - 2 * way, :, passing]
            if kind == 0
            else term_in.at[group, 1 - way, :, passing],
            relay_send.at[kind],
            (kv_recv if kind == 0 else term_recv).at[group, 1 - way],
            {"lat": routes[way][2], "lon": beside},
        )

    def detour_in(group, way, kind):
        which = group // 2 - 1
        return remote(
            (edge_out, part_out)[kind].at[group, way],
            detour.at[kind, which, 1 - way],
            (edge_send, part_send)[kind].at[way],
            detour_recv.at[kind, which, 1 - way],
            {"lat": lat + inward, "lon": (left, right)[way]},
        )

    def detour_out(group, origin, kind):
        which = group // 2 - 1
        return remote(
            detour.at[kind, which, origin],
            (edge_in, part_in)[kind].at[group, origin],
            detour_send.at[kind, which, origin],
            (edge_recv, part_recv)[kind].at[group, origin],
            {"lat": lat - inward},
        )

    def to_sides(group, kind):
        aside = is_hot & ((group == 2) | (group == 4))
        for way in range(2):
            @pl.when(jnp.logical_not(aside))
            def _():
                (edge_copy, part_copy)[kind](group, way).start()

            @pl.when(aside)
            def _():
                detour_in(group, way, kind).start()

    def pass_aside(group, kind):
        for origin in range(2):
            detour_in(group, 1 - origin, kind).wait_recv()
            detour_out(group, origin, kind).start()

    def relayed(group, kind):
        return True if kind == 0 else group < GROUPS - 2

    def to_tiles(group, kind, act):
        copy = (kv_copy, term_copy)[kind]
        for way in range(2):
            crossing = (lat == routes[way][0]) & relayed(group, kind)

            @pl.when(exists[way] & jnp.logical_not(crossing))
            def _():
                act(copy(group, way, whole))

            @pl.when(crossing)
            def _():
                if kind == 1 or way == 1:
                    act(copy(group, way, direct))
                act(pass_copy(group, way, kind))

    def from_tiles(group, kind):
        copy = (kv_copy, term_copy)[kind]
        for origin in range(2):
            @pl.when(exists[origin])
            def _():
                copy(group, 1 - origin, whole).wait_recv()

    def forward(group, kind):
        for way in range(2):
            @pl.when((lat == routes[way][1]) & relayed(group, kind))
            def _():
                pass_copy(group, way, kind).wait_recv()
                relay_copy(group, way, kind).start()

    def start(copy):
        copy.start()

    def send_edges(group):
        for which in range(2):
            for image in range(images):
                def half(start, low):
                    block = near[group, which, image, start : start + 16].astype(jnp.float32)
                    return block[low : low + HALO]

                edge_out[group, 0, which, image] = jnp.concatenate(
                    [half(0, 0), half(32, 0)], axis=0
                ).astype(jnp.bfloat16)
                edge_out[group, 1, which, image] = jnp.concatenate(
                    [half(16, HALO), half(48, HALO)], axis=0
                ).astype(jnp.bfloat16)
        to_sides(group, 0)

    def send_group(group, carry):
        copies = own_copies(group)
        copies[0].wait()
        copies[1].wait()
        to_tiles(group, 0, start)
        copies[2].wait()
        copies[3].wait()

        @pl.when(group < AHEAD)
        def _():
            send_edges(group)

        return carry

    lax.fori_loop(0, GROUPS, send_group, 0)

    def send_above(group, carry):
        kv_copy(group, 0, direct).start()
        return carry

    for way in range(2):
        @pl.when(jnp.logical_not(exists[way]))
        def _():
            far[:, 2 * way] = jnp.zeros((GROUPS, 2, images, tokens, group_lanes), jnp.bfloat16)
            term_in[:, way] = jnp.zeros((GROUPS, 2, images, tokens, group_lanes), jnp.bfloat16)

    def listed(target):
        found = (
            (lists_ref[0, lat] == target)
            | (lists_ref[1, lat] == target)
            | (lists_ref[2, lat] == target)
        ) & (target >= 0)
        return jnp.where(found, 1, 0)

    def mask(shape, key_axis):
        key = lax.broadcasted_iota(jnp.int32, shape, key_axis)
        query = lax.broadcasted_iota(jnp.int32, shape, 1 - key_axis)
        key_tile = key >> 6
        key_col = key & 31
        edge = query - tokens
        is_own = query < tokens
        from_left = edge < 2 * HALO
        query_col = jnp.where(
            is_own, query & 31, jnp.where(from_left, (edge & 7) - HALO, 32 + (edge & 7))
        )
        query_row = jnp.where(is_own, query >> 5, (edge >> 3) & 1)
        width = jnp.where(query_row == 0, widths_ref[2 * lat], widths_ref[2 * lat + 1])
        active = jnp.where(
            key_tile == 0, listed(lat - 1), jnp.where(key_tile == 1, listed(lat), listed(lat + 1))
        )
        visible = (jnp.abs(query_col - key_col) <= width) & (active == 1) & (edge < 4 * HALO)
        return jnp.where(visible, 0.0, HIDDEN)

    for copy in small_copies:
        copy.wait()
    bias[...] = mask(bias.shape, 0)

    places = [(image, head) for image in range(images) for head in range(group_heads)]

    def from_near(group, which, image, head):
        at = pl.ds(head * HDIM, HDIM)
        edges = [edge_in[group, origin, which, image, :, at] for origin in range(2)]
        rest = jnp.zeros((2 * tokens - seen, HDIM), jnp.bfloat16)
        return jnp.concatenate([near[group, which, image, :, at]] + edges + [rest], axis=0)

    def from_far(group, which, image, head):
        at = pl.ds(head * HDIM, HDIM)
        return jnp.concatenate([far[group, slot, which, image, :, at] for slot in range(3)], axis=0)

    to_log2 = scale * math.log2(math.e)
    seen = tokens + 4 * HALO

    def scores(group):
        tops, sums, balances = [], [], []
        for item, (image, head) in enumerate(places):
            values = from_far(group, 1, image, head)
            raw = nt(from_far(group, 0, image, head), from_near(group, 0, image, head))
            raw = raw * to_log2 + bias[...]
            dp = nt(values, from_near(group, 1, image, head))
            top = jnp.maximum(jnp.max(raw, axis=0, keepdims=True), FLOOR)
            e = jnp.exp2(raw - top)
            slot = group * group_items + item
            exps[slot] = e
            dps[slot] = dp
            mixed[slot] = nn(jnp.transpose(e.astype(jnp.bfloat16))[0:seen], values)
            tops.append(top)
            sums.append(jnp.sum(e, axis=0, keepdims=True))
            balances.append(jnp.sum(e * dp, axis=0, keepdims=True))
        for kind, found in enumerate((tops, sums, balances)):
            rows = found + [jnp.zeros_like(found[0])] * (8 - len(found))
            stats[group, kind] = jnp.concatenate(rows, axis=0)
        for way, moves in enumerate((((0, 0, 8), (32, 8, 8), (64, 16, 16)), ((24, 0, 8), (56, 8, 8), (80, 16, 16)))):
            packed = jnp.zeros((8, HDIM), jnp.float32)
            for kind in range(3):
                for old, new, size in moves:
                    packed = window(stats[group, kind], old, 32 * kind + new, size, packed)
            stats_out[way, group] = packed
        for way in range(2):
            stat_copy(group, way).start()

    def wait_stats(group):
        for way in range(2):
            stat_copy(group, way).wait_recv()

    def combine(group):
        others = []
        for kind in range(3):
            other = jnp.full((8, HDIM), FLOOR if kind == 0 else 0.0, jnp.float32)
            for origin, moves in enumerate((((0, 64, 16), (16, 0, 8), (24, 32, 8)), ((0, 80, 16), (16, 24, 8), (24, 56, 8)))):
                for old, new, size in moves:
                    other = window(stats_in[origin, group], 32 * kind + old, new, size, other)
            others.append(other)
        top, total, balance = (stats[group, kind] for kind in range(3))
        top2, total2, balance2 = others
        high = jnp.maximum(top, top2)
        part = jnp.exp2(top - high)
        part2 = jnp.exp2(top2 - high)
        inverse = 1.0 / jnp.maximum(part * total + part2 * total2, 0.5)
        factor = part * inverse
        factors[group, 0] = factor
        factors[group, 1] = (part * balance + part2 * balance2) * inverse
        columns[group] = jnp.transpose(factor)

    def gradients(group):
        for item, (image, head) in enumerate(places):
            at = pl.ds(head * HDIM, HDIM)
            slot = group * group_items + item
            keys = from_far(group, 0, image, head)
            queries, grads = (from_near(group, which, image, head) for which in range(2))
            w = exps[slot] * factors[group, 0, item : item + 1, :]
            ds = w * (dps[slot] - factors[group, 1, item : item + 1, :])
            w = w.astype(jnp.bfloat16)
            ds = ds.astype(jnp.bfloat16)
            dk = nn(ds, queries) * scale
            dv = nn(w, grads)
            att = mixed[slot] * columns[group, 0:seen, item : item + 1]
            dq = nn(jnp.transpose(ds)[0:seen], keys) * scale
            for which, x in enumerate((dk, dv)):
                far_acc[group, which, image, :, at] = x[tokens : 2 * tokens]
                term_out[group, 0, which, image, :, at] = x[0:tokens].astype(jnp.bfloat16)
                term_out[group, 1, which, image, :, at] = x[2 * tokens :].astype(jnp.bfloat16)
            for which, x in enumerate((att, dq)):
                near_acc[group, which, image, :, at] = x[0:tokens]
                for way in range(2):
                    low = tokens + 2 * HALO * way
                    part_out[group, way, which, image, :, at] = x[low : low + 2 * HALO].astype(jnp.bfloat16)
        to_tiles(group, 1, start)
        to_sides(group, 1)

    def finish(group):
        for way in range(2):
            part_copy(group, way).wait_recv()
        from_tiles(group, 1)
        at = lanes(group)
        for image in range(images):
            for which in range(2):
                acc = near_acc[group, which, image]
                add_l = part_in[group, 0, which, image].astype(jnp.float32)
                add_r = part_in[group, 1, which, image].astype(jnp.float32)
                rows = []
                for r in range(2):
                    here = acc[32 * r : 32 * r + 32]
                    rows.append(here[0:8] + add_l[8 * r : 8 * r + 8])
                    rows.append(here[8:24])
                    rows.append(here[24:32] + add_r[8 * r : 8 * r + 8])
                outs[which, image, :, at] = jnp.concatenate(rows, axis=0).astype(jnp.bfloat16)
            for which in range(2):
                total = far_acc[group, which, image]
                for way in range(2):
                    total = total + term_in[group, way, which, image].astype(jnp.float32)
                outs[2 + which, image, :, at] = total.astype(jnp.bfloat16)

    def step(index, carry):
        @pl.when(index < GROUPS // 2)
        def _():
            forward(2 * index, 0)
            forward(2 * index + 1, 0)

        for group in (2, 4):
            @pl.when(is_detour & (index == group + 1))
            def _():
                pass_aside(group, 0)

        @pl.when(index < GROUPS)
        def _():
            from_tiles(index, 0)
            for origin in range(2):
                edge_copy(index, 1 - origin).wait_recv()

            scores(index)

            @pl.when(index + AHEAD < GROUPS)
            def _():
                send_edges(index + AHEAD)

        @pl.when((index >= BEHIND + 2) & (index < GROUPS + BEHIND))
        def _():
            forward(index - BEHIND - 2, 1)

        @pl.when(index >= BEHIND)
        def _():
            wait_stats(index - BEHIND)
            combine(index - BEHIND)
            gradients(index - BEHIND)

        return carry

    @pl.when(below_middle | (lat == 0))
    def _():
        pl.semaphore_wait(ready, 1)

    @pl.when(below_middle)
    def _():
        lax.fori_loop(0, GROUPS, send_above, 0)

    lax.fori_loop(0, GROUPS + BEHIND, step, 0)

    @pl.when(is_detour)
    def _():
        for group in (2, 4):
            pass_aside(group, 1)

    def last(group, carry):
        finish(group)
        return carry

    lax.fori_loop(0, GROUPS, last, 0)

    def sent(source, sem):
        remote(source, source, sem, sem, sides[0]).wait_send()

    @pl.when(is_detour)
    def _():
        for kind in range(2):
            for group in (2, 4):
                for origin in range(2):
                    detour_out(group, origin, kind).wait_send()

    for way in range(2):
        for source, sem in (
            (edge_out.at[:, way], edge_send.at[way]),
            (part_out.at[:, way], part_send.at[way]),
            (stats_out.at[way, :, 0:group_items], stat_send.at[way]),
        ):
            sent(source, sem)
        crossing = lat == routes[way][0]

        @pl.when(exists[way] & jnp.logical_not(crossing))
        def _():
            sent(far.at[:, 1], kv_send.at[way])
            sent(term_out.at[:, way], term_send.at[way])

        @pl.when(crossing)
        def _():
            sent(far.at[:, 1, :, direct], kv_send.at[way])
            sent(far.at[:, 1, :, passing], pass_send.at[0])
            sent(term_out.at[0 : GROUPS - 2, way, :, direct], half_send.at[way])
            sent(term_out.at[0 : GROUPS - 2, way, :, passing], pass_send.at[1])
            sent(term_out.at[GROUPS - 2 :, way], term_send.at[way])

        @pl.when(lat == routes[way][1])
        def _():
            sent(relay.at[0], relay_send.at[0])
            sent(relay.at[1, 0 : GROUPS - 2], relay_send.at[1])


def split_kernel(stacked, *refs):
    outs, sem = refs[:4], refs[4]
    copies = [pltpu.make_async_copy(stacked.at[i], outs[i], sem.at[i]) for i in range(4)]
    for copy in copies:
        copy.start()
    for copy in copies:
        copy.wait()


def solution(mesh):
    lon_count = mesh.shape["lon"]
    lat_count = mesh.shape["lat"]

    def on_device(queries, key_states, value_states, out_grad, block_lists, row_widths):
        images, rows, columns, channels = queries.shape
        tokens = rows * columns
        flat = (images, tokens, channels)
        items = images * channels // HDIM
        lanes = channels // GROUPS
        bf16, f32 = jnp.bfloat16, jnp.float32
        hbm_spec = pl.BlockSpec(memory_space=pltpu.HBM)
        vmem_spec = pl.BlockSpec(memory_space=pltpu.VMEM)
        dma = pltpu.SemaphoreType.DMA
        stacked = pl.pallas_call(
            functools.partial(kernel, lon_count, lat_count),
            out_shape=pltpu.VMEM((4,) + flat, bf16),
            in_specs=[hbm_spec] * 6,
            out_specs=vmem_spec,
            scratch_shapes=[
                pltpu.VMEM((GROUPS, 2, images, tokens, lanes), bf16),
                pltpu.VMEM((GROUPS, 2, 2, images, 2 * HALO, lanes), bf16),
                pltpu.VMEM((GROUPS, 3, 2, images, tokens, lanes), bf16),
                pltpu.VMEM((GROUPS, 2, 2, images, 2 * HALO, lanes), bf16),
                pltpu.VMEM((3 * tokens, 2 * tokens), f32),
                pltpu.VMEM((items, 3 * tokens, 2 * tokens), f32),
                pltpu.VMEM((items, 3 * tokens, 2 * tokens), f32),
                pltpu.VMEM((GROUPS, 3, 8, 2 * tokens), f32),
                pltpu.VMEM((2, GROUPS, 8, 2 * tokens), f32),
                pltpu.VMEM((2, GROUPS, 8, 2 * tokens), f32),
                pltpu.VMEM((GROUPS, 2, 8, 2 * tokens), f32),
                pltpu.VMEM((GROUPS, 2 * tokens, 8), f32),
                pltpu.VMEM((items, tokens + 4 * HALO, HDIM), f32),
                pltpu.VMEM((GROUPS, 2, images, tokens, lanes), f32),
                pltpu.VMEM((GROUPS, 2, 2, images, 2 * HALO, lanes), bf16),
                pltpu.VMEM((GROUPS, 2, 2, images, 2 * HALO, lanes), bf16),
                pltpu.VMEM((GROUPS, 2, images, tokens, lanes), f32),
                pltpu.VMEM((GROUPS, 2, 2, images, tokens, lanes), bf16),
                pltpu.VMEM((GROUPS, 2, 2, images, tokens, lanes), bf16),
                pltpu.VMEM((2, GROUPS, 2, images - images // 2, tokens, lanes), bf16),
                pltpu.VMEM((2, DETOURS, 2, 2, images, 2 * HALO, lanes), bf16),
                pltpu.SMEM(block_lists.shape[::-1], jnp.int32),
                pltpu.SMEM(row_widths.shape, jnp.int32),
                dma((2,)),
                dma((GROUPS, 4)),
                dma((2,)),
                dma((GROUPS, 2)),
                dma((2,)),
                dma((GROUPS, 2)),
                dma((2,)),
                dma((GROUPS, 2)),
                dma((2,)),
                dma((GROUPS, 2)),
                dma((2,)),
                dma((2,)),
                dma((GROUPS, 2)),
                dma((2,)),
                dma((GROUPS, 2)),
                dma((2,)),
                dma((2, DETOURS, 2)),
                dma((2, DETOURS, 2)),
                pltpu.SemaphoreType.REGULAR,
            ],
            compiler_params=pltpu.CompilerParams(
                collective_id=0, has_side_effects=True, vmem_limit_bytes=60 * 1024 * 1024
            ),
            cost_estimate=pl.CostEstimate(
                flops=12 * items * 192 * 128 * 128,
                bytes_accessed=8 * images * tokens * channels * 2,
                transcendentals=items * 192 * 128,
            ),
        )(
            block_lists.T,
            row_widths,
            queries.reshape(flat),
            key_states.reshape(flat),
            value_states.reshape(flat),
            out_grad.reshape(flat),
        )
        results = pl.pallas_call(
            split_kernel,
            out_shape=[jax.ShapeDtypeStruct(flat, bf16)] * 4,
            in_specs=[pl.BlockSpec(memory_space=pl.ANY)],
            out_specs=[hbm_spec] * 4,
            scratch_shapes=[dma((4,))],
            compiler_params=pltpu.CompilerParams(vmem_limit_bytes=8 * 1024 * 1024),
        )(stacked)
        return tuple(x.reshape(queries.shape) for x in results)

    split = P(None, "lat", "lon", None)
    return jax.shard_map(
        on_device,
        mesh=mesh,
        in_specs=(split, split, split, split, P(), P()),
        out_specs=(split, split, split, split),
        check_vma=False,
    )
```
